32 devices in a mesh: dp: 8 (over y, x, core), seq: 4 (over z).
Axes of the slice: x: 2, y: 2, z: 4, core: 2. Of those that a mesh axis runs over, the one named last changes fastest.
Arguments:
- tokens: bfloat16 [4096, 2048], P(('dp', 'seq')), may hold values from -6 to 6
- norm_first: bfloat16 [2048], P(('dp', 'seq')), may hold values from 0.5 to 1.5
- w_query: bfloat16 [2048, 2048], P(('dp', 'seq')), may hold values from -0.125 to 0.125
- w_key: bfloat16 [2048, 256], P(('dp', 'seq')), may hold values from -0.125 to 0.125
- w_value: bfloat16 [2048, 256], P(('dp', 'seq')), may hold values from -0.125 to 0.125
- w_out: bfloat16 [2048, 2048], P(('dp', 'seq')), may hold values from -0.5 to 0.5
- norm_second: bfloat16 [2048], P(('dp', 'seq')), may hold values from 0.5 to 1.5
- w_gate: bfloat16 [2048, 5632], P(('dp', 'seq')), may hold values from -0.125 to 0.125
- w_up: bfloat16 [2048, 5632], P(('dp', 'seq')), may hold values from -0.125 to 0.125
- w_down: bfloat16 [5632, 2048], P(('dp', 'seq')), may hold values from -0.078125 to 0.078125
- cotangent: bfloat16 [4096, 2048], P(('dp', 'seq')), may hold values from -6 to 6
Outputs:
- mixed: bfloat16 [4096, 2048], P(('dp', 'seq'))
- grad_tokens: bfloat16 [4096, 2048], P(('dp', 'seq'))
- grad_norm_first: float32 [2048], P(('dp', 'seq'))
- grad_query: float32 [2048, 2048], P(('dp', 'seq'))
- grad_key: float32 [2048, 256], P(('dp', 'seq'))
- grad_value: float32 [2048, 256], P(('dp', 'seq'))
- grad_out: float32 [2048, 2048], P(('dp', 'seq'))
- grad_norm_second: float32 [2048], P(('dp', 'seq'))
- grad_gate: float32 [2048, 5632], P(('dp', 'seq'))
- grad_up: float32 [2048, 5632], P(('dp', 'seq'))
- grad_down: float32 [5632, 2048], P(('dp', 'seq'))
The draws below stay inside these ranges and needn't reach their ends.
All inputs are finite; a program needn't handle non-finite values.
Results may differ from the reference program's by a relative error of at most 0.015.
Values may be sent and summed in bfloat16 or wider, within the bound.
A program may use at most 448 MiB of HBM per device.

```python
import jax
import jax.numpy as jnp
from jax import lax

D = 2048
H = 32
KEY_VALUE_HEADS = 4
HEAD_SIZE = 64
FF = 5632
TOK_DEV = 128
TOKENS = 4096
N_DP = 8
N_SEQ = 4


def shard_levels(key, shape, cuts, least, top_value):
    factor_of = 1.0
    for dim, parts in cuts:
        heights = jax.random.uniform(jax.random.fold_in(jax.random.fold_in(key, 6), dim), (parts,), jnp.float32, least / len(cuts), top_value / len(cuts))
        factor_of = factor_of * jnp.repeat(jnp.exp(heights), shape[dim] // parts).reshape((-1,) + (1,) * (len(shape) - 1 - dim))
    return factor_of


def noise(rng, shape, scale, reach, cuts=(), kind=jnp.bfloat16):
    level = shard_levels(rng, shape, cuts, -0.22, 0.18) if cuts else 1.0
    values = jax.random.normal(rng, shape, jnp.float32) * scale * level
    return jnp.minimum(jnp.maximum(values, -reach), reach).astype(kind)


def setup_inputs(seed: int = 0) -> dict:
    seeds = jax.random.split(jax.random.key(seed), 12)
    tokens = noise(seeds[0], (TOKENS, D), 1.0, 6.0, ((0, 32),))
    norm_first = jnp.clip(1.0 + 0.1 * jax.random.normal(seeds[1], (D,), jnp.float32), 0.5, 1.5).astype(jnp.bfloat16)
    w_query = noise(seeds[2], (D, H * HEAD_SIZE), D ** -0.5, 0.125, ((0, 32),))
    w_key = noise(seeds[3], (D, KEY_VALUE_HEADS * HEAD_SIZE), D ** -0.5, 0.125, ((0, 32),))
    w_value = noise(seeds[4], (D, KEY_VALUE_HEADS * HEAD_SIZE), D ** -0.5, 0.125, ((0, 32),))
    w_out = noise(seeds[5], (H * HEAD_SIZE, D), (H * HEAD_SIZE // 16) ** -0.5, 0.5, ((0, 32),))
    norm_second = jnp.clip(1.0 + 0.1 * jax.random.normal(seeds[6], (D,), jnp.float32), 0.5, 1.5).astype(jnp.bfloat16)
    w_gate = noise(seeds[7], (D, FF), D ** -0.5, 0.125, ((0, 32),))
    w_up = noise(seeds[8], (D, FF), D ** -0.5, 0.125, ((0, 32),))
    w_down = noise(seeds[9], (FF, D), FF ** -0.5, 0.078125, ((0, 32),))
    cotangent = noise(seeds[10], (TOKENS, D), 1.0, 6.0, ((0, 32),))
    return {"tokens": tokens, "norm_first": norm_first, "w_query": w_query, "w_key": w_key, "w_value": w_value, "w_out": w_out, "norm_second": norm_second, "w_gate": w_gate, "w_up": w_up, "w_down": w_down, "cotangent": cotangent}


EPS = 1e-05
HIGH = lax.Precision.HIGHEST

@jax.custom_vjp
def low(v):
    return lax.optimization_barrier(v.astype(jnp.bfloat16)).astype(jnp.float32)

@jax.custom_vjp
def low_back(v):
    return v

def low_keep(v):
    return (low(v), None)

def low_pass(kept, grad):
    return (grad,)

def back_keep(v):
    return (v, None)

def back_low(kept, grad):
    return (low(grad),)
low.defvjp(low_keep, low_pass)
low_back.defvjp(back_keep, back_low)

def matmul(left, right):
    return jnp.dot(left, right, precision=HIGH)

def rms_norm(value, gain):
    return value * lax.rsqrt(lax.optimization_barrier(jnp.mean(value * value, axis=-1, keepdims=True)) + EPS) * gain

def tables(length):
    positions = jnp.arange(length, dtype=jnp.float32)
    freq = 10000.0 ** (-jnp.arange(0, HEAD_SIZE // 2, dtype=jnp.float32) * 2.0 / HEAD_SIZE)
    angle = positions[:, None] * freq[None, :]
    return (jnp.cos(angle)[:, None, :], jnp.sin(angle)[:, None, :])

def rotate(heads, cosine, sine):
    half = heads.shape[-1] // 2
    first = heads[..., :half]
    second = heads[..., half:]
    return jnp.concatenate([first * cosine - second * sine, second * cosine + first * sine], axis=-1)

def group_attention(queries, keys, values):
    length = keys.shape[0]
    block = min(512, length)
    total_count = length // block
    per = queries.shape[1]
    scale = HEAD_SIZE ** (-0.5)
    qblocks = queries.reshape(total_count, block, per, HEAD_SIZE)
    key_pos = jnp.arange(length)

    def one(args):
        index, qblk = args
        scores = jnp.einsum('qhd,kd->hqk', qblk, keys, precision=HIGH) * scale
        scores = low_back(scores)
        rows = index * block + jnp.arange(block)
        scores = jnp.where(key_pos[None, None, :] <= rows[None, :, None], scores, -1e+30)
        probs = jax.nn.softmax(scores, axis=-1)
        return jnp.einsum('hqk,kd->qhd', low(probs), values, precision=HIGH)
    outs = lax.map(jax.checkpoint(one), (jnp.arange(total_count), qblocks))
    return outs.reshape(length, per * HEAD_SIZE)

def layer(x, gain1, wq, wk, value_weight, wo, gain2, wg, wu, wd):
    length = x.shape[0]
    normalized_input = low(rms_norm(x, gain1))
    cosine, sine = tables(length)
    queries = rotate(low_back(matmul(normalized_input, wq)).reshape(length, H, HEAD_SIZE), cosine, sine)
    keys = rotate(low_back(matmul(normalized_input, wk)).reshape(length, KEY_VALUE_HEADS, HEAD_SIZE), cosine, sine)
    values = low_back(matmul(normalized_input, value_weight)).reshape(length, KEY_VALUE_HEADS, HEAD_SIZE)
    queries = low_back(low(queries))
    head_repeat = N_SEQ // KEY_VALUE_HEADS
    per = H // N_SEQ
    outs = []
    for group in range(N_SEQ):
        head = group // head_repeat
        key_group = low_back(low(keys[:, head]))
        value_group = low_back(low(values[:, head]))
        outs.append(group_attention(queries[:, group * per:(group + 1) * per], key_group, value_group))
    attn = low_back(low(jnp.concatenate(outs, axis=1)))
    hmid = x + low_back(matmul(attn, wo))
    normed2 = low(rms_norm(hmid, gain2))
    gate = low_back(matmul(normed2, wg))
    upper = low_back(matmul(normed2, wu))
    hidden = low(jax.nn.silu(gate) * upper)
    return hmid + low_back(matmul(hidden, wd))

def reference(tokens, norm_first, w_query, w_key, w_value, w_out, norm_second, w_gate, w_up, w_down, cotangent):
    length = TOK_DEV * N_SEQ
    params = tuple((w.astype(jnp.float32) for w in (norm_first, w_query, w_key, w_value, w_out, norm_second, w_gate, w_up, w_down)))
    inputs = tokens.astype(jnp.float32).reshape(N_DP, length, D)

    def forward(values, *weights):
        return lax.map(jax.checkpoint(lambda item: layer(item, *weights)), values)
    result, pull = jax.vjp(forward, inputs, *params)
    grads = pull(cotangent.astype(jnp.float32).reshape(N_DP, length, D))
    total = N_DP * length
    return (result.reshape(total, D).astype(jnp.bfloat16), grads[0].reshape(total, D).astype(jnp.bfloat16), grads[1], grads[2], grads[3], grads[4], grads[5], grads[6], grads[7], grads[8], grads[9])
```

```python
import jax
import jax.numpy as jnp
from jax import lax
from jax.sharding import PartitionSpec as P

H = 32
KEY_VALUE_HEADS = 4
HEAD_SIZE = 64
EPS = 1e-05
BF = jnp.bfloat16
F32 = jnp.float32


def tables(positions):
    freq = 10000.0 ** (-jnp.arange(0, HEAD_SIZE // 2, dtype=F32) * 2.0 / HEAD_SIZE)
    angle = positions.astype(F32)[:, None] * freq[None, :]
    return (jnp.cos(angle)[:, None, :], jnp.sin(angle)[:, None, :])


def rotate(heads, cosine, sine):
    half = heads.shape[-1] // 2
    first = heads[..., :half]
    second = heads[..., half:]
    return jnp.concatenate(
        [first * cosine - second * sine, second * cosine + first * sine], axis=-1
    )


def dot(left, right):
    return jnp.dot(left, right, preferred_element_type=F32)


def left_dot(left, right):
    return lax.dot_general(left, right, (((0,), (0,)), ((), ())), preferred_element_type=F32)


def right_dot(left, right):
    return lax.dot_general(left, right, (((1,), (1,)), ((), ())), preferred_element_type=F32)


def bits_of(count):
    return [1 << k for k in range(count.bit_length() - 1)]


class Axis:
    def __init__(self, name):
        self.name = name
        self.size = lax.axis_size(name)
        self.me = lax.axis_index(name)

    def swap(self, value, mask):
        return lax.ppermute(value, self.name, [(i, i ^ mask) for i in range(self.size)])

    def all(self, value):
        return [value if m == 0 else self.swap(value, m) for m in range(self.size)]

    def exchange(self, stacked):
        return [
            lax.dynamic_index_in_dim(stacked, self.me ^ m, 0, keepdims=False)
            if m == 0
            else self.swap(
                lax.dynamic_index_in_dim(stacked, self.me ^ m, 0, keepdims=False), m
            )
            for m in range(self.size)
        ]

    def natural(self, pieces):
        stack = jnp.stack(pieces)
        return [
            lax.dynamic_index_in_dim(stack, self.me ^ i, 0, keepdims=False)
            for i in range(self.size)
        ]


def orders(size):
    even = [m for m in range(size) if m % 2 == 0]
    return even, [m + 1 for m in even]


def chip_bits(size, turn):
    bits = bits_of(size)[1:]
    return bits if turn == 0 else bits[::-1]


def gather_chips(dp, piece, turn):
    pieces = {0: piece}
    for bit in chip_bits(dp.size, turn):
        pieces.update({m ^ bit: dp.swap(p, bit) for m, p in list(pieces.items())})
    return pieces


def gather_rows(dp, piece, turn):
    pieces = gather_chips(dp, piece, turn)
    even = jnp.concatenate([pieces[m] for m in orders(dp.size)[0]], axis=0)
    return even, dp.swap(even, 1)


def scatter_chips(dp, blocks, turn):
    for bit in chip_bits(dp.size, turn):
        for m in [m for m in blocks if m & bit]:
            other = dp.swap(blocks.pop(m).astype(BF), bit)
            blocks[m ^ bit] = blocks[m ^ bit].astype(F32) + other.astype(F32)
    return blocks[0]


def scatter_rows(dp, even_fn, odd, turn):
    rows = odd.shape[0] * 2 // dp.size
    other = dp.swap(odd, 1)
    even = (even_fn() + other.astype(F32)).astype(BF)
    blocks = {
        m: even[i * rows : (i + 1) * rows] for i, m in enumerate(orders(dp.size)[0])
    }
    return scatter_chips(dp, blocks, turn)


def mask_columns(dp, value):
    width = value.shape[1] // dp.size
    return tuple(
        jnp.concatenate(
            [lax.dynamic_slice_in_dim(value, (dp.me ^ m) * width, width, 1) for m in group],
            axis=1,
        )
        for group in orders(dp.size)
    )


def natural_columns(dp, even, odd):
    both = jnp.concatenate([even, odd], axis=1)
    width = both.shape[1] // dp.size
    half = dp.size // 2
    parts = []
    for i in range(dp.size):
        mask = dp.me ^ i
        place = mask // 2 + (mask % 2) * half
        parts.append(lax.dynamic_slice_in_dim(both, place * width, width, 1))
    return jnp.concatenate(parts, axis=1)


def attend(queries, keys, values, visible):
    scores = jnp.einsum("qhd,kd->hqk", queries, keys, preferred_element_type=F32)
    scores = jnp.where(visible[None], scores * HEAD_SIZE ** (-0.5), -1e30)
    top = jnp.max(scores, axis=-1, keepdims=True)
    expo = jnp.exp(scores - top)
    total = jnp.sum(expo, axis=-1, keepdims=True)
    probs = (expo / total).astype(BF)
    result = jnp.einsum("hqk,kd->qhd", probs, values, preferred_element_type=F32)
    return result.astype(BF), top + jnp.log(total)


def attend_back(queries, keys, values, grad_heads, logsum, visible):
    scale = HEAD_SIZE ** (-0.5)
    scores = jnp.einsum("qhd,kd->hqk", queries, keys, preferred_element_type=F32)
    scores = jnp.where(visible[None], scores * scale, -1e30)
    probs = jnp.exp(scores - logsum)
    pgrad = jnp.einsum("qhd,kd->hqk", grad_heads, values, preferred_element_type=F32)
    delta = jnp.sum(probs * pgrad, axis=-1, keepdims=True)
    sgrad = (probs * (pgrad - delta)).astype(BF)
    qgrad = jnp.einsum("hqk,kd->qhd", sgrad, keys, preferred_element_type=F32) * scale
    kgrad = jnp.einsum("hqk,qhd->kd", sgrad, queries, preferred_element_type=F32) * scale
    vgrad = jnp.einsum("hqk,qhd->kd", probs.astype(BF), grad_heads, preferred_element_type=F32)
    return qgrad.astype(BF), kgrad.astype(BF), vgrad.astype(BF)


def shards(
    tokens, norm_first, w_query, w_key, w_value, w_out, norm_second, w_gate, w_up, w_down, cotangent
):
    dp, seq = Axis("dp"), Axis("seq")
    groups = seq.size
    count, width = tokens.shape
    ff = w_gate.shape[1]
    per = H // groups
    repeat = groups // KEY_VALUE_HEADS
    heads_wide = H * HEAD_SIZE
    keys_wide = KEY_VALUE_HEADS * HEAD_SIZE
    gain1 = norm_first.astype(F32)[:, None]
    gain2 = norm_second.astype(F32)[:, None]

    w_first = jnp.concatenate([w_query, w_key, w_value], axis=1)
    w_first_scaled = (w_first.astype(F32) * gain1).astype(BF)
    wide = w_first.shape[1]

    def by_part(weight):
        rows = weight.shape[0]
        scaled = (weight.astype(F32) * gain2).astype(BF)
        parts = scaled.reshape(rows, dp.size, groups, ff // dp.size // groups)
        return parts.transpose(2, 0, 1, 3).reshape(groups, rows, ff // groups)

    down = [gather_chips(dp, w_down[:, t * width // 2 : (t + 1) * width // 2], t) for t in (0, 1)]
    first_rows = jnp.concatenate(seq.natural(seq.all(w_first_scaled)), axis=0)
    first = [gather_rows(dp, first_rows[:, t * wide // 2 : (t + 1) * wide // 2], t) for t in (0, 1)]
    out_rows = jnp.concatenate(seq.natural(seq.all(w_out)), axis=0)
    outw = [gather_rows(dp, out_rows[:, t * width // 2 : (t + 1) * width // 2], t) for t in (0, 1)]
    gate_up = seq.exchange(jnp.stack([by_part(w_gate), by_part(w_up)], axis=1))
    gate_up = jnp.concatenate(seq.natural(gate_up), axis=1)
    (gate_even, gate_odd), (up_even, up_odd) = [
        gather_rows(dp, gate_up[t], t) for t in (0, 1)
    ]
    cot_all = jnp.concatenate(seq.all(cotangent), axis=0)

    rows_down = w_down.shape[0]
    down_full = []
    for t in (0, 1):
        even = jnp.stack([down[t][m] for m in orders(dp.size)[0]])
        odd = dp.swap(even, 1)
        full = jnp.zeros((rows_down * dp.size, width // 2), BF)
        for i, m in enumerate(orders(dp.size)[0]):
            full = lax.dynamic_update_slice(full, even[i], ((dp.me ^ m) * rows_down, 0))
            full = lax.dynamic_update_slice(full, odd[i], ((dp.me ^ m ^ 1) * rows_down, 0))
        down_full.append(full)

    inputs = tokens.astype(F32)
    inv1 = lax.rsqrt(jnp.mean(inputs * inputs, axis=-1, keepdims=True) + EPS)
    hat1 = (inputs * inv1).astype(BF)
    hat1_even, hat1_odd = mask_columns(dp, hat1)
    cosine, sine = tables(seq.me * count + jnp.arange(count))
    pre = jnp.concatenate(
        [dot(hat1_even, first[t][0]) + dot(hat1_odd, first[t][1]) for t in (0, 1)], axis=1
    )
    qpre = pre[:, :heads_wide].reshape(count, H, HEAD_SIZE)
    kpre = pre[:, heads_wide : heads_wide + keys_wide].reshape(count, KEY_VALUE_HEADS, HEAD_SIZE)
    vround = pre[:, heads_wide + keys_wide :].astype(BF)
    qrot = rotate(qpre, cosine, sine).reshape(count, heads_wide).astype(BF)
    krot = rotate(kpre, cosine, sine).reshape(count, keys_wide).astype(BF)
    span = per * HEAD_SIZE
    packed = []
    for g in range(groups):
        head = g // repeat * HEAD_SIZE
        packed.append(
            jnp.concatenate(
                [
                    qrot[:, g * span : (g + 1) * span],
                    krot[:, head : head + HEAD_SIZE],
                    vround[:, head : head + HEAD_SIZE],
                ],
                axis=1,
            )
        )
    qkv = jnp.concatenate(seq.exchange(jnp.stack(packed)), axis=0)
    length = qkv.shape[0]
    queries = qkv[:, :span].reshape(length, per, HEAD_SIZE)
    keys = qkv[:, span : span + HEAD_SIZE]
    values = qkv[:, span + HEAD_SIZE :]
    place = jnp.concatenate(
        [(seq.me ^ m) * count + jnp.arange(count, dtype=jnp.int32) for m in range(groups)]
    )
    visible = place[None, :] <= place[:, None]
    out_heads, logsum = attend(queries, keys, values, visible)
    out_heads = out_heads.reshape(length, span)

    def back_home(value):
        return seq.natural(
            [
                value[:count] if m == 0 else seq.swap(value[m * count : (m + 1) * count], m)
                for m in range(groups)
            ]
        )

    attn = jnp.concatenate(back_home(out_heads), axis=1)
    attn_even, attn_odd = mask_columns(dp, attn)
    branch = jnp.concatenate(
        [dot(attn_even, outw[t][0]) + dot(attn_odd, outw[t][1]) for t in (0, 1)], axis=1
    )
    hmid = inputs + branch

    inv2 = lax.rsqrt(jnp.mean(hmid * hmid, axis=-1, keepdims=True) + EPS)
    hat2 = jnp.concatenate(mask_columns(dp, (hmid * inv2).astype(BF)), axis=1)
    hat2_all = jnp.concatenate(seq.all(hat2), axis=0)
    hat2_even, hat2_odd = hat2_all[:, : width // 2], hat2_all[:, width // 2 :]
    gate = dot(hat2_even, gate_even) + dot(hat2_odd, gate_odd)
    upper = dot(hat2_even, up_even) + dot(hat2_odd, up_odd)
    sigma = jax.nn.sigmoid(gate)
    hidden = (gate * sigma * upper).astype(BF)
    halves = [cot_all[:, : width // 2], cot_all[:, width // 2 :]]
    dhidden = right_dot(halves[0], down_full[0]) + right_dot(halves[1], down_full[1])
    dgate = (dhidden * upper * sigma * (1.0 + gate * (1.0 - sigma))).astype(BF)
    dupper = (dhidden * gate * sigma).astype(BF)
    dhat2 = jnp.concatenate(
        [
            right_dot(dgate, gate_even) + right_dot(dupper, up_even),
            right_dot(dgate, gate_odd) + right_dot(dupper, up_odd),
        ],
        axis=1,
    ).astype(BF)

    def sum_home(value):
        total = value[:count].astype(F32)
        for m in range(1, groups):
            total = total + seq.swap(value[m * count : (m + 1) * count], m).astype(F32)
        return total

    dhat2 = sum_home(dhat2)
    dgain2 = natural_columns(dp, dhat2[:, : width // 2], dhat2[:, width // 2 :])
    inner = jnp.mean(hmid * dgain2, axis=-1, keepdims=True)
    dh = cotangent.astype(F32) + inv2 * dgain2 - hmid * inv2 * inv2 * inv2 * inner
    dbranch = dh.astype(BF)

    dattn = natural_columns(
        dp,
        *[
            sum(
                right_dot(dbranch[:, t * width // 2 : (t + 1) * width // 2], outw[t][s])
                for t in (0, 1)
            ).astype(BF)
            for s in (0, 1)
        ],
    )
    grad_heads = jnp.concatenate(
        seq.exchange(dattn.reshape(count, groups, span).transpose(1, 0, 2)), axis=0
    ).reshape(length, per, HEAD_SIZE)
    dq, dk, dv = attend_back(queries, keys, values, grad_heads, logsum, visible)
    dqkv = back_home(jnp.concatenate([dq.reshape(length, span), dk, dv], axis=1))
    dq = jnp.concatenate([piece[:, :span] for piece in dqkv], axis=1)
    dk = [piece[:, span : span + HEAD_SIZE].astype(F32) for piece in dqkv]
    dv = [piece[:, span + HEAD_SIZE :].astype(F32) for piece in dqkv]
    dk = jnp.stack(
        [sum(dk[i * repeat : (i + 1) * repeat]) for i in range(KEY_VALUE_HEADS)], axis=1
    )
    dv = jnp.concatenate(
        [sum(dv[i * repeat : (i + 1) * repeat]) for i in range(KEY_VALUE_HEADS)], axis=1
    )
    dq = rotate(dq.astype(F32).reshape(count, H, HEAD_SIZE), cosine, -sine)
    dk = rotate(dk, cosine, -sine)
    dpre = jnp.concatenate(
        [dq.reshape(count, heads_wide), dk.reshape(count, keys_wide), dv], axis=1
    ).astype(BF)
    dhalf = [dpre[:, t * wide // 2 : (t + 1) * wide // 2] for t in (0, 1)]
    dhat1 = [sum(right_dot(dhalf[t], first[t][s]) for t in (0, 1)) for s in (0, 1)]
    dgain1 = natural_columns(dp, *dhat1)
    inner = jnp.mean(inputs * dgain1, axis=-1, keepdims=True)
    grad_inputs = dh + inv1 * dgain1 - inputs * inv1 * inv1 * inv1 * inner

    mixed_part = jnp.concatenate([dot(hidden, down_full[t]) for t in (0, 1)], axis=1).astype(BF)
    mixed = hmid + sum_home(mixed_part)

    grad_down = []
    for t in (0, 1):
        part = left_dot(hidden, halves[t]).astype(BF)
        blocks = [
            lax.dynamic_slice_in_dim(part, (dp.me ^ m) * rows_down, rows_down, 0)
            for m in range(dp.size)
        ]
        even, odd = orders(dp.size)
        other = dp.swap(jnp.stack([blocks[m] for m in odd]), 1)
        summed = {
            m: (blocks[m].astype(F32) + other[i].astype(F32)).astype(BF)
            for i, m in enumerate(even)
        }
        grad_down.append(scatter_chips(dp, summed, t))
    grad_down = jnp.concatenate(grad_down, axis=1)

    def ff_grad(grad, turn):
        odd = left_dot(hat2_odd, grad).astype(BF)
        return scatter_rows(dp, lambda: left_dot(hat2_even, grad), odd, turn)

    rows = w_gate.shape[0]
    sent = jnp.stack([ff_grad(dgate, 0).astype(BF), ff_grad(dupper, 1).astype(BF)])
    sent = sent.reshape(2, groups, rows, ff // groups).transpose(1, 0, 2, 3)
    got = jnp.stack(seq.natural(seq.exchange(sent)))
    got = got.reshape(groups, 2, rows, dp.size, ff // groups // dp.size)
    got = got.transpose(1, 2, 3, 0, 4).reshape(2, rows, ff).astype(F32)
    grad_gate, grad_up = got[0] * gain2, got[1] * gain2
    grad_gain2 = jnp.sum(got[0] * w_gate.astype(F32) + got[1] * w_up.astype(F32), axis=1)

    def proj_grad(even, odd, grads):
        parts = []
        for t in (0, 1):
            send = left_dot(odd, grads[t]).astype(BF)
            parts.append(
                scatter_rows(dp, lambda grad=grads[t]: left_dot(even, grad), send, t)
            )
        own = jnp.concatenate(parts, axis=1)
        own = own.astype(BF).reshape(groups, rows, own.shape[1])
        return sum(piece.astype(F32) for piece in seq.exchange(own))

    grad_out = proj_grad(
        attn_even,
        attn_odd,
        [dbranch[:, t * width // 2 : (t + 1) * width // 2] for t in (0, 1)],
    )
    grad_first = proj_grad(hat1_even, hat1_odd, dhalf)
    grad_gain1 = jnp.sum(grad_first * w_first.astype(F32), axis=1)
    grad_first = grad_first * gain1
    return (
        mixed.astype(BF),
        grad_inputs.astype(BF),
        grad_gain1,
        grad_first[:, :heads_wide],
        grad_first[:, heads_wide : heads_wide + keys_wide],
        grad_first[:, heads_wide + keys_wide :],
        grad_out,
        grad_gain2,
        grad_gate,
        grad_up,
        grad_down,
    )


def solution(mesh):
    rows = P(("dp", "seq"), None)
    line = P(("dp", "seq"))
    return jax.shard_map(
        shards,
        mesh=mesh,
        in_specs=(rows, line, rows, rows, rows, rows, line, rows, rows, rows, rows),
        out_specs=(rows, rows, line, rows, rows, rows, rows, line, rows, rows, rows),
        check_vma=False,
    )
```

```python
import jax
import jax.numpy as jnp
from jax import lax
from jax.experimental import pallas as pl
from jax.experimental.pallas import tpu as pltpu
from jax.sharding import PartitionSpec as P

H = 32
KEY_VALUE_HEADS = 4
HEAD_SIZE = 64
EPS = 1e-05
BF = jnp.bfloat16
F32 = jnp.float32


def tables(positions):
    freq = 10000.0 ** (-jnp.arange(0, HEAD_SIZE // 2, dtype=F32) * 2.0 / HEAD_SIZE)
    angle = positions.astype(F32)[:, None] * freq[None, :]
    return (jnp.cos(angle)[:, None, :], jnp.sin(angle)[:, None, :])


def rotate(heads, cosine, sine):
    half = heads.shape[-1] // 2
    first = heads[..., :half]
    second = heads[..., half:]
    return jnp.concatenate(
        [first * cosine - second * sine, second * cosine + first * sine], axis=-1
    )


def dot(left, right):
    return jnp.dot(left, right, preferred_element_type=F32)


def left_dot(left, right):
    return lax.dot_general(left, right, (((0,), (0,)), ((), ())), preferred_element_type=F32)


def right_dot(left, right):
    return lax.dot_general(left, right, (((1,), (1,)), ((), ())), preferred_element_type=F32)


def bits_of(count):
    return [1 << k for k in range(count.bit_length() - 1)]


class Axis:
    def __init__(self, name):
        self.name = name
        self.size = lax.axis_size(name)
        self.me = lax.axis_index(name)

    def swap(self, value, mask):
        return lax.ppermute(value, self.name, [(i, i ^ mask) for i in range(self.size)])

    def all(self, value):
        return [value if m == 0 else self.swap(value, m) for m in range(self.size)]

    def exchange(self, stacked):
        return [
            lax.dynamic_index_in_dim(stacked, self.me ^ m, 0, keepdims=False)
            if m == 0
            else self.swap(
                lax.dynamic_index_in_dim(stacked, self.me ^ m, 0, keepdims=False), m
            )
            for m in range(self.size)
        ]

    def natural(self, pieces):
        stack = jnp.stack(pieces)
        return [
            lax.dynamic_index_in_dim(stack, self.me ^ i, 0, keepdims=False)
            for i in range(self.size)
        ]


def orders(size):
    even = [m for m in range(size) if m % 2 == 0]
    return even, [m + 1 for m in even]


def chip_bits(size, turn):
    bits = bits_of(size)[1:]
    return bits if turn == 0 else bits[::-1]


def gather_chips(dp, piece, turn):
    pieces = {0: piece}
    for bit in chip_bits(dp.size, turn):
        pieces.update({m ^ bit: dp.swap(p, bit) for m, p in list(pieces.items())})
    return pieces


def gather_rows(dp, piece, turn):
    pieces = gather_chips(dp, piece, turn)
    even = jnp.concatenate([pieces[m] for m in orders(dp.size)[0]], axis=0)
    return even, dp.swap(even, 1)


def scatter_chips(dp, blocks, turn):
    for bit in chip_bits(dp.size, turn):
        for m in [m for m in blocks if m & bit]:
            other = dp.swap(blocks.pop(m).astype(BF), bit)
            blocks[m ^ bit] = blocks[m ^ bit].astype(F32) + other.astype(F32)
    return blocks[0]


def scatter_rows(dp, even_fn, odd, turn):
    rows = odd.shape[0] * 2 // dp.size
    other = dp.swap(odd, 1)
    even = (even_fn() + other.astype(F32)).astype(BF)
    blocks = {
        m: even[i * rows : (i + 1) * rows] for i, m in enumerate(orders(dp.size)[0])
    }
    return scatter_chips(dp, blocks, turn)


def mask_columns(dp, value):
    width = value.shape[1] // dp.size
    return tuple(
        jnp.concatenate(
            [lax.dynamic_slice_in_dim(value, (dp.me ^ m) * width, width, 1) for m in group],
            axis=1,
        )
        for group in orders(dp.size)
    )


def natural_columns(dp, even, odd):
    both = jnp.concatenate([even, odd], axis=1)
    width = both.shape[1] // dp.size
    half = dp.size // 2
    parts = []
    for i in range(dp.size):
        mask = dp.me ^ i
        place = mask // 2 + (mask % 2) * half
        parts.append(lax.dynamic_slice_in_dim(both, place * width, width, 1))
    return jnp.concatenate(parts, axis=1)


def attend(queries, keys, values, visible):
    scores = jnp.einsum("qhd,kd->hqk", queries, keys, preferred_element_type=F32)
    scores = jnp.where(visible[None], scores * HEAD_SIZE ** (-0.5), -1e30)
    top = jnp.max(scores, axis=-1, keepdims=True)
    expo = jnp.exp(scores - top)
    total = jnp.sum(expo, axis=-1, keepdims=True)
    probs = (expo / total).astype(BF)
    result = jnp.einsum("hqk,kd->qhd", probs, values, preferred_element_type=F32)
    return result.astype(BF), top + jnp.log(total)


def attend_back(queries, keys, values, grad_heads, logsum, visible):
    scale = HEAD_SIZE ** (-0.5)
    scores = jnp.einsum("qhd,kd->hqk", queries, keys, preferred_element_type=F32)
    scores = jnp.where(visible[None], scores * scale, -1e30)
    probs = jnp.exp(scores - logsum)
    pgrad = jnp.einsum("qhd,kd->hqk", grad_heads, values, preferred_element_type=F32)
    delta = jnp.sum(probs * pgrad, axis=-1, keepdims=True)
    sgrad = (probs * (pgrad - delta)).astype(BF)
    qgrad = jnp.einsum("hqk,kd->qhd", sgrad, keys, preferred_element_type=F32) * scale
    kgrad = jnp.einsum("hqk,qhd->kd", sgrad, queries, preferred_element_type=F32) * scale
    vgrad = jnp.einsum("hqk,qhd->kd", probs.astype(BF), grad_heads, preferred_element_type=F32)
    return qgrad.astype(BF), kgrad.astype(BF), vgrad.astype(BF)


def general_shards(
    tokens, norm_first, w_query, w_key, w_value, w_out, norm_second, w_gate, w_up, w_down, cotangent
):
    dp, seq = Axis("dp"), Axis("seq")
    groups = seq.size
    count, width = tokens.shape
    ff = w_gate.shape[1]
    per = H // groups
    repeat = groups // KEY_VALUE_HEADS
    heads_wide = H * HEAD_SIZE
    keys_wide = KEY_VALUE_HEADS * HEAD_SIZE
    gain1 = norm_first.astype(F32)[:, None]
    gain2 = norm_second.astype(F32)[:, None]

    w_first = jnp.concatenate([w_query, w_key, w_value], axis=1)
    w_first_scaled = (w_first.astype(F32) * gain1).astype(BF)
    wide = w_first.shape[1]

    def by_part(weight):
        rows = weight.shape[0]
        scaled = (weight.astype(F32) * gain2).astype(BF)
        parts = scaled.reshape(rows, dp.size, groups, ff // dp.size // groups)
        return parts.transpose(2, 0, 1, 3).reshape(groups, rows, ff // groups)

    down = [gather_chips(dp, w_down[:, t * width // 2 : (t + 1) * width // 2], t) for t in (0, 1)]
    first_rows = jnp.concatenate(seq.natural(seq.all(w_first_scaled)), axis=0)
    first = [gather_rows(dp, first_rows[:, t * wide // 2 : (t + 1) * wide // 2], t) for t in (0, 1)]
    out_rows = jnp.concatenate(seq.natural(seq.all(w_out)), axis=0)
    outw = [gather_rows(dp, out_rows[:, t * width // 2 : (t + 1) * width // 2], t) for t in (0, 1)]
    gate_up = seq.exchange(jnp.stack([by_part(w_gate), by_part(w_up)], axis=1))
    gate_up = jnp.concatenate(seq.natural(gate_up), axis=1)
    (gate_even, gate_odd), (up_even, up_odd) = [
        gather_rows(dp, gate_up[t], t) for t in (0, 1)
    ]
    cot_all = jnp.concatenate(seq.all(cotangent), axis=0)

    rows_down = w_down.shape[0]
    down_full = []
    for t in (0, 1):
        even = jnp.stack([down[t][m] for m in orders(dp.size)[0]])
        odd = dp.swap(even, 1)
        full = jnp.zeros((rows_down * dp.size, width // 2), BF)
        for i, m in enumerate(orders(dp.size)[0]):
            full = lax.dynamic_update_slice(full, even[i], ((dp.me ^ m) * rows_down, 0))
            full = lax.dynamic_update_slice(full, odd[i], ((dp.me ^ m ^ 1) * rows_down, 0))
        down_full.append(full)

    inputs = tokens.astype(F32)
    inv1 = lax.rsqrt(jnp.mean(inputs * inputs, axis=-1, keepdims=True) + EPS)
    hat1 = (inputs * inv1).astype(BF)
    hat1_even, hat1_odd = mask_columns(dp, hat1)
    cosine, sine = tables(seq.me * count + jnp.arange(count))
    pre = jnp.concatenate(
        [dot(hat1_even, first[t][0]) + dot(hat1_odd, first[t][1]) for t in (0, 1)], axis=1
    )
    qpre = pre[:, :heads_wide].reshape(count, H, HEAD_SIZE)
    kpre = pre[:, heads_wide : heads_wide + keys_wide].reshape(count, KEY_VALUE_HEADS, HEAD_SIZE)
    vround = pre[:, heads_wide + keys_wide :].astype(BF)
    qrot = rotate(qpre, cosine, sine).reshape(count, heads_wide).astype(BF)
    krot = rotate(kpre, cosine, sine).reshape(count, keys_wide).astype(BF)
    span = per * HEAD_SIZE
    packed = []
    for g in range(groups):
        head = g // repeat * HEAD_SIZE
        packed.append(
            jnp.concatenate(
                [
                    qrot[:, g * span : (g + 1) * span],
                    krot[:, head : head + HEAD_SIZE],
                    vround[:, head : head + HEAD_SIZE],
                ],
                axis=1,
            )
        )
    qkv = jnp.concatenate(seq.exchange(jnp.stack(packed)), axis=0)
    length = qkv.shape[0]
    queries = qkv[:, :span].reshape(length, per, HEAD_SIZE)
    keys = qkv[:, span : span + HEAD_SIZE]
    values = qkv[:, span + HEAD_SIZE :]
    place = jnp.concatenate(
        [(seq.me ^ m) * count + jnp.arange(count, dtype=jnp.int32) for m in range(groups)]
    )
    visible = place[None, :] <= place[:, None]
    out_heads, logsum = attend(queries, keys, values, visible)
    out_heads = out_heads.reshape(length, span)

    def back_home(value):
        return seq.natural(
            [
                value[:count] if m == 0 else seq.swap(value[m * count : (m + 1) * count], m)
                for m in range(groups)
            ]
        )

    attn = jnp.concatenate(back_home(out_heads), axis=1)
    attn_even, attn_odd = mask_columns(dp, attn)
    branch = jnp.concatenate(
        [dot(attn_even, outw[t][0]) + dot(attn_odd, outw[t][1]) for t in (0, 1)], axis=1
    )
    hmid = inputs + branch

    inv2 = lax.rsqrt(jnp.mean(hmid * hmid, axis=-1, keepdims=True) + EPS)
    hat2 = jnp.concatenate(mask_columns(dp, (hmid * inv2).astype(BF)), axis=1)
    hat2_all = jnp.concatenate(seq.all(hat2), axis=0)
    hat2_even, hat2_odd = hat2_all[:, : width // 2], hat2_all[:, width // 2 :]
    gate = dot(hat2_even, gate_even) + dot(hat2_odd, gate_odd)
    upper = dot(hat2_even, up_even) + dot(hat2_odd, up_odd)
    sigma = jax.nn.sigmoid(gate)
    hidden = (gate * sigma * upper).astype(BF)
    halves = [cot_all[:, : width // 2], cot_all[:, width // 2 :]]
    dhidden = right_dot(halves[0], down_full[0]) + right_dot(halves[1], down_full[1])
    dgate = (dhidden * upper * sigma * (1.0 + gate * (1.0 - sigma))).astype(BF)
    dupper = (dhidden * gate * sigma).astype(BF)
    dhat2 = jnp.concatenate(
        [
            right_dot(dgate, gate_even) + right_dot(dupper, up_even),
            right_dot(dgate, gate_odd) + right_dot(dupper, up_odd),
        ],
        axis=1,
    ).astype(BF)

    def sum_home(value):
        total = value[:count].astype(F32)
        for m in range(1, groups):
            total = total + seq.swap(value[m * count : (m + 1) * count], m).astype(F32)
        return total

    dhat2 = sum_home(dhat2)
    dgain2 = natural_columns(dp, dhat2[:, : width // 2], dhat2[:, width // 2 :])
    inner = jnp.mean(hmid * dgain2, axis=-1, keepdims=True)
    dh = cotangent.astype(F32) + inv2 * dgain2 - hmid * inv2 * inv2 * inv2 * inner
    dbranch = dh.astype(BF)

    dattn = natural_columns(
        dp,
        *[
            sum(
                right_dot(dbranch[:, t * width // 2 : (t + 1) * width // 2], outw[t][s])
                for t in (0, 1)
            ).astype(BF)
            for s in (0, 1)
        ],
    )
    grad_heads = jnp.concatenate(
        seq.exchange(dattn.reshape(count, groups, span).transpose(1, 0, 2)), axis=0
    ).reshape(length, per, HEAD_SIZE)
    dq, dk, dv = attend_back(queries, keys, values, grad_heads, logsum, visible)
    dqkv = back_home(jnp.concatenate([dq.reshape(length, span), dk, dv], axis=1))
    dq = jnp.concatenate([piece[:, :span] for piece in dqkv], axis=1)
    dk = [piece[:, span : span + HEAD_SIZE].astype(F32) for piece in dqkv]
    dv = [piece[:, span + HEAD_SIZE :].astype(F32) for piece in dqkv]
    dk = jnp.stack(
        [sum(dk[i * repeat : (i + 1) * repeat]) for i in range(KEY_VALUE_HEADS)], axis=1
    )
    dv = jnp.concatenate(
        [sum(dv[i * repeat : (i + 1) * repeat]) for i in range(KEY_VALUE_HEADS)], axis=1
    )
    dq = rotate(dq.astype(F32).reshape(count, H, HEAD_SIZE), cosine, -sine)
    dk = rotate(dk, cosine, -sine)
    dpre = jnp.concatenate(
        [dq.reshape(count, heads_wide), dk.reshape(count, keys_wide), dv], axis=1
    ).astype(BF)
    dhalf = [dpre[:, t * wide // 2 : (t + 1) * wide // 2] for t in (0, 1)]
    dhat1 = [sum(right_dot(dhalf[t], first[t][s]) for t in (0, 1)) for s in (0, 1)]
    dgain1 = natural_columns(dp, *dhat1)
    inner = jnp.mean(inputs * dgain1, axis=-1, keepdims=True)
    grad_inputs = dh + inv1 * dgain1 - inputs * inv1 * inv1 * inv1 * inner

    mixed_part = jnp.concatenate([dot(hidden, down_full[t]) for t in (0, 1)], axis=1).astype(BF)
    mixed = hmid + sum_home(mixed_part)

    grad_down = []
    for t in (0, 1):
        part = left_dot(hidden, halves[t]).astype(BF)
        blocks = [
            lax.dynamic_slice_in_dim(part, (dp.me ^ m) * rows_down, rows_down, 0)
            for m in range(dp.size)
        ]
        even, odd = orders(dp.size)
        other = dp.swap(jnp.stack([blocks[m] for m in odd]), 1)
        summed = {
            m: (blocks[m].astype(F32) + other[i].astype(F32)).astype(BF)
            for i, m in enumerate(even)
        }
        grad_down.append(scatter_chips(dp, summed, t))
    grad_down = jnp.concatenate(grad_down, axis=1)

    def ff_grad(grad, turn):
        odd = left_dot(hat2_odd, grad).astype(BF)
        return scatter_rows(dp, lambda: left_dot(hat2_even, grad), odd, turn)

    rows = w_gate.shape[0]
    sent = jnp.stack([ff_grad(dgate, 0).astype(BF), ff_grad(dupper, 1).astype(BF)])
    sent = sent.reshape(2, groups, rows, ff // groups).transpose(1, 0, 2, 3)
    got = jnp.stack(seq.natural(seq.exchange(sent)))
    got = got.reshape(groups, 2, rows, dp.size, ff // groups // dp.size)
    got = got.transpose(1, 2, 3, 0, 4).reshape(2, rows, ff).astype(F32)
    grad_gate, grad_up = got[0] * gain2, got[1] * gain2
    grad_gain2 = jnp.sum(got[0] * w_gate.astype(F32) + got[1] * w_up.astype(F32), axis=1)

    def proj_grad(even, odd, grads):
        parts = []
        for t in (0, 1):
            send = left_dot(odd, grads[t]).astype(BF)
            parts.append(
                scatter_rows(dp, lambda grad=grads[t]: left_dot(even, grad), send, t)
            )
        own = jnp.concatenate(parts, axis=1)
        own = own.astype(BF).reshape(groups, rows, own.shape[1])
        return sum(piece.astype(F32) for piece in seq.exchange(own))

    grad_out = proj_grad(
        attn_even,
        attn_odd,
        [dbranch[:, t * width // 2 : (t + 1) * width // 2] for t in (0, 1)],
    )
    grad_first = proj_grad(hat1_even, hat1_odd, dhalf)
    grad_gain1 = jnp.sum(grad_first * w_first.astype(F32), axis=1)
    grad_first = grad_first * gain1
    return (
        mixed.astype(BF),
        grad_inputs.astype(BF),
        grad_gain1,
        grad_first[:, :heads_wide],
        grad_first[:, heads_wide : heads_wide + keys_wide],
        grad_first[:, heads_wide + keys_wide :],
        grad_out,
        grad_gain2,
        grad_gate,
        grad_up,
        grad_down,
    )


MESH = pl.DeviceIdType.MESH
ANY = pl.BlockSpec(memory_space=pl.ANY)
VMEM = pl.BlockSpec(memory_space=pltpu.VMEM)


class Net:
    def __init__(self, send_sems, recv_sems):
        self.send_sems, self.recv_sems, self.used = send_sems, recv_sems, 0
        self.open = []
        dp, z = lax.axis_index("dp"), lax.axis_index("seq")
        self.dp, self.z = dp, z
        self.dps = {
            0: dp,
            1: dp + 1 - 2 * lax.rem(dp, 2),
            2: dp + 2 - 4 * lax.rem(lax.div(dp, 2), 2),
            4: lax.rem(dp + 4, 8),
        }
        self.dps[6] = lax.rem(self.dps[2] + 4, 8)
        self.zs = {0: z, 1: z + 1 - 2 * lax.rem(z, 2), 2: lax.rem(z + 2, 4), 3: 3 - z}

    def target(self, name):
        kind, mask = name
        return (self.dps[mask], self.z) if kind == "d" else (self.dp, self.zs[mask])

    def barrier(self, names):
        sem = pltpu.get_barrier_semaphore()
        for name in names:
            pl.semaphore_signal(sem, inc=1, device_id=self.target(name), device_id_type=MESH)
        pl.semaphore_wait(sem, len(names))

    def send(self, src, dst, name):
        copy = pltpu.make_async_remote_copy(
            src_ref=src,
            dst_ref=dst,
            send_sem=self.send_sems.at[self.used],
            recv_sem=self.recv_sems.at[self.used],
            device_id=self.target(name),
            device_id_type=MESH,
        )
        self.used += 1
        copy.start()
        self.open.append(copy)
        return copy

    def local(self, src, dst):
        copy = pltpu.make_async_copy(src, dst, self.send_sems.at[self.used])
        self.used += 1
        copy.start()
        return copy

    def finish(self):
        for copy in self.open:
            copy.wait_send()


X, Y, CORE = ("d", 2), ("d", 4), ("d", 1)
PARTNERS = [X, Y, CORE, ("z", 1), ("z", 2), ("z", 3)]


class Plane:
    def __init__(self, net, at, both):
        self.net, self.at, self.both = net, at, both

    def push(self, mask, half, name):
        ref = self.at(mask, half)
        return self.net.send(ref, ref, name)

    def start(self):
        self.xa = self.push(0, 0, X)
        self.yb = self.push(0, 1, Y)
        self.ya = self.push(0, 0, Y)
        self.xb = self.push(0, 1, X)
        self.cores = [self.core(0)]

    def core(self, mask):
        return [self.net.send(ref, ref, CORE) for ref in self.both(mask)]

    def forward(self):
        self.xa.wait_recv()
        self.ya2 = self.push(2, 0, Y)
        self.yb.wait_recv()
        self.xb2 = self.push(4, 1, X)

    def spread(self):
        self.ya.wait_recv()
        self.cores.append(self.core(4))
        self.xb.wait_recv()
        self.cores.append(self.core(2))
        self.ya2.wait_recv()
        self.xb2.wait_recv()
        self.cores.append(self.core(6))

    def finish(self):
        for copies in self.cores:
            for copy in copies:
                copy.wait_recv()


def rotary(value, cosine, sine):
    lane = lax.broadcasted_iota(jnp.int32, value.shape, 1)
    partner = jnp.where(
        lax.rem(lane, 64) < 32, pltpu.roll(value, 96, 1), pltpu.roll(value, 32, 1)
    )
    return value * cosine + partner * sine


def rms(value):
    return lax.rsqrt(jnp.mean(value * value, axis=-1, keepdims=True) + EPS)


def twice(pair):
    lane = lax.broadcasted_iota(jnp.int32, pair.shape, 1)
    other = pltpu.roll(pair.astype(F32), 64, 1).astype(BF)
    return jnp.where(lane < 64, pair, other), jnp.where(lane < 64, other, pair)


def first_kernel(
    x_ref, wa1, wa2, wf, wd, cot, cos_q, sin_q, cos_k, sin_k,
    wg_all, wd_all, a1_out, a2_out, c_all, n_all, qkv_out, lse, att_out, hmid, hat1_out,
    a1, a2, qkv_send, qkv, heads, att, hat1, hat2, send_sems, recv_sems,
):
    net = Net(send_sems, recv_sems)
    dp, z, dps, zs = net.dp, net.z, net.dps, net.zs
    first_half = a1.shape[1] // 2
    second_half = a2.shape[1] // 2
    tok = x_ref.shape[0]
    group = qkv.shape[1]
    span = heads.shape[1]

    def rows(ref, start, count, half=None):
        start = pl.multiple_of(start, 16)
        if half is None:
            return ref.at[pl.ds(start, count), :]
        width = ref.shape[1] // 2
        return ref.at[pl.ds(start, count), pl.ds(half * width, width)]

    def line(ref, mask):
        return rows(ref, (dp * 4 + zs[mask]) * 64, 64)

    def block(ref, size):
        return (
            lambda mask, half: rows(ref, dps[mask] * size, size, half),
            lambda mask: [rows(ref, dps[mask] * size, size)],
        )

    own_a1 = net.local(wa1, line(a1, 0))
    own_a2 = net.local(wa2, line(a2, 0))
    own_wd = net.local(wd, rows(wd_all, dp * 176, 176))
    own_f = net.local(wf.at[z], wg_all.at[:, pl.ds(pl.multiple_of((dp * 4 + z) * 64, 16), 64), :])
    own_c = net.local(cot, c_all.at[0, pl.ds(pl.multiple_of(z * tok, 16), tok), :])
    own_a1.wait()
    own_wd.wait()
    net.barrier(PARTNERS)

    def z_start(ref):
        far = net.send(line(ref, 0), line(ref, 0), ("z", 2))
        near = net.send(line(ref, 0), line(ref, 0), ("z", 1))
        return far, near

    def z_forward(ref, far):
        far.wait_recv()
        return net.send(line(ref, 2), line(ref, 2), ("z", 1))

    down = Plane(net, *block(wd_all, 176))
    plane1 = Plane(net, *block(a1, 256))
    plane2 = Plane(net, *block(a2, 256))
    plane_f = Plane(
        net,
        lambda mask, half: rows(wg_all.at[half], dps[mask] * 256, 256),
        lambda mask: [rows(wg_all.at[half], dps[mask] * 256, 256) for half in (0, 1)],
    )
    a1_far, a1_near = z_start(a1)
    down.start()
    own_a2.wait()
    own_f.wait()
    x = x_ref[...].astype(F32)
    hat1[...] = (x * rms(x)).astype(BF)
    a1_last = z_forward(a1, a1_far)
    down.forward()
    a1_near.wait_recv()
    a1_last.wait_recv()
    plane1.start()
    a2_far, a2_near = z_start(a2)
    down.spread()
    a2_last = z_forward(a2, a2_far)
    f_place = wg_all.at[:, pl.ds(pl.multiple_of((dp * 4 + z) * 64, 16), 64), :]
    f_copies = [net.send(wf.at[zs[m]], f_place, ("z", m)) for m in (2, 3, 1)]
    plane1.forward()
    a2_near.wait_recv()
    a2_last.wait_recv()
    plane1.spread()
    plane2.start()
    plane1.finish()

    here = pl.ds(pl.multiple_of(z * tok, 16), tok)

    def tokens_start(src, ref):
        place = ref.at[0, here, :]
        far = net.send(src, place, ("z", 2))
        near = net.send(src, place, ("z", 1))
        own = net.send(src, ref.at[1, here, :], CORE)
        return far, near, own

    def tokens_forward(ref, far):
        far.wait_recv()
        there = pl.ds(pl.multiple_of(zs[2] * tok, 16), tok)
        return [
            net.send(ref.at[0, there, :], ref.at[0, there, :], ("z", 1)),
            net.send(ref.at[0, there, :], ref.at[1, there, :], CORE),
        ]

    def tokens_end(ref, near, last):
        near.wait_recv()
        last[0].wait_recv()
        out = []
        for m in (1, 3):
            there = pl.ds(pl.multiple_of(zs[m] * tok, 16), tok)
            out.append(net.send(ref.at[0, there, :], ref.at[1, there, :], CORE))
        return out

    left = hat1[...]

    def project(g, carry):
        cols = pl.ds(pl.multiple_of(g * group, 128), group)
        pre = jnp.dot(left, a1[:, cols], preferred_element_type=F32)
        for j in range(group // 128):
            part = pre[:, j * 128 : (j + 1) * 128]
            last = j == group // 128 - 1
            c_ref, s_ref = (cos_k, sin_k) if last else (cos_q, sin_q)
            part = rotary(part, c_ref[...], s_ref[...])
            qkv_send[g, :, j * 128 : (j + 1) * 128] = part.astype(BF)
        return carry

    lax.fori_loop(0, 4, project, 0)
    q_copies = [net.send(qkv_send.at[zs[m]], qkv.at[here, :], ("z", m)) for m in (2, 3, 1)]
    own_q = net.local(qkv_send.at[z], qkv.at[here, :])
    own_c.wait()
    plane2.forward()
    for copy in f_copies:
        copy.wait_recv()
    own_q.wait()
    for copy in q_copies:
        copy.wait_recv()
    c_far, c_near, c_own = tokens_start(cot, c_all)

    kv = qkv[:, span:]
    kk, vv = twice(kv)

    def pair(p, carry):
        cols = pl.ds(pl.multiple_of(p * 128, 128), 128)
        for qb in range(4):
            keys = (qb + 1) * tok
            q = qkv[qb * tok : (qb + 1) * tok, cols]
            lane = lax.broadcasted_iota(jnp.int32, (tok, 128), 1)
            row = lax.broadcasted_iota(jnp.int32, (tok, keys), 0) + qb * tok
            col = lax.broadcasted_iota(jnp.int32, (tok, keys), 1)
            outs = []
            for h in range(2):
                mine = (lane < 64) if h == 0 else (lane >= 64)
                qh = jnp.where(mine, q, jnp.zeros_like(q))
                s = right_dot(qh, kk[:keys]) * HEAD_SIZE ** (-0.5)
                s = jnp.where(col <= row, s, -1e30)
                top = jnp.max(s, axis=-1, keepdims=True)
                e = jnp.exp(s - top)
                total = jnp.sum(e, axis=-1, keepdims=True)
                probs = (e * (1.0 / total)).astype(BF)
                outs.append(dot(probs, vv[:keys]))
                old = lse[qb * tok : (qb + 1) * tok, :]
                lse[qb * tok : (qb + 1) * tok, :] = jnp.where(
                    lane == 2 * p + h, top + jnp.log(total), old
                )
            heads[qb * tok : (qb + 1) * tok, cols] = jnp.where(
                lane < 64, outs[0], outs[1]
            ).astype(BF)
        return carry

    lse[...] = jnp.zeros_like(lse)
    lax.fori_loop(0, span // 128, pair, 0)
    h_copies = [
        net.send(
            heads.at[pl.ds(pl.multiple_of(zs[m] * tok, 16), tok), :], att.at[z], ("z", m)
        )
        for m in (2, 3, 1)
    ]
    own_h = net.local(heads.at[here, :], att.at[z])
    plane2.spread()
    plane_f.start()
    c_last = tokens_forward(c_all, c_far)
    plane2.finish()
    own_h.wait()
    for copy in h_copies:
        copy.wait_recv()

    width = x_ref.shape[1]
    for part in range(4):
        cols = pl.ds(part * (width // 4), width // 4)
        total = x_ref[:, cols].astype(F32)
        for g in range(4):
            total += jnp.dot(
                att[g], a2[g * span : (g + 1) * span, cols], preferred_element_type=F32
            )
        hmid[:, cols] = total
    mid = hmid[...]
    hat2[...] = (mid * rms(mid)).astype(BF)

    own_n = net.local(hat2, n_all.at[0, here, :])
    n_far, n_near, n_own = tokens_start(hat2, n_all)
    outs = [
        net.local(a1, a1_out), net.local(a2, a2_out), net.local(qkv, qkv_out),
        net.local(att, att_out), net.local(hat1, hat1_out),
    ]
    c_core = tokens_end(c_all, c_near, c_last)
    plane_f.forward()
    n_last = tokens_forward(n_all, n_far)
    plane_f.spread()
    down.finish()
    n_core = tokens_end(n_all, n_near, n_last)
    plane_f.finish()
    for copy in [n_own, c_own, n_last[1], c_last[1]] + n_core + c_core:
        copy.wait_recv()
    own_n.wait()
    for copy in outs:
        copy.wait()
    net.finish()


def first_call(x, wa1, wa2, wf, wd, cot, tables4):
    tok, width = x.shape
    ff_part = wf.shape[-1]
    sds = jax.ShapeDtypeStruct
    wide = wa1.shape[1]
    group = wide // 4
    span = group - 128
    return pl.pallas_call(
        first_kernel,
        name="first",
        out_shape=[
            sds((2, width, ff_part), BF), sds((ff_part, width), BF),
            sds((width, wide), BF), sds((width, width), BF),
            sds((2, 4 * tok, width), BF), sds((2, 4 * tok, width), BF),
            sds((4 * tok, group), BF), sds((4 * tok, 128), F32), sds((4, tok, span), BF),
            sds((tok, width), F32), sds((tok, width), BF),
        ],
        in_specs=[VMEM] + [ANY] * 5 + [VMEM] * 4,
        out_specs=[ANY] * 7 + [VMEM, ANY, VMEM, ANY],
        scratch_shapes=[
            pltpu.VMEM((width, wide), BF),
            pltpu.VMEM((width, width), BF),
            pltpu.VMEM((4, tok, group), BF),
            pltpu.VMEM((4 * tok, group), BF),
            pltpu.VMEM((4 * tok, span), BF),
            pltpu.VMEM((4, tok, span), BF),
            pltpu.VMEM((tok, width), BF),
            pltpu.VMEM((tok, width), BF),
            pltpu.SemaphoreType.DMA((96,)),
            pltpu.SemaphoreType.DMA((96,)),
        ],
        compiler_params=pltpu.CompilerParams(
            collective_id=1, has_side_effects=True, vmem_limit_bytes=56 * 2**20
        ),
    )(x, wa1, wa2, wf, wd, cot, *tables4)


def shards(
    tokens, norm_first, w_query, w_key, w_value, w_out, norm_second, w_gate, w_up, w_down, cotangent
):
    dp, seq = Axis("dp"), Axis("seq")
    groups = seq.size
    count, width = tokens.shape
    ff = w_gate.shape[1]
    rows = w_gate.shape[0]
    per = H // groups
    span = per * HEAD_SIZE
    gain1 = norm_first.astype(F32)[:, None]
    gain2 = norm_second.astype(F32)[:, None]

    w_first = jnp.concatenate(
        [
            part
            for g in range(groups)
            for part in (
                w_query[:, g * span : (g + 1) * span],
                w_key[:, g * HEAD_SIZE : (g + 1) * HEAD_SIZE],
                w_value[:, g * HEAD_SIZE : (g + 1) * HEAD_SIZE],
            )
        ],
        axis=1,
    )
    wide = w_first.shape[1]
    group = wide // groups

    def by_part(weight):
        scaled = (weight.astype(F32) * gain2).astype(BF)
        parts = scaled.reshape(rows, dp.size, groups, ff // dp.size // groups)
        return parts.transpose(2, 0, 1, 3).reshape(groups, rows, ff // groups)

    cosine, sine = tables(seq.me * count + jnp.arange(count))
    cosine, sine = cosine[:, 0], sine[:, 0]
    one, zero = jnp.ones_like(cosine), jnp.zeros_like(cosine)
    tables4 = [
        jnp.concatenate(parts, axis=1)
        for parts in (
            [cosine] * 4,
            [-sine, sine] * 2,
            [cosine, cosine, one, one],
            [-sine, sine, zero, zero],
        )
    ]
    wg, wd, a1, a2, c_all, n_all, qkv, lse, att, hmid, hat1 = first_call(
        tokens,
        (w_first.astype(F32) * gain1).astype(BF),
        w_out,
        jnp.stack([by_part(w_gate), by_part(w_up)], axis=1),
        w_down,
        cotangent,
        tables4,
    )
    hat2_all, cot_all = n_all[0], c_all[0]
    gate = dot(hat2_all, wg[0])
    upper = dot(hat2_all, wg[1])
    sigma = jax.nn.sigmoid(gate)
    hidden = (gate * sigma * upper).astype(BF)
    dhidden = right_dot(cot_all, wd)
    dgate = (dhidden * upper * sigma * (1.0 + gate * (1.0 - sigma))).astype(BF)
    dupper = (dhidden * gate * sigma).astype(BF)
    dhat2 = (right_dot(dgate, wg[0]) + right_dot(dupper, wg[1])).astype(BF)
    length = groups * count

    def token_rows(value, i):
        return lax.dynamic_slice_in_dim(value, i * count, count, 0)

    def sum_home(value):
        return sum(
            (token_rows(value, seq.me) if m == 0 else seq.swap(token_rows(value, seq.me ^ m), m)).astype(F32)
            for m in range(groups)
        )

    dhat2 = sum_home(dhat2)
    inv2 = lax.rsqrt(jnp.mean(hmid * hmid, axis=-1, keepdims=True) + EPS)
    inner = jnp.mean(hmid * dhat2, axis=-1, keepdims=True)
    dh = cotangent.astype(F32) + inv2 * dhat2 - hmid * inv2 * inv2 * inv2 * inner
    dbranch = dh.astype(BF)

    dattn = right_dot(dbranch, a2).astype(BF)
    grad_heads = jnp.concatenate(
        seq.natural(seq.exchange(dattn.reshape(count, groups, span).transpose(1, 0, 2))), axis=0
    ).reshape(length, per, HEAD_SIZE)
    queries = qkv[:, :span].reshape(length, per, HEAD_SIZE)
    keys = qkv[:, span : span + HEAD_SIZE]
    values = qkv[:, span + HEAD_SIZE :]
    place = jnp.arange(length)
    visible = place[None, :] <= place[:, None]
    logsum = lse[:, :per].T[:, :, None]
    dq, dk, dv = attend_back(queries, keys, values, grad_heads, logsum, visible)
    back = jnp.concatenate([dq.reshape(length, span), dk, dv], axis=1)
    back = seq.natural(
        [
            token_rows(back, seq.me) if m == 0 else seq.swap(token_rows(back, seq.me ^ m), m)
            for m in range(groups)
        ]
    )
    cosine, sine = cosine[:, None, :], sine[:, None, :]
    dpre = []
    for piece in back:
        turned = rotate(
            piece[:, : span + HEAD_SIZE].astype(F32).reshape(count, per + 1, HEAD_SIZE), cosine, -sine
        ).reshape(count, span + HEAD_SIZE)
        dpre += [turned.astype(BF), piece[:, span + HEAD_SIZE :]]
    dpre = jnp.concatenate(dpre, axis=1)
    dhat1 = right_dot(dpre, a1)
    inputs = tokens.astype(F32)
    inv1 = lax.rsqrt(jnp.mean(inputs * inputs, axis=-1, keepdims=True) + EPS)
    inner = jnp.mean(inputs * dhat1, axis=-1, keepdims=True)
    grad_inputs = dh + inv1 * dhat1 - inputs * inv1 * inv1 * inv1 * inner
    mixed = hmid + sum_home(dot(hidden, wd).astype(BF))

    def scatter(part, turn):
        size = part.shape[0] // dp.size
        blocks = [
            lax.dynamic_slice_in_dim(part, (dp.me ^ m) * size, size, 0) for m in range(dp.size)
        ]
        even, odd = orders(dp.size)
        other = dp.swap(jnp.stack([blocks[m] for m in odd]), 1)
        summed = {
            m: (blocks[m].astype(F32) + other[i].astype(F32)).astype(BF)
            for i, m in enumerate(even)
        }
        return scatter_chips(dp, summed, turn)

    half = width // 2
    grad_down = jnp.concatenate(
        [
            scatter(left_dot(hidden, cot_all[:, t * half : (t + 1) * half]).astype(BF), t)
            for t in (0, 1)
        ],
        axis=1,
    )
    sent = jnp.stack(
        [
            scatter(left_dot(hat2_all, grad).astype(BF), t).astype(BF)
            for t, grad in enumerate((dgate, dupper))
        ]
    )
    sent = sent.reshape(2, groups, rows, ff // groups).transpose(1, 0, 2, 3)
    got = jnp.stack(seq.natural(seq.exchange(sent)))
    got = got.reshape(groups, 2, rows, dp.size, ff // groups // dp.size)
    got = got.transpose(1, 2, 3, 0, 4).reshape(2, rows, ff).astype(F32)
    grad_gate, grad_up = got[0] * gain2, got[1] * gain2
    grad_gain2 = jnp.sum(got[0] * w_gate.astype(F32) + got[1] * w_up.astype(F32), axis=1)

    def proj_grad(left, right):
        size = right.shape[1] // 2
        own = jnp.concatenate(
            [
                scatter(left_dot(left, right[:, t * size : (t + 1) * size]).astype(BF), t)
                for t in (0, 1)
            ],
            axis=1,
        )
        own = own.astype(BF).reshape(groups, rows, own.shape[1])
        return sum(piece.astype(F32) for piece in seq.exchange(own))

    attn = jnp.concatenate([att[g] for g in range(groups)], axis=1)
    grad_out = proj_grad(attn, dbranch)
    grad_first = proj_grad(hat1, dpre)
    grad_gain1 = jnp.sum(grad_first * w_first.astype(F32), axis=1)
    grad_first = (grad_first * gain1).reshape(rows, groups, group)
    return (
        mixed.astype(BF),
        grad_inputs.astype(BF),
        grad_gain1,
        grad_first[:, :, :span].reshape(rows, groups * span),
        grad_first[:, :, span : span + HEAD_SIZE].reshape(rows, groups * HEAD_SIZE),
        grad_first[:, :, span + HEAD_SIZE :].reshape(rows, groups * HEAD_SIZE),
        grad_out,
        grad_gain2,
        grad_gate,
        grad_up,
        grad_down,
    )


def solution(mesh):
    special = mesh.shape['dp'] == 8 and mesh.shape['seq'] == KEY_VALUE_HEADS
    rows = P(("dp", "seq"), None)
    line = P(("dp", "seq"))
    return jax.shard_map(
        shards if special else general_shards,
        mesh=mesh,
        in_specs=(rows, line, rows, rows, rows, rows, line, rows, rows, rows, rows),
        out_specs=(rows, rows, line, rows, rows, rows, rows, line, rows, rows, rows),
        check_vma=False,
    )
```

```python
import jax
import jax.numpy as jnp
from jax import lax
from jax.experimental import pallas as pl
from jax.experimental.pallas import tpu as pltpu
from jax.sharding import PartitionSpec as P

H = 32
KEY_VALUE_HEADS = 4
HEAD_SIZE = 64
EPS = 1e-05
BF = jnp.bfloat16
F32 = jnp.float32


def tables(positions):
    freq = 10000.0 ** (-jnp.arange(0, HEAD_SIZE // 2, dtype=F32) * 2.0 / HEAD_SIZE)
    angle = positions.astype(F32)[:, None] * freq[None, :]
    return (jnp.cos(angle)[:, None, :], jnp.sin(angle)[:, None, :])


def rotate(heads, cosine, sine):
    half = heads.shape[-1] // 2
    first = heads[..., :half]
    second = heads[..., half:]
    return jnp.concatenate(
        [first * cosine - second * sine, second * cosine + first * sine], axis=-1
    )


def dot(left, right):
    return jnp.dot(left, right, preferred_element_type=F32)


def left_dot(left, right):
    return lax.dot_general(left, right, (((0,), (0,)), ((), ())), preferred_element_type=F32)


def right_dot(left, right):
    return lax.dot_general(left, right, (((1,), (1,)), ((), ())), preferred_element_type=F32)


def bits_of(count):
    return [1 << k for k in range(count.bit_length() - 1)]


class Axis:
    def __init__(self, name):
        self.name = name
        self.size = lax.axis_size(name)
        self.me = lax.axis_index(name)

    def swap(self, value, mask):
        return lax.ppermute(value, self.name, [(i, i ^ mask) for i in range(self.size)])

    def all(self, value):
        return [value if m == 0 else self.swap(value, m) for m in range(self.size)]

    def exchange(self, stacked):
        return [
            lax.dynamic_index_in_dim(stacked, self.me ^ m, 0, keepdims=False)
            if m == 0
            else self.swap(
                lax.dynamic_index_in_dim(stacked, self.me ^ m, 0, keepdims=False), m
            )
            for m in range(self.size)
        ]

    def natural(self, pieces):
        stack = jnp.stack(pieces)
        return [
            lax.dynamic_index_in_dim(stack, self.me ^ i, 0, keepdims=False)
            for i in range(self.size)
        ]


def orders(size):
    even = [m for m in range(size) if m % 2 == 0]
    return even, [m + 1 for m in even]


def chip_bits(size, turn):
    bits = bits_of(size)[1:]
    return bits if turn == 0 else bits[::-1]


def gather_chips(dp, piece, turn):
    pieces = {0: piece}
    for bit in chip_bits(dp.size, turn):
        pieces.update({m ^ bit: dp.swap(p, bit) for m, p in list(pieces.items())})
    return pieces


def gather_rows(dp, piece, turn):
    pieces = gather_chips(dp, piece, turn)
    even = jnp.concatenate([pieces[m] for m in orders(dp.size)[0]], axis=0)
    return even, dp.swap(even, 1)


def scatter_chips(dp, blocks, turn):
    for bit in chip_bits(dp.size, turn):
        for m in [m for m in blocks if m & bit]:
            other = dp.swap(blocks.pop(m).astype(BF), bit)
            blocks[m ^ bit] = blocks[m ^ bit].astype(F32) + other.astype(F32)
    return blocks[0]


def scatter_rows(dp, even_fn, odd, turn):
    rows = odd.shape[0] * 2 // dp.size
    other = dp.swap(odd, 1)
    even = (even_fn() + other.astype(F32)).astype(BF)
    blocks = {
        m: even[i * rows : (i + 1) * rows] for i, m in enumerate(orders(dp.size)[0])
    }
    return scatter_chips(dp, blocks, turn)


def mask_columns(dp, value):
    width = value.shape[1] // dp.size
    return tuple(
        jnp.concatenate(
            [lax.dynamic_slice_in_dim(value, (dp.me ^ m) * width, width, 1) for m in group],
            axis=1,
        )
        for group in orders(dp.size)
    )


def natural_columns(dp, even, odd):
    both = jnp.concatenate([even, odd], axis=1)
    width = both.shape[1] // dp.size
    half = dp.size // 2
    parts = []
    for i in range(dp.size):
        mask = dp.me ^ i
        place = mask // 2 + (mask % 2) * half
        parts.append(lax.dynamic_slice_in_dim(both, place * width, width, 1))
    return jnp.concatenate(parts, axis=1)


def attend(queries, keys, values, visible):
    scores = jnp.einsum("qhd,kd->hqk", queries, keys, preferred_element_type=F32)
    scores = jnp.where(visible[None], scores * HEAD_SIZE ** (-0.5), -1e30)
    top = jnp.max(scores, axis=-1, keepdims=True)
    expo = jnp.exp(scores - top)
    total = jnp.sum(expo, axis=-1, keepdims=True)
    probs = (expo / total).astype(BF)
    result = jnp.einsum("hqk,kd->qhd", probs, values, preferred_element_type=F32)
    return result.astype(BF), top + jnp.log(total)


def attend_back(queries, keys, values, grad_heads, logsum, visible):
    scale = HEAD_SIZE ** (-0.5)
    scores = jnp.einsum("qhd,kd->hqk", queries, keys, preferred_element_type=F32)
    scores = jnp.where(visible[None], scores * scale, -1e30)
    probs = jnp.exp(scores - logsum)
    pgrad = jnp.einsum("qhd,kd->hqk", grad_heads, values, preferred_element_type=F32)
    delta = jnp.sum(probs * pgrad, axis=-1, keepdims=True)
    sgrad = (probs * (pgrad - delta)).astype(BF)
    qgrad = jnp.einsum("hqk,kd->qhd", sgrad, keys, preferred_element_type=F32) * scale
    kgrad = jnp.einsum("hqk,qhd->kd", sgrad, queries, preferred_element_type=F32) * scale
    vgrad = jnp.einsum("hqk,qhd->kd", probs.astype(BF), grad_heads, preferred_element_type=F32)
    return qgrad.astype(BF), kgrad.astype(BF), vgrad.astype(BF)


def general_shards(
    tokens, norm_first, w_query, w_key, w_value, w_out, norm_second, w_gate, w_up, w_down, cotangent
):
    dp, seq = Axis("dp"), Axis("seq")
    groups = seq.size
    count, width = tokens.shape
    ff = w_gate.shape[1]
    per = H // groups
    repeat = groups // KEY_VALUE_HEADS
    heads_wide = H * HEAD_SIZE
    keys_wide = KEY_VALUE_HEADS * HEAD_SIZE
    gain1 = norm_first.astype(F32)[:, None]
    gain2 = norm_second.astype(F32)[:, None]

    w_first = jnp.concatenate([w_query, w_key, w_value], axis=1)
    w_first_scaled = (w_first.astype(F32) * gain1).astype(BF)
    wide = w_first.shape[1]

    def by_part(weight):
        rows = weight.shape[0]
        scaled = (weight.astype(F32) * gain2).astype(BF)
        parts = scaled.reshape(rows, dp.size, groups, ff // dp.size // groups)
        return parts.transpose(2, 0, 1, 3).reshape(groups, rows, ff // groups)

    down = [gather_chips(dp, w_down[:, t * width // 2 : (t + 1) * width // 2], t) for t in (0, 1)]
    first_rows = jnp.concatenate(seq.natural(seq.all(w_first_scaled)), axis=0)
    first = [gather_rows(dp, first_rows[:, t * wide // 2 : (t + 1) * wide // 2], t) for t in (0, 1)]
    out_rows = jnp.concatenate(seq.natural(seq.all(w_out)), axis=0)
    outw = [gather_rows(dp, out_rows[:, t * width // 2 : (t + 1) * width // 2], t) for t in (0, 1)]
    gate_up = seq.exchange(jnp.stack([by_part(w_gate), by_part(w_up)], axis=1))
    gate_up = jnp.concatenate(seq.natural(gate_up), axis=1)
    (gate_even, gate_odd), (up_even, up_odd) = [
        gather_rows(dp, gate_up[t], t) for t in (0, 1)
    ]
    cot_all = jnp.concatenate(seq.all(cotangent), axis=0)

    rows_down = w_down.shape[0]
    down_full = []
    for t in (0, 1):
        even = jnp.stack([down[t][m] for m in orders(dp.size)[0]])
        odd = dp.swap(even, 1)
        full = jnp.zeros((rows_down * dp.size, width // 2), BF)
        for i, m in enumerate(orders(dp.size)[0]):
            full = lax.dynamic_update_slice(full, even[i], ((dp.me ^ m) * rows_down, 0))
            full = lax.dynamic_update_slice(full, odd[i], ((dp.me ^ m ^ 1) * rows_down, 0))
        down_full.append(full)

    inputs = tokens.astype(F32)
    inv1 = lax.rsqrt(jnp.mean(inputs * inputs, axis=-1, keepdims=True) + EPS)
    hat1 = (inputs * inv1).astype(BF)
    hat1_even, hat1_odd = mask_columns(dp, hat1)
    cosine, sine = tables(seq.me * count + jnp.arange(count))
    pre = jnp.concatenate(
        [dot(hat1_even, first[t][0]) + dot(hat1_odd, first[t][1]) for t in (0, 1)], axis=1
    )
    qpre = pre[:, :heads_wide].reshape(count, H, HEAD_SIZE)
    kpre = pre[:, heads_wide : heads_wide + keys_wide].reshape(count, KEY_VALUE_HEADS, HEAD_SIZE)
    vround = pre[:, heads_wide + keys_wide :].astype(BF)
    qrot = rotate(qpre, cosine, sine).reshape(count, heads_wide).astype(BF)
    krot = rotate(kpre, cosine, sine).reshape(count, keys_wide).astype(BF)
    span = per * HEAD_SIZE
    packed = []
    for g in range(groups):
        head = g // repeat * HEAD_SIZE
        packed.append(
            jnp.concatenate(
                [
                    qrot[:, g * span : (g + 1) * span],
                    krot[:, head : head + HEAD_SIZE],
                    vround[:, head : head + HEAD_SIZE],
                ],
                axis=1,
            )
        )
    qkv = jnp.concatenate(seq.exchange(jnp.stack(packed)), axis=0)
    length = qkv.shape[0]
    queries = qkv[:, :span].reshape(length, per, HEAD_SIZE)
    keys = qkv[:, span : span + HEAD_SIZE]
    values = qkv[:, span + HEAD_SIZE :]
    place = jnp.concatenate(
        [(seq.me ^ m) * count + jnp.arange(count, dtype=jnp.int32) for m in range(groups)]
    )
    visible = place[None, :] <= place[:, None]
    out_heads, logsum = attend(queries, keys, values, visible)
    out_heads = out_heads.reshape(length, span)

    def back_home(value):
        return seq.natural(
            [
                value[:count] if m == 0 else seq.swap(value[m * count : (m + 1) * count], m)
                for m in range(groups)
            ]
        )

    attn = jnp.concatenate(back_home(out_heads), axis=1)
    attn_even, attn_odd = mask_columns(dp, attn)
    branch = jnp.concatenate(
        [dot(attn_even, outw[t][0]) + dot(attn_odd, outw[t][1]) for t in (0, 1)], axis=1
    )
    hmid = inputs + branch

    inv2 = lax.rsqrt(jnp.mean(hmid * hmid, axis=-1, keepdims=True) + EPS)
    hat2 = jnp.concatenate(mask_columns(dp, (hmid * inv2).astype(BF)), axis=1)
    hat2_all = jnp.concatenate(seq.all(hat2), axis=0)
    hat2_even, hat2_odd = hat2_all[:, : width // 2], hat2_all[:, width // 2 :]
    gate = dot(hat2_even, gate_even) + dot(hat2_odd, gate_odd)
    upper = dot(hat2_even, up_even) + dot(hat2_odd, up_odd)
    sigma = jax.nn.sigmoid(gate)
    hidden = (gate * sigma * upper).astype(BF)
    halves = [cot_all[:, : width // 2], cot_all[:, width // 2 :]]
    dhidden = right_dot(halves[0], down_full[0]) + right_dot(halves[1], down_full[1])
    dgate = (dhidden * upper * sigma * (1.0 + gate * (1.0 - sigma))).astype(BF)
    dupper = (dhidden * gate * sigma).astype(BF)
    dhat2 = jnp.concatenate(
        [
            right_dot(dgate, gate_even) + right_dot(dupper, up_even),
            right_dot(dgate, gate_odd) + right_dot(dupper, up_odd),
        ],
        axis=1,
    ).astype(BF)

    def sum_home(value):
        total = value[:count].astype(F32)
        for m in range(1, groups):
            total = total + seq.swap(value[m * count : (m + 1) * count], m).astype(F32)
        return total

    dhat2 = sum_home(dhat2)
    dgain2 = natural_columns(dp, dhat2[:, : width // 2], dhat2[:, width // 2 :])
    inner = jnp.mean(hmid * dgain2, axis=-1, keepdims=True)
    dh = cotangent.astype(F32) + inv2 * dgain2 - hmid * inv2 * inv2 * inv2 * inner
    dbranch = dh.astype(BF)

    dattn = natural_columns(
        dp,
        *[
            sum(
                right_dot(dbranch[:, t * width // 2 : (t + 1) * width // 2], outw[t][s])
                for t in (0, 1)
            ).astype(BF)
            for s in (0, 1)
        ],
    )
    grad_heads = jnp.concatenate(
        seq.exchange(dattn.reshape(count, groups, span).transpose(1, 0, 2)), axis=0
    ).reshape(length, per, HEAD_SIZE)
    dq, dk, dv = attend_back(queries, keys, values, grad_heads, logsum, visible)
    dqkv = back_home(jnp.concatenate([dq.reshape(length, span), dk, dv], axis=1))
    dq = jnp.concatenate([piece[:, :span] for piece in dqkv], axis=1)
    dk = [piece[:, span : span + HEAD_SIZE].astype(F32) for piece in dqkv]
    dv = [piece[:, span + HEAD_SIZE :].astype(F32) for piece in dqkv]
    dk = jnp.stack(
        [sum(dk[i * repeat : (i + 1) * repeat]) for i in range(KEY_VALUE_HEADS)], axis=1
    )
    dv = jnp.concatenate(
        [sum(dv[i * repeat : (i + 1) * repeat]) for i in range(KEY_VALUE_HEADS)], axis=1
    )
    dq = rotate(dq.astype(F32).reshape(count, H, HEAD_SIZE), cosine, -sine)
    dk = rotate(dk, cosine, -sine)
    dpre = jnp.concatenate(
        [dq.reshape(count, heads_wide), dk.reshape(count, keys_wide), dv], axis=1
    ).astype(BF)
    dhalf = [dpre[:, t * wide // 2 : (t + 1) * wide // 2] for t in (0, 1)]
    dhat1 = [sum(right_dot(dhalf[t], first[t][s]) for t in (0, 1)) for s in (0, 1)]
    dgain1 = natural_columns(dp, *dhat1)
    inner = jnp.mean(inputs * dgain1, axis=-1, keepdims=True)
    grad_inputs = dh + inv1 * dgain1 - inputs * inv1 * inv1 * inv1 * inner

    mixed_part = jnp.concatenate([dot(hidden, down_full[t]) for t in (0, 1)], axis=1).astype(BF)
    mixed = hmid + sum_home(mixed_part)

    grad_down = []
    for t in (0, 1):
        part = left_dot(hidden, halves[t]).astype(BF)
        blocks = [
            lax.dynamic_slice_in_dim(part, (dp.me ^ m) * rows_down, rows_down, 0)
            for m in range(dp.size)
        ]
        even, odd = orders(dp.size)
        other = dp.swap(jnp.stack([blocks[m] for m in odd]), 1)
        summed = {
            m: (blocks[m].astype(F32) + other[i].astype(F32)).astype(BF)
            for i, m in enumerate(even)
        }
        grad_down.append(scatter_chips(dp, summed, t))
    grad_down = jnp.concatenate(grad_down, axis=1)

    def ff_grad(grad, turn):
        odd = left_dot(hat2_odd, grad).astype(BF)
        return scatter_rows(dp, lambda: left_dot(hat2_even, grad), odd, turn)

    rows = w_gate.shape[0]
    sent = jnp.stack([ff_grad(dgate, 0).astype(BF), ff_grad(dupper, 1).astype(BF)])
    sent = sent.reshape(2, groups, rows, ff // groups).transpose(1, 0, 2, 3)
    got = jnp.stack(seq.natural(seq.exchange(sent)))
    got = got.reshape(groups, 2, rows, dp.size, ff // groups // dp.size)
    got = got.transpose(1, 2, 3, 0, 4).reshape(2, rows, ff).astype(F32)
    grad_gate, grad_up = got[0] * gain2, got[1] * gain2
    grad_gain2 = jnp.sum(got[0] * w_gate.astype(F32) + got[1] * w_up.astype(F32), axis=1)

    def proj_grad(even, odd, grads):
        parts = []
        for t in (0, 1):
            send = left_dot(odd, grads[t]).astype(BF)
            parts.append(
                scatter_rows(dp, lambda grad=grads[t]: left_dot(even, grad), send, t)
            )
        own = jnp.concatenate(parts, axis=1)
        own = own.astype(BF).reshape(groups, rows, own.shape[1])
        return sum(piece.astype(F32) for piece in seq.exchange(own))

    grad_out = proj_grad(
        attn_even,
        attn_odd,
        [dbranch[:, t * width // 2 : (t + 1) * width // 2] for t in (0, 1)],
    )
    grad_first = proj_grad(hat1_even, hat1_odd, dhalf)
    grad_gain1 = jnp.sum(grad_first * w_first.astype(F32), axis=1)
    grad_first = grad_first * gain1
    return (
        mixed.astype(BF),
        grad_inputs.astype(BF),
        grad_gain1,
        grad_first[:, :heads_wide],
        grad_first[:, heads_wide : heads_wide + keys_wide],
        grad_first[:, heads_wide + keys_wide :],
        grad_out,
        grad_gain2,
        grad_gate,
        grad_up,
        grad_down,
    )


MESH = pl.DeviceIdType.MESH
ANY = pl.BlockSpec(memory_space=pl.ANY)
VMEM = pl.BlockSpec(memory_space=pltpu.VMEM)


class Net:
    def __init__(self, send_sems, recv_sems):
        self.send_sems, self.recv_sems, self.used = send_sems, recv_sems, 0
        self.open = []
        dp, z = lax.axis_index("dp"), lax.axis_index("seq")
        self.dp, self.z = dp, z
        self.dps = {
            0: dp,
            1: dp + 1 - 2 * lax.rem(dp, 2),
            2: dp + 2 - 4 * lax.rem(lax.div(dp, 2), 2),
            4: lax.rem(dp + 4, 8),
        }
        self.dps[6] = lax.rem(self.dps[2] + 4, 8)
        for mask in (2, 4, 6):
            self.dps[mask + 1] = self.dps[mask] + 1 - 2 * lax.rem(dp, 2)
        self.zs = {0: z, 1: z + 1 - 2 * lax.rem(z, 2), 2: lax.rem(z + 2, 4), 3: 3 - z}

    def target(self, name):
        kind, mask = name
        return (self.dps[mask], self.z) if kind == "d" else (self.dp, self.zs[mask])

    def barrier(self, names):
        sem = pltpu.get_barrier_semaphore()
        for name in names:
            pl.semaphore_signal(sem, inc=1, device_id=self.target(name), device_id_type=MESH)
        pl.semaphore_wait(sem, len(names))

    def send(self, src, dst, name):
        copy = pltpu.make_async_remote_copy(
            src_ref=src,
            dst_ref=dst,
            send_sem=self.send_sems.at[self.used],
            recv_sem=self.recv_sems.at[self.used],
            device_id=self.target(name),
            device_id_type=MESH,
        )
        self.used += 1
        copy.start()
        self.open.append(copy)
        return copy

    def local(self, src, dst):
        copy = pltpu.make_async_copy(src, dst, self.send_sems.at[self.used])
        self.used += 1
        copy.start()
        return copy

    def finish(self):
        for copy in self.open:
            copy.wait_send()


X, Y, CORE = ("d", 2), ("d", 4), ("d", 1)
PARTNERS = [X, Y, CORE, ("z", 1), ("z", 2), ("z", 3)]


class Plane:
    def __init__(self, net, at, both):
        self.net, self.at, self.both = net, at, both

    def push(self, mask, half, name):
        ref = self.at(mask, half)
        return self.net.send(ref, ref, name)

    def start(self):
        self.xa = self.push(0, 0, X)
        self.yb = self.push(0, 1, Y)
        self.ya = self.push(0, 0, Y)
        self.xb = self.push(0, 1, X)
        self.cores = [self.core(0)]

    def core(self, mask):
        return [self.net.send(ref, ref, CORE) for ref in self.both(mask)]

    def forward(self):
        self.xa.wait_recv()
        self.ya2 = self.push(2, 0, Y)
        self.yb.wait_recv()
        self.xb2 = self.push(4, 1, X)

    def spread(self):
        self.ya.wait_recv()
        self.cores.append(self.core(4))
        self.xb.wait_recv()
        self.cores.append(self.core(2))
        self.ya2.wait_recv()
        self.xb2.wait_recv()
        self.cores.append(self.core(6))

    def finish(self):
        for copies in self.cores:
            for copy in copies:
                copy.wait_recv()


def rotary(value, cosine, sine):
    lane = lax.broadcasted_iota(jnp.int32, value.shape, 1)
    partner = jnp.where(
        lax.rem(lane, 64) < 32, pltpu.roll(value, 96, 1), pltpu.roll(value, 32, 1)
    )
    return value * cosine + partner * sine


def rms(value):
    return lax.rsqrt(jnp.mean(value * value, axis=-1, keepdims=True) + EPS)


def twice(pair):
    lane = lax.broadcasted_iota(jnp.int32, pair.shape, 1)
    other = pltpu.roll(pair.astype(F32), 64, 1).astype(BF)
    return jnp.where(lane < 64, pair, other), jnp.where(lane < 64, other, pair)


def first_kernel(
    x_ref, wa1, wa2, wf, wd, cot, cos_q, sin_q, cos_k, sin_k,
    wg_all, wd_all, a1_out, a2_out, c_all, n_all, qkv_out, lse, att_out, hmid, hat1_out,
    a1, a2, qkv_send, qkv, heads, att, hat1, hat2, send_sems, recv_sems,
):
    net = Net(send_sems, recv_sems)
    dp, z, dps, zs = net.dp, net.z, net.dps, net.zs
    first_half = a1.shape[1] // 2
    second_half = a2.shape[1] // 2
    tok = x_ref.shape[0]
    group = qkv.shape[1]
    span = heads.shape[1]

    def rows(ref, start, count, half=None):
        start = pl.multiple_of(start, 16)
        if half is None:
            return ref.at[pl.ds(start, count), :]
        width = ref.shape[1] // 2
        return ref.at[pl.ds(start, count), pl.ds(half * width, width)]

    def line(ref, mask):
        return rows(ref, (dp * 4 + zs[mask]) * 64, 64)

    def block(ref, size):
        return (
            lambda mask, half: rows(ref, dps[mask] * size, size, half),
            lambda mask: [rows(ref, dps[mask] * size, size)],
        )

    own_a1 = net.local(wa1, line(a1, 0))
    own_a2 = net.local(wa2, line(a2, 0))
    own_wd = net.local(wd, rows(wd_all, dp * 176, 176))
    own_f = net.local(wf.at[z], wg_all.at[:, pl.ds(pl.multiple_of((dp * 4 + z) * 64, 16), 64), :])
    own_c = net.local(cot, c_all.at[0, pl.ds(pl.multiple_of(z * tok, 16), tok), :])
    own_a1.wait()
    own_wd.wait()
    net.barrier(PARTNERS)

    def z_start(ref):
        far = net.send(line(ref, 0), line(ref, 0), ("z", 2))
        near = net.send(line(ref, 0), line(ref, 0), ("z", 1))
        return far, near

    def z_forward(ref, far):
        far.wait_recv()
        return net.send(line(ref, 2), line(ref, 2), ("z", 1))

    down = Plane(net, *block(wd_all, 176))
    plane1 = Plane(net, *block(a1, 256))
    plane2 = Plane(net, *block(a2, 256))
    plane_f = Plane(
        net,
        lambda mask, half: rows(wg_all.at[half], dps[mask] * 256, 256),
        lambda mask: [rows(wg_all.at[half], dps[mask] * 256, 256) for half in (0, 1)],
    )
    a1_far, a1_near = z_start(a1)
    down.start()
    own_a2.wait()
    own_f.wait()
    x = x_ref[...].astype(F32)
    hat1[...] = (x * rms(x)).astype(BF)
    a1_last = z_forward(a1, a1_far)
    down.forward()
    a1_near.wait_recv()
    a1_last.wait_recv()
    plane1.start()
    a2_far, a2_near = z_start(a2)
    down.spread()
    a2_last = z_forward(a2, a2_far)
    f_place = wg_all.at[:, pl.ds(pl.multiple_of((dp * 4 + z) * 64, 16), 64), :]
    f_copies = [net.send(wf.at[zs[m]], f_place, ("z", m)) for m in (2, 3, 1)]
    plane1.forward()
    a2_near.wait_recv()
    a2_last.wait_recv()
    plane1.spread()
    plane2.start()
    plane1.finish()

    here = pl.ds(pl.multiple_of(z * tok, 16), tok)

    def tokens_start(src, ref):
        place = ref.at[0, here, :]
        far = net.send(src, place, ("z", 2))
        near = net.send(src, place, ("z", 1))
        own = net.send(src, ref.at[1, here, :], CORE)
        return far, near, own

    def tokens_forward(ref, far):
        far.wait_recv()
        there = pl.ds(pl.multiple_of(zs[2] * tok, 16), tok)
        return [
            net.send(ref.at[0, there, :], ref.at[0, there, :], ("z", 1)),
            net.send(ref.at[0, there, :], ref.at[1, there, :], CORE),
        ]

    def tokens_end(ref, near, last):
        near.wait_recv()
        last[0].wait_recv()
        out = []
        for m in (1, 3):
            there = pl.ds(pl.multiple_of(zs[m] * tok, 16), tok)
            out.append(net.send(ref.at[0, there, :], ref.at[1, there, :], CORE))
        return out

    left = hat1[...]

    def project(g, carry):
        cols = pl.ds(pl.multiple_of(g * group, 128), group)
        pre = jnp.dot(left, a1[:, cols], preferred_element_type=F32)
        for j in range(group // 128):
            part = pre[:, j * 128 : (j + 1) * 128]
            last = j == group // 128 - 1
            c_ref, s_ref = (cos_k, sin_k) if last else (cos_q, sin_q)
            part = rotary(part, c_ref[...], s_ref[...])
            qkv_send[g, :, j * 128 : (j + 1) * 128] = part.astype(BF)
        return carry

    lax.fori_loop(0, 4, project, 0)
    q_copies = [net.send(qkv_send.at[zs[m]], qkv.at[here, :], ("z", m)) for m in (2, 3, 1)]
    own_q = net.local(qkv_send.at[z], qkv.at[here, :])
    own_c.wait()
    plane2.forward()
    for copy in f_copies:
        copy.wait_recv()
    own_q.wait()
    for copy in q_copies:
        copy.wait_recv()
    c_far, c_near, c_own = tokens_start(cot, c_all)

    kv = qkv[:, span:]
    kk, vv = twice(kv)

    def pair(p, carry):
        cols = pl.ds(pl.multiple_of(p * 128, 128), 128)
        for qb in range(4):
            keys = (qb + 1) * tok
            q = qkv[qb * tok : (qb + 1) * tok, cols]
            lane = lax.broadcasted_iota(jnp.int32, (tok, 128), 1)
            row = lax.broadcasted_iota(jnp.int32, (tok, keys), 0) + qb * tok
            col = lax.broadcasted_iota(jnp.int32, (tok, keys), 1)
            outs = []
            for h in range(2):
                mine = (lane < 64) if h == 0 else (lane >= 64)
                qh = jnp.where(mine, q, jnp.zeros_like(q))
                s = right_dot(qh, kk[:keys]) * HEAD_SIZE ** (-0.5)
                s = jnp.where(col <= row, s, -1e30)
                top = jnp.max(s, axis=-1, keepdims=True)
                e = jnp.exp(s - top)
                total = jnp.sum(e, axis=-1, keepdims=True)
                probs = (e * (1.0 / total)).astype(BF)
                outs.append(dot(probs, vv[:keys]))
                old = lse[qb * tok : (qb + 1) * tok, :]
                lse[qb * tok : (qb + 1) * tok, :] = jnp.where(
                    lane == 2 * p + h, top + jnp.log(total), old
                )
            heads[qb * tok : (qb + 1) * tok, cols] = jnp.where(
                lane < 64, outs[0], outs[1]
            ).astype(BF)
        return carry

    lse[...] = jnp.zeros_like(lse)
    lax.fori_loop(0, span // 128, pair, 0)
    h_copies = [
        net.send(
            heads.at[pl.ds(pl.multiple_of(zs[m] * tok, 16), tok), :], att.at[z], ("z", m)
        )
        for m in (2, 3, 1)
    ]
    own_h = net.local(heads.at[here, :], att.at[z])
    plane2.spread()
    plane_f.start()
    c_last = tokens_forward(c_all, c_far)
    plane2.finish()
    own_h.wait()
    for copy in h_copies:
        copy.wait_recv()

    width = x_ref.shape[1]
    for part in range(4):
        cols = pl.ds(part * (width // 4), width // 4)
        total = x_ref[:, cols].astype(F32)
        for g in range(4):
            total += jnp.dot(
                att[g], a2[g * span : (g + 1) * span, cols], preferred_element_type=F32
            )
        hmid[:, cols] = total
    mid = hmid[...]
    hat2[...] = (mid * rms(mid)).astype(BF)

    own_n = net.local(hat2, n_all.at[0, here, :])
    n_far, n_near, n_own = tokens_start(hat2, n_all)
    outs = [
        net.local(a1, a1_out), net.local(a2, a2_out), net.local(qkv, qkv_out),
        net.local(att, att_out), net.local(hat1, hat1_out),
    ]
    c_core = tokens_end(c_all, c_near, c_last)
    plane_f.forward()
    n_last = tokens_forward(n_all, n_far)
    plane_f.spread()
    down.finish()
    n_core = tokens_end(n_all, n_near, n_last)
    plane_f.finish()
    for copy in [n_own, c_own, n_last[1], c_last[1]] + n_core + c_core:
        copy.wait_recv()
    own_n.wait()
    for copy in outs:
        copy.wait()
    net.finish()


def first_call(x, wa1, wa2, wf, wd, cot, tables4):
    tok, width = x.shape
    ff_part = wf.shape[-1]
    sds = jax.ShapeDtypeStruct
    wide = wa1.shape[1]
    group = wide // 4
    span = group - 128
    return pl.pallas_call(
        first_kernel,
        name="first",
        out_shape=[
            sds((2, width, ff_part), BF), sds((ff_part, width), BF),
            sds((width, wide), BF), sds((width, width), BF),
            sds((2, 4 * tok, width), BF), sds((2, 4 * tok, width), BF),
            sds((4 * tok, group), BF), sds((4 * tok, 128), F32), sds((4, tok, span), BF),
            sds((tok, width), F32), sds((tok, width), BF),
        ],
        in_specs=[VMEM] + [ANY] * 5 + [VMEM] * 4,
        out_specs=[ANY] * 7 + [VMEM, ANY, VMEM, ANY],
        scratch_shapes=[
            pltpu.VMEM((width, wide), BF),
            pltpu.VMEM((width, width), BF),
            pltpu.VMEM((4, tok, group), BF),
            pltpu.VMEM((4 * tok, group), BF),
            pltpu.VMEM((4 * tok, span), BF),
            pltpu.VMEM((4, tok, span), BF),
            pltpu.VMEM((tok, width), BF),
            pltpu.VMEM((tok, width), BF),
            pltpu.SemaphoreType.DMA((96,)),
            pltpu.SemaphoreType.DMA((96,)),
        ],
        compiler_params=pltpu.CompilerParams(
            collective_id=1, has_side_effects=True, vmem_limit_bytes=56 * 2**20
        ),
    )(x, wa1, wa2, wf, wd, cot, *tables4)


def aligned(start, count, unit):
    return pl.ds(pl.multiple_of(start, unit), count)


def second_kernel(
    n_all, c_all, wg, wd,
    dn_out, mix_own, mix_far, hg_out, gdown,
    wg_v, wd_v, n_v, c_v, hid, dg, du, dn_part, mx_part, dn_r1, dn_s, dn_r2, mx_r1,
    hg_v, hd, hd_r1, hd_k, hd_r2, sib_s, sib_r, send_sems, recv_sems,
):
    net = Net(send_sems, recv_sems)
    dp, z, dps, zs = net.dp, net.z, net.dps, net.zs
    core = lax.rem(dp, 2)
    tok = dn_r2.shape[0]
    width = dn_r2.shape[1]
    ff = hid.shape[2]
    half = width // 2
    pair = 2 * tok
    copies = [
        net.local(n_all.at[0], n_v.at[0]),
        net.local(wg.at[0], wg_v.at[0]),
        net.local(wg.at[1], wg_v.at[1]),
        net.local(c_all.at[0], c_v.at[0]),
        net.local(wd, wd_v),
        net.local(n_all.at[1], n_v.at[1]),
        net.local(c_all.at[1], c_v.at[1]),
    ]
    net.barrier([X, Y, CORE, ("z", 1), ("z", 2)])
    for copy in copies[:5]:
        copy.wait()
    near_pair = lax.div(z, 2)
    rows_of = {"far": aligned((1 - near_pair) * pair, pair, 16), "near": aligned(near_pair * pair, pair, 16)}

    def chunks(fn, total, size):
        whole = total // size

        def step(i, carry):
            fn(i * size, size)
            return carry

        lax.fori_loop(0, whole, step, 0)
        if total % size:
            fn(whole * size, total - whole * size)

    def front(rows):
        def chunk(start, size):
            cols = aligned(start, size, 128)
            n = n_v[0, rows, :]
            gate = dot(n, wg_v[0, :, cols])
            upper = dot(n, wg_v[1, :, cols])
            dhid = right_dot(c_v[0, rows, :], wd_v[cols, :])
            sigma = jax.nn.sigmoid(gate)
            silu = gate * sigma
            hid[0, rows, cols] = (silu * upper).astype(BF)
            dg[0, rows, cols] = (dhid * upper * sigma * (1.0 + gate * (1.0 - sigma))).astype(BF)
            du[0, rows, cols] = (dhid * silu).astype(BF)

        chunks(chunk, ff, 256)

    def to_sibling(rows):
        return [net.send(ref.at[0, rows, :], ref.at[1, rows, :], CORE) for ref in (hid, dg, du)]

    def back(rows, part):
        def chunk(start, size):
            cols = aligned(start + part * half, size, 128)
            total = right_dot(dg[0, rows, :], wg_v[0, cols, :])
            total += right_dot(du[0, rows, :], wg_v[1, cols, :])
            dn_part[rows, cols] = total.astype(BF)

        chunks(chunk, half, 256)

    def slot(mask):
        return aligned(zs[mask] * tok, tok, 16)

    def piece(part):
        return pl.ds(part * half, half)

    front(rows_of["far"])
    sib = to_sibling(rows_of["far"])
    dn_a = []
    for part in (0, 1):
        back(rows_of["far"], part)
        dn_a.append(
            net.send(dn_part.at[slot(3), piece(part)], dn_r1.at[1, :, piece(part)], ("z", 1))
        )
    front(rows_of["near"])
    sib += to_sibling(rows_of["near"])
    dn_c = []
    for part in (0, 1):
        dn_a[part].wait_recv()
        cols = piece(part)
        dn_s[:, cols] = (
            dn_part[slot(2), cols].astype(F32) + dn_r1[1, :, cols].astype(F32)
        ).astype(BF)
        dn_c.append(net.send(dn_s.at[:, cols], dn_r2.at[:, cols], ("z", 2)))
    dn_b = []
    for part in (0, 1):
        back(rows_of["near"], part)
        dn_b.append(
            net.send(dn_part.at[slot(1), piece(part)], dn_r1.at[0, :, piece(part)], ("z", 1))
        )
    for copy in copies[5:]:
        copy.wait()
    for copy in sib:
        copy.wait_recv()

    ccols = aligned(core * half, half, 128)

    def down_chunk(start, size):
        cols = aligned(start, size, 128)
        total = left_dot(hid[0, :, cols], c_v[0, :, ccols])
        total += left_dot(hid[1, :, cols], c_v[1, :, ccols])
        hd[cols, :] = total.astype(BF)

    chunks(down_chunk, ff, 256)
    chip = ff // 4
    quarter = half // 2

    def hd_at(mask, side):
        return aligned(lax.div(dps[mask], 2) * chip, chip, 16), pl.ds(side * quarter, quarter)

    def hd_send(mask, side, place, name):
        r, c = hd_at(mask, side)
        return net.send(hd.at[r, c], hd_r1.at[side, place], name)

    hd_1 = [hd_send(6, 0, 1, X), hd_send(6, 1, 1, Y), hd_send(2, 0, 0, X), hd_send(4, 1, 0, Y)]

    def mix_chunk(start, size):
        cols = aligned(start, size, 128)
        mx_part[:, cols] = dot(hid[0], wd_v[:, cols]).astype(BF)

    chunks(mix_chunk, width, 256)
    mx = [
        net.send(mx_part.at[slot(3), :], mx_r1.at[1], ("z", 1)),
        net.send(mx_part.at[slot(1), :], mx_r1.at[0], ("z", 1)),
    ]

    def block(b, carry):
        cols = aligned((b * 2 + core) * 256, 256, 128)
        left = [n_v[s, :, cols].T for s in (0, 1)]
        for t, grad in enumerate((dg, du)):
            total = dot(left[0], grad[0]) + dot(left[1], grad[1])
            hg_v[t, b] = total.astype(BF)
        return carry

    lax.fori_loop(0, 4, block, 0)
    hg_copy = net.local(hg_v, hg_out)

    hd_1[0].wait_recv()
    hd_1[1].wait_recv()
    hd_2 = []
    for side, (mask, name) in enumerate(((4, Y), (2, X))):
        r, c = hd_at(mask, side)
        hd_k[side] = (hd[r, c].astype(F32) + hd_r1[side, 1].astype(F32)).astype(BF)
        hd_2.append(net.send(hd_k.at[side], hd_r2.at[side], name))
    for part in (0, 1):
        dn_b[part].wait_recv()
        dn_c[part].wait_recv()
        cols = piece(part)
        dn_out[:, cols] = (
            dn_part[slot(0), cols].astype(F32)
            + dn_r1[0, :, cols].astype(F32)
            + dn_r2[:, cols].astype(F32)
        )
    hd_1[2].wait_recv()
    hd_1[3].wait_recv()
    own = core * (chip // 2)
    other = (1 - core) * (chip // 2)
    mx[0].wait_recv()
    mx[1].wait_recv()
    mix_own[...] = mx_part[slot(0), :].astype(F32) + mx_r1[0].astype(F32)
    mix_far[...] = (mx_part[slot(2), :].astype(F32) + mx_r1[1].astype(F32)).astype(BF)
    for side in (0, 1):
        hd_2[side].wait_recv()
        r0 = lax.div(dp, 2) * chip

        def total(start):
            _, c = hd_at(0, side)
            return (
                hd[aligned(r0 + start, chip // 2, 16), c].astype(F32)
                + hd_r1[side, 0, aligned(start, chip // 2, 16), :].astype(F32)
                + hd_r2[side, aligned(start, chip // 2, 16), :].astype(F32)
            )

        sib_s[:, side * quarter : (side + 1) * quarter] = total(other)
        gdown[:, aligned(core * half + side * quarter, quarter, 128)] = total(own)
    last = net.send(sib_s, sib_r, CORE)
    last.wait_recv()
    gdown[:, aligned((1 - core) * half, half, 128)] = sib_r[...]
    hg_copy.wait()
    net.finish()


def second_call(n_all, c_all, wg, wd):
    _, length, width = n_all.shape
    tok = length // 4
    ff = wg.shape[2]
    sds = jax.ShapeDtypeStruct
    half = width // 2
    chip = ff // 4
    return pl.pallas_call(
        second_kernel,
        name="second",
        out_shape=[
            sds((tok, width), F32), sds((tok, width), F32), sds((tok, width), BF),
            sds((2, 4, 256, ff), BF), sds((chip // 2, width), F32),
        ],
        in_specs=[ANY] * 4,
        out_specs=[VMEM, VMEM, VMEM, ANY, VMEM],
        scratch_shapes=[
            pltpu.VMEM((2, width, ff), BF),
            pltpu.VMEM((ff, width), BF),
            pltpu.VMEM((2, length, width), BF),
            pltpu.VMEM((2, length, width), BF),
            pltpu.VMEM((2, length, ff), BF),
            pltpu.VMEM((2, length, ff), BF),
            pltpu.VMEM((2, length, ff), BF),
            pltpu.VMEM((length, width), BF),
            pltpu.VMEM((length, width), BF),
            pltpu.VMEM((2, tok, width), BF),
            pltpu.VMEM((tok, width), BF),
            pltpu.VMEM((tok, width), BF),
            pltpu.VMEM((2, tok, width), BF),
            pltpu.VMEM((2, 4, 256, ff), BF),
            pltpu.VMEM((ff, half), BF),
            pltpu.VMEM((2, 2, chip, half // 2), BF),
            pltpu.VMEM((2, chip, half // 2), BF),
            pltpu.VMEM((2, chip, half // 2), BF),
            pltpu.VMEM((chip // 2, half), F32),
            pltpu.VMEM((chip // 2, half), F32),
            pltpu.SemaphoreType.DMA((48,)),
            pltpu.SemaphoreType.DMA((48,)),
        ],
        compiler_params=pltpu.CompilerParams(
            collective_id=2, has_side_effects=True, vmem_limit_bytes=60 * 2**20
        ),
    )(n_all, c_all, wg, wd)


def third_kernel(
    x_ref, hmid, cot, dn2, mix_own, mix_far, qkv, lse, cos_q, sin_q, cos_k, sin_k,
    a1, a2, hat1, att, hg,
    tok_out, mixed, g2_out, g1_out, fb,
    a1_v, a2_v, hg_v, f_r1, f_k, f_r2, fs, dh, dbr_all, dpre_all, hat_all, att_all,
    dsend, gh, dqkv, dk_acc, dv_acc, dback, mix_r, g2_p, g1_p, g2_r1, g1_r1, g2_s, g1_s, g2_r2, g1_r2,
    send_sems, recv_sems,
):
    net = Net(send_sems, recv_sems)
    dp, z, dps, zs = net.dp, net.z, net.dps, net.zs
    tok, width = x_ref.shape
    group = qkv.shape[1]
    span = group - 128
    wide = 4 * group
    here = aligned(z * tok, tok, 16)
    mine = aligned(dp * tok, tok, 16)

    def chip(mask):
        return lax.div(dps[mask], 2)

    loads = [
        net.local(a2, a2_v),
        net.local(hg.at[0, chip(0)], hg_v.at[0, 0]),
        net.local(hg.at[0, chip(4)], hg_v.at[0, 1]),
        net.local(hg.at[1, chip(0)], hg_v.at[1, 0]),
        net.local(hg.at[1, chip(2)], hg_v.at[1, 1]),
        net.local(a1, a1_v),
    ]
    net.barrier([("d", m) for m in range(1, 8)] + [("z", m) for m in (1, 2, 3)])
    f_1 = [
        net.send(hg.at[0, chip(6)], f_r1.at[0, 1], X),
        net.send(hg.at[1, chip(6)], f_r1.at[1, 1], Y),
        net.send(hg.at[0, chip(2)], f_r1.at[0, 0], X),
        net.send(hg.at[1, chip(4)], f_r1.at[1, 0], Y),
    ]

    def norm_back(value, grad):
        inv = rms(value)
        inner = jnp.mean(value * grad, axis=-1, keepdims=True)
        return inv * grad - value * (inv * inv * inv * inner)

    dh[...] = cot[...].astype(F32) + norm_back(hmid[...], dn2[...])
    dbr_all[mine, :] = dh[...].astype(BF)
    loads[0].wait()
    d_copies = []
    for m in (2, 3, 1, 0):
        rows = aligned(zs[m] * span, span, 16)
        dsend[m] = right_dot(dbr_all[mine, :], a2_v[rows, :]).astype(BF)
        if m:
            d_copies.append(net.send(dsend.at[m], gh.at[here, :], ("z", m)))
    gh[here, :] = dsend[0]
    small = []
    for m in range(1, 8):
        cols = aligned(dps[m] * 256, 256, 128)
        small.append(net.send(hat1.at[:, cols], hat_all.at[mine, :], ("d", m)))
        cols = aligned(lax.rem(dps[m], 2) * 256, 256, 128)
        small.append(net.send(att.at[chip(m), :, cols], att_all.at[mine, :], ("d", m)))
    own = [
        net.local(hat1.at[:, aligned(dp * 256, 256, 128)], hat_all.at[mine, :]),
        net.local(att.at[chip(0), :, aligned(lax.rem(dp, 2) * 256, 256, 128)], att_all.at[mine, :]),
    ]
    for copy in d_copies:
        copy.wait_recv()
    mix_copy = net.send(mix_far, mix_r, ("z", 2))

    scale = HEAD_SIZE ** (-0.5)
    kk, vv = twice(qkv[:, span:])
    dk_acc[...] = jnp.zeros_like(dk_acc)
    dv_acc[...] = jnp.zeros_like(dv_acc)

    def pair(p, carry):
        cols = aligned(p * 128, 128, 128)
        for qb in range(4):
            keys = (qb + 1) * tok
            rows = slice(qb * tok, (qb + 1) * tok)
            q = qkv[rows, cols]
            g = gh[rows, cols]
            lane = lax.broadcasted_iota(jnp.int32, (tok, 128), 1)
            row = lax.broadcasted_iota(jnp.int32, (tok, keys), 0) + qb * tok
            col = lax.broadcasted_iota(jnp.int32, (tok, keys), 1)
            outs = []
            for h in range(2):
                lanes = (lane < 64) if h == 0 else (lane >= 64)
                qh = jnp.where(lanes, q, jnp.zeros_like(q))
                gg = jnp.where(lanes, g, jnp.zeros_like(g))
                log = jnp.sum(
                    jnp.where(lane == 2 * p + h, lse[rows, :], 0.0), axis=-1, keepdims=True
                )
                s = right_dot(qh, kk[:keys]) * scale
                probs = jnp.exp(jnp.where(col <= row, s, -1e30) - log)
                pg = right_dot(gg, vv[:keys])
                delta = jnp.sum(probs * pg, axis=-1, keepdims=True)
                ds = (probs * (pg - delta)).astype(BF)
                outs.append(dot(ds, kk[:keys]) * scale)
                dk_acc[:keys, :] += left_dot(ds, qh)
                dv_acc[:keys, :] += left_dot(probs.astype(BF), gg)
            dqkv[rows, cols] = jnp.where(lane < 64, outs[0], outs[1]).astype(BF)
        return carry

    lax.fori_loop(0, span // 128, pair, 0)
    dk = dk_acc[...]
    dv = dv_acc[...]
    lane = lax.broadcasted_iota(jnp.int32, dk.shape, 1)
    dqkv[:, span:] = jnp.where(
        lane < 64, (dk + pltpu.roll(dk, 64, 1)) * scale, dv + pltpu.roll(dv, 64, 1)
    ).astype(BF)
    b_copies = [
        net.send(dqkv.at[aligned(zs[m] * tok, tok, 16), :], dback.at[z], ("z", m))
        for m in (2, 3, 1)
    ]
    dback[z] = dqkv[here, :]

    for copy in loads[1:]:
        copy.wait()
    f_2 = []
    for t, name in ((0, Y), (1, X)):
        f_1[t].wait_recv()
        f_k[t] = (hg_v[t, 1].astype(F32) + f_r1[t, 1].astype(F32)).astype(BF)
        f_2.append(net.send(f_k.at[t], f_r2.at[t], name))

    def slots(ref, size):
        w = ref.shape[1] // 2
        return (
            lambda mask, half: ref.at[aligned(dps[mask] * size, size, 16), pl.ds(half * w, w)],
            lambda mask: [ref.at[aligned(dps[mask] * size, size, 16), :]],
        )

    plane_b = Plane(net, *slots(dbr_all, tok))
    plane_p = Plane(net, *slots(dpre_all, tok))
    plane_b.start()
    for copy in b_copies:
        copy.wait_recv()
    for g in range(4):
        for j in range(group // 128):
            last = j == group // 128 - 1
            c_ref, s_ref = (cos_k, sin_k) if last else (cos_q, sin_q)
            part = dback[g, :, j * 128 : (j + 1) * 128].astype(F32)
            start = g * group + j * 128
            dpre_all[mine, start : start + 128] = rotary(part, c_ref[...], -s_ref[...]).astype(BF)
    plane_p.start()
    plane_b.forward()

    def dhat_chunk(i, carry):
        cols = aligned(i * 256, 256, 128)
        dn2[:, cols] = right_dot(dpre_all[mine, :], a1_v[cols, :])
        return carry

    lax.fori_loop(0, width // 256, dhat_chunk, 0)
    tok_out[...] = (dh[...] + norm_back(x_ref[...].astype(F32), dn2[...])).astype(BF)
    plane_p.forward()

    f_1[2].wait_recv()
    f_1[3].wait_recv()
    f_copies = []
    for t in (0, 1):
        f_2[t].wait_recv()
        total = hg_v[t, 0].astype(F32) + f_r1[t, 0].astype(F32) + f_r2[t].astype(F32)
        for i in range(4):
            fs[i, t] = total[i * 64 : (i + 1) * 64, :].astype(BF)
    f_copies = [net.send(fs.at[zs[m]], fb.at[z], ("z", m)) for m in (2, 3, 1)]
    fb[z] = fs[z]

    def z_rows(mask):
        return aligned(zs[mask] * 64, 64, 16)

    def z_start(part, r1):
        return (
            net.send(part.at[z_rows(3), :], r1.at[1], ("z", 1)),
            net.send(part.at[z_rows(1), :], r1.at[0], ("z", 1)),
        )

    def z_middle(sent, part, r1, s, r2):
        sent[0].wait_recv()
        s[...] = (part[z_rows(2), :].astype(F32) + r1[1].astype(F32)).astype(BF)
        return net.send(s, r2, ("z", 2))

    def z_end(sent, far, part, r1, r2, out):
        sent[1].wait_recv()
        far.wait_recv()
        out[...] = part[z_rows(0), :].astype(F32) + r1[0].astype(F32) + r2[...].astype(F32)

    def product(left, right, out):
        turned = left[...].T

        def chunk(i, carry):
            cols = aligned(i * 512, 512, 128)
            out[:, cols] = dot(turned, right[:, cols]).astype(BF)
            return carry

        lax.fori_loop(0, right.shape[1] // 512, chunk, 0)

    for copy in own:
        copy.wait()
    for copy in small:
        copy.wait_recv()
    plane_b.spread()
    plane_b.finish()
    product(att_all, dbr_all, g2_p)
    g2_1 = z_start(g2_p, g2_r1)
    mix_copy.wait_recv()
    mixed[...] = (hmid[...] + mix_own[...] + mix_r[...].astype(F32)).astype(BF)
    plane_p.spread()
    plane_p.finish()
    product(hat_all, dpre_all, g1_p)
    g1_1 = z_start(g1_p, g1_r1)
    g2_2 = z_middle(g2_1, g2_p, g2_r1, g2_s, g2_r2)
    g1_2 = z_middle(g1_1, g1_p, g1_r1, g1_s, g1_r2)
    z_end(g2_1, g2_2, g2_p, g2_r1, g2_r2, g2_out)
    z_end(g1_1, g1_2, g1_p, g1_r1, g1_r2, g1_out)
    for copy in f_copies:
        copy.wait_recv()
    net.finish()


def third_call(x, hmid, cot, dn2, mix_own, mix_far, qkv, lse, tables4, a1, a2, hat1, att, hg):
    tok, width = x.shape
    group = qkv.shape[1]
    wide = 4 * group
    span = group - 128
    ff = hg.shape[-1]
    sds = jax.ShapeDtypeStruct
    v = pltpu.VMEM
    return pl.pallas_call(
        third_kernel,
        name="third",
        out_shape=[
            sds((tok, width), BF), sds((tok, width), BF), sds((64, width), F32),
            sds((64, wide), F32), sds((4, 2, 64, ff), BF),
        ],
        in_specs=[VMEM] * 12 + [ANY] * 5,
        out_specs=[VMEM] * 5,
        scratch_shapes=[
            v((width, wide), BF), v((width, width), BF), v((2, 2, 256, ff), BF),
            v((2, 2, 256, ff), BF), v((2, 256, ff), BF), v((2, 256, ff), BF), v((4, 2, 64, ff), BF),
            v((tok, width), F32), v((8 * tok, width), BF), v((8 * tok, wide), BF),
            v((8 * tok, 256), BF), v((8 * tok, 256), BF),
            v((4, tok, span), BF), v((4 * tok, span), BF), v((4 * tok, group), BF),
            v((4 * tok, 128), F32), v((4 * tok, 128), F32), v((4, tok, group), BF),
            v((tok, width), BF),
            v((256, width), BF), v((256, wide), BF), v((2, 64, width), BF), v((2, 64, wide), BF),
            v((64, width), BF), v((64, wide), BF), v((64, width), BF), v((64, wide), BF),
            pltpu.SemaphoreType.DMA((80,)),
            pltpu.SemaphoreType.DMA((80,)),
        ],
        compiler_params=pltpu.CompilerParams(
            collective_id=3, has_side_effects=True, vmem_limit_bytes=60 * 2**20
        ),
    )(x, hmid, cot, dn2, mix_own, mix_far, qkv, lse, *tables4, a1, a2, hat1, att, hg)


def last_kernel(
    fb, g1, w_first, w_gate, w_up, gain1, gain2,
    gq, gk, gv, g_gate, g_up, g_gain1, g_gain2,
):
    grad = g1[...]
    g_gain1[...] = jnp.sum(grad * w_first[...].astype(F32), axis=1, keepdims=True)
    grad = grad * gain1[...]
    group = grad.shape[1] // 4
    span = group - 128
    lane = lax.broadcasted_iota(jnp.int32, (grad.shape[0], 128), 1)
    for g in range(4):
        gq[:, g * span : (g + 1) * span] = grad[:, g * group : g * group + span]
    for g in (0, 2):
        one = grad[:, g * group + span : (g + 1) * group]
        two = grad[:, (g + 1) * group + span : (g + 2) * group]
        gk[:, g * 64 : g * 64 + 128] = jnp.where(lane < 64, one, pltpu.roll(two, 64, 1))
        gv[:, g * 64 : g * 64 + 128] = jnp.where(lane < 64, pltpu.roll(one, 64, 1), two)
    size = fb.shape[-1] // 8
    total = jnp.zeros_like(g_gain2)
    for t, (out, weight) in enumerate(((g_gate, w_gate), (g_up, w_up))):
        for d in range(0, 8, 2):
            parts = [
                fb[i, t, :, e * size : (e + 1) * size].astype(F32) for e in (d, d + 1) for i in range(4)
            ]
            joined = jnp.concatenate(parts, axis=1)
            cols = pl.ds(d * 4 * size, 8 * size)
            total += jnp.sum(joined * weight[:, cols].astype(F32), axis=1, keepdims=True)
            out[:, cols] = joined * gain2[...]
    g_gain2[...] = total


def last_call(fb, g1, w_first, w_gate, w_up, gain1, gain2):
    rows, ff = w_gate.shape
    width = w_first.shape[1] - 512
    sds = jax.ShapeDtypeStruct
    return pl.pallas_call(
        last_kernel,
        name="last",
        out_shape=[
            sds((rows, width), F32), sds((rows, 256), F32), sds((rows, 256), F32),
            sds((rows, ff), F32), sds((rows, ff), F32), sds((rows, 1), F32), sds((rows, 1), F32),
        ],
        in_specs=[VMEM] * 7,
        out_specs=[VMEM] * 7,
        compiler_params=pltpu.CompilerParams(vmem_limit_bytes=40 * 2**20),
    )(fb, g1, w_first, w_gate, w_up, gain1, gain2)


def shards(
    tokens, norm_first, w_query, w_key, w_value, w_out, norm_second, w_gate, w_up, w_down, cotangent
):
    dp, seq = Axis("dp"), Axis("seq")
    groups = seq.size
    count, width = tokens.shape
    ff = w_gate.shape[1]
    rows = w_gate.shape[0]
    per = H // groups
    span = per * HEAD_SIZE
    gain1 = norm_first.astype(F32)[:, None]
    gain2 = norm_second.astype(F32)[:, None]

    w_first = jnp.concatenate(
        [
            part
            for g in range(groups)
            for part in (
                w_query[:, g * span : (g + 1) * span],
                w_key[:, g * HEAD_SIZE : (g + 1) * HEAD_SIZE],
                w_value[:, g * HEAD_SIZE : (g + 1) * HEAD_SIZE],
            )
        ],
        axis=1,
    )
    wide = w_first.shape[1]
    group = wide // groups

    def by_part(weight):
        scaled = (weight.astype(F32) * gain2).astype(BF)
        parts = scaled.reshape(rows, dp.size, groups, ff // dp.size // groups)
        return parts.transpose(2, 0, 1, 3).reshape(groups, rows, ff // groups)

    cosine, sine = tables(seq.me * count + jnp.arange(count))
    cosine, sine = cosine[:, 0], sine[:, 0]
    one, zero = jnp.ones_like(cosine), jnp.zeros_like(cosine)
    tables4 = [
        jnp.concatenate(parts, axis=1)
        for parts in (
            [cosine] * 4,
            [-sine, sine] * 2,
            [cosine, cosine, one, one],
            [-sine, sine, zero, zero],
        )
    ]
    wg, wd, a1, a2, c_all, n_all, qkv, lse, att, hmid, hat1 = first_call(
        tokens,
        (w_first.astype(F32) * gain1).astype(BF),
        w_out,
        jnp.stack([by_part(w_gate), by_part(w_up)], axis=1),
        w_down,
        cotangent,
        tables4,
    )
    dhat2, mix_own, mix_far, hg, grad_down = second_call(n_all, c_all, wg, wd)
    grad_tokens, mixed, grad_out, grad_first, parts = third_call(
        tokens, hmid, cotangent, dhat2, mix_own, mix_far, qkv, lse, tables4, a1, a2, hat1, att, hg
    )
    grad_query, grad_key, grad_value, grad_gate, grad_up, grad_gain1, grad_gain2 = last_call(
        parts, grad_first, w_first, w_gate, w_up, gain1, gain2
    )
    return (
        mixed,
        grad_tokens,
        grad_gain1[:, 0],
        grad_query,
        grad_key,
        grad_value,
        grad_out,
        grad_gain2[:, 0],
        grad_gate,
        grad_up,
        grad_down,
    )


def solution(mesh):
    special = mesh.shape['dp'] == 8 and mesh.shape['seq'] == KEY_VALUE_HEADS
    rows = P(("dp", "seq"), None)
    line = P(("dp", "seq"))
    return jax.shard_map(
        shards if special else general_shards,
        mesh=mesh,
        in_specs=(rows, line, rows, rows, rows, rows, line, rows, rows, rows, rows),
        out_specs=(rows, rows, line, rows, rows, rows, rows, line, rows, rows, rows),
        check_vma=False,
    )
```

```python
import jax
import jax.numpy as jnp
from jax import lax
from jax.experimental import pallas as pl
from jax.experimental.pallas import tpu as pltpu
from jax.sharding import PartitionSpec as P

H = 32
KEY_VALUE_HEADS = 4
HEAD_SIZE = 64
EPS = 1e-05
BF = jnp.bfloat16
F32 = jnp.float32


def tables(positions):
    freq = 10000.0 ** (-jnp.arange(0, HEAD_SIZE // 2, dtype=F32) * 2.0 / HEAD_SIZE)
    angle = positions.astype(F32)[:, None] * freq[None, :]
    return (jnp.cos(angle)[:, None, :], jnp.sin(angle)[:, None, :])


def rotate(heads, cosine, sine):
    half = heads.shape[-1] // 2
    first = heads[..., :half]
    second = heads[..., half:]
    return jnp.concatenate(
        [first * cosine - second * sine, second * cosine + first * sine], axis=-1
    )


def dot(left, right):
    return jnp.dot(left, right, preferred_element_type=F32)


def left_dot(left, right):
    return lax.dot_general(left, right, (((0,), (0,)), ((), ())), preferred_element_type=F32)


def right_dot(left, right):
    return lax.dot_general(left, right, (((1,), (1,)), ((), ())), preferred_element_type=F32)


def bits_of(count):
    return [1 << k for k in range(count.bit_length() - 1)]


class Axis:
    def __init__(self, name):
        self.name = name
        self.size = lax.axis_size(name)
        self.me = lax.axis_index(name)

    def swap(self, value, mask):
        return lax.ppermute(value, self.name, [(i, i ^ mask) for i in range(self.size)])

    def all(self, value):
        return [value if m == 0 else self.swap(value, m) for m in range(self.size)]

    def exchange(self, stacked):
        return [
            lax.dynamic_index_in_dim(stacked, self.me ^ m, 0, keepdims=False)
            if m == 0
            else self.swap(
                lax.dynamic_index_in_dim(stacked, self.me ^ m, 0, keepdims=False), m
            )
            for m in range(self.size)
        ]

    def natural(self, pieces):
        stack = jnp.stack(pieces)
        return [
            lax.dynamic_index_in_dim(stack, self.me ^ i, 0, keepdims=False)
            for i in range(self.size)
        ]


def orders(size):
    even = [m for m in range(size) if m % 2 == 0]
    return even, [m + 1 for m in even]


def chip_bits(size, turn):
    bits = bits_of(size)[1:]
    return bits if turn == 0 else bits[::-1]


def gather_chips(dp, piece, turn):
    pieces = {0: piece}
    for bit in chip_bits(dp.size, turn):
        pieces.update({m ^ bit: dp.swap(p, bit) for m, p in list(pieces.items())})
    return pieces


def gather_rows(dp, piece, turn):
    pieces = gather_chips(dp, piece, turn)
    even = jnp.concatenate([pieces[m] for m in orders(dp.size)[0]], axis=0)
    return even, dp.swap(even, 1)


def scatter_chips(dp, blocks, turn):
    for bit in chip_bits(dp.size, turn):
        for m in [m for m in blocks if m & bit]:
            other = dp.swap(blocks.pop(m).astype(BF), bit)
            blocks[m ^ bit] = blocks[m ^ bit].astype(F32) + other.astype(F32)
    return blocks[0]


def scatter_rows(dp, even_fn, odd, turn):
    rows = odd.shape[0] * 2 // dp.size
    other = dp.swap(odd, 1)
    even = (even_fn() + other.astype(F32)).astype(BF)
    blocks = {
        m: even[i * rows : (i + 1) * rows] for i, m in enumerate(orders(dp.size)[0])
    }
    return scatter_chips(dp, blocks, turn)


def mask_columns(dp, value):
    width = value.shape[1] // dp.size
    return tuple(
        jnp.concatenate(
            [lax.dynamic_slice_in_dim(value, (dp.me ^ m) * width, width, 1) for m in group],
            axis=1,
        )
        for group in orders(dp.size)
    )


def natural_columns(dp, even, odd):
    both = jnp.concatenate([even, odd], axis=1)
    width = both.shape[1] // dp.size
    half = dp.size // 2
    parts = []
    for i in range(dp.size):
        mask = dp.me ^ i
        place = mask // 2 + (mask % 2) * half
        parts.append(lax.dynamic_slice_in_dim(both, place * width, width, 1))
    return jnp.concatenate(parts, axis=1)


def attend(queries, keys, values, visible):
    scores = jnp.einsum("qhd,kd->hqk", queries, keys, preferred_element_type=F32)
    scores = jnp.where(visible[None], scores * HEAD_SIZE ** (-0.5), -1e30)
    top = jnp.max(scores, axis=-1, keepdims=True)
    expo = jnp.exp(scores - top)
    total = jnp.sum(expo, axis=-1, keepdims=True)
    probs = (expo / total).astype(BF)
    result = jnp.einsum("hqk,kd->qhd", probs, values, preferred_element_type=F32)
    return result.astype(BF), top + jnp.log(total)


def attend_back(queries, keys, values, grad_heads, logsum, visible):
    scale = HEAD_SIZE ** (-0.5)
    scores = jnp.einsum("qhd,kd->hqk", queries, keys, preferred_element_type=F32)
    scores = jnp.where(visible[None], scores * scale, -1e30)
    probs = jnp.exp(scores - logsum)
    pgrad = jnp.einsum("qhd,kd->hqk", grad_heads, values, preferred_element_type=F32)
    delta = jnp.sum(probs * pgrad, axis=-1, keepdims=True)
    sgrad = (probs * (pgrad - delta)).astype(BF)
    qgrad = jnp.einsum("hqk,kd->qhd", sgrad, keys, preferred_element_type=F32) * scale
    kgrad = jnp.einsum("hqk,qhd->kd", sgrad, queries, preferred_element_type=F32) * scale
    vgrad = jnp.einsum("hqk,qhd->kd", probs.astype(BF), grad_heads, preferred_element_type=F32)
    return qgrad.astype(BF), kgrad.astype(BF), vgrad.astype(BF)


def general_shards(
    tokens, norm_first, w_query, w_key, w_value, w_out, norm_second, w_gate, w_up, w_down, cotangent
):
    dp, seq = Axis("dp"), Axis("seq")
    groups = seq.size
    count, width = tokens.shape
    ff = w_gate.shape[1]
    per = H // groups
    repeat = groups // KEY_VALUE_HEADS
    heads_wide = H * HEAD_SIZE
    keys_wide = KEY_VALUE_HEADS * HEAD_SIZE
    gain1 = norm_first.astype(F32)[:, None]
    gain2 = norm_second.astype(F32)[:, None]

    w_first = jnp.concatenate([w_query, w_key, w_value], axis=1)
    w_first_scaled = (w_first.astype(F32) * gain1).astype(BF)
    wide = w_first.shape[1]

    def by_part(weight):
        rows = weight.shape[0]
        scaled = (weight.astype(F32) * gain2).astype(BF)
        parts = scaled.reshape(rows, dp.size, groups, ff // dp.size // groups)
        return parts.transpose(2, 0, 1, 3).reshape(groups, rows, ff // groups)

    down = [gather_chips(dp, w_down[:, t * width // 2 : (t + 1) * width // 2], t) for t in (0, 1)]
    first_rows = jnp.concatenate(seq.natural(seq.all(w_first_scaled)), axis=0)
    first = [gather_rows(dp, first_rows[:, t * wide // 2 : (t + 1) * wide // 2], t) for t in (0, 1)]
    out_rows = jnp.concatenate(seq.natural(seq.all(w_out)), axis=0)
    outw = [gather_rows(dp, out_rows[:, t * width // 2 : (t + 1) * width // 2], t) for t in (0, 1)]
    gate_up = seq.exchange(jnp.stack([by_part(w_gate), by_part(w_up)], axis=1))
    gate_up = jnp.concatenate(seq.natural(gate_up), axis=1)
    (gate_even, gate_odd), (up_even, up_odd) = [
        gather_rows(dp, gate_up[t], t) for t in (0, 1)
    ]
    cot_all = jnp.concatenate(seq.all(cotangent), axis=0)

    rows_down = w_down.shape[0]
    down_full = []
    for t in (0, 1):
        even = jnp.stack([down[t][m] for m in orders(dp.size)[0]])
        odd = dp.swap(even, 1)
        full = jnp.zeros((rows_down * dp.size, width // 2), BF)
        for i, m in enumerate(orders(dp.size)[0]):
            full = lax.dynamic_update_slice(full, even[i], ((dp.me ^ m) * rows_down, 0))
            full = lax.dynamic_update_slice(full, odd[i], ((dp.me ^ m ^ 1) * rows_down, 0))
        down_full.append(full)

    inputs = tokens.astype(F32)
    inv1 = lax.rsqrt(jnp.mean(inputs * inputs, axis=-1, keepdims=True) + EPS)
    hat1 = (inputs * inv1).astype(BF)
    hat1_even, hat1_odd = mask_columns(dp, hat1)
    cosine, sine = tables(seq.me * count + jnp.arange(count))
    pre = jnp.concatenate(
        [dot(hat1_even, first[t][0]) + dot(hat1_odd, first[t][1]) for t in (0, 1)], axis=1
    )
    qpre = pre[:, :heads_wide].reshape(count, H, HEAD_SIZE)
    kpre = pre[:, heads_wide : heads_wide + keys_wide].reshape(count, KEY_VALUE_HEADS, HEAD_SIZE)
    vround = pre[:, heads_wide + keys_wide :].astype(BF)
    qrot = rotate(qpre, cosine, sine).reshape(count, heads_wide).astype(BF)
    krot = rotate(kpre, cosine, sine).reshape(count, keys_wide).astype(BF)
    span = per * HEAD_SIZE
    packed = []
    for g in range(groups):
        head = g // repeat * HEAD_SIZE
        packed.append(
            jnp.concatenate(
                [
                    qrot[:, g * span : (g + 1) * span],
                    krot[:, head : head + HEAD_SIZE],
                    vround[:, head : head + HEAD_SIZE],
                ],
                axis=1,
            )
        )
    qkv = jnp.concatenate(seq.exchange(jnp.stack(packed)), axis=0)
    length = qkv.shape[0]
    queries = qkv[:, :span].reshape(length, per, HEAD_SIZE)
    keys = qkv[:, span : span + HEAD_SIZE]
    values = qkv[:, span + HEAD_SIZE :]
    place = jnp.concatenate(
        [(seq.me ^ m) * count + jnp.arange(count, dtype=jnp.int32) for m in range(groups)]
    )
    visible = place[None, :] <= place[:, None]
    out_heads, logsum = attend(queries, keys, values, visible)
    out_heads = out_heads.reshape(length, span)

    def back_home(value):
        return seq.natural(
            [
                value[:count] if m == 0 else seq.swap(value[m * count : (m + 1) * count], m)
                for m in range(groups)
            ]
        )

    attn = jnp.concatenate(back_home(out_heads), axis=1)
    attn_even, attn_odd = mask_columns(dp, attn)
    branch = jnp.concatenate(
        [dot(attn_even, outw[t][0]) + dot(attn_odd, outw[t][1]) for t in (0, 1)], axis=1
    )
    hmid = inputs + branch

    inv2 = lax.rsqrt(jnp.mean(hmid * hmid, axis=-1, keepdims=True) + EPS)
    hat2 = jnp.concatenate(mask_columns(dp, (hmid * inv2).astype(BF)), axis=1)
    hat2_all = jnp.concatenate(seq.all(hat2), axis=0)
    hat2_even, hat2_odd = hat2_all[:, : width // 2], hat2_all[:, width // 2 :]
    gate = dot(hat2_even, gate_even) + dot(hat2_odd, gate_odd)
    upper = dot(hat2_even, up_even) + dot(hat2_odd, up_odd)
    sigma = jax.nn.sigmoid(gate)
    hidden = (gate * sigma * upper).astype(BF)
    halves = [cot_all[:, : width // 2], cot_all[:, width // 2 :]]
    dhidden = right_dot(halves[0], down_full[0]) + right_dot(halves[1], down_full[1])
    dgate = (dhidden * upper * sigma * (1.0 + gate * (1.0 - sigma))).astype(BF)
    dupper = (dhidden * gate * sigma).astype(BF)
    dhat2 = jnp.concatenate(
        [
            right_dot(dgate, gate_even) + right_dot(dupper, up_even),
            right_dot(dgate, gate_odd) + right_dot(dupper, up_odd),
        ],
        axis=1,
    ).astype(BF)

    def sum_home(value):
        total = value[:count].astype(F32)
        for m in range(1, groups):
            total = total + seq.swap(value[m * count : (m + 1) * count], m).astype(F32)
        return total

    dhat2 = sum_home(dhat2)
    dgain2 = natural_columns(dp, dhat2[:, : width // 2], dhat2[:, width // 2 :])
    inner = jnp.mean(hmid * dgain2, axis=-1, keepdims=True)
    dh = cotangent.astype(F32) + inv2 * dgain2 - hmid * inv2 * inv2 * inv2 * inner
    dbranch = dh.astype(BF)

    dattn = natural_columns(
        dp,
        *[
            sum(
                right_dot(dbranch[:, t * width // 2 : (t + 1) * width // 2], outw[t][s])
                for t in (0, 1)
            ).astype(BF)
            for s in (0, 1)
        ],
    )
    grad_heads = jnp.concatenate(
        seq.exchange(dattn.reshape(count, groups, span).transpose(1, 0, 2)), axis=0
    ).reshape(length, per, HEAD_SIZE)
    dq, dk, dv = attend_back(queries, keys, values, grad_heads, logsum, visible)
    dqkv = back_home(jnp.concatenate([dq.reshape(length, span), dk, dv], axis=1))
    dq = jnp.concatenate([piece[:, :span] for piece in dqkv], axis=1)
    dk = [piece[:, span : span + HEAD_SIZE].astype(F32) for piece in dqkv]
    dv = [piece[:, span + HEAD_SIZE :].astype(F32) for piece in dqkv]
    dk = jnp.stack(
        [sum(dk[i * repeat : (i + 1) * repeat]) for i in range(KEY_VALUE_HEADS)], axis=1
    )
    dv = jnp.concatenate(
        [sum(dv[i * repeat : (i + 1) * repeat]) for i in range(KEY_VALUE_HEADS)], axis=1
    )
    dq = rotate(dq.astype(F32).reshape(count, H, HEAD_SIZE), cosine, -sine)
    dk = rotate(dk, cosine, -sine)
    dpre = jnp.concatenate(
        [dq.reshape(count, heads_wide), dk.reshape(count, keys_wide), dv], axis=1
    ).astype(BF)
    dhalf = [dpre[:, t * wide // 2 : (t + 1) * wide // 2] for t in (0, 1)]
    dhat1 = [sum(right_dot(dhalf[t], first[t][s]) for t in (0, 1)) for s in (0, 1)]
    dgain1 = natural_columns(dp, *dhat1)
    inner = jnp.mean(inputs * dgain1, axis=-1, keepdims=True)
    grad_inputs = dh + inv1 * dgain1 - inputs * inv1 * inv1 * inv1 * inner

    mixed_part = jnp.concatenate([dot(hidden, down_full[t]) for t in (0, 1)], axis=1).astype(BF)
    mixed = hmid + sum_home(mixed_part)

    grad_down = []
    for t in (0, 1):
        part = left_dot(hidden, halves[t]).astype(BF)
        blocks = [
            lax.dynamic_slice_in_dim(part, (dp.me ^ m) * rows_down, rows_down, 0)
            for m in range(dp.size)
        ]
        even, odd = orders(dp.size)
        other = dp.swap(jnp.stack([blocks[m] for m in odd]), 1)
        summed = {
            m: (blocks[m].astype(F32) + other[i].astype(F32)).astype(BF)
            for i, m in enumerate(even)
        }
        grad_down.append(scatter_chips(dp, summed, t))
    grad_down = jnp.concatenate(grad_down, axis=1)

    def ff_grad(grad, turn):
        odd = left_dot(hat2_odd, grad).astype(BF)
        return scatter_rows(dp, lambda: left_dot(hat2_even, grad), odd, turn)

    rows = w_gate.shape[0]
    sent = jnp.stack([ff_grad(dgate, 0).astype(BF), ff_grad(dupper, 1).astype(BF)])
    sent = sent.reshape(2, groups, rows, ff // groups).transpose(1, 0, 2, 3)
    got = jnp.stack(seq.natural(seq.exchange(sent)))
    got = got.reshape(groups, 2, rows, dp.size, ff // groups // dp.size)
    got = got.transpose(1, 2, 3, 0, 4).reshape(2, rows, ff).astype(F32)
    grad_gate, grad_up = got[0] * gain2, got[1] * gain2
    grad_gain2 = jnp.sum(got[0] * w_gate.astype(F32) + got[1] * w_up.astype(F32), axis=1)

    def proj_grad(even, odd, grads):
        parts = []
        for t in (0, 1):
            send = left_dot(odd, grads[t]).astype(BF)
            parts.append(
                scatter_rows(dp, lambda grad=grads[t]: left_dot(even, grad), send, t)
            )
        own = jnp.concatenate(parts, axis=1)
        own = own.astype(BF).reshape(groups, rows, own.shape[1])
        return sum(piece.astype(F32) for piece in seq.exchange(own))

    grad_out = proj_grad(
        attn_even,
        attn_odd,
        [dbranch[:, t * width // 2 : (t + 1) * width // 2] for t in (0, 1)],
    )
    grad_first = proj_grad(hat1_even, hat1_odd, dhalf)
    grad_gain1 = jnp.sum(grad_first * w_first.astype(F32), axis=1)
    grad_first = grad_first * gain1
    return (
        mixed.astype(BF),
        grad_inputs.astype(BF),
        grad_gain1,
        grad_first[:, :heads_wide],
        grad_first[:, heads_wide : heads_wide + keys_wide],
        grad_first[:, heads_wide + keys_wide :],
        grad_out,
        grad_gain2,
        grad_gate,
        grad_up,
        grad_down,
    )


MESH = pl.DeviceIdType.MESH
ANY = pl.BlockSpec(memory_space=pl.ANY)
VMEM = pl.BlockSpec(memory_space=pltpu.VMEM)


class Net:
    def __init__(self, send_sems, recv_sems):
        self.send_sems, self.recv_sems, self.used = send_sems, recv_sems, 0
        self.open = []
        dp, z = lax.axis_index("dp"), lax.axis_index("seq")
        self.dp, self.z = dp, z
        self.dps = {
            0: dp,
            1: dp + 1 - 2 * lax.rem(dp, 2),
            2: dp + 2 - 4 * lax.rem(lax.div(dp, 2), 2),
            4: lax.rem(dp + 4, 8),
        }
        self.dps[6] = lax.rem(self.dps[2] + 4, 8)
        for mask in (2, 4, 6):
            self.dps[mask + 1] = self.dps[mask] + 1 - 2 * lax.rem(dp, 2)
        self.zs = {0: z, 1: z + 1 - 2 * lax.rem(z, 2), 2: lax.rem(z + 2, 4), 3: 3 - z}

    def target(self, name):
        kind, mask = name
        return (self.dps[mask], self.z) if kind == "d" else (self.dp, self.zs[mask])

    def barrier(self, names):
        sem = pltpu.get_barrier_semaphore()
        for name in names:
            pl.semaphore_signal(sem, inc=1, device_id=self.target(name), device_id_type=MESH)
        pl.semaphore_wait(sem, len(names))

    def send(self, src, dst, name):
        copy = pltpu.make_async_remote_copy(
            src_ref=src,
            dst_ref=dst,
            send_sem=self.send_sems.at[self.used],
            recv_sem=self.recv_sems.at[self.used],
            device_id=self.target(name),
            device_id_type=MESH,
        )
        self.used += 1
        copy.start()
        self.open.append(copy)
        return copy

    def local(self, src, dst):
        copy = pltpu.make_async_copy(src, dst, self.send_sems.at[self.used])
        self.used += 1
        copy.start()
        return copy

    def finish(self):
        for copy in self.open:
            copy.wait_send()


X, Y, CORE = ("d", 2), ("d", 4), ("d", 1)
PARTNERS = [X, Y, CORE, ("z", 1), ("z", 2), ("z", 3)]


class Plane:
    def __init__(self, net, at, both):
        self.net, self.at, self.both = net, at, both

    def push(self, mask, half, name):
        ref = self.at(mask, half)
        return self.net.send(ref, ref, name)

    def start(self):
        self.xa = self.push(0, 0, X)
        self.yb = self.push(0, 1, Y)
        self.ya = self.push(0, 0, Y)
        self.xb = self.push(0, 1, X)
        self.cores = [self.core(0)]

    def core(self, mask):
        return [self.net.send(ref, ref, CORE) for ref in self.both(mask)]

    def forward(self):
        self.xa.wait_recv()
        self.ya2 = self.push(2, 0, Y)
        self.yb.wait_recv()
        self.xb2 = self.push(4, 1, X)

    def spread(self):
        self.ya.wait_recv()
        self.cores.append(self.core(4))
        self.xb.wait_recv()
        self.cores.append(self.core(2))
        self.ya2.wait_recv()
        self.xb2.wait_recv()
        self.cores.append(self.core(6))

    def finish(self):
        for copies in self.cores:
            for copy in copies:
                copy.wait_recv()


def rotary(value, cosine, sine):
    lane = lax.broadcasted_iota(jnp.int32, value.shape, 1)
    partner = jnp.where(
        lax.rem(lane, 64) < 32, pltpu.roll(value, 96, 1), pltpu.roll(value, 32, 1)
    )
    return value * cosine + partner * sine


def rms(value):
    return lax.rsqrt(jnp.mean(value * value, axis=-1, keepdims=True) + EPS)


def twice(pair):
    lane = lax.broadcasted_iota(jnp.int32, pair.shape, 1)
    other = pltpu.roll(pair.astype(F32), 64, 1).astype(BF)
    return jnp.where(lane < 64, pair, other), jnp.where(lane < 64, other, pair)


def aligned(start, count, unit):
    return pl.ds(pl.multiple_of(start, unit), count)


class Sums:
    def __init__(self, net, part, r1, mid, r2):
        self.net, self.part, self.r1, self.mid, self.r2 = net, part, r1, mid, r2
        self.width = r2.shape[-1]

    def cols(self, side):
        return pl.ds(side * self.width, self.width)

    def block(self, mask):
        return lax.div(self.net.dps[mask], 2)

    def push(self, mask, side, place, name):
        src = self.part.at[self.block(mask), :, self.cols(side)]
        return self.net.send(src, self.r1.at[side, place], name)

    def first(self, mask):
        if mask == 6:
            self.near = [self.push(6, 0, 1, X), self.push(6, 1, 1, Y)]
        elif mask == 2:
            self.own = [self.push(2, 0, 0, X)]
        elif mask == 4:
            self.own.append(self.push(4, 1, 0, Y))

    def second(self):
        self.far = []
        for side, (mask, name) in enumerate(((4, Y), (2, X))):
            self.near[side].wait_recv()
            mine = self.part[self.block(mask), :, self.cols(side)]
            self.mid[side] = (mine.astype(F32) + self.r1[side, 1].astype(F32)).astype(BF)
            self.far.append(self.net.send(self.mid.at[side], self.r2.at[side], name))

    def total(self, side):
        self.own[side].wait_recv()
        self.far[side].wait_recv()
        mine = self.part[self.block(0), :, self.cols(side)]
        return mine.astype(F32) + self.r1[side, 0].astype(F32) + self.r2[side].astype(F32)


def first_kernel(
    x_ref, wq, wk, wv, gain1, w_gate, w_up, gain2, cos_q, sin_q, cos_k, sin_k, wo, wd, cot,
    wg_all, wd_all, wq_out, wo_out, hat_out, c_all, n_all, qkv_out, att_out, lse, hmid,
    wq_s, wf, wq_v, wo_v, hat, qkv_send, qkv, heads, att, part, r1, mid, r2, hat2,
    send_sems, recv_sems,
):
    net = Net(send_sems, recv_sems)
    dp, z, dps, zs = net.dp, net.z, net.dps, net.zs
    tok, width = x_ref.shape
    group = qkv.shape[1]
    span = heads.shape[1]
    ff = wf.shape[-1]
    core, chip = lax.rem(dp, 2), lax.div(dp, 2)
    here = aligned(z * tok, tok, 16)

    own = [
        net.local(wo, wo_v.at[core, z]),
        net.local(wd, wd_all.at[aligned(dp * 176, 176, 16), :]),
        net.local(cot, c_all.at[0, here, :]),
    ]
    net.barrier(PARTNERS + [("d", 6)])

    scale = gain1[...]
    lane = lax.broadcasted_iota(jnp.int32, (wq.shape[0], 128), 1)
    for g in range(4):
        wq_s[g, :, :span] = (wq[:, g * span : (g + 1) * span].astype(F32) * scale).astype(BF)
        start = g // 2 * 128
        k = wk[:, start : start + 128].astype(F32)
        v = wv[:, start : start + 128].astype(F32)
        if g % 2 == 0:
            both = jnp.where(lane < 64, k, pltpu.roll(v, 64, 1))
        else:
            both = jnp.where(lane < 64, pltpu.roll(k, 64, 1), v)
        wq_s[g, :, span:] = (both * scale).astype(BF)

    def chip_of(mask):
        return lax.div(dps[mask], 2)

    w_1 = [
        net.send(wq_s.at[chip_of(m)], wq_v.at[chip, core, z], ("d", m)) for m in (6, 2, 4)
    ]
    own_q = net.local(wq_s.at[chip], wq_v.at[chip, core, z])
    x = x_ref[...].astype(F32)
    hat[chip] = (x * rms(x)).astype(BF)

    def half_of(ref, side):
        w = ref.shape[-1] // 2
        return pl.ds(side * w, w)

    def block(ref, size, cores):
        def at(mask, side):
            return ref.at[aligned(dps[mask] * size, size, 16), half_of(ref, side)]

        return at, lambda mask: [ref.at[aligned(dps[mask] * size, size, 16), :]] if cores else []

    plane_h = Plane(net, lambda m, s: hat.at[chip_of(m), :, half_of(hat, s)], lambda m: [])
    plane_h.start()
    down = Plane(net, *block(wd_all, 176, True))
    own[1].wait()
    down.start()

    scale = gain2[...]
    size = ff // 8
    for t, weight in enumerate((w_gate, w_up)):
        for i in range(4):
            parts = [weight[:, (d * 4 + i) * size : (d * 4 + i + 1) * size] for d in range(8)]
            joined = jnp.concatenate([p.astype(F32) for p in parts], axis=1)
            wf[i, t] = (joined * scale).astype(BF)
    own_f = net.local(wf.at[z], wg_all.at[:, aligned((dp * 4 + z) * 64, 64, 16), :])

    own_q.wait()
    for copy in w_1:
        copy.wait_recv()

    def wq_at(mask):
        return wq_v.at[:, core, zs[mask]]

    def wo_at(mask):
        return wo_v.at[core, zs[mask]]

    class Line:
        def __init__(self, at):
            self.at = at
            self.far = self.push(0, ("z", 2))
            self.near = self.push(0, ("z", 1))
            self.cores = [self.push(0, CORE)]

        def push(self, mask, name):
            return net.send(self.at(mask), self.at(mask), name)

        def forward(self):
            self.far.wait_recv()
            self.last = self.push(2, ("z", 1))
            self.cores.append(self.push(2, CORE))

        def spread(self):
            self.near.wait_recv()
            self.cores.append(self.push(1, CORE))
            self.last.wait_recv()
            self.cores.append(self.push(3, CORE))

        def finish(self):
            for copy in self.cores:
                copy.wait_recv()

    line_q = Line(wq_at)
    plane_h.forward()
    line_q.forward()
    f_place = wg_all.at[:, aligned((dp * 4 + z) * 64, 64, 16), :]
    f_copies = [net.send(wf.at[zs[m]], f_place, ("z", m)) for m in (2, 3, 1)]
    plane_h.spread()
    line_q.spread()
    own[0].wait()
    line_o = Line(wo_at)
    down.forward()
    line_q.finish()

    weight = wq_v[...].reshape(width, group)

    def project(s, carry):
        pre = jnp.dot(hat[s], weight, preferred_element_type=F32)
        for j in range(group // 128):
            last = j == group // 128 - 1
            c_ref, s_ref = (cos_k, sin_k) if last else (cos_q, sin_q)
            value = rotary(pre[:, j * 128 : (j + 1) * 128], c_ref[...], s_ref[...])
            qkv_send[s, :, j * 128 : (j + 1) * 128] = value.astype(BF)
        return carry

    lax.fori_loop(0, 4, project, 0)
    q_copies = [net.send(qkv_send.at[zs[m]], qkv.at[here, :], ("z", m)) for m in (2, 3, 1)]
    own_q = net.local(qkv_send.at[z], qkv.at[here, :])
    line_o.forward()
    down.spread()
    own_f.wait()
    for copy in f_copies:
        copy.wait_recv()
    plane_f = Plane(
        net,
        lambda m, s: wg_all.at[s, aligned(dps[m] * 256, 256, 16), :],
        lambda m: [wg_all.at[s, aligned(dps[m] * 256, 256, 16), :] for s in (0, 1)],
    )
    plane_f.start()
    own_q.wait()
    for copy in q_copies:
        copy.wait_recv()

    kk, vv = twice(qkv[:, span:])

    def pair(p, carry):
        cols = aligned(p * 128, 128, 128)
        for qb in range(4):
            keys = (qb + 1) * tok
            q = qkv[qb * tok : (qb + 1) * tok, cols]
            lane = lax.broadcasted_iota(jnp.int32, (tok, 128), 1)
            row = lax.broadcasted_iota(jnp.int32, (tok, keys), 0) + qb * tok
            col = lax.broadcasted_iota(jnp.int32, (tok, keys), 1)
            outs = []
            for h in range(2):
                mine = (lane < 64) if h == 0 else (lane >= 64)
                qh = jnp.where(mine, q, jnp.zeros_like(q))
                s = right_dot(qh, kk[:keys]) * HEAD_SIZE ** (-0.5)
                s = jnp.where(col <= row, s, -1e30)
                top = jnp.max(s, axis=-1, keepdims=True)
                e = jnp.exp(s - top)
                total = jnp.sum(e, axis=-1, keepdims=True)
                probs = (e * (1.0 / total)).astype(BF)
                outs.append(dot(probs, vv[:keys]))
                old = lse[qb * tok : (qb + 1) * tok, :]
                lse[qb * tok : (qb + 1) * tok, :] = jnp.where(
                    lane == 2 * p + h, top + jnp.log(total), old
                )
            heads[qb * tok : (qb + 1) * tok, cols] = jnp.where(
                lane < 64, outs[0], outs[1]
            ).astype(BF)
        return carry

    lse[...] = jnp.zeros_like(lse)
    lax.fori_loop(0, span // 128, pair, 0)
    h_copies = [
        net.send(heads.at[aligned(zs[m] * tok, tok, 16), :], att.at[z], ("z", m))
        for m in (2, 3, 1)
    ]
    own_h = net.local(heads.at[here, :], att.at[z])

    def tokens_start(src, ref):
        place = ref.at[0, here, :]
        far = net.send(src, place, ("z", 2))
        near = net.send(src, place, ("z", 1))
        return far, near, net.send(src, ref.at[1, here, :], CORE)

    def tokens_push(ref, mask, name):
        there = aligned(zs[mask] * tok, tok, 16)
        return net.send(ref.at[0, there, :], ref.at[1 if name == CORE else 0, there, :], name)

    def tokens_forward(ref, far):
        far.wait_recv()
        return [tokens_push(ref, 2, ("z", 1)), tokens_push(ref, 2, CORE)]

    def tokens_end(ref, near, last):
        near.wait_recv()
        last[0].wait_recv()
        return [tokens_push(ref, m, CORE) for m in (1, 3)]

    line_o.spread()
    line_o.finish()
    own_h.wait()
    for copy in h_copies:
        copy.wait_recv()
    c_far, c_near, c_own = tokens_start(cot, c_all)

    sums = Sums(net, part, r1, mid, r2)
    for m in (6, 2, 4, 0):
        s = chip_of(m)
        for c in range(4):
            cols = pl.ds(c * (width // 4), width // 4)
            weight = wo_v[:, :, :, cols].reshape(span, width // 4)
            part[s, :, cols] = dot(att[s], weight).astype(BF)
        sums.first(m)
    sums.second()
    plane_f.forward()
    own[2].wait()
    c_last = tokens_forward(c_all, c_far)
    for side in (0, 1):
        cols = half_of(hmid, side)
        hmid[:, cols] = x_ref[:, cols].astype(F32) + sums.total(side)
    value = hmid[...]
    hat2[...] = (value * rms(value)).astype(BF)
    own_n = net.local(hat2, n_all.at[0, here, :])
    n_far, n_near, n_own = tokens_start(hat2, n_all)
    outs = [
        net.local(wq_v, wq_out), net.local(wo_v, wo_out), net.local(qkv, qkv_out),
        net.local(att, att_out), net.local(hat, hat_out),
    ]
    c_core = tokens_end(c_all, c_near, c_last)
    n_last = tokens_forward(n_all, n_far)
    plane_f.spread()
    n_core = tokens_end(n_all, n_near, n_last)
    down.finish()
    plane_f.finish()
    for copy in [n_own, c_own, n_last[1], c_last[1]] + n_core + c_core:
        copy.wait_recv()
    own_n.wait()
    for copy in outs:
        copy.wait()
    net.finish()


def first_call(x, wq, wk, wv, gain1, w_gate, w_up, gain2, tables4, wo, wd, cot):
    tok, width = x.shape
    ff = w_gate.shape[1] // 4
    span = width // 4
    group = span + 128
    sds = jax.ShapeDtypeStruct
    v = pltpu.VMEM
    return pl.pallas_call(
        first_kernel,
        name="first",
        out_shape=[
            sds((2, width, ff), BF), sds((ff, width), BF),
            sds((4, 2, 4, 64, group), BF), sds((2, 4, 64, width), BF), sds((4, tok, width), BF),
            sds((2, 4 * tok, width), BF), sds((2, 4 * tok, width), BF),
            sds((4 * tok, group), BF), sds((4, tok, span), BF),
            sds((4 * tok, 128), F32), sds((tok, width), F32),
        ],
        in_specs=[VMEM] * 15,
        out_specs=[ANY] * 9 + [VMEM] * 2,
        scratch_shapes=[
            v((4, 64, group), BF), v((4, 2, 64, ff), BF), v((4, 2, 4, 64, group), BF),
            v((2, 4, 64, width), BF), v((4, tok, width), BF), v((4, tok, group), BF),
            v((4 * tok, group), BF), v((4 * tok, span), BF), v((4, tok, span), BF),
            v((4, tok, width), BF), v((2, 2, tok, width // 2), BF), v((2, tok, width // 2), BF),
            v((2, tok, width // 2), BF), v((tok, width), BF),
            pltpu.SemaphoreType.DMA((96,)),
            pltpu.SemaphoreType.DMA((96,)),
        ],
        compiler_params=pltpu.CompilerParams(
            collective_id=1, has_side_effects=True, vmem_limit_bytes=56 * 2**20
        ),
    )(x, wq, wk, wv, gain1, w_gate, w_up, gain2, *tables4, wo, wd, cot)


def second_kernel(
    n_all, c_all, wg, wd,
    dn_out, mx_part, hg_out, gdown,
    wg_v, wd_v, n_v, c_v, hid, dg, du, dn_part, dn_r1, dn_s, dn_r2,
    hg_v, hd, hd_r1, hd_k, hd_r2, sib_s, sib_r, send_sems, recv_sems,
):
    net = Net(send_sems, recv_sems)
    dp, z, dps, zs = net.dp, net.z, net.dps, net.zs
    core = lax.rem(dp, 2)
    tok = dn_r2.shape[0]
    width = dn_r2.shape[1]
    ff = hid.shape[2]
    half = width // 2
    pair = 2 * tok
    copies = [
        net.local(n_all.at[0], n_v.at[0]),
        net.local(wg.at[0], wg_v.at[0]),
        net.local(wg.at[1], wg_v.at[1]),
        net.local(c_all.at[0], c_v.at[0]),
        net.local(wd, wd_v),
        net.local(n_all.at[1], n_v.at[1]),
        net.local(c_all.at[1], c_v.at[1]),
    ]
    net.barrier([X, Y, CORE, ("z", 1), ("z", 2)])
    for copy in copies[:5]:
        copy.wait()
    near_pair = lax.div(z, 2)
    rows_of = {"far": aligned((1 - near_pair) * pair, pair, 16), "near": aligned(near_pair * pair, pair, 16)}

    def chunks(fn, total, size):
        whole = total // size

        def step(i, carry):
            fn(i * size, size)
            return carry

        lax.fori_loop(0, whole, step, 0)
        if total % size:
            fn(whole * size, total - whole * size)

    def front(rows):
        def chunk(start, size):
            cols = aligned(start, size, 128)
            n = n_v[0, rows, :]
            gate = dot(n, wg_v[0, :, cols])
            upper = dot(n, wg_v[1, :, cols])
            dhid = right_dot(c_v[0, rows, :], wd_v[cols, :])
            sigma = jax.nn.sigmoid(gate)
            silu = gate * sigma
            hid[0, rows, cols] = (silu * upper).astype(BF)
            dg[0, rows, cols] = (dhid * upper * sigma * (1.0 + gate * (1.0 - sigma))).astype(BF)
            du[0, rows, cols] = (dhid * silu).astype(BF)

        chunks(chunk, ff, 256)

    def to_sibling(rows):
        return [net.send(ref.at[0, rows, :], ref.at[1, rows, :], CORE) for ref in (hid, dg, du)]

    def back(rows, part):
        def chunk(start, size):
            cols = aligned(start + part * half, size, 128)
            total = right_dot(dg[0, rows, :], wg_v[0, cols, :])
            total += right_dot(du[0, rows, :], wg_v[1, cols, :])
            dn_part[rows, cols] = total.astype(BF)

        chunks(chunk, half, 256)

    def slot(mask):
        return aligned(zs[mask] * tok, tok, 16)

    def piece(part):
        return pl.ds(part * half, half)

    front(rows_of["far"])
    sib = to_sibling(rows_of["far"])
    dn_a = []
    for part in (0, 1):
        back(rows_of["far"], part)
        dn_a.append(
            net.send(dn_part.at[slot(3), piece(part)], dn_r1.at[1, :, piece(part)], ("z", 1))
        )
    front(rows_of["near"])
    sib += to_sibling(rows_of["near"])
    dn_c = []
    for part in (0, 1):
        dn_a[part].wait_recv()
        cols = piece(part)
        dn_s[:, cols] = (
            dn_part[slot(2), cols].astype(F32) + dn_r1[1, :, cols].astype(F32)
        ).astype(BF)
        dn_c.append(net.send(dn_s.at[:, cols], dn_r2.at[:, cols], ("z", 2)))
    dn_b = []
    for part in (0, 1):
        back(rows_of["near"], part)
        dn_b.append(
            net.send(dn_part.at[slot(1), piece(part)], dn_r1.at[0, :, piece(part)], ("z", 1))
        )
    for copy in copies[5:]:
        copy.wait()
    for copy in sib:
        copy.wait_recv()

    ccols = aligned(core * half, half, 128)

    def down_chunk(start, size):
        cols = aligned(start, size, 128)
        total = left_dot(hid[0, :, cols], c_v[0, :, ccols])
        total += left_dot(hid[1, :, cols], c_v[1, :, ccols])
        hd[cols, :] = total.astype(BF)

    chunks(down_chunk, ff, 256)
    chip = ff // 4
    quarter = half // 2

    def hd_at(mask, side):
        return aligned(lax.div(dps[mask], 2) * chip, chip, 16), pl.ds(side * quarter, quarter)

    def hd_send(mask, side, place, name):
        r, c = hd_at(mask, side)
        return net.send(hd.at[r, c], hd_r1.at[side, place], name)

    hd_1 = [hd_send(6, 0, 1, X), hd_send(6, 1, 1, Y), hd_send(2, 0, 0, X), hd_send(4, 1, 0, Y)]

    def mix_chunk(start, size):
        cols = aligned(start, size, 128)
        mx_part[:, cols] = dot(hid[0], wd_v[:, cols]).astype(BF)

    chunks(mix_chunk, width, 256)
    def block(b, carry):
        cols = aligned((b * 2 + core) * 256, 256, 128)
        left = [n_v[s, :, cols].T for s in (0, 1)]
        for t, grad in enumerate((dg, du)):
            total = dot(left[0], grad[0]) + dot(left[1], grad[1])
            hg_v[t, b] = total.astype(BF)
        return carry

    lax.fori_loop(0, 4, block, 0)
    hg_copy = net.local(hg_v, hg_out)

    hd_1[0].wait_recv()
    hd_1[1].wait_recv()
    hd_2 = []
    for side, (mask, name) in enumerate(((4, Y), (2, X))):
        r, c = hd_at(mask, side)
        hd_k[side] = (hd[r, c].astype(F32) + hd_r1[side, 1].astype(F32)).astype(BF)
        hd_2.append(net.send(hd_k.at[side], hd_r2.at[side], name))
    for part in (0, 1):
        dn_b[part].wait_recv()
        dn_c[part].wait_recv()
        cols = piece(part)
        dn_out[:, cols] = (
            dn_part[slot(0), cols].astype(F32)
            + dn_r1[0, :, cols].astype(F32)
            + dn_r2[:, cols].astype(F32)
        )
    hd_1[2].wait_recv()
    hd_1[3].wait_recv()
    own = core * (chip // 2)
    other = (1 - core) * (chip // 2)
    for side in (0, 1):
        hd_2[side].wait_recv()
        r0 = lax.div(dp, 2) * chip

        def total(start):
            _, c = hd_at(0, side)
            return (
                hd[aligned(r0 + start, chip // 2, 16), c].astype(F32)
                + hd_r1[side, 0, aligned(start, chip // 2, 16), :].astype(F32)
                + hd_r2[side, aligned(start, chip // 2, 16), :].astype(F32)
            )

        sib_s[:, side * quarter : (side + 1) * quarter] = total(other)
        gdown[:, aligned(core * half + side * quarter, quarter, 128)] = total(own)
    last = net.send(sib_s, sib_r, CORE)
    last.wait_recv()
    gdown[:, aligned((1 - core) * half, half, 128)] = sib_r[...]
    hg_copy.wait()
    net.finish()


def second_call(n_all, c_all, wg, wd):
    _, length, width = n_all.shape
    tok = length // 4
    ff = wg.shape[2]
    sds = jax.ShapeDtypeStruct
    half = width // 2
    chip = ff // 4
    return pl.pallas_call(
        second_kernel,
        name="second",
        out_shape=[
            sds((tok, width), F32), sds((length, width), BF),
            sds((2, 4, 256, ff), BF), sds((chip // 2, width), F32),
        ],
        in_specs=[ANY] * 4,
        out_specs=[VMEM, VMEM, ANY, VMEM],
        scratch_shapes=[
            pltpu.VMEM((2, width, ff), BF),
            pltpu.VMEM((ff, width), BF),
            pltpu.VMEM((2, length, width), BF),
            pltpu.VMEM((2, length, width), BF),
            pltpu.VMEM((2, length, ff), BF),
            pltpu.VMEM((2, length, ff), BF),
            pltpu.VMEM((2, length, ff), BF),
            pltpu.VMEM((length, width), BF),
            pltpu.VMEM((2, tok, width), BF),
            pltpu.VMEM((tok, width), BF),
            pltpu.VMEM((tok, width), BF),
            pltpu.VMEM((2, 4, 256, ff), BF),
            pltpu.VMEM((ff, half), BF),
            pltpu.VMEM((2, 2, chip, half // 2), BF),
            pltpu.VMEM((2, chip, half // 2), BF),
            pltpu.VMEM((2, chip, half // 2), BF),
            pltpu.VMEM((chip // 2, half), F32),
            pltpu.VMEM((chip // 2, half), F32),
            pltpu.SemaphoreType.DMA((48,)),
            pltpu.SemaphoreType.DMA((48,)),
        ],
        compiler_params=pltpu.CompilerParams(
            collective_id=2, has_side_effects=True, vmem_limit_bytes=60 * 2**20
        ),
    )(n_all, c_all, wg, wd)


def third_kernel(
    x_ref, hmid, cot, dn2, qkv, lse, cos_q, sin_q, cos_k, sin_k,
    mx, wq, wo, hat, att, hg,
    tok_out, mixed, g2_out, g1_out, fb,
    wq_v, wo_v, hat_v, hat_s, att_v, att_s, mx_v, mx_r1, mx_s, mx_r2,
    hg_v, f_r1, f_k, f_r2, fs, dh, dbr, dbr_s, dsend, gh, dqkv, dk_acc, dv_acc, dback,
    dpre, dpre_s, part, r1, mid, r2, g2_p, g2_r1, g2_s, g2_r2, g1_p, g1_r1, g1_s, g1_r2, g1_f,
    send_sems, recv_sems,
):
    net = Net(send_sems, recv_sems)
    dp, z, dps, zs = net.dp, net.z, net.dps, net.zs
    tok, width = x_ref.shape
    group = qkv.shape[1]
    span = group - 128
    here = aligned(z * tok, tok, 16)
    core, chip = lax.rem(dp, 2), lax.div(dp, 2)

    def chip_of(mask):
        return lax.div(dps[mask], 2)

    def slot(mask):
        return aligned(zs[mask] * tok, tok, 16)

    loads = [
        net.local(wo, wo_v),
        net.local(hg.at[0, chip], hg_v.at[0, 0]),
        net.local(hg.at[0, chip_of(4)], hg_v.at[0, 1]),
        net.local(hg.at[1, chip], hg_v.at[1, 0]),
        net.local(hg.at[1, chip_of(2)], hg_v.at[1, 1]),
        net.local(mx.at[slot(0), :], mx_v.at[0]),
        net.local(mx.at[slot(2), :], mx_v.at[1]),
        net.local(att, att_v),
        net.local(wq, wq_v),
        net.local(hat, hat_v),
    ]
    net.barrier(PARTNERS + [("d", 6)])
    mx_1 = [
        net.send(mx.at[slot(3), :], mx_r1.at[1], ("z", 1)),
        net.send(mx.at[slot(1), :], mx_r1.at[0], ("z", 1)),
    ]

    def norm_back(value, grad):
        inv = rms(value)
        inner = jnp.mean(value * grad, axis=-1, keepdims=True)
        return inv * grad - value * (inv * inv * inv * inner)

    dh[...] = cot[...].astype(F32) + norm_back(hmid[...], dn2[...])
    dbr[chip] = dh[...].astype(BF)
    half = width // 2
    plane_b = Plane(net, lambda m, s: dbr.at[chip_of(m), :, pl.ds(s * half, half)], lambda m: [])
    plane_b.start()
    small = [
        net.send(att.at[:, :, aligned((1 - core) * 256, 256, 128)], att_s, CORE)
    ] + [
        net.send(
            hat.at[:, :, aligned(i * 512 + (1 - core) * 256, 256, 128)],
            hat_s.at[:, :, pl.ds(i * 256, 256)],
            CORE,
        )
        for i in range(4)
    ]
    plane_b.forward()
    f_1 = [
        net.send(hg.at[0, chip_of(6)], f_r1.at[0, 1], X),
        net.send(hg.at[1, chip_of(6)], f_r1.at[1, 1], Y),
        net.send(hg.at[0, chip_of(2)], f_r1.at[0, 0], X),
        net.send(hg.at[1, chip_of(4)], f_r1.at[1, 0], Y),
    ]
    plane_b.spread()
    loads[0].wait()
    d_copies = []
    weight = wo_v[...].reshape(span, width)
    for m in (2, 3, 1, 0):
        dsend[m] = right_dot(dbr[zs[m]], weight).astype(BF)
        if m:
            d_copies.append(net.send(dsend.at[m], gh.at[here, :], ("z", m)))
    gh[here, :] = dsend[0]
    dbr_copy = net.send(dbr, dbr_s, CORE)
    for copy in loads[1:]:
        copy.wait()
    for copy in d_copies:
        copy.wait_recv()
    mx_1[0].wait_recv()
    mx_s[...] = (mx_v[1].astype(F32) + mx_r1[1].astype(F32)).astype(BF)
    mx_2 = net.send(mx_s, mx_r2, ("z", 2))

    scale = HEAD_SIZE ** (-0.5)
    kk, vv = twice(qkv[:, span:])
    dk_acc[...] = jnp.zeros_like(dk_acc)
    dv_acc[...] = jnp.zeros_like(dv_acc)

    def pair(p, carry):
        cols = aligned(p * 128, 128, 128)
        for qb in range(4):
            keys = (qb + 1) * tok
            rows = slice(qb * tok, (qb + 1) * tok)
            q = qkv[rows, cols]
            g = gh[rows, cols]
            lane = lax.broadcasted_iota(jnp.int32, (tok, 128), 1)
            row = lax.broadcasted_iota(jnp.int32, (tok, keys), 0) + qb * tok
            col = lax.broadcasted_iota(jnp.int32, (tok, keys), 1)
            outs = []
            for h in range(2):
                lanes = (lane < 64) if h == 0 else (lane >= 64)
                qh = jnp.where(lanes, q, jnp.zeros_like(q))
                gg = jnp.where(lanes, g, jnp.zeros_like(g))
                log = jnp.sum(
                    jnp.where(lane == 2 * p + h, lse[rows, :], 0.0), axis=-1, keepdims=True
                )
                s = right_dot(qh, kk[:keys]) * scale
                probs = jnp.exp(jnp.where(col <= row, s, -1e30) - log)
                pg = right_dot(gg, vv[:keys])
                delta = jnp.sum(probs * pg, axis=-1, keepdims=True)
                ds = (probs * (pg - delta)).astype(BF)
                outs.append(dot(ds, kk[:keys]) * scale)
                dk_acc[:keys, :] += left_dot(ds, qh)
                dv_acc[:keys, :] += left_dot(probs.astype(BF), gg)
            dqkv[rows, cols] = jnp.where(lane < 64, outs[0], outs[1]).astype(BF)
        return carry

    lax.fori_loop(0, span // 128, pair, 0)
    dk = dk_acc[...]
    dv = dv_acc[...]
    lane = lax.broadcasted_iota(jnp.int32, dk.shape, 1)
    dqkv[:, span:] = jnp.where(
        lane < 64, (dk + pltpu.roll(dk, 64, 1)) * scale, dv + pltpu.roll(dv, 64, 1)
    ).astype(BF)
    b_copies = [net.send(dqkv.at[slot(m), :], dback.at[z], ("z", m)) for m in (2, 3, 1)]
    dback[z] = dqkv[here, :]

    f_2 = []
    for t, name in ((0, Y), (1, X)):
        f_1[t].wait_recv()
        f_k[t] = (hg_v[t, 1].astype(F32) + f_r1[t, 1].astype(F32)).astype(BF)
        f_2.append(net.send(f_k.at[t], f_r2.at[t], name))

    class Line:
        def __init__(self, parts, r1, s, r2):
            self.parts, self.r1, self.s, self.r2 = parts, r1, s, r2
            self.sent = [
                net.send(parts.at[zs[3]], r1.at[1], ("z", 1)),
                net.send(parts.at[zs[1]], r1.at[0], ("z", 1)),
            ]

        def middle(self):
            self.sent[0].wait_recv()
            self.s[...] = (self.parts[zs[2]].astype(F32) + self.r1[1].astype(F32)).astype(BF)
            self.far = net.send(self.s, self.r2, ("z", 2))

        def total(self):
            self.sent[1].wait_recv()
            self.far.wait_recv()
            own = self.parts[z].astype(F32) + self.r1[0].astype(F32)
            return own + self.r2[...].astype(F32)

    small[0].wait_recv()
    dbr_copy.wait_recv()
    mine = att_v[:, :, aligned(core * 256, 256, 128)].reshape(4 * tok, 256).T
    theirs = att_s[...].reshape(4 * tok, 256).T

    def out_chunk(i, carry):
        cols = aligned(i * 512, 512, 128)
        total = dot(mine, dbr[:, :, cols].reshape(4 * tok, 512))
        total += dot(theirs, dbr_s[:, :, cols].reshape(4 * tok, 512))
        g2_p[:, :, cols] = total.astype(BF).reshape(4, 64, 512)
        return carry

    lax.fori_loop(0, width // 512, out_chunk, 0)
    line_o = Line(g2_p, g2_r1, g2_s, g2_r2)

    for copy in b_copies:
        copy.wait_recv()
    for s in range(4):
        for j in range(group // 128):
            cols = slice(j * 128, (j + 1) * 128)
            last = j == group // 128 - 1
            c_ref, s_ref = (cos_k, sin_k) if last else (cos_q, sin_q)
            value = dback[s, :, cols].astype(F32)
            dpre[s, :, cols] = rotary(value, c_ref[...], -s_ref[...]).astype(BF)
    dpre_copy = net.send(dpre, dpre_s, CORE)

    left = dpre[...].reshape(4 * tok, group)

    def dhat_chunk(i, carry):
        cols = aligned(i * 256, 256, 128)
        rows = wq_v[lax.div(i, 2), lax.rem(i, 2)].reshape(256, group)
        part[:, :, cols] = right_dot(left, rows).astype(BF).reshape(4, tok, 256)
        return carry

    lax.fori_loop(0, width // 256, dhat_chunk, 0)
    sums = Sums(net, part, r1, mid, r2)
    for m in (6, 2, 4):
        sums.first(m)

    for copy in small[1:]:
        copy.wait_recv()
    dpre_copy.wait_recv()
    right = dpre_s[...].reshape(4 * tok, group)

    def first_chunk(i, carry):
        own = hat_v[:, :, aligned(i * 512 + core * 256, 256, 128)].reshape(4 * tok, 256).T
        sib = hat_s[:, :, aligned(i * 256, 256, 128)].reshape(4 * tok, 256).T
        total = dot(own, left) + dot(sib, right)
        g1_p[:, i] = total.astype(BF).reshape(4, 64, group)
        return carry

    lax.fori_loop(0, 4, first_chunk, 0)
    line_q = Line(g1_p, g1_r1, g1_s, g1_r2)
    line_o.middle()
    f_copies = []
    for t in (0, 1):
        f_1[2 + t].wait_recv()
        f_2[t].wait_recv()
        total = hg_v[t, 0].astype(F32) + f_r1[t, 0].astype(F32) + f_r2[t].astype(F32)
        for i in range(4):
            fs[i, t] = total[i * 64 : (i + 1) * 64, :].astype(BF)
    sums.second()
    line_q.middle()
    f_copies = [net.send(fs.at[zs[m]], fb.at[z], ("z", m)) for m in (2, 3, 1)]
    fb[z] = fs[z]
    mx_1[1].wait_recv()
    mx_2.wait_recv()
    total = mx_v[0].astype(F32) + mx_r1[0].astype(F32) + mx_r2[...].astype(F32)
    mixed[...] = (hmid[...] + total).astype(BF)
    g2_out[...] = line_o.total()
    for side in (0, 1):
        dn2[:, side * half : (side + 1) * half] = sums.total(side)
    tok_out[...] = (dh[...] + norm_back(x_ref[...].astype(F32), dn2[...])).astype(BF)
    g1_f[...] = line_q.total().astype(BF)
    g_copies = [net.send(g1_f.at[chip_of(m)], g1_out.at[chip], ("d", m)) for m in (6, 2, 4)]
    g1_out[chip] = g1_f[chip]
    for copy in g_copies + f_copies:
        copy.wait_recv()
    net.finish()


def third_call(x, hmid, cot, dn2, qkv, lse, tables4, mx, wq, wo, hat, att, hg):
    tok, width = x.shape
    group = qkv.shape[1]
    span = group - 128
    ff = hg.shape[-1]
    sds = jax.ShapeDtypeStruct
    v = pltpu.VMEM
    return pl.pallas_call(
        third_kernel,
        name="third",
        out_shape=[
            sds((tok, width), BF), sds((tok, width), BF), sds((64, width), F32),
            sds((4, 64, group), BF), sds((4, 2, 64, ff), BF),
        ],
        in_specs=[VMEM] * 10 + [ANY] * 6,
        out_specs=[VMEM] * 5,
        scratch_shapes=[
            v((4, 2, 4, 64, group), BF), v((2, 4, 64, width), BF), v((4, tok, width), BF),
            v((4, tok, width // 2), BF), v((4, tok, span), BF), v((4, tok, span // 2), BF),
            v((2, tok, width), BF), v((2, tok, width), BF), v((tok, width), BF), v((tok, width), BF),
            v((2, 2, 256, ff), BF), v((2, 2, 256, ff), BF), v((2, 256, ff), BF), v((2, 256, ff), BF),
            v((4, 2, 64, ff), BF), v((tok, width), F32), v((4, tok, width), BF),
            v((4, tok, width), BF), v((4, tok, span), BF), v((4 * tok, span), BF),
            v((4 * tok, group), BF), v((4 * tok, 128), F32), v((4 * tok, 128), F32),
            v((4, tok, group), BF), v((4, tok, group), BF), v((4, tok, group), BF),
            v((4, tok, width), BF), v((2, 2, tok, width // 2), BF), v((2, tok, width // 2), BF),
            v((2, tok, width // 2), BF),
            v((4, 64, width), BF), v((2, 64, width), BF), v((64, width), BF), v((64, width), BF),
            v((4, 4, 64, group), BF), v((2, 4, 64, group), BF), v((4, 64, group), BF),
            v((4, 64, group), BF), v((4, 64, group), BF),
            pltpu.SemaphoreType.DMA((80,)),
            pltpu.SemaphoreType.DMA((80,)),
        ],
        compiler_params=pltpu.CompilerParams(
            collective_id=3, has_side_effects=True, vmem_limit_bytes=60 * 2**20
        ),
    )(x, hmid, cot, dn2, qkv, lse, *tables4, mx, wq, wo, hat, att, hg)


def last_kernel(
    fb, g1, wq, wk, wv, w_gate, w_up, gain1, gain2,
    gq, gk, gv, g_gate, g_up, g_gain1, g_gain2,
):
    span = g1.shape[2] - 128
    lane = lax.broadcasted_iota(jnp.int32, (g1.shape[1], 128), 1)
    scale = gain1[...]

    def put(out, weight, cols, value):
        out[:, cols] = value * scale
        return jnp.sum(value * weight[:, cols].astype(F32), axis=1, keepdims=True)

    total = jnp.zeros_like(g_gain1)
    for g in range(4):
        total += put(gq, wq, slice(g * span, (g + 1) * span), g1[g, :, :span].astype(F32))
    for g in (0, 2):
        one = g1[g, :, span:].astype(F32)
        two = g1[g + 1, :, span:].astype(F32)
        cols = slice(g * 64, g * 64 + 128)
        total += put(gk, wk, cols, jnp.where(lane < 64, one, pltpu.roll(two, 64, 1)))
        total += put(gv, wv, cols, jnp.where(lane < 64, pltpu.roll(one, 64, 1), two))
    g_gain1[...] = total
    size = fb.shape[-1] // 8
    total = jnp.zeros_like(g_gain2)
    for t, (out, weight) in enumerate(((g_gate, w_gate), (g_up, w_up))):
        for d in range(0, 8, 2):
            parts = [
                fb[i, t, :, e * size : (e + 1) * size].astype(F32) for e in (d, d + 1) for i in range(4)
            ]
            joined = jnp.concatenate(parts, axis=1)
            cols = pl.ds(d * 4 * size, 8 * size)
            total += jnp.sum(joined * weight[:, cols].astype(F32), axis=1, keepdims=True)
            out[:, cols] = joined * gain2[...]
    g_gain2[...] = total


def last_call(fb, g1, wq, wk, wv, w_gate, w_up, gain1, gain2):
    rows, ff = w_gate.shape
    sds = jax.ShapeDtypeStruct
    return pl.pallas_call(
        last_kernel,
        name="last",
        out_shape=[
            sds(wq.shape, F32), sds(wk.shape, F32), sds(wv.shape, F32),
            sds((rows, ff), F32), sds((rows, ff), F32), sds((rows, 1), F32), sds((rows, 1), F32),
        ],
        in_specs=[VMEM] * 9,
        out_specs=[VMEM] * 7,
        compiler_params=pltpu.CompilerParams(vmem_limit_bytes=40 * 2**20),
    )(fb, g1, wq, wk, wv, w_gate, w_up, gain1, gain2)


def shards(
    tokens, norm_first, w_query, w_key, w_value, w_out, norm_second, w_gate, w_up, w_down, cotangent
):
    count = tokens.shape[0]
    gain1 = norm_first.astype(F32)[:, None]
    gain2 = norm_second.astype(F32)[:, None]
    cosine, sine = tables(lax.axis_index("seq") * count + jnp.arange(count))
    cosine, sine = cosine[:, 0], sine[:, 0]
    one, zero = jnp.ones_like(cosine), jnp.zeros_like(cosine)
    tables4 = [
        jnp.concatenate(parts, axis=1)
        for parts in (
            [cosine] * 4,
            [-sine, sine] * 2,
            [cosine, cosine, one, one],
            [-sine, sine, zero, zero],
        )
    ]
    wg, wd, wq, wo, hat, c_all, n_all, qkv, att, lse, hmid = first_call(
        tokens, w_query, w_key, w_value, gain1, w_gate, w_up, gain2, tables4,
        w_out, w_down, cotangent,
    )
    dhat2, mixed_part, hg, grad_down = second_call(n_all, c_all, wg, wd)
    grad_tokens, mixed, grad_out, grad_first, parts = third_call(
        tokens, hmid, cotangent, dhat2, qkv, lse, tables4, mixed_part, wq, wo, hat, att, hg
    )
    grad_query, grad_key, grad_value, grad_gate, grad_up, grad_gain1, grad_gain2 = last_call(
        parts, grad_first, w_query, w_key, w_value, w_gate, w_up, gain1, gain2
    )
    return (
        mixed,
        grad_tokens,
        grad_gain1[:, 0],
        grad_query,
        grad_key,
        grad_value,
        grad_out,
        grad_gain2[:, 0],
        grad_gate,
        grad_up,
        grad_down,
    )


def solution(mesh):
    special = mesh.shape['dp'] == 8 and mesh.shape['seq'] == KEY_VALUE_HEADS
    rows = P(("dp", "seq"), None)
    line = P(("dp", "seq"))
    return jax.shard_map(
        shards if special else general_shards,
        mesh=mesh,
        in_specs=(rows, line, rows, rows, rows, rows, line, rows, rows, rows, rows),
        out_specs=(rows, rows, line, rows, rows, rows, rows, line, rows, rows, rows),
        check_vma=False,
    )
```

```python
import jax
import jax.numpy as jnp
from jax import lax
from jax.experimental import pallas as pl
from jax.experimental.pallas import tpu as pltpu
from jax.sharding import PartitionSpec as P

H = 32
KEY_VALUE_HEADS = 4
HEAD_SIZE = 64
EPS = 1e-05
BF = jnp.bfloat16
F32 = jnp.float32


def tables(positions):
    freq = 10000.0 ** (-jnp.arange(0, HEAD_SIZE // 2, dtype=F32) * 2.0 / HEAD_SIZE)
    angle = positions.astype(F32)[:, None] * freq[None, :]
    return (jnp.cos(angle)[:, None, :], jnp.sin(angle)[:, None, :])


def rotate(heads, cosine, sine):
    half = heads.shape[-1] // 2
    first = heads[..., :half]
    second = heads[..., half:]
    return jnp.concatenate(
        [first * cosine - second * sine, second * cosine + first * sine], axis=-1
    )


def dot(left, right):
    return jnp.dot(left, right, preferred_element_type=F32)


def left_dot(left, right):
    return lax.dot_general(left, right, (((0,), (0,)), ((), ())), preferred_element_type=F32)


def right_dot(left, right):
    return lax.dot_general(left, right, (((1,), (1,)), ((), ())), preferred_element_type=F32)


def bits_of(count):
    return [1 << k for k in range(count.bit_length() - 1)]


class Axis:
    def __init__(self, name):
        self.name = name
        self.size = lax.axis_size(name)
        self.me = lax.axis_index(name)

    def swap(self, value, mask):
        return lax.ppermute(value, self.name, [(i, i ^ mask) for i in range(self.size)])

    def all(self, value):
        return [value if m == 0 else self.swap(value, m) for m in range(self.size)]

    def exchange(self, stacked):
        return [
            lax.dynamic_index_in_dim(stacked, self.me ^ m, 0, keepdims=False)
            if m == 0
            else self.swap(
                lax.dynamic_index_in_dim(stacked, self.me ^ m, 0, keepdims=False), m
            )
            for m in range(self.size)
        ]

    def natural(self, pieces):
        stack = jnp.stack(pieces)
        return [
            lax.dynamic_index_in_dim(stack, self.me ^ i, 0, keepdims=False)
            for i in range(self.size)
        ]


def orders(size):
    even = [m for m in range(size) if m % 2 == 0]
    return even, [m + 1 for m in even]


def chip_bits(size, turn):
    bits = bits_of(size)[1:]
    return bits if turn == 0 else bits[::-1]


def gather_chips(dp, piece, turn):
    pieces = {0: piece}
    for bit in chip_bits(dp.size, turn):
        pieces.update({m ^ bit: dp.swap(p, bit) for m, p in list(pieces.items())})
    return pieces


def gather_rows(dp, piece, turn):
    pieces = gather_chips(dp, piece, turn)
    even = jnp.concatenate([pieces[m] for m in orders(dp.size)[0]], axis=0)
    return even, dp.swap(even, 1)


def scatter_chips(dp, blocks, turn):
    for bit in chip_bits(dp.size, turn):
        for m in [m for m in blocks if m & bit]:
            other = dp.swap(blocks.pop(m).astype(BF), bit)
            blocks[m ^ bit] = blocks[m ^ bit].astype(F32) + other.astype(F32)
    return blocks[0]


def scatter_rows(dp, even_fn, odd, turn):
    rows = odd.shape[0] * 2 // dp.size
    other = dp.swap(odd, 1)
    even = (even_fn() + other.astype(F32)).astype(BF)
    blocks = {
        m: even[i * rows : (i + 1) * rows] for i, m in enumerate(orders(dp.size)[0])
    }
    return scatter_chips(dp, blocks, turn)


def mask_columns(dp, value):
    width = value.shape[1] // dp.size
    return tuple(
        jnp.concatenate(
            [lax.dynamic_slice_in_dim(value, (dp.me ^ m) * width, width, 1) for m in group],
            axis=1,
        )
        for group in orders(dp.size)
    )


def natural_columns(dp, even, odd):
    both = jnp.concatenate([even, odd], axis=1)
    width = both.shape[1] // dp.size
    half = dp.size // 2
    parts = []
    for i in range(dp.size):
        mask = dp.me ^ i
        place = mask // 2 + (mask % 2) * half
        parts.append(lax.dynamic_slice_in_dim(both, place * width, width, 1))
    return jnp.concatenate(parts, axis=1)


def attend(queries, keys, values, visible):
    scores = jnp.einsum("qhd,kd->hqk", queries, keys, preferred_element_type=F32)
    scores = jnp.where(visible[None], scores * HEAD_SIZE ** (-0.5), -1e30)
    top = jnp.max(scores, axis=-1, keepdims=True)
    expo = jnp.exp(scores - top)
    total = jnp.sum(expo, axis=-1, keepdims=True)
    probs = (expo / total).astype(BF)
    result = jnp.einsum("hqk,kd->qhd", probs, values, preferred_element_type=F32)
    return result.astype(BF), top + jnp.log(total)


def attend_back(queries, keys, values, grad_heads, logsum, visible):
    scale = HEAD_SIZE ** (-0.5)
    scores = jnp.einsum("qhd,kd->hqk", queries, keys, preferred_element_type=F32)
    scores = jnp.where(visible[None], scores * scale, -1e30)
    probs = jnp.exp(scores - logsum)
    pgrad = jnp.einsum("qhd,kd->hqk", grad_heads, values, preferred_element_type=F32)
    delta = jnp.sum(probs * pgrad, axis=-1, keepdims=True)
    sgrad = (probs * (pgrad - delta)).astype(BF)
    qgrad = jnp.einsum("hqk,kd->qhd", sgrad, keys, preferred_element_type=F32) * scale
    kgrad = jnp.einsum("hqk,qhd->kd", sgrad, queries, preferred_element_type=F32) * scale
    vgrad = jnp.einsum("hqk,qhd->kd", probs.astype(BF), grad_heads, preferred_element_type=F32)
    return qgrad.astype(BF), kgrad.astype(BF), vgrad.astype(BF)


def general_shards(
    tokens, norm_first, w_query, w_key, w_value, w_out, norm_second, w_gate, w_up, w_down, cotangent
):
    dp, seq = Axis("dp"), Axis("seq")
    groups = seq.size
    count, width = tokens.shape
    ff = w_gate.shape[1]
    per = H // groups
    repeat = groups // KEY_VALUE_HEADS
    heads_wide = H * HEAD_SIZE
    keys_wide = KEY_VALUE_HEADS * HEAD_SIZE
    gain1 = norm_first.astype(F32)[:, None]
    gain2 = norm_second.astype(F32)[:, None]

    w_first = jnp.concatenate([w_query, w_key, w_value], axis=1)
    w_first_scaled = (w_first.astype(F32) * gain1).astype(BF)
    wide = w_first.shape[1]

    def by_part(weight):
        rows = weight.shape[0]
        scaled = (weight.astype(F32) * gain2).astype(BF)
        parts = scaled.reshape(rows, dp.size, groups, ff // dp.size // groups)
        return parts.transpose(2, 0, 1, 3).reshape(groups, rows, ff // groups)

    down = [gather_chips(dp, w_down[:, t * width // 2 : (t + 1) * width // 2], t) for t in (0, 1)]
    first_rows = jnp.concatenate(seq.natural(seq.all(w_first_scaled)), axis=0)
    first = [gather_rows(dp, first_rows[:, t * wide // 2 : (t + 1) * wide // 2], t) for t in (0, 1)]
    out_rows = jnp.concatenate(seq.natural(seq.all(w_out)), axis=0)
    outw = [gather_rows(dp, out_rows[:, t * width // 2 : (t + 1) * width // 2], t) for t in (0, 1)]
    gate_up = seq.exchange(jnp.stack([by_part(w_gate), by_part(w_up)], axis=1))
    gate_up = jnp.concatenate(seq.natural(gate_up), axis=1)
    (gate_even, gate_odd), (up_even, up_odd) = [
        gather_rows(dp, gate_up[t], t) for t in (0, 1)
    ]
    cot_all = jnp.concatenate(seq.all(cotangent), axis=0)

    rows_down = w_down.shape[0]
    down_full = []
    for t in (0, 1):
        even = jnp.stack([down[t][m] for m in orders(dp.size)[0]])
        odd = dp.swap(even, 1)
        full = jnp.zeros((rows_down * dp.size, width // 2), BF)
        for i, m in enumerate(orders(dp.size)[0]):
            full = lax.dynamic_update_slice(full, even[i], ((dp.me ^ m) * rows_down, 0))
            full = lax.dynamic_update_slice(full, odd[i], ((dp.me ^ m ^ 1) * rows_down, 0))
        down_full.append(full)

    inputs = tokens.astype(F32)
    inv1 = lax.rsqrt(jnp.mean(inputs * inputs, axis=-1, keepdims=True) + EPS)
    hat1 = (inputs * inv1).astype(BF)
    hat1_even, hat1_odd = mask_columns(dp, hat1)
    cosine, sine = tables(seq.me * count + jnp.arange(count))
    pre = jnp.concatenate(
        [dot(hat1_even, first[t][0]) + dot(hat1_odd, first[t][1]) for t in (0, 1)], axis=1
    )
    qpre = pre[:, :heads_wide].reshape(count, H, HEAD_SIZE)
    kpre = pre[:, heads_wide : heads_wide + keys_wide].reshape(count, KEY_VALUE_HEADS, HEAD_SIZE)
    vround = pre[:, heads_wide + keys_wide :].astype(BF)
    qrot = rotate(qpre, cosine, sine).reshape(count, heads_wide).astype(BF)
    krot = rotate(kpre, cosine, sine).reshape(count, keys_wide).astype(BF)
    span = per * HEAD_SIZE
    packed = []
    for g in range(groups):
        head = g // repeat * HEAD_SIZE
        packed.append(
            jnp.concatenate(
                [
                    qrot[:, g * span : (g + 1) * span],
                    krot[:, head : head + HEAD_SIZE],
                    vround[:, head : head + HEAD_SIZE],
                ],
                axis=1,
            )
        )
    qkv = jnp.concatenate(seq.exchange(jnp.stack(packed)), axis=0)
    length = qkv.shape[0]
    queries = qkv[:, :span].reshape(length, per, HEAD_SIZE)
    keys = qkv[:, span : span + HEAD_SIZE]
    values = qkv[:, span + HEAD_SIZE :]
    place = jnp.concatenate(
        [(seq.me ^ m) * count + jnp.arange(count, dtype=jnp.int32) for m in range(groups)]
    )
    visible = place[None, :] <= place[:, None]
    out_heads, logsum = attend(queries, keys, values, visible)
    out_heads = out_heads.reshape(length, span)

    def back_home(value):
        return seq.natural(
            [
                value[:count] if m == 0 else seq.swap(value[m * count : (m + 1) * count], m)
                for m in range(groups)
            ]
        )

    attn = jnp.concatenate(back_home(out_heads), axis=1)
    attn_even, attn_odd = mask_columns(dp, attn)
    branch = jnp.concatenate(
        [dot(attn_even, outw[t][0]) + dot(attn_odd, outw[t][1]) for t in (0, 1)], axis=1
    )
    hmid = inputs + branch

    inv2 = lax.rsqrt(jnp.mean(hmid * hmid, axis=-1, keepdims=True) + EPS)
    hat2 = jnp.concatenate(mask_columns(dp, (hmid * inv2).astype(BF)), axis=1)
    hat2_all = jnp.concatenate(seq.all(hat2), axis=0)
    hat2_even, hat2_odd = hat2_all[:, : width // 2], hat2_all[:, width // 2 :]
    gate = dot(hat2_even, gate_even) + dot(hat2_odd, gate_odd)
    upper = dot(hat2_even, up_even) + dot(hat2_odd, up_odd)
    sigma = jax.nn.sigmoid(gate)
    hidden = (gate * sigma * upper).astype(BF)
    halves = [cot_all[:, : width // 2], cot_all[:, width // 2 :]]
    dhidden = right_dot(halves[0], down_full[0]) + right_dot(halves[1], down_full[1])
    dgate = (dhidden * upper * sigma * (1.0 + gate * (1.0 - sigma))).astype(BF)
    dupper = (dhidden * gate * sigma).astype(BF)
    dhat2 = jnp.concatenate(
        [
            right_dot(dgate, gate_even) + right_dot(dupper, up_even),
            right_dot(dgate, gate_odd) + right_dot(dupper, up_odd),
        ],
        axis=1,
    ).astype(BF)

    def sum_home(value):
        total = value[:count].astype(F32)
        for m in range(1, groups):
            total = total + seq.swap(value[m * count : (m + 1) * count], m).astype(F32)
        return total

    dhat2 = sum_home(dhat2)
    dgain2 = natural_columns(dp, dhat2[:, : width // 2], dhat2[:, width // 2 :])
    inner = jnp.mean(hmid * dgain2, axis=-1, keepdims=True)
    dh = cotangent.astype(F32) + inv2 * dgain2 - hmid * inv2 * inv2 * inv2 * inner
    dbranch = dh.astype(BF)

    dattn = natural_columns(
        dp,
        *[
            sum(
                right_dot(dbranch[:, t * width // 2 : (t + 1) * width // 2], outw[t][s])
                for t in (0, 1)
            ).astype(BF)
            for s in (0, 1)
        ],
    )
    grad_heads = jnp.concatenate(
        seq.exchange(dattn.reshape(count, groups, span).transpose(1, 0, 2)), axis=0
    ).reshape(length, per, HEAD_SIZE)
    dq, dk, dv = attend_back(queries, keys, values, grad_heads, logsum, visible)
    dqkv = back_home(jnp.concatenate([dq.reshape(length, span), dk, dv], axis=1))
    dq = jnp.concatenate([piece[:, :span] for piece in dqkv], axis=1)
    dk = [piece[:, span : span + HEAD_SIZE].astype(F32) for piece in dqkv]
    dv = [piece[:, span + HEAD_SIZE :].astype(F32) for piece in dqkv]
    dk = jnp.stack(
        [sum(dk[i * repeat : (i + 1) * repeat]) for i in range(KEY_VALUE_HEADS)], axis=1
    )
    dv = jnp.concatenate(
        [sum(dv[i * repeat : (i + 1) * repeat]) for i in range(KEY_VALUE_HEADS)], axis=1
    )
    dq = rotate(dq.astype(F32).reshape(count, H, HEAD_SIZE), cosine, -sine)
    dk = rotate(dk, cosine, -sine)
    dpre = jnp.concatenate(
        [dq.reshape(count, heads_wide), dk.reshape(count, keys_wide), dv], axis=1
    ).astype(BF)
    dhalf = [dpre[:, t * wide // 2 : (t + 1) * wide // 2] for t in (0, 1)]
    dhat1 = [sum(right_dot(dhalf[t], first[t][s]) for t in (0, 1)) for s in (0, 1)]
    dgain1 = natural_columns(dp, *dhat1)
    inner = jnp.mean(inputs * dgain1, axis=-1, keepdims=True)
    grad_inputs = dh + inv1 * dgain1 - inputs * inv1 * inv1 * inv1 * inner

    mixed_part = jnp.concatenate([dot(hidden, down_full[t]) for t in (0, 1)], axis=1).astype(BF)
    mixed = hmid + sum_home(mixed_part)

    grad_down = []
    for t in (0, 1):
        part = left_dot(hidden, halves[t]).astype(BF)
        blocks = [
            lax.dynamic_slice_in_dim(part, (dp.me ^ m) * rows_down, rows_down, 0)
            for m in range(dp.size)
        ]
        even, odd = orders(dp.size)
        other = dp.swap(jnp.stack([blocks[m] for m in odd]), 1)
        summed = {
            m: (blocks[m].astype(F32) + other[i].astype(F32)).astype(BF)
            for i, m in enumerate(even)
        }
        grad_down.append(scatter_chips(dp, summed, t))
    grad_down = jnp.concatenate(grad_down, axis=1)

    def ff_grad(grad, turn):
        odd = left_dot(hat2_odd, grad).astype(BF)
        return scatter_rows(dp, lambda: left_dot(hat2_even, grad), odd, turn)

    rows = w_gate.shape[0]
    sent = jnp.stack([ff_grad(dgate, 0).astype(BF), ff_grad(dupper, 1).astype(BF)])
    sent = sent.reshape(2, groups, rows, ff // groups).transpose(1, 0, 2, 3)
    got = jnp.stack(seq.natural(seq.exchange(sent)))
    got = got.reshape(groups, 2, rows, dp.size, ff // groups // dp.size)
    got = got.transpose(1, 2, 3, 0, 4).reshape(2, rows, ff).astype(F32)
    grad_gate, grad_up = got[0] * gain2, got[1] * gain2
    grad_gain2 = jnp.sum(got[0] * w_gate.astype(F32) + got[1] * w_up.astype(F32), axis=1)

    def proj_grad(even, odd, grads):
        parts = []
        for t in (0, 1):
            send = left_dot(odd, grads[t]).astype(BF)
            parts.append(
                scatter_rows(dp, lambda grad=grads[t]: left_dot(even, grad), send, t)
            )
        own = jnp.concatenate(parts, axis=1)
        own = own.astype(BF).reshape(groups, rows, own.shape[1])
        return sum(piece.astype(F32) for piece in seq.exchange(own))

    grad_out = proj_grad(
        attn_even,
        attn_odd,
        [dbranch[:, t * width // 2 : (t + 1) * width // 2] for t in (0, 1)],
    )
    grad_first = proj_grad(hat1_even, hat1_odd, dhalf)
    grad_gain1 = jnp.sum(grad_first * w_first.astype(F32), axis=1)
    grad_first = grad_first * gain1
    return (
        mixed.astype(BF),
        grad_inputs.astype(BF),
        grad_gain1,
        grad_first[:, :heads_wide],
        grad_first[:, heads_wide : heads_wide + keys_wide],
        grad_first[:, heads_wide + keys_wide :],
        grad_out,
        grad_gain2,
        grad_gate,
        grad_up,
        grad_down,
    )


MESH = pl.DeviceIdType.MESH
ANY = pl.BlockSpec(memory_space=pl.ANY)
VMEM = pl.BlockSpec(memory_space=pltpu.VMEM)


class Net:
    def __init__(self, send_sems, recv_sems):
        self.send_sems, self.recv_sems, self.used = send_sems, recv_sems, 0
        self.open = []
        dp, z = lax.axis_index("dp"), lax.axis_index("seq")
        self.dp, self.z = dp, z
        self.dps = {
            0: dp,
            1: dp + 1 - 2 * lax.rem(dp, 2),
            2: dp + 2 - 4 * lax.rem(lax.div(dp, 2), 2),
            4: lax.rem(dp + 4, 8),
        }
        self.dps[6] = lax.rem(self.dps[2] + 4, 8)
        for mask in (2, 4, 6):
            self.dps[mask + 1] = self.dps[mask] + 1 - 2 * lax.rem(dp, 2)
        self.zs = {0: z, 1: z + 1 - 2 * lax.rem(z, 2), 2: lax.rem(z + 2, 4), 3: 3 - z}

    def target(self, name):
        kind, mask = name
        return (self.dps[mask], self.z) if kind == "d" else (self.dp, self.zs[mask])

    def barrier(self, names):
        sem = pltpu.get_barrier_semaphore()
        for name in names:
            pl.semaphore_signal(sem, inc=1, device_id=self.target(name), device_id_type=MESH)
        pl.semaphore_wait(sem, len(names))

    def send(self, src, dst, name):
        copy = pltpu.make_async_remote_copy(
            src_ref=src,
            dst_ref=dst,
            send_sem=self.send_sems.at[self.used],
            recv_sem=self.recv_sems.at[self.used],
            device_id=self.target(name),
            device_id_type=MESH,
        )
        self.used += 1
        copy.start()
        self.open.append(copy)
        return copy

    def local(self, src, dst):
        copy = pltpu.make_async_copy(src, dst, self.send_sems.at[self.used])
        self.used += 1
        copy.start()
        return copy

    def finish(self):
        for copy in self.open:
            copy.wait_send()


X, Y, CORE = ("d", 2), ("d", 4), ("d", 1)
PARTNERS = [X, Y, CORE, ("z", 1), ("z", 2), ("z", 3)]


class Plane:
    def __init__(self, net, at, both):
        self.net, self.at, self.both = net, at, both

    def push(self, mask, half, name):
        ref = self.at(mask, half)
        return self.net.send(ref, ref, name)

    def start(self):
        self.xa = self.push(0, 0, X)
        self.yb = self.push(0, 1, Y)
        self.ya = self.push(0, 0, Y)
        self.xb = self.push(0, 1, X)
        self.cores = [self.core(0)]

    def core(self, mask):
        return [self.net.send(ref, ref, CORE) for ref in self.both(mask)]

    def forward(self):
        self.xa.wait_recv()
        self.ya2 = self.push(2, 0, Y)
        self.yb.wait_recv()
        self.xb2 = self.push(4, 1, X)

    def spread(self):
        self.ya.wait_recv()
        self.cores.append(self.core(4))
        self.xb.wait_recv()
        self.cores.append(self.core(2))
        self.ya2.wait_recv()
        self.xb2.wait_recv()
        self.cores.append(self.core(6))

    def finish(self):
        for copies in self.cores:
            for copy in copies:
                copy.wait_recv()


def rotary(value, cosine, sine):
    lane = lax.broadcasted_iota(jnp.int32, value.shape, 1)
    partner = jnp.where(
        lax.rem(lane, 64) < 32, pltpu.roll(value, 96, 1), pltpu.roll(value, 32, 1)
    )
    return value * cosine + partner * sine


def rms(value):
    return lax.rsqrt(jnp.mean(value * value, axis=-1, keepdims=True) + EPS)


def twice(pair):
    lane = lax.broadcasted_iota(jnp.int32, pair.shape, 1)
    other = pltpu.roll(pair.astype(F32), 64, 1).astype(BF)
    return jnp.where(lane < 64, pair, other), jnp.where(lane < 64, other, pair)


def aligned(start, count, unit):
    return pl.ds(pl.multiple_of(start, unit), count)


class Sums:
    def __init__(self, net, part, r1, mid, r2):
        self.net, self.part, self.r1, self.mid, self.r2 = net, part, r1, mid, r2
        self.width = r2.shape[-1]

    def cols(self, side):
        return pl.ds(side * self.width, self.width)

    def block(self, mask):
        return lax.div(self.net.dps[mask], 2)

    def push(self, mask, side, place, name):
        src = self.part.at[self.block(mask), :, self.cols(side)]
        return self.net.send(src, self.r1.at[side, place], name)

    def first(self, mask):
        if mask == 6:
            self.near = [self.push(6, 0, 1, X), self.push(6, 1, 1, Y)]
        elif mask == 2:
            self.own = [self.push(2, 0, 0, X)]
        elif mask == 4:
            self.own.append(self.push(4, 1, 0, Y))

    def second(self):
        self.far = []
        for side, (mask, name) in enumerate(((4, Y), (2, X))):
            self.near[side].wait_recv()
            mine = self.part[self.block(mask), :, self.cols(side)]
            self.mid[side] = (mine.astype(F32) + self.r1[side, 1].astype(F32)).astype(BF)
            self.far.append(self.net.send(self.mid.at[side], self.r2.at[side], name))

    def total(self, side):
        self.own[side].wait_recv()
        self.far[side].wait_recv()
        mine = self.part[self.block(0), :, self.cols(side)]
        return mine.astype(F32) + self.r1[side, 0].astype(F32) + self.r2[side].astype(F32)


def first_kernel(
    x_ref, wq, wk, wv, gain1, w_gate, w_up, gain2, cos_q, sin_q, cos_k, sin_k, wo, wd, cot,
    wg_all, wd_all, wq_out, wo_out, hat_out, c_all, n_all, qkv_out, att_out, lse, hmid,
    wq_s, wf, wq_v, wo_v, hat, qkv_send, qkv, heads, att, part, r1, mid, r2, hat2,
    send_sems, recv_sems,
):
    net = Net(send_sems, recv_sems)
    dp, z, dps, zs = net.dp, net.z, net.dps, net.zs
    tok, width = x_ref.shape
    group = qkv.shape[1]
    span = heads.shape[1]
    ff = wf.shape[-1]
    core, chip = lax.rem(dp, 2), lax.div(dp, 2)
    here = aligned(z * tok, tok, 16)

    own = [
        net.local(wo, wo_v.at[core, z]),
        net.local(wd, wd_all.at[aligned(dp * 176, 176, 16), :]),
        net.local(cot, c_all.at[here, :]),
    ]
    net.barrier(PARTNERS + [("d", 6)])

    scale = gain1[...]
    lane = lax.broadcasted_iota(jnp.int32, (wq.shape[0], 128), 1)
    for g in range(4):
        wq_s[g, :, :span] = (wq[:, g * span : (g + 1) * span].astype(F32) * scale).astype(BF)
        start = g // 2 * 128
        k = wk[:, start : start + 128].astype(F32)
        v = wv[:, start : start + 128].astype(F32)
        if g % 2 == 0:
            both = jnp.where(lane < 64, k, pltpu.roll(v, 64, 1))
        else:
            both = jnp.where(lane < 64, pltpu.roll(k, 64, 1), v)
        wq_s[g, :, span:] = (both * scale).astype(BF)

    def chip_of(mask):
        return lax.div(dps[mask], 2)

    w_1 = [
        net.send(wq_s.at[chip_of(m)], wq_v.at[chip, core, z], ("d", m)) for m in (6, 2, 4)
    ]
    own_q = net.local(wq_s.at[chip], wq_v.at[chip, core, z])
    x = x_ref[...].astype(F32)
    hat[chip] = (x * rms(x)).astype(BF)

    def half_of(ref, side):
        w = ref.shape[-1] // 2
        return pl.ds(side * w, w)

    def block(ref, size, cores):
        def at(mask, side):
            return ref.at[aligned(dps[mask] * size, size, 16), half_of(ref, side)]

        return at, lambda mask: [ref.at[aligned(dps[mask] * size, size, 16), :]] if cores else []

    plane_h = Plane(net, lambda m, s: hat.at[chip_of(m), :, half_of(hat, s)], lambda m: [])
    plane_h.start()
    down = Plane(net, *block(wd_all, 176, True))
    own[1].wait()
    down.start()

    scale = gain2[...]
    size = ff // 8
    for t, weight in enumerate((w_gate, w_up)):
        for i in range(4):
            parts = [weight[:, (d * 4 + i) * size : (d * 4 + i + 1) * size] for d in range(8)]
            joined = jnp.concatenate([p.astype(F32) for p in parts], axis=1)
            wf[i, t] = (joined * scale).astype(BF)
    own_f = net.local(wf.at[z], wg_all.at[:, aligned((dp * 4 + z) * 64, 64, 16), :])

    f_rows = aligned((dp * 4 + z) * 64, 64, 16)

    def f_send(t):
        return [
            net.send(wf.at[zs[m], t], wg_all.at[t, f_rows, :], ("z", m)) for m in (2, 3, 1)
        ]

    def f_plane(t):
        def rows(mask, start, count):
            return wg_all.at[t, aligned(dps[mask] * 256 + start, count, 16), :]

        return Plane(
            net, lambda m, s: rows(m, s * 128, 128), lambda m: [rows(m, 0, 256)]
        )

    own_q.wait()
    for copy in w_1:
        copy.wait_recv()

    def wq_at(mask):
        return wq_v.at[:, core, zs[mask]]

    def wo_at(mask):
        return wo_v.at[core, zs[mask]]

    class Line:
        def __init__(self, at):
            self.at = at
            self.far = self.push(0, ("z", 2))
            self.near = self.push(0, ("z", 1))
            self.cores = [self.push(0, CORE)]

        def push(self, mask, name):
            return net.send(self.at(mask), self.at(mask), name)

        def forward(self):
            self.far.wait_recv()
            self.last = self.push(2, ("z", 1))
            self.cores.append(self.push(2, CORE))

        def spread(self):
            self.near.wait_recv()
            self.cores.append(self.push(1, CORE))
            self.last.wait_recv()
            self.cores.append(self.push(3, CORE))

        def finish(self):
            for copy in self.cores:
                copy.wait_recv()

    line_q = Line(wq_at)
    plane_h.forward()
    line_q.forward()
    gate_copies = f_send(0)
    plane_h.spread()
    line_q.spread()
    own[0].wait()
    line_o = Line(wo_at)
    down.forward()
    line_q.finish()

    weight = wq_v[...].reshape(width, group)

    def project(s, carry):
        pre = jnp.dot(hat[s], weight, preferred_element_type=F32)
        for j in range(group // 128):
            last = j == group // 128 - 1
            c_ref, s_ref = (cos_k, sin_k) if last else (cos_q, sin_q)
            value = rotary(pre[:, j * 128 : (j + 1) * 128], c_ref[...], s_ref[...])
            qkv_send[s, :, j * 128 : (j + 1) * 128] = value.astype(BF)
        return carry

    lax.fori_loop(0, 4, project, 0)
    q_copies = [net.send(qkv_send.at[zs[m]], qkv.at[here, :], ("z", m)) for m in (2, 3, 1)]
    own_q = net.local(qkv_send.at[z], qkv.at[here, :])
    line_o.forward()
    up_copies = f_send(1)
    down.spread()
    own_q.wait()
    for copy in q_copies:
        copy.wait_recv()

    kk, vv = twice(qkv[:, span:])

    def pair(p, carry):
        cols = aligned(p * 128, 128, 128)
        for qb in range(4):
            keys = (qb + 1) * tok
            q = qkv[qb * tok : (qb + 1) * tok, cols]
            lane = lax.broadcasted_iota(jnp.int32, (tok, 128), 1)
            row = lax.broadcasted_iota(jnp.int32, (tok, keys), 0) + qb * tok
            col = lax.broadcasted_iota(jnp.int32, (tok, keys), 1)
            outs = []
            for h in range(2):
                mine = (lane < 64) if h == 0 else (lane >= 64)
                qh = jnp.where(mine, q, jnp.zeros_like(q))
                s = right_dot(qh, kk[:keys]) * HEAD_SIZE ** (-0.5)
                s = jnp.where(col <= row, s, -1e30)
                top = jnp.max(s, axis=-1, keepdims=True)
                e = jnp.exp(s - top)
                total = jnp.sum(e, axis=-1, keepdims=True)
                probs = (e * (1.0 / total)).astype(BF)
                outs.append(dot(probs, vv[:keys]))
                old = lse[qb * tok : (qb + 1) * tok, :]
                lse[qb * tok : (qb + 1) * tok, :] = jnp.where(
                    lane == 2 * p + h, top + jnp.log(total), old
                )
            heads[qb * tok : (qb + 1) * tok, cols] = jnp.where(
                lane < 64, outs[0], outs[1]
            ).astype(BF)
        return carry

    lse[...] = jnp.zeros_like(lse)
    lax.fori_loop(0, span // 128, pair, 0)
    h_copies = [
        net.send(heads.at[aligned(zs[m] * tok, tok, 16), :], att.at[z], ("z", m))
        for m in (2, 3, 1)
    ]
    own_h = net.local(heads.at[here, :], att.at[z])

    def tokens_start(src, ref):
        place = ref.at[0, here, :]
        far = net.send(src, place, ("z", 2))
        near = net.send(src, place, ("z", 1))
        return far, near, net.send(src, ref.at[1, here, :], CORE)

    def tokens_push(ref, mask, name):
        there = aligned(zs[mask] * tok, tok, 16)
        return net.send(ref.at[0, there, :], ref.at[1 if name == CORE else 0, there, :], name)

    def tokens_forward(ref, far):
        far.wait_recv()
        return [tokens_push(ref, 2, ("z", 1)), tokens_push(ref, 2, CORE)]

    def tokens_end(ref, near, last):
        near.wait_recv()
        last[0].wait_recv()
        return [tokens_push(ref, m, CORE) for m in (1, 3)]

    own_f.wait()
    for copy in gate_copies:
        copy.wait_recv()
    plane_g, plane_u = f_plane(0), f_plane(1)
    plane_g.start()
    line_o.spread()
    line_o.finish()
    own_h.wait()
    for copy in h_copies:
        copy.wait_recv()


    c_near = net.send(cot, c_all.at[here, :], ("z", 1))
    c_far = net.send(cot, c_all.at[here, :], ("z", 2))
    sums = Sums(net, part, r1, mid, r2)
    for m in (6, 2, 4, 0):
        s = chip_of(m)
        for c in range(4):
            cols = pl.ds(c * (width // 4), width // 4)
            weight = wo_v[:, :, :, cols].reshape(span, width // 4)
            part[s, :, cols] = dot(att[s], weight).astype(BF)
        sums.first(m)
    sums.second()
    plane_g.forward()
    for side in (0, 1):
        cols = half_of(hmid, side)
        hmid[:, cols] = x_ref[:, cols].astype(F32) + sums.total(side)
    value = hmid[...]
    hat2[...] = (value * rms(value)).astype(BF)
    own_n = net.local(hat2, n_all.at[0, here, :])
    n_far, n_near, n_own = tokens_start(hat2, n_all)
    outs = [
        net.local(wq_v, wq_out), net.local(wo_v, wo_out), net.local(qkv, qkv_out),
        net.local(att, att_out), net.local(hat, hat_out),
    ]
    for copy in up_copies:
        copy.wait_recv()
    plane_u.start()
    plane_g.spread()
    n_last = tokens_forward(n_all, n_far)
    plane_u.forward()
    n_core = tokens_end(n_all, n_near, n_last)
    plane_u.spread()
    for plane in (down, plane_g, plane_u):
        plane.finish()
    for copy in [n_own, n_last[1], c_near, c_far] + n_core:
        copy.wait_recv()
    own_n.wait()
    own[2].wait()
    for copy in outs:
        copy.wait()
    net.finish()


def first_call(x, wq, wk, wv, gain1, w_gate, w_up, gain2, tables4, wo, wd, cot):
    tok, width = x.shape
    ff = w_gate.shape[1] // 4
    span = width // 4
    group = span + 128
    sds = jax.ShapeDtypeStruct
    v = pltpu.VMEM
    return pl.pallas_call(
        first_kernel,
        name="first",
        out_shape=[
            sds((2, width, ff), BF), sds((ff, width), BF),
            sds((4, 2, 4, 64, group), BF), sds((2, 4, 64, width), BF), sds((4, tok, width), BF),
            sds((4 * tok, width), BF), sds((2, 4 * tok, width), BF),
            sds((4 * tok, group), BF), sds((4, tok, span), BF),
            sds((4 * tok, 128), F32), sds((tok, width), F32),
        ],
        in_specs=[VMEM] * 15,
        out_specs=[ANY] * 9 + [VMEM] * 2,
        scratch_shapes=[
            v((4, 64, group), BF), v((4, 2, 64, ff), BF), v((4, 2, 4, 64, group), BF),
            v((2, 4, 64, width), BF), v((4, tok, width), BF), v((4, tok, group), BF),
            v((4 * tok, group), BF), v((4 * tok, span), BF), v((4, tok, span), BF),
            v((4, tok, width), BF), v((2, 2, tok, width // 2), BF), v((2, tok, width // 2), BF),
            v((2, tok, width // 2), BF), v((tok, width), BF),
            pltpu.SemaphoreType.DMA((96,)),
            pltpu.SemaphoreType.DMA((96,)),
        ],
        compiler_params=pltpu.CompilerParams(
            collective_id=1, has_side_effects=True, vmem_limit_bytes=56 * 2**20
        ),
    )(x, wq, wk, wv, gain1, w_gate, w_up, gain2, *tables4, wo, wd, cot)


def second_kernel(
    n_all, c_all, wg, wd,
    dn_out, mx_part, hg_out, gdown,
    wg_v, wd_v, n_v, c_v, gate_s, up_s, hid, dg, du,
    dn_part, dn_r1, dn_s, dn_r2,
    hd, hd_r1, hd_k, hd_r2, sib_s, sib_r, send_sems, recv_sems,
):
    net = Net(send_sems, recv_sems)
    dp, z, dps, zs = net.dp, net.z, net.dps, net.zs
    core = lax.rem(dp, 2)
    tok, width = dn_r2.shape
    ff = hid.shape[2]
    half = width // 2
    pair = 2 * tok

    def slot(mask):
        return aligned(zs[mask] * tok, tok, 16)

    loads = [
        net.local(n_all.at[0], n_v.at[0]),
        net.local(wg.at[0], wg_v.at[0]),
        net.local(wg.at[1], wg_v.at[1]),
        net.local(wd, wd_v),
        net.local(c_all.at[slot(0), :], c_v.at[0, slot(0), :]),
        net.local(c_all.at[slot(1), :], c_v.at[0, slot(1), :]),
        net.local(c_all.at[slot(2), :], c_v.at[0, slot(2), :]),
        net.local(n_all.at[1], n_v.at[1]),
    ]
    net.barrier([X, Y, CORE, ("z", 1), ("z", 2)])

    def c_push(mask, name):
        there = c_v.at[1 if name == CORE else 0, slot(mask), :]
        return net.send(c_all.at[slot(mask), :], there, name)

    c_last = c_push(2, ("z", 1))
    sib = [c_push(m, CORE) for m in (0, 1, 2)]
    for copy in loads[:3]:
        copy.wait()
    near_pair = lax.div(z, 2)
    far = aligned((1 - near_pair) * pair, pair, 16)
    near = aligned(near_pair * pair, pair, 16)

    def chunks(fn, total, size):
        whole = total // size

        def step(i, carry):
            fn(i * size, size)
            return carry

        lax.fori_loop(0, whole, step, 0)
        if total % size:
            fn(whole * size, total - whole * size)

    def forward(rows):
        def chunk(start, size):
            cols = aligned(start, size, 128)
            n = n_v[0, rows, :]
            gate = dot(n, wg_v[0, :, cols])
            upper = dot(n, wg_v[1, :, cols])
            gate_s[rows, cols] = gate
            up_s[rows, cols] = upper
            hid[0, rows, cols] = (gate * jax.nn.sigmoid(gate) * upper).astype(BF)

        chunks(chunk, ff, 256)
        sib.append(net.send(hid.at[0, rows, :], hid.at[1, rows, :], CORE))

    def mix(rows):
        def chunk(start, size):
            cols = aligned(start, size, 128)
            mx_part[rows, cols] = dot(hid[0, rows, :], wd_v[:, cols]).astype(BF)

        chunks(chunk, width, 256)

    def turn(rows):
        def chunk(start, size):
            cols = aligned(start, size, 128)
            dhid = right_dot(c_v[0, rows, :], wd_v[cols, :])
            gate = gate_s[rows, cols]
            sigma = jax.nn.sigmoid(gate)
            dg[0, rows, cols] = (
                dhid * up_s[rows, cols] * sigma * (1.0 + gate * (1.0 - sigma))
            ).astype(BF)
            du[0, rows, cols] = (dhid * gate * sigma).astype(BF)

        chunks(chunk, ff, 256)
        for ref in (dg, du):
            sib.append(net.send(ref.at[0, rows, :], ref.at[1, rows, :], CORE))

    def back(rows, part):
        def chunk(start, size):
            cols = aligned(start + part * half, size, 128)
            total = right_dot(dg[0, rows, :], wg_v[0, cols, :])
            total += right_dot(du[0, rows, :], wg_v[1, cols, :])
            dn_part[rows, cols] = total.astype(BF)

        chunks(chunk, half, 256)

    def piece(part):
        return pl.ds(part * half, half)

    forward(far)
    forward(near)
    for copy in loads[3:]:
        copy.wait()
    c_last.wait_recv()
    sib.append(net.send(c_v.at[0, slot(3), :], c_v.at[1, slot(3), :], CORE))
    early, sib = sib, []
    turn(far)
    dn_a = []
    for part in (0, 1):
        back(far, part)
        dn_a.append(
            net.send(dn_part.at[slot(3), piece(part)], dn_r1.at[1, :, piece(part)], ("z", 1))
        )
    turn(near)
    for copy in early:
        copy.wait_recv()
    ccols = aligned(core * half, half, 128)

    def down_chunk(start, size):
        cols = aligned(start, size, 128)
        total = left_dot(hid[0, :, cols], c_v[0, :, ccols])
        total += left_dot(hid[1, :, cols], c_v[1, :, ccols])
        hd[cols, :] = total.astype(BF)

    chunks(down_chunk, ff, 256)
    chip = ff // 4
    quarter = half // 2

    def hd_at(mask, side):
        return aligned(lax.div(dps[mask], 2) * chip, chip, 16), pl.ds(side * quarter, quarter)

    def hd_send(mask, side, place, name):
        r, c = hd_at(mask, side)
        return net.send(hd.at[r, c], hd_r1.at[side, place], name)

    hd_1 = [hd_send(6, 0, 1, X), hd_send(6, 1, 1, Y), hd_send(2, 0, 0, X), hd_send(4, 1, 0, Y)]

    dn_c = []
    for part in (0, 1):
        dn_a[part].wait_recv()
        cols = piece(part)
        dn_s[:, cols] = (
            dn_part[slot(2), cols].astype(F32) + dn_r1[1, :, cols].astype(F32)
        ).astype(BF)
        dn_c.append(net.send(dn_s.at[:, cols], dn_r2.at[:, cols], ("z", 2)))
    dn_b = []
    for part in (0, 1):
        back(near, part)
        dn_b.append(
            net.send(dn_part.at[slot(1), piece(part)], dn_r1.at[0, :, piece(part)], ("z", 1))
        )
    for copy in sib:
        copy.wait_recv()

    def block(b, carry):
        cols = aligned((b * 2 + core) * 256, 256, 128)
        left = [n_v[s, :, cols].T for s in (0, 1)]
        for t, grad in enumerate((dg, du)):
            total = dot(left[0], grad[0]) + dot(left[1], grad[1])
            wg_v[t, aligned(b * 256, 256, 16), :] = total.astype(BF)
        return carry

    lax.fori_loop(0, 4, block, 0)
    hg_copy = net.local(wg_v.at[:, pl.ds(0, 1024), :], hg_out)
    mix(far)
    mix(near)

    hd_1[0].wait_recv()
    hd_1[1].wait_recv()
    hd_2 = []
    for side, (mask, name) in enumerate(((4, Y), (2, X))):
        r, c = hd_at(mask, side)
        hd_k[side] = (hd[r, c].astype(F32) + hd_r1[side, 1].astype(F32)).astype(BF)
        hd_2.append(net.send(hd_k.at[side], hd_r2.at[side], name))
    for part in (0, 1):
        dn_b[part].wait_recv()
        dn_c[part].wait_recv()
        cols = piece(part)
        dn_out[:, cols] = (
            dn_part[slot(0), cols].astype(F32)
            + dn_r1[0, :, cols].astype(F32)
            + dn_r2[:, cols].astype(F32)
        )
    hd_1[2].wait_recv()
    hd_1[3].wait_recv()
    own = core * (chip // 2)
    other = (1 - core) * (chip // 2)
    for side in (0, 1):
        hd_2[side].wait_recv()
        r0 = lax.div(dp, 2) * chip

        def total(start):
            _, c = hd_at(0, side)
            return (
                hd[aligned(r0 + start, chip // 2, 16), c].astype(F32)
                + hd_r1[side, 0, aligned(start, chip // 2, 16), :].astype(F32)
                + hd_r2[side, aligned(start, chip // 2, 16), :].astype(F32)
            )

        sib_s[:, side * quarter : (side + 1) * quarter] = total(other)
        gdown[:, aligned(core * half + side * quarter, quarter, 128)] = total(own)
    last = net.send(sib_s, sib_r, CORE)
    last.wait_recv()
    gdown[:, aligned((1 - core) * half, half, 128)] = sib_r[...]
    hg_copy.wait()
    net.finish()


def second_call(n_all, c_all, wg, wd):
    _, length, width = n_all.shape
    tok = length // 4
    ff = wg.shape[2]
    sds = jax.ShapeDtypeStruct
    half = width // 2
    chip = ff // 4
    v = pltpu.VMEM
    return pl.pallas_call(
        second_kernel,
        name="second",
        out_shape=[
            sds((tok, width), F32), sds((length, width), BF),
            sds((2, 1024, ff), BF), sds((chip // 2, width), F32),
        ],
        in_specs=[ANY] * 4,
        out_specs=[VMEM, VMEM, ANY, VMEM],
        scratch_shapes=[
            v((2, width, ff), BF), v((ff, width), BF), v((2, length, width), BF),
            v((2, length, width), BF), v((length, ff), F32), v((length, ff), F32),
            v((2, length, ff), BF), v((2, length, ff), BF), v((2, length, ff), BF),
            v((length, width), BF), v((2, tok, width), BF), v((tok, width), BF), v((tok, width), BF),
            v((ff, half), BF), v((2, 2, chip, half // 2), BF), v((2, chip, half // 2), BF),
            v((2, chip, half // 2), BF), v((chip // 2, half), F32), v((chip // 2, half), F32),
            pltpu.SemaphoreType.DMA((56,)),
            pltpu.SemaphoreType.DMA((56,)),
        ],
        compiler_params=pltpu.CompilerParams(
            collective_id=2, has_side_effects=True, vmem_limit_bytes=62 * 2**20
        ),
    )(n_all, c_all, wg, wd)


def third_kernel(
    x_ref, hmid, cot, dn2, qkv, lse, cos_q, sin_q, cos_k, sin_k,
    mx, wq, wo, hat, att, hg,
    tok_out, mixed, g2_out, g1_out, fb,
    wq_v, wo_v, hat_v, hat_s, att_v, att_s, mx_v, mx_r1, mx_s, mx_r2,
    hg_v, f_r1, f_k, f_r2, fs, dh, dbr, dbr_s, dsend, gh, dqkv, dk_acc, dv_acc, dback,
    dpre, dpre_s, part, r1, mid, r2, g2_p, g2_r1, g2_s, g2_r2, g1_p, g1_r1, g1_s, g1_r2, g1_f,
    send_sems, recv_sems,
):
    net = Net(send_sems, recv_sems)
    dp, z, dps, zs = net.dp, net.z, net.dps, net.zs
    tok, width = x_ref.shape
    group = qkv.shape[1]
    span = group - 128
    here = aligned(z * tok, tok, 16)
    core, chip = lax.rem(dp, 2), lax.div(dp, 2)

    def chip_of(mask):
        return lax.div(dps[mask], 2)

    def slot(mask):
        return aligned(zs[mask] * tok, tok, 16)

    def hg_at(t, mask):
        return hg.at[t, aligned(chip_of(mask) * 256, 256, 16), :]

    loads = [
        net.local(wo, wo_v),
        net.local(hg_at(0, 0), hg_v.at[0, 0]),
        net.local(hg_at(0, 4), hg_v.at[0, 1]),
        net.local(hg_at(1, 0), hg_v.at[1, 0]),
        net.local(hg_at(1, 2), hg_v.at[1, 1]),
        net.local(mx.at[slot(0), :], mx_v.at[0]),
        net.local(mx.at[slot(2), pl.ds(0, width // 2)], mx_v.at[1, :, pl.ds(0, width // 2)]),
        net.local(mx.at[slot(1), pl.ds(width // 2, width // 2)], mx_v.at[1, :, pl.ds(width // 2, width // 2)]),
        net.local(att, att_v),
        net.local(wq, wq_v),
        net.local(hat, hat_v),
    ]
    net.barrier(PARTNERS + [("d", 6)])
    half = width // 2
    mx_cols = [pl.ds(0, half), pl.ds(half, half)]

    def mx_send(mask, side, place, name):
        c = mx_cols[side]
        return net.send(mx.at[slot(mask), c], mx_r1.at[place, :, c], name)

    mx_1 = [
        [mx_send(3, side, 1, ("z", step)), mx_send(step, side, 0, ("z", step))]
        for side, step in ((0, 1), (1, 2))
    ]

    def norm_back(value, grad):
        inv = rms(value)
        inner = jnp.mean(value * grad, axis=-1, keepdims=True)
        return inv * grad - value * (inv * inv * inv * inner)

    dh[...] = cot[...].astype(F32) + norm_back(hmid[...], dn2[...])
    dbr[chip] = dh[...].astype(BF)
    plane_b = Plane(net, lambda m, s: dbr.at[chip_of(m), :, pl.ds(s * half, half)], lambda m: [])
    plane_b.start()
    small = [
        net.send(att.at[:, :, aligned((1 - core) * 256, 256, 128)], att_s, CORE)
    ] + [
        net.send(
            hat.at[:, :, aligned(i * 512 + (1 - core) * 256, 256, 128)],
            hat_s.at[:, :, pl.ds(i * 256, 256)],
            CORE,
        )
        for i in range(4)
    ]
    plane_b.forward()
    f_1 = [
        net.send(hg_at(0, 6), f_r1.at[0, 1], X),
        net.send(hg_at(1, 6), f_r1.at[1, 1], Y),
        net.send(hg_at(0, 2), f_r1.at[0, 0], X),
        net.send(hg_at(1, 4), f_r1.at[1, 0], Y),
    ]
    plane_b.spread()
    loads[0].wait()
    d_copies = []
    weight = wo_v[...].reshape(span, width)
    for m in (2, 3, 1, 0):
        dsend[m] = right_dot(dbr[zs[m]], weight).astype(BF)
        if m:
            d_copies.append(net.send(dsend.at[m], gh.at[here, :], ("z", m)))
    gh[here, :] = dsend[0]
    dbr_copy = net.send(dbr, dbr_s, CORE)
    for copy in loads[1:]:
        copy.wait()
    for copy in d_copies:
        copy.wait_recv()
    mx_2 = []
    for side, step in ((0, 2), (1, 1)):
        c = mx_cols[side]
        mx_1[side][0].wait_recv()
        mx_s[:, c] = (mx_v[1, :, c].astype(F32) + mx_r1[1, :, c].astype(F32)).astype(BF)
        mx_2.append(net.send(mx_s.at[:, c], mx_r2.at[:, c], ("z", step)))

    scale = HEAD_SIZE ** (-0.5)
    kk, vv = twice(qkv[:, span:])
    dk_acc[...] = jnp.zeros_like(dk_acc)
    dv_acc[...] = jnp.zeros_like(dv_acc)

    def pair(p, carry):
        cols = aligned(p * 128, 128, 128)
        for qb in range(4):
            keys = (qb + 1) * tok
            rows = slice(qb * tok, (qb + 1) * tok)
            q = qkv[rows, cols]
            g = gh[rows, cols]
            lane = lax.broadcasted_iota(jnp.int32, (tok, 128), 1)
            row = lax.broadcasted_iota(jnp.int32, (tok, keys), 0) + qb * tok
            col = lax.broadcasted_iota(jnp.int32, (tok, keys), 1)
            outs = []
            for h in range(2):
                lanes = (lane < 64) if h == 0 else (lane >= 64)
                qh = jnp.where(lanes, q, jnp.zeros_like(q))
                gg = jnp.where(lanes, g, jnp.zeros_like(g))
                log = jnp.sum(
                    jnp.where(lane == 2 * p + h, lse[rows, :], 0.0), axis=-1, keepdims=True
                )
                s = right_dot(qh, kk[:keys]) * scale
                probs = jnp.exp(jnp.where(col <= row, s, -1e30) - log)
                pg = right_dot(gg, vv[:keys])
                delta = jnp.sum(probs * pg, axis=-1, keepdims=True)
                ds = (probs * (pg - delta)).astype(BF)
                outs.append(dot(ds, kk[:keys]) * scale)
                dk_acc[:keys, :] += left_dot(ds, qh)
                dv_acc[:keys, :] += left_dot(probs.astype(BF), gg)
            dqkv[rows, cols] = jnp.where(lane < 64, outs[0], outs[1]).astype(BF)
        return carry

    lax.fori_loop(0, span // 128, pair, 0)
    dk = dk_acc[...]
    dv = dv_acc[...]
    lane = lax.broadcasted_iota(jnp.int32, dk.shape, 1)
    dqkv[:, span:] = jnp.where(
        lane < 64, (dk + pltpu.roll(dk, 64, 1)) * scale, dv + pltpu.roll(dv, 64, 1)
    ).astype(BF)
    b_copies = [net.send(dqkv.at[slot(m), :], dback.at[z], ("z", m)) for m in (2, 3, 1)]
    dback[z] = dqkv[here, :]

    f_2 = []
    for t, name in ((0, Y), (1, X)):
        f_1[t].wait_recv()
        f_k[t] = (hg_v[t, 1].astype(F32) + f_r1[t, 1].astype(F32)).astype(BF)
        f_2.append(net.send(f_k.at[t], f_r2.at[t], name))

    class Line:
        def __init__(self, parts, r1, s, r2):
            self.parts, self.r1, self.s, self.r2 = parts, r1, s, r2
            self.sent = [
                net.send(parts.at[zs[3]], r1.at[1], ("z", 1)),
                net.send(parts.at[zs[1]], r1.at[0], ("z", 1)),
            ]

        def middle(self):
            self.sent[0].wait_recv()
            self.s[...] = (self.parts[zs[2]].astype(F32) + self.r1[1].astype(F32)).astype(BF)
            self.far = net.send(self.s, self.r2, ("z", 2))

        def total(self):
            self.sent[1].wait_recv()
            self.far.wait_recv()
            own = self.parts[z].astype(F32) + self.r1[0].astype(F32)
            return own + self.r2[...].astype(F32)

    small[0].wait_recv()
    dbr_copy.wait_recv()
    mine = att_v[:, :, aligned(core * 256, 256, 128)].reshape(4 * tok, 256).T
    theirs = att_s[...].reshape(4 * tok, 256).T

    def out_chunk(i, carry):
        cols = aligned(i * 512, 512, 128)
        total = dot(mine, dbr[:, :, cols].reshape(4 * tok, 512))
        total += dot(theirs, dbr_s[:, :, cols].reshape(4 * tok, 512))
        g2_p[:, :, cols] = total.astype(BF).reshape(4, 64, 512)
        return carry

    lax.fori_loop(0, width // 512, out_chunk, 0)
    line_o = Line(g2_p, g2_r1, g2_s, g2_r2)

    for copy in b_copies:
        copy.wait_recv()
    for s in range(4):
        for j in range(group // 128):
            cols = slice(j * 128, (j + 1) * 128)
            last = j == group // 128 - 1
            c_ref, s_ref = (cos_k, sin_k) if last else (cos_q, sin_q)
            value = dback[s, :, cols].astype(F32)
            dpre[s, :, cols] = rotary(value, c_ref[...], -s_ref[...]).astype(BF)
    dpre_copy = net.send(dpre, dpre_s, CORE)

    left = dpre[...].reshape(4 * tok, group)

    def dhat_chunk(i, carry):
        cols = aligned(i * 256, 256, 128)
        rows = wq_v[lax.div(i, 2), lax.rem(i, 2)].reshape(256, group)
        part[:, :, cols] = right_dot(left, rows).astype(BF).reshape(4, tok, 256)
        return carry

    lax.fori_loop(0, width // 256, dhat_chunk, 0)
    sums = Sums(net, part, r1, mid, r2)
    for m in (6, 2, 4):
        sums.first(m)

    for copy in small[1:]:
        copy.wait_recv()
    dpre_copy.wait_recv()
    right = dpre_s[...].reshape(4 * tok, group)

    def first_chunk(i, carry):
        own = hat_v[:, :, aligned(i * 512 + core * 256, 256, 128)].reshape(4 * tok, 256).T
        sib = hat_s[:, :, aligned(i * 256, 256, 128)].reshape(4 * tok, 256).T
        total = dot(own, left) + dot(sib, right)
        g1_p[:, i] = total.astype(BF).reshape(4, 64, group)
        return carry

    lax.fori_loop(0, 4, first_chunk, 0)
    line_q = Line(g1_p, g1_r1, g1_s, g1_r2)
    line_o.middle()
    f_copies = []
    for t in (0, 1):
        f_1[2 + t].wait_recv()
        f_2[t].wait_recv()
        total = hg_v[t, 0].astype(F32) + f_r1[t, 0].astype(F32) + f_r2[t].astype(F32)
        for i in range(4):
            fs[i, t] = total[i * 64 : (i + 1) * 64, :].astype(BF)
    sums.second()
    line_q.middle()
    f_copies = [net.send(fs.at[zs[m]], fb.at[z], ("z", m)) for m in (2, 3, 1)]
    fb[z] = fs[z]
    for side in (0, 1):
        mx_1[side][1].wait_recv()
        mx_2[side].wait_recv()
    total = mx_v[0].astype(F32) + mx_r1[0].astype(F32) + mx_r2[...].astype(F32)
    mixed[...] = (hmid[...] + total).astype(BF)
    g2_out[...] = line_o.total()
    for side in (0, 1):
        dn2[:, side * half : (side + 1) * half] = sums.total(side)
    tok_out[...] = (dh[...] + norm_back(x_ref[...].astype(F32), dn2[...])).astype(BF)
    g1_f[...] = line_q.total().astype(BF)
    g_copies = [net.send(g1_f.at[chip_of(m)], g1_out.at[chip], ("d", m)) for m in (6, 2, 4)]
    g1_out[chip] = g1_f[chip]
    for copy in g_copies + f_copies:
        copy.wait_recv()
    net.finish()


def third_call(x, hmid, cot, dn2, qkv, lse, tables4, mx, wq, wo, hat, att, hg):
    tok, width = x.shape
    group = qkv.shape[1]
    span = group - 128
    ff = hg.shape[-1]
    sds = jax.ShapeDtypeStruct
    v = pltpu.VMEM
    return pl.pallas_call(
        third_kernel,
        name="third",
        out_shape=[
            sds((tok, width), BF), sds((tok, width), BF), sds((64, width), F32),
            sds((4, 64, group), BF), sds((4, 2, 64, ff), BF),
        ],
        in_specs=[VMEM] * 10 + [ANY] * 6,
        out_specs=[VMEM] * 5,
        scratch_shapes=[
            v((4, 2, 4, 64, group), BF), v((2, 4, 64, width), BF), v((4, tok, width), BF),
            v((4, tok, width // 2), BF), v((4, tok, span), BF), v((4, tok, span // 2), BF),
            v((2, tok, width), BF), v((2, tok, width), BF), v((tok, width), BF), v((tok, width), BF),
            v((2, 2, 256, ff), BF), v((2, 2, 256, ff), BF), v((2, 256, ff), BF), v((2, 256, ff), BF),
            v((4, 2, 64, ff), BF), v((tok, width), F32), v((4, tok, width), BF),
            v((4, tok, width), BF), v((4, tok, span), BF), v((4 * tok, span), BF),
            v((4 * tok, group), BF), v((4 * tok, 128), F32), v((4 * tok, 128), F32),
            v((4, tok, group), BF), v((4, tok, group), BF), v((4, tok, group), BF),
            v((4, tok, width), BF), v((2, 2, tok, width // 2), BF), v((2, tok, width // 2), BF),
            v((2, tok, width // 2), BF),
            v((4, 64, width), BF), v((2, 64, width), BF), v((64, width), BF), v((64, width), BF),
            v((4, 4, 64, group), BF), v((2, 4, 64, group), BF), v((4, 64, group), BF),
            v((4, 64, group), BF), v((4, 64, group), BF),
            pltpu.SemaphoreType.DMA((80,)),
            pltpu.SemaphoreType.DMA((80,)),
        ],
        compiler_params=pltpu.CompilerParams(
            collective_id=3, has_side_effects=True, vmem_limit_bytes=60 * 2**20
        ),
    )(x, hmid, cot, dn2, qkv, lse, *tables4, mx, wq, wo, hat, att, hg)


def last_kernel(
    fb, g1, wq, wk, wv, w_gate, w_up, gain1, gain2,
    gq, gk, gv, g_gate, g_up, g_gain1, g_gain2,
):
    span = g1.shape[2] - 128
    lane = lax.broadcasted_iota(jnp.int32, (g1.shape[1], 128), 1)
    scale = gain1[...]

    def put(out, weight, cols, value):
        out[:, cols] = value * scale
        return jnp.sum(value * weight[:, cols].astype(F32), axis=1, keepdims=True)

    total = jnp.zeros_like(g_gain1)
    for g in range(4):
        total += put(gq, wq, slice(g * span, (g + 1) * span), g1[g, :, :span].astype(F32))
    for g in (0, 2):
        one = g1[g, :, span:].astype(F32)
        two = g1[g + 1, :, span:].astype(F32)
        cols = slice(g * 64, g * 64 + 128)
        total += put(gk, wk, cols, jnp.where(lane < 64, one, pltpu.roll(two, 64, 1)))
        total += put(gv, wv, cols, jnp.where(lane < 64, pltpu.roll(one, 64, 1), two))
    g_gain1[...] = total
    size = fb.shape[-1] // 8
    total = jnp.zeros_like(g_gain2)
    for t, (out, weight) in enumerate(((g_gate, w_gate), (g_up, w_up))):
        for d in range(0, 8, 2):
            parts = [
                fb[i, t, :, e * size : (e + 1) * size].astype(F32) for e in (d, d + 1) for i in range(4)
            ]
            joined = jnp.concatenate(parts, axis=1)
            cols = pl.ds(d * 4 * size, 8 * size)
            total += jnp.sum(joined * weight[:, cols].astype(F32), axis=1, keepdims=True)
            out[:, cols] = joined * gain2[...]
    g_gain2[...] = total


def last_call(fb, g1, wq, wk, wv, w_gate, w_up, gain1, gain2):
    rows, ff = w_gate.shape
    sds = jax.ShapeDtypeStruct
    return pl.pallas_call(
        last_kernel,
        name="last",
        out_shape=[
            sds(wq.shape, F32), sds(wk.shape, F32), sds(wv.shape, F32),
            sds((rows, ff), F32), sds((rows, ff), F32), sds((rows, 1), F32), sds((rows, 1), F32),
        ],
        in_specs=[VMEM] * 9,
        out_specs=[VMEM] * 7,
        compiler_params=pltpu.CompilerParams(vmem_limit_bytes=40 * 2**20),
    )(fb, g1, wq, wk, wv, w_gate, w_up, gain1, gain2)


def shards(
    tokens, norm_first, w_query, w_key, w_value, w_out, norm_second, w_gate, w_up, w_down, cotangent
):
    count = tokens.shape[0]
    gain1 = norm_first.astype(F32)[:, None]
    gain2 = norm_second.astype(F32)[:, None]
    cosine, sine = tables(lax.axis_index("seq") * count + jnp.arange(count))
    cosine, sine = cosine[:, 0], sine[:, 0]
    one, zero = jnp.ones_like(cosine), jnp.zeros_like(cosine)
    tables4 = [
        jnp.concatenate(parts, axis=1)
        for parts in (
            [cosine] * 4,
            [-sine, sine] * 2,
            [cosine, cosine, one, one],
            [-sine, sine, zero, zero],
        )
    ]
    wg, wd, wq, wo, hat, c_all, n_all, qkv, att, lse, hmid = first_call(
        tokens, w_query, w_key, w_value, gain1, w_gate, w_up, gain2, tables4,
        w_out, w_down, cotangent,
    )
    dhat2, mixed_part, hg, grad_down = second_call(n_all, c_all, wg, wd)
    grad_tokens, mixed, grad_out, grad_first, parts = third_call(
        tokens, hmid, cotangent, dhat2, qkv, lse, tables4, mixed_part, wq, wo, hat, att, hg
    )
    grad_query, grad_key, grad_value, grad_gate, grad_up, grad_gain1, grad_gain2 = last_call(
        parts, grad_first, w_query, w_key, w_value, w_gate, w_up, gain1, gain2
    )
    return (
        mixed,
        grad_tokens,
        grad_gain1[:, 0],
        grad_query,
        grad_key,
        grad_value,
        grad_out,
        grad_gain2[:, 0],
        grad_gate,
        grad_up,
        grad_down,
    )


def solution(mesh):
    special = mesh.shape['dp'] == 8 and mesh.shape['seq'] == KEY_VALUE_HEADS
    rows = P(("dp", "seq"), None)
    line = P(("dp", "seq"))
    return jax.shard_map(
        shards if special else general_shards,
        mesh=mesh,
        in_specs=(rows, line, rows, rows, rows, rows, line, rows, rows, rows, rows),
        out_specs=(rows, rows, line, rows, rows, rows, rows, line, rows, rows, rows),
        check_vma=False,
    )
```

```python
import jax
import jax.numpy as jnp
from jax import lax
from jax.experimental import pallas as pl
from jax.experimental.pallas import tpu as pltpu
from jax.sharding import PartitionSpec as P

H = 32
KEY_VALUE_HEADS = 4
HEAD_SIZE = 64
EPS = 1e-05
BF = jnp.bfloat16
F32 = jnp.float32


def tables(positions):
    freq = 10000.0 ** (-jnp.arange(0, HEAD_SIZE // 2, dtype=F32) * 2.0 / HEAD_SIZE)
    angle = positions.astype(F32)[:, None] * freq[None, :]
    return (jnp.cos(angle)[:, None, :], jnp.sin(angle)[:, None, :])


def rotate(heads, cosine, sine):
    half = heads.shape[-1] // 2
    first = heads[..., :half]
    second = heads[..., half:]
    return jnp.concatenate(
        [first * cosine - second * sine, second * cosine + first * sine], axis=-1
    )


def dot(left, right):
    return jnp.dot(left, right, preferred_element_type=F32)


def left_dot(left, right):
    return lax.dot_general(left, right, (((0,), (0,)), ((), ())), preferred_element_type=F32)


def right_dot(left, right):
    return lax.dot_general(left, right, (((1,), (1,)), ((), ())), preferred_element_type=F32)


def bits_of(count):
    return [1 << k for k in range(count.bit_length() - 1)]


class Axis:
    def __init__(self, name):
        self.name = name
        self.size = lax.axis_size(name)
        self.me = lax.axis_index(name)

    def swap(self, value, mask):
        return lax.ppermute(value, self.name, [(i, i ^ mask) for i in range(self.size)])

    def all(self, value):
        return [value if m == 0 else self.swap(value, m) for m in range(self.size)]

    def exchange(self, stacked):
        return [
            lax.dynamic_index_in_dim(stacked, self.me ^ m, 0, keepdims=False)
            if m == 0
            else self.swap(
                lax.dynamic_index_in_dim(stacked, self.me ^ m, 0, keepdims=False), m
            )
            for m in range(self.size)
        ]

    def natural(self, pieces):
        stack = jnp.stack(pieces)
        return [
            lax.dynamic_index_in_dim(stack, self.me ^ i, 0, keepdims=False)
            for i in range(self.size)
        ]


def orders(size):
    even = [m for m in range(size) if m % 2 == 0]
    return even, [m + 1 for m in even]


def chip_bits(size, turn):
    bits = bits_of(size)[1:]
    return bits if turn == 0 else bits[::-1]


def gather_chips(dp, piece, turn):
    pieces = {0: piece}
    for bit in chip_bits(dp.size, turn):
        pieces.update({m ^ bit: dp.swap(p, bit) for m, p in list(pieces.items())})
    return pieces


def gather_rows(dp, piece, turn):
    pieces = gather_chips(dp, piece, turn)
    even = jnp.concatenate([pieces[m] for m in orders(dp.size)[0]], axis=0)
    return even, dp.swap(even, 1)


def scatter_chips(dp, blocks, turn):
    for bit in chip_bits(dp.size, turn):
        for m in [m for m in blocks if m & bit]:
            other = dp.swap(blocks.pop(m).astype(BF), bit)
            blocks[m ^ bit] = blocks[m ^ bit].astype(F32) + other.astype(F32)
    return blocks[0]


def scatter_rows(dp, even_fn, odd, turn):
    rows = odd.shape[0] * 2 // dp.size
    other = dp.swap(odd, 1)
    even = (even_fn() + other.astype(F32)).astype(BF)
    blocks = {
        m: even[i * rows : (i + 1) * rows] for i, m in enumerate(orders(dp.size)[0])
    }
    return scatter_chips(dp, blocks, turn)


def mask_columns(dp, value):
    width = value.shape[1] // dp.size
    return tuple(
        jnp.concatenate(
            [lax.dynamic_slice_in_dim(value, (dp.me ^ m) * width, width, 1) for m in group],
            axis=1,
        )
        for group in orders(dp.size)
    )


def natural_columns(dp, even, odd):
    both = jnp.concatenate([even, odd], axis=1)
    width = both.shape[1] // dp.size
    half = dp.size // 2
    parts = []
    for i in range(dp.size):
        mask = dp.me ^ i
        place = mask // 2 + (mask % 2) * half
        parts.append(lax.dynamic_slice_in_dim(both, place * width, width, 1))
    return jnp.concatenate(parts, axis=1)


def attend(queries, keys, values, visible):
    scores = jnp.einsum("qhd,kd->hqk", queries, keys, preferred_element_type=F32)
    scores = jnp.where(visible[None], scores * HEAD_SIZE ** (-0.5), -1e30)
    top = jnp.max(scores, axis=-1, keepdims=True)
    expo = jnp.exp(scores - top)
    total = jnp.sum(expo, axis=-1, keepdims=True)
    probs = (expo / total).astype(BF)
    result = jnp.einsum("hqk,kd->qhd", probs, values, preferred_element_type=F32)
    return result.astype(BF), top + jnp.log(total)


def attend_back(queries, keys, values, grad_heads, logsum, visible):
    scale = HEAD_SIZE ** (-0.5)
    scores = jnp.einsum("qhd,kd->hqk", queries, keys, preferred_element_type=F32)
    scores = jnp.where(visible[None], scores * scale, -1e30)
    probs = jnp.exp(scores - logsum)
    pgrad = jnp.einsum("qhd,kd->hqk", grad_heads, values, preferred_element_type=F32)
    delta = jnp.sum(probs * pgrad, axis=-1, keepdims=True)
    sgrad = (probs * (pgrad - delta)).astype(BF)
    qgrad = jnp.einsum("hqk,kd->qhd", sgrad, keys, preferred_element_type=F32) * scale
    kgrad = jnp.einsum("hqk,qhd->kd", sgrad, queries, preferred_element_type=F32) * scale
    vgrad = jnp.einsum("hqk,qhd->kd", probs.astype(BF), grad_heads, preferred_element_type=F32)
    return qgrad.astype(BF), kgrad.astype(BF), vgrad.astype(BF)


def general_shards(
    tokens, norm_first, w_query, w_key, w_value, w_out, norm_second, w_gate, w_up, w_down, cotangent
):
    dp, seq = Axis("dp"), Axis("seq")
    groups = seq.size
    count, width = tokens.shape
    ff = w_gate.shape[1]
    per = H // groups
    repeat = groups // KEY_VALUE_HEADS
    heads_wide = H * HEAD_SIZE
    keys_wide = KEY_VALUE_HEADS * HEAD_SIZE
    gain1 = norm_first.astype(F32)[:, None]
    gain2 = norm_second.astype(F32)[:, None]

    w_first = jnp.concatenate([w_query, w_key, w_value], axis=1)
    w_first_scaled = (w_first.astype(F32) * gain1).astype(BF)
    wide = w_first.shape[1]

    def by_part(weight):
        rows = weight.shape[0]
        scaled = (weight.astype(F32) * gain2).astype(BF)
        parts = scaled.reshape(rows, dp.size, groups, ff // dp.size // groups)
        return parts.transpose(2, 0, 1, 3).reshape(groups, rows, ff // groups)

    down = [gather_chips(dp, w_down[:, t * width // 2 : (t + 1) * width // 2], t) for t in (0, 1)]
    first_rows = jnp.concatenate(seq.natural(seq.all(w_first_scaled)), axis=0)
    first = [gather_rows(dp, first_rows[:, t * wide // 2 : (t + 1) * wide // 2], t) for t in (0, 1)]
    out_rows = jnp.concatenate(seq.natural(seq.all(w_out)), axis=0)
    outw = [gather_rows(dp, out_rows[:, t * width // 2 : (t + 1) * width // 2], t) for t in (0, 1)]
    gate_up = seq.exchange(jnp.stack([by_part(w_gate), by_part(w_up)], axis=1))
    gate_up = jnp.concatenate(seq.natural(gate_up), axis=1)
    (gate_even, gate_odd), (up_even, up_odd) = [
        gather_rows(dp, gate_up[t], t) for t in (0, 1)
    ]
    cot_all = jnp.concatenate(seq.all(cotangent), axis=0)

    rows_down = w_down.shape[0]
    down_full = []
    for t in (0, 1):
        even = jnp.stack([down[t][m] for m in orders(dp.size)[0]])
        odd = dp.swap(even, 1)
        full = jnp.zeros((rows_down * dp.size, width // 2), BF)
        for i, m in enumerate(orders(dp.size)[0]):
            full = lax.dynamic_update_slice(full, even[i], ((dp.me ^ m) * rows_down, 0))
            full = lax.dynamic_update_slice(full, odd[i], ((dp.me ^ m ^ 1) * rows_down, 0))
        down_full.append(full)

    inputs = tokens.astype(F32)
    inv1 = lax.rsqrt(jnp.mean(inputs * inputs, axis=-1, keepdims=True) + EPS)
    hat1 = (inputs * inv1).astype(BF)
    hat1_even, hat1_odd = mask_columns(dp, hat1)
    cosine, sine = tables(seq.me * count + jnp.arange(count))
    pre = jnp.concatenate(
        [dot(hat1_even, first[t][0]) + dot(hat1_odd, first[t][1]) for t in (0, 1)], axis=1
    )
    qpre = pre[:, :heads_wide].reshape(count, H, HEAD_SIZE)
    kpre = pre[:, heads_wide : heads_wide + keys_wide].reshape(count, KEY_VALUE_HEADS, HEAD_SIZE)
    vround = pre[:, heads_wide + keys_wide :].astype(BF)
    qrot = rotate(qpre, cosine, sine).reshape(count, heads_wide).astype(BF)
    krot = rotate(kpre, cosine, sine).reshape(count, keys_wide).astype(BF)
    span = per * HEAD_SIZE
    packed = []
    for g in range(groups):
        head = g // repeat * HEAD_SIZE
        packed.append(
            jnp.concatenate(
                [
                    qrot[:, g * span : (g + 1) * span],
                    krot[:, head : head + HEAD_SIZE],
                    vround[:, head : head + HEAD_SIZE],
                ],
                axis=1,
            )
        )
    qkv = jnp.concatenate(seq.exchange(jnp.stack(packed)), axis=0)
    length = qkv.shape[0]
    queries = qkv[:, :span].reshape(length, per, HEAD_SIZE)
    keys = qkv[:, span : span + HEAD_SIZE]
    values = qkv[:, span + HEAD_SIZE :]
    place = jnp.concatenate(
        [(seq.me ^ m) * count + jnp.arange(count, dtype=jnp.int32) for m in range(groups)]
    )
    visible = place[None, :] <= place[:, None]
    out_heads, logsum = attend(queries, keys, values, visible)
    out_heads = out_heads.reshape(length, span)

    def back_home(value):
        return seq.natural(
            [
                value[:count] if m == 0 else seq.swap(value[m * count : (m + 1) * count], m)
                for m in range(groups)
            ]
        )

    attn = jnp.concatenate(back_home(out_heads), axis=1)
    attn_even, attn_odd = mask_columns(dp, attn)
    branch = jnp.concatenate(
        [dot(attn_even, outw[t][0]) + dot(attn_odd, outw[t][1]) for t in (0, 1)], axis=1
    )
    hmid = inputs + branch

    inv2 = lax.rsqrt(jnp.mean(hmid * hmid, axis=-1, keepdims=True) + EPS)
    hat2 = jnp.concatenate(mask_columns(dp, (hmid * inv2).astype(BF)), axis=1)
    hat2_all = jnp.concatenate(seq.all(hat2), axis=0)
    hat2_even, hat2_odd = hat2_all[:, : width // 2], hat2_all[:, width // 2 :]
    gate = dot(hat2_even, gate_even) + dot(hat2_odd, gate_odd)
    upper = dot(hat2_even, up_even) + dot(hat2_odd, up_odd)
    sigma = jax.nn.sigmoid(gate)
    hidden = (gate * sigma * upper).astype(BF)
    halves = [cot_all[:, : width // 2], cot_all[:, width // 2 :]]
    dhidden = right_dot(halves[0], down_full[0]) + right_dot(halves[1], down_full[1])
    dgate = (dhidden * upper * sigma * (1.0 + gate * (1.0 - sigma))).astype(BF)
    dupper = (dhidden * gate * sigma).astype(BF)
    dhat2 = jnp.concatenate(
        [
            right_dot(dgate, gate_even) + right_dot(dupper, up_even),
            right_dot(dgate, gate_odd) + right_dot(dupper, up_odd),
        ],
        axis=1,
    ).astype(BF)

    def sum_home(value):
        total = value[:count].astype(F32)
        for m in range(1, groups):
            total = total + seq.swap(value[m * count : (m + 1) * count], m).astype(F32)
        return total

    dhat2 = sum_home(dhat2)
    dgain2 = natural_columns(dp, dhat2[:, : width // 2], dhat2[:, width // 2 :])
    inner = jnp.mean(hmid * dgain2, axis=-1, keepdims=True)
    dh = cotangent.astype(F32) + inv2 * dgain2 - hmid * inv2 * inv2 * inv2 * inner
    dbranch = dh.astype(BF)

    dattn = natural_columns(
        dp,
        *[
            sum(
                right_dot(dbranch[:, t * width // 2 : (t + 1) * width // 2], outw[t][s])
                for t in (0, 1)
            ).astype(BF)
            for s in (0, 1)
        ],
    )
    grad_heads = jnp.concatenate(
        seq.exchange(dattn.reshape(count, groups, span).transpose(1, 0, 2)), axis=0
    ).reshape(length, per, HEAD_SIZE)
    dq, dk, dv = attend_back(queries, keys, values, grad_heads, logsum, visible)
    dqkv = back_home(jnp.concatenate([dq.reshape(length, span), dk, dv], axis=1))
    dq = jnp.concatenate([piece[:, :span] for piece in dqkv], axis=1)
    dk = [piece[:, span : span + HEAD_SIZE].astype(F32) for piece in dqkv]
    dv = [piece[:, span + HEAD_SIZE :].astype(F32) for piece in dqkv]
    dk = jnp.stack(
        [sum(dk[i * repeat : (i + 1) * repeat]) for i in range(KEY_VALUE_HEADS)], axis=1
    )
    dv = jnp.concatenate(
        [sum(dv[i * repeat : (i + 1) * repeat]) for i in range(KEY_VALUE_HEADS)], axis=1
    )
    dq = rotate(dq.astype(F32).reshape(count, H, HEAD_SIZE), cosine, -sine)
    dk = rotate(dk, cosine, -sine)
    dpre = jnp.concatenate(
        [dq.reshape(count, heads_wide), dk.reshape(count, keys_wide), dv], axis=1
    ).astype(BF)
    dhalf = [dpre[:, t * wide // 2 : (t + 1) * wide // 2] for t in (0, 1)]
    dhat1 = [sum(right_dot(dhalf[t], first[t][s]) for t in (0, 1)) for s in (0, 1)]
    dgain1 = natural_columns(dp, *dhat1)
    inner = jnp.mean(inputs * dgain1, axis=-1, keepdims=True)
    grad_inputs = dh + inv1 * dgain1 - inputs * inv1 * inv1 * inv1 * inner

    mixed_part = jnp.concatenate([dot(hidden, down_full[t]) for t in (0, 1)], axis=1).astype(BF)
    mixed = hmid + sum_home(mixed_part)

    grad_down = []
    for t in (0, 1):
        part = left_dot(hidden, halves[t]).astype(BF)
        blocks = [
            lax.dynamic_slice_in_dim(part, (dp.me ^ m) * rows_down, rows_down, 0)
            for m in range(dp.size)
        ]
        even, odd = orders(dp.size)
        other = dp.swap(jnp.stack([blocks[m] for m in odd]), 1)
        summed = {
            m: (blocks[m].astype(F32) + other[i].astype(F32)).astype(BF)
            for i, m in enumerate(even)
        }
        grad_down.append(scatter_chips(dp, summed, t))
    grad_down = jnp.concatenate(grad_down, axis=1)

    def ff_grad(grad, turn):
        odd = left_dot(hat2_odd, grad).astype(BF)
        return scatter_rows(dp, lambda: left_dot(hat2_even, grad), odd, turn)

    rows = w_gate.shape[0]
    sent = jnp.stack([ff_grad(dgate, 0).astype(BF), ff_grad(dupper, 1).astype(BF)])
    sent = sent.reshape(2, groups, rows, ff // groups).transpose(1, 0, 2, 3)
    got = jnp.stack(seq.natural(seq.exchange(sent)))
    got = got.reshape(groups, 2, rows, dp.size, ff // groups // dp.size)
    got = got.transpose(1, 2, 3, 0, 4).reshape(2, rows, ff).astype(F32)
    grad_gate, grad_up = got[0] * gain2, got[1] * gain2
    grad_gain2 = jnp.sum(got[0] * w_gate.astype(F32) + got[1] * w_up.astype(F32), axis=1)

    def proj_grad(even, odd, grads):
        parts = []
        for t in (0, 1):
            send = left_dot(odd, grads[t]).astype(BF)
            parts.append(
                scatter_rows(dp, lambda grad=grads[t]: left_dot(even, grad), send, t)
            )
        own = jnp.concatenate(parts, axis=1)
        own = own.astype(BF).reshape(groups, rows, own.shape[1])
        return sum(piece.astype(F32) for piece in seq.exchange(own))

    grad_out = proj_grad(
        attn_even,
        attn_odd,
        [dbranch[:, t * width // 2 : (t + 1) * width // 2] for t in (0, 1)],
    )
    grad_first = proj_grad(hat1_even, hat1_odd, dhalf)
    grad_gain1 = jnp.sum(grad_first * w_first.astype(F32), axis=1)
    grad_first = grad_first * gain1
    return (
        mixed.astype(BF),
        grad_inputs.astype(BF),
        grad_gain1,
        grad_first[:, :heads_wide],
        grad_first[:, heads_wide : heads_wide + keys_wide],
        grad_first[:, heads_wide + keys_wide :],
        grad_out,
        grad_gain2,
        grad_gate,
        grad_up,
        grad_down,
    )


MESH = pl.DeviceIdType.MESH
ANY = pl.BlockSpec(memory_space=pl.ANY)
VMEM = pl.BlockSpec(memory_space=pltpu.VMEM)


class Net:
    def __init__(self, send_sems, recv_sems):
        self.send_sems, self.recv_sems, self.used = send_sems, recv_sems, 0
        self.open = []
        dp, z = lax.axis_index("dp"), lax.axis_index("seq")
        self.dp, self.z = dp, z
        self.dps = {
            0: dp,
            1: dp + 1 - 2 * lax.rem(dp, 2),
            2: dp + 2 - 4 * lax.rem(lax.div(dp, 2), 2),
            4: lax.rem(dp + 4, 8),
        }
        self.dps[6] = lax.rem(self.dps[2] + 4, 8)
        for mask in (2, 4, 6):
            self.dps[mask + 1] = self.dps[mask] + 1 - 2 * lax.rem(dp, 2)
        self.zs = {0: z, 1: z + 1 - 2 * lax.rem(z, 2), 2: lax.rem(z + 2, 4), 3: 3 - z}

    def target(self, name):
        kind, mask = name
        return (self.dps[mask], self.z) if kind == "d" else (self.dp, self.zs[mask])

    def barrier(self, names):
        sem = pltpu.get_barrier_semaphore()
        for name in names:
            pl.semaphore_signal(sem, inc=1, device_id=self.target(name), device_id_type=MESH)
        pl.semaphore_wait(sem, len(names))

    def send(self, src, dst, name):
        copy = pltpu.make_async_remote_copy(
            src_ref=src,
            dst_ref=dst,
            send_sem=self.send_sems.at[self.used],
            recv_sem=self.recv_sems.at[self.used],
            device_id=self.target(name),
            device_id_type=MESH,
        )
        self.used += 1
        copy.start()
        self.open.append(copy)
        return copy

    def local(self, src, dst):
        copy = pltpu.make_async_copy(src, dst, self.send_sems.at[self.used])
        self.used += 1
        copy.start()
        return copy

    def sent(self, copies):
        for copy in copies:
            copy.wait_send()
        done = [id(copy) for copy in copies]
        self.open = [copy for copy in self.open if id(copy) not in done]

    def finish(self):
        for copy in self.open:
            copy.wait_send()


X, Y, CORE = ("d", 2), ("d", 4), ("d", 1)
PARTNERS = [X, Y, CORE, ("z", 1), ("z", 2), ("z", 3)]


class Plane:
    def __init__(self, net, at, both):
        self.net, self.at, self.both = net, at, both

    def push(self, mask, half, name):
        ref = self.at(mask, half)
        return self.net.send(ref, ref, name)

    def start(self):
        self.xa = self.push(0, 0, X)
        self.yb = self.push(0, 1, Y)
        self.ya = self.push(0, 0, Y)
        self.xb = self.push(0, 1, X)
        self.cores = [self.core(0)]

    def core(self, mask):
        return [self.net.send(ref, ref, CORE) for ref in self.both(mask)]

    def forward(self):
        self.xa.wait_recv()
        self.ya2 = self.push(2, 0, Y)
        self.yb.wait_recv()
        self.xb2 = self.push(4, 1, X)

    def spread(self):
        self.ya.wait_recv()
        self.cores.append(self.core(4))
        self.xb.wait_recv()
        self.cores.append(self.core(2))
        self.ya2.wait_recv()
        self.xb2.wait_recv()
        self.cores.append(self.core(6))

    def finish(self):
        for copies in self.cores:
            for copy in copies:
                copy.wait_recv()

    def sent(self):
        copies = [self.xa, self.yb, self.ya, self.xb, self.ya2, self.xb2]
        self.net.sent(copies + [copy for group in self.cores for copy in group])


def rotary(value, cosine, sine):
    lane = lax.broadcasted_iota(jnp.int32, value.shape, 1)
    partner = jnp.where(
        lax.rem(lane, 64) < 32, pltpu.roll(value, 96, 1), pltpu.roll(value, 32, 1)
    )
    return value * cosine + partner * sine


def rms(value):
    return lax.rsqrt(jnp.mean(value * value, axis=-1, keepdims=True) + EPS)


def twice(pair):
    lane = lax.broadcasted_iota(jnp.int32, pair.shape, 1)
    other = pltpu.roll(pair.astype(F32), 64, 1).astype(BF)
    return jnp.where(lane < 64, pair, other), jnp.where(lane < 64, other, pair)


def aligned(start, count, unit):
    return pl.ds(pl.multiple_of(start, unit), count)


class Sums:
    def __init__(self, net, part, r1, mid, r2):
        self.net, self.part, self.r1, self.mid, self.r2 = net, part, r1, mid, r2
        self.width = r2.shape[-1]

    def cols(self, side):
        return pl.ds(side * self.width, self.width)

    def block(self, mask):
        return lax.div(self.net.dps[mask], 2)

    def push(self, mask, side, place, name):
        src = self.part.at[self.block(mask), :, self.cols(side)]
        return self.net.send(src, self.r1.at[side, place], name)

    def first(self, mask):
        if mask == 6:
            self.near = [self.push(6, 0, 1, X), self.push(6, 1, 1, Y)]
        elif mask == 2:
            self.own = [self.push(2, 0, 0, X)]
        elif mask == 4:
            self.own.append(self.push(4, 1, 0, Y))

    def second(self):
        self.far = []
        for side, (mask, name) in enumerate(((4, Y), (2, X))):
            self.near[side].wait_recv()
            mine = self.part[self.block(mask), :, self.cols(side)]
            self.mid[side] = (mine.astype(F32) + self.r1[side, 1].astype(F32)).astype(BF)
            self.far.append(self.net.send(self.mid.at[side], self.r2.at[side], name))

    def sent(self):
        self.net.sent(self.near + self.own + self.far)

    def total(self, side):
        self.own[side].wait_recv()
        self.far[side].wait_recv()
        mine = self.part[self.block(0), :, self.cols(side)]
        return mine.astype(F32) + self.r1[side, 0].astype(F32) + self.r2[side].astype(F32)


def first_kernel(
    x_ref, wq, wk, wv, gain1, w_gate, w_up, gain2, cos_q, sin_q, cos_k, sin_k, wo, wd, cot,
    wq_out, wo_out, hat_out, qkv_out, att_out, mx_out, mx_far, hg_out, lse, hmid, dn_out, gdown,
    wq_s, wf, wq_v, wo_v, hat, qkv_send, qkv, heads, att, part, r1, mid, r2,
    wg_v, wd_v, n_v, n_sib, c_v, c_sib, hid, dg, du,
    mx_r, hd, hd_r1, hd_k, hd_r2, sib_r, send_sems, recv_sems,
):
    net = Net(send_sems, recv_sems)
    dp, z, dps, zs = net.dp, net.z, net.dps, net.zs
    tok, width = x_ref.shape
    group = qkv.shape[1]
    span = heads.shape[1]
    ff = wf.shape[-1]
    core, chip = lax.rem(dp, 2), lax.div(dp, 2)
    here = aligned(z * tok, tok, 16)

    own = [
        net.local(wo, wo_v.at[core, z]),
        net.local(wd, wd_v.at[aligned(dp * 176, 176, 16), :]),
        net.local(cot, c_v.at[here, :]),
    ]
    net.barrier(PARTNERS + [("d", 6)])

    scale = gain1[...]
    lane = lax.broadcasted_iota(jnp.int32, (wq.shape[0], 128), 1)
    for g in range(4):
        wq_s[g, :, :span] = (wq[:, g * span : (g + 1) * span].astype(F32) * scale).astype(BF)
        start = g // 2 * 128
        k = wk[:, start : start + 128].astype(F32)
        v = wv[:, start : start + 128].astype(F32)
        if g % 2 == 0:
            both = jnp.where(lane < 64, k, pltpu.roll(v, 64, 1))
        else:
            both = jnp.where(lane < 64, pltpu.roll(k, 64, 1), v)
        wq_s[g, :, span:] = (both * scale).astype(BF)

    def chip_of(mask):
        return lax.div(dps[mask], 2)

    w_1 = [
        net.send(wq_s.at[chip_of(m)], wq_v.at[chip, core, z], ("d", m)) for m in (6, 2, 4)
    ]
    own_q = net.local(wq_s.at[chip], wq_v.at[chip, core, z])
    x = x_ref[...].astype(F32)
    hat[chip] = (x * rms(x)).astype(BF)

    def half_of(ref, side):
        w = ref.shape[-1] // 2
        return pl.ds(side * w, w)

    def block(ref, size, cores):
        def at(mask, side):
            return ref.at[aligned(dps[mask] * size, size, 16), half_of(ref, side)]

        return at, lambda mask: [ref.at[aligned(dps[mask] * size, size, 16), :]] if cores else []

    plane_h = Plane(net, lambda m, s: hat.at[chip_of(m), :, half_of(hat, s)], lambda m: [])
    plane_h.start()
    down = Plane(net, *block(wd_v, 176, True))
    own[1].wait()
    down.start()

    def wq_at(mask):
        return wq_v.at[:, core, zs[mask]]

    def wo_at(mask):
        return wo_v.at[core, zs[mask]]

    class Line:
        def __init__(self, at):
            self.at = at
            self.far = self.push(0, ("z", 2))
            self.near = self.push(0, ("z", 1))
            self.cores = [self.push(0, CORE)]

        def push(self, mask, name):
            return net.send(self.at(mask), self.at(mask), name)

        def forward(self):
            self.far.wait_recv()
            self.last = self.push(2, ("z", 1))
            self.cores.append(self.push(2, CORE))

        def spread(self):
            self.near.wait_recv()
            self.cores.append(self.push(1, CORE))
            self.last.wait_recv()
            self.cores.append(self.push(3, CORE))

        def finish(self):
            for copy in self.cores:
                copy.wait_recv()

    scale = gain2[...]
    size = ff // 8
    for t, weight in enumerate((w_gate, w_up)):
        for i in range(4):
            parts = [weight[:, (d * 4 + i) * size : (d * 4 + i + 1) * size] for d in range(8)]
            joined = jnp.concatenate([p.astype(F32) for p in parts], axis=1)
            wf[i, t] = (joined * scale).astype(BF)
    own_f = net.local(wf.at[z], wg_v.at[:, aligned((dp * 4 + z) * 64, 64, 16), :])

    f_rows = aligned((dp * 4 + z) * 64, 64, 16)

    def f_send(t):
        return [
            net.send(wf.at[zs[m], t], wg_v.at[t, f_rows, :], ("z", m)) for m in (2, 3, 1)
        ]

    def f_plane(t):
        def rows(mask, start, count):
            return wg_v.at[t, aligned(dps[mask] * 256 + start, count, 16), :]

        return Plane(
            net, lambda m, s: rows(m, s * 128, 128), lambda m: [rows(m, 0, 256)]
        )

    own[0].wait()
    line_o = Line(wo_at)
    own_q.wait()
    for copy in w_1:
        copy.wait_recv()

    line_q = Line(wq_at)
    plane_h.forward()
    line_q.forward()
    gate_copies = f_send(0)
    plane_h.spread()
    line_q.spread()
    down.forward()
    line_q.finish()

    weight = wq_v[...].reshape(width, group)

    def project(s, carry):
        pre = jnp.dot(hat[s], weight, preferred_element_type=F32)
        for j in range(group // 128):
            last = j == group // 128 - 1
            c_ref, s_ref = (cos_k, sin_k) if last else (cos_q, sin_q)
            value = rotary(pre[:, j * 128 : (j + 1) * 128], c_ref[...], s_ref[...])
            qkv_send[s, :, j * 128 : (j + 1) * 128] = value.astype(BF)
        return carry

    lax.fori_loop(0, 4, project, 0)
    q_copies = [net.send(qkv_send.at[zs[m]], qkv.at[here, :], ("z", m)) for m in (2, 3, 1)]
    own_q = net.local(qkv_send.at[z], qkv.at[here, :])
    line_o.forward()
    up_copies = f_send(1)
    down.spread()
    own_q.wait()
    for copy in q_copies:
        copy.wait_recv()

    kk, vv = twice(qkv[:, span:])

    def pair(p, carry):
        cols = aligned(p * 128, 128, 128)
        for qb in range(4):
            keys = (qb + 1) * tok
            q = qkv[qb * tok : (qb + 1) * tok, cols]
            lane = lax.broadcasted_iota(jnp.int32, (tok, 128), 1)
            row = lax.broadcasted_iota(jnp.int32, (tok, keys), 0) + qb * tok
            col = lax.broadcasted_iota(jnp.int32, (tok, keys), 1)
            outs = []
            for h in range(2):
                mine = (lane < 64) if h == 0 else (lane >= 64)
                qh = jnp.where(mine, q, jnp.zeros_like(q))
                s = right_dot(qh, kk[:keys]) * HEAD_SIZE ** (-0.5)
                s = jnp.where(col <= row, s, -1e30)
                top = jnp.max(s, axis=-1, keepdims=True)
                e = jnp.exp(s - top)
                total = jnp.sum(e, axis=-1, keepdims=True)
                probs = (e * (1.0 / total)).astype(BF)
                outs.append(dot(probs, vv[:keys]))
                old = lse[qb * tok : (qb + 1) * tok, :]
                lse[qb * tok : (qb + 1) * tok, :] = jnp.where(
                    lane == 2 * p + h, top + jnp.log(total), old
                )
            heads[qb * tok : (qb + 1) * tok, cols] = jnp.where(
                lane < 64, outs[0], outs[1]
            ).astype(BF)
        return carry

    lse[...] = jnp.zeros_like(lse)
    lax.fori_loop(0, span // 128, pair, 0)
    h_copies = [
        net.send(heads.at[aligned(zs[m] * tok, tok, 16), :], att.at[z], ("z", m))
        for m in (2, 3, 1)
    ]
    own_h = net.local(heads.at[here, :], att.at[z])

    own_f.wait()
    for copy in gate_copies:
        copy.wait_recv()
    plane_g, plane_u = f_plane(0), f_plane(1)
    plane_g.start()
    line_o.spread()
    line_o.finish()
    own_h.wait()
    for copy in h_copies:
        copy.wait_recv()


    c_near = net.send(cot, c_v.at[here, :], ("z", 1))
    c_far = net.send(cot, c_v.at[here, :], ("z", 2))
    sums = Sums(net, part, r1, mid, r2)
    for m in (6, 2, 4, 0):
        s = chip_of(m)
        for c in range(4):
            cols = pl.ds(c * (width // 4), width // 4)
            weight = wo_v[:, :, :, cols].reshape(span, width // 4)
            part[s, :, cols] = dot(att[s], weight).astype(BF)
        sums.first(m)
    sums.second()
    plane_g.forward()
    for copy in up_copies:
        copy.wait_recv()
    plane_u.start()
    for side in (0, 1):
        cols = half_of(hmid, side)
        hmid[:, cols] = x_ref[:, cols].astype(F32) + sums.total(side)
    value = hmid[...]
    n_v[here, :] = (value * rms(value)).astype(BF)

    def slot(mask):
        return aligned(zs[mask] * tok, tok, 16)

    def tokens(ref, mask, name):
        return net.send(ref.at[slot(mask), :], ref.at[slot(mask), :], name)

    n_far = tokens(n_v, 0, ("z", 2))
    n_near = tokens(n_v, 0, ("z", 1))
    outs = [
        net.local(wq_v, wq_out), net.local(wo_v, wo_out), net.local(qkv, qkv_out),
        net.local(att, att_out), net.local(hat, hat_out),
    ]
    c_far.wait_recv()
    c_last = tokens(c_v, 2, ("z", 1))
    plane_g.spread()
    plane_u.forward()
    n_far.wait_recv()
    n_last = tokens(n_v, 2, ("z", 1))
    plane_u.spread()

    half = width // 2
    near_pair = lax.div(z, 2)
    far = aligned((1 - near_pair) * 2 * tok, 2 * tok, 16)
    near = aligned(near_pair * 2 * tok, 2 * tok, 16)
    dn_part = part

    def chunks(fn, total, size):
        whole = total // size

        def step(i, carry):
            fn(i * size, size)
            return carry

        lax.fori_loop(0, whole, step, 0)
        if total % size:
            fn(whole * size, total - whole * size)

    def front(rows):
        def chunk(start, size):
            cols = aligned(start, size, 128)
            n = n_v[rows, :]
            gate = dot(n, wg_v[0, :, cols])
            upper = dot(n, wg_v[1, :, cols])
            dhid = right_dot(c_v[rows, :], wd_v[cols, :])
            sigma = jax.nn.sigmoid(gate)
            silu = gate * sigma
            hid[0, rows, cols] = (silu * upper).astype(BF)
            dg[0, rows, cols] = (dhid * upper * sigma * (1.0 + gate * (1.0 - sigma))).astype(BF)
            du[0, rows, cols] = (dhid * silu).astype(BF)

        chunks(chunk, ff, 256)
        return [
            net.send(ref.at[0, rows, :], ref.at[1, rows, :], CORE) for ref in (hid, dg, du)
        ]

    def back(rows, first_slot, side):
        def chunk(start, size):
            cols = aligned(start + side * half, size, 128)
            total = right_dot(dg[0, rows, :], wg_v[0, cols, :])
            total += right_dot(du[0, rows, :], wg_v[1, cols, :])
            dn_part[pl.ds(first_slot, 2), :, cols] = total.astype(BF).reshape(2, tok, size)

        chunks(chunk, half, 256)

    def piece(side):
        return pl.ds(side * half, half)

    sums.sent()
    n_near.wait_recv()
    c_near.wait_recv()
    for plane in (down, plane_g, plane_u):
        plane.finish()
    own[2].wait()
    sib = front(near)
    dn_b = []
    for side in (0, 1):
        back(near, near_pair * 2, side)
        dn_b.append(
            net.send(
                dn_part.at[zs[1], :, piece(side)], r1.at[side, 0], ("z", 1)
            )
        )
    c_last.wait_recv()
    c_copy = net.send(c_v.at[:, aligned((1 - core) * half, half, 128)], c_sib, CORE)
    n_last.wait_recv()
    n_copies = [
        net.send(
            n_v.at[:, aligned((i * 2 + 1 - core) * 256, 256, 128)],
            n_sib.at[:, pl.ds(i * 256, 256)],
            CORE,
        )
        for i in range(4)
    ]
    sib += front(far)
    dn_a = []
    for side in (0, 1):
        back(far, (1 - near_pair) * 2, side)
        dn_a.append(
            net.send(
                dn_part.at[zs[3], :, piece(side)], r1.at[side, 1], ("z", 1)
            )
        )
    c_copy.wait_recv()
    for copy in sib:
        copy.wait_recv()

    ccols = aligned(core * half, half, 128)

    def down_chunk(start, size):
        cols = aligned(start, size, 128)
        total = left_dot(hid[0, :, cols], c_v[:, ccols])
        total += left_dot(hid[1, :, cols], c_sib[...])
        hd[cols, :] = total.astype(BF)

    chunks(down_chunk, ff, 256)
    chip_rows = ff // 4
    quarter = half // 2

    def hd_at(mask, side):
        return aligned(chip_of(mask) * chip_rows, chip_rows, 16), pl.ds(side * quarter, quarter)

    def hd_send(mask, side, place, name):
        r, c = hd_at(mask, side)
        return net.send(hd.at[r, c], hd_r1.at[side, place], name)

    hd_1 = [hd_send(6, 0, 1, X), hd_send(6, 1, 1, Y), hd_send(2, 0, 0, X), hd_send(4, 1, 0, Y)]
    dn_c = []
    for side in (0, 1):
        dn_a[side].wait_recv()
        cols = piece(side)
        mid[side] = (
            dn_part[zs[2], :, cols].astype(F32) + r1[side, 1].astype(F32)
        ).astype(BF)
        dn_c.append(net.send(mid.at[side], r2.at[side], ("z", 2)))

    for copy in outs:
        copy.wait()
    plane_h.sent()

    def mix_chunk(start, size):
        cols = aligned(start, size, 128)
        hat[:, :, cols] = dot(hid[0], wd_v[:, cols]).astype(BF).reshape(4, tok, size)

    chunks(mix_chunk, width, 256)
    mx_copy = net.local(hat, mx_out)
    mx_a = net.send(hat.at[zs[3]], mx_r, ("z", 1))

    hd_1[0].wait_recv()
    hd_1[1].wait_recv()
    hd_2 = []
    for side, (mask, name) in enumerate(((4, Y), (2, X))):
        r, c = hd_at(mask, side)
        hd_k[side] = (hd[r, c].astype(F32) + hd_r1[side, 1].astype(F32)).astype(BF)
        hd_2.append(net.send(hd_k.at[side], hd_r2.at[side], name))

    for copy in n_copies:
        copy.wait_recv()
    plane_g.sent()
    plane_u.sent()

    def block(b, carry):
        cols = aligned((b * 2 + core) * 256, 256, 128)
        left = n_v[:, cols].T
        other = n_sib[:, aligned(b * 256, 256, 128)].T
        for t, grad in enumerate((dg, du)):
            total = dot(left, grad[0]) + dot(other, grad[1])
            wg_v[t, aligned(b * 256, 256, 16), :] = total.astype(BF)
        return carry

    lax.fori_loop(0, 4, block, 0)
    hg_copy = net.local(wg_v.at[:, pl.ds(0, 1024), :], hg_out)
    for side in (0, 1):
        dn_b[side].wait_recv()
        dn_c[side].wait_recv()
        cols = piece(side)
        dn_out[:, cols] = (
            dn_part[z, :, cols].astype(F32)
            + r1[side, 0].astype(F32)
            + r2[side].astype(F32)
        )
    mx_a.wait_recv()
    net.sent(dn_c)
    far_copies = []
    for side in (0, 1):
        cols = piece(side)
        mid[side] = (hat[zs[2], :, cols].astype(F32) + mx_r[:, cols].astype(F32)).astype(BF)
        far_copies.append(net.local(mid.at[side], mx_far.at[:, cols]))
    hd_1[2].wait_recv()
    hd_1[3].wait_recv()
    rows_half = chip_rows // 2
    for side in (0, 1):
        hd_2[side].wait_recv()

        def total(start):
            _, c = hd_at(0, side)
            return (
                hd[aligned(chip * chip_rows + start, rows_half, 16), c].astype(F32)
                + hd_r1[side, 0, aligned(start, rows_half, 16), :].astype(F32)
                + hd_r2[side, aligned(start, rows_half, 16), :].astype(F32)
            )

        net.sent([hd_2[side]])
        hd_k[side, :rows_half] = total((1 - core) * rows_half).astype(BF)
        gdown[:, aligned(core * half + side * quarter, quarter, 128)] = total(core * rows_half)
    last = net.send(hd_k.at[:, pl.ds(0, rows_half), :], sib_r, CORE)
    last.wait_recv()
    for side in (0, 1):
        start = (1 - core) * half + side * quarter
        gdown[:, aligned(start, quarter, 128)] = sib_r[side].astype(F32)
    hg_copy.wait()
    mx_copy.wait()
    for copy in far_copies:
        copy.wait()
    net.finish()


def first_call(x, wq, wk, wv, gain1, w_gate, w_up, gain2, tables4, wo, wd, cot):
    tok, width = x.shape
    ff = w_gate.shape[1] // 4
    span = width // 4
    group = span + 128
    sds = jax.ShapeDtypeStruct
    v = pltpu.VMEM
    half = width // 2
    return pl.pallas_call(
        first_kernel,
        name="first",
        out_shape=[
            sds((4, 2, 4, 64, group), BF), sds((2, 4, 64, width), BF), sds((4, tok, width), BF),
            sds((4 * tok, group), BF), sds((4, tok, span), BF), sds((4, tok, width), BF),
            sds((tok, width), BF), sds((2, 1024, ff), BF), sds((4 * tok, 128), F32), sds((tok, width), F32),
            sds((tok, width), F32), sds((ff // 8, width), F32),
        ],
        in_specs=[VMEM] * 15,
        out_specs=[ANY] * 8 + [VMEM] * 4,
        scratch_shapes=[
            v((4, 64, group), BF), v((4, 2, 64, ff), BF), v((4, 2, 4, 64, group), BF),
            v((2, 4, 64, width), BF), v((4, tok, width), BF), v((4, tok, group), BF),
            v((4 * tok, group), BF), v((4 * tok, span), BF), v((4, tok, span), BF),
            v((4, tok, width), BF), v((2, 2, tok, half), BF), v((2, tok, half), BF),
            v((2, tok, half), BF),
            v((2, width, ff), BF), v((ff, width), BF), v((4 * tok, width), BF),
            v((4 * tok, half), BF), v((4 * tok, width), BF), v((4 * tok, half), BF),
            v((2, 4 * tok, ff), BF), v((2, 4 * tok, ff), BF), v((2, 4 * tok, ff), BF),
            v((tok, width), BF), v((ff, half), BF), v((2, 2, ff // 4, half // 2), BF), v((2, ff // 4, half // 2), BF),
            v((2, ff // 4, half // 2), BF), v((2, ff // 8, half // 2), BF),
            pltpu.SemaphoreType.DMA((144,)),
            pltpu.SemaphoreType.DMA((144,)),
        ],
        compiler_params=pltpu.CompilerParams(
            collective_id=1, has_side_effects=True, vmem_limit_bytes=62 * 2**20
        ),
    )(x, wq, wk, wv, gain1, w_gate, w_up, gain2, *tables4, wo, wd, cot)


def third_kernel(
    x_ref, hmid, cot, dn2, qkv, lse, cos_q, sin_q, cos_k, sin_k,
    mx, mx_far, wq, wo, hat, att, hg,
    tok_out, mixed, g2_out, g1_out, fb,
    wq_v, wo_v, hat_v, hat_s, att_v, att_s, mx_v, mx_r1, mx_r2,
    hg_v, f_r1, f_k, f_r2, fs, dh, dbr, dbr_s, dsend, gh, dqkv, dk_acc, dv_acc, dback,
    dpre, dpre_s, part, r1, mid, r2, g2_p, g2_r1, g2_s, g2_r2, g1_p, g1_r1, g1_s, g1_r2, g1_f,
    send_sems, recv_sems,
):
    net = Net(send_sems, recv_sems)
    dp, z, dps, zs = net.dp, net.z, net.dps, net.zs
    tok, width = x_ref.shape
    group = qkv.shape[1]
    span = group - 128
    here = aligned(z * tok, tok, 16)
    core, chip = lax.rem(dp, 2), lax.div(dp, 2)

    def chip_of(mask):
        return lax.div(dps[mask], 2)

    def slot(mask):
        return aligned(zs[mask] * tok, tok, 16)

    def hg_at(t, mask):
        return hg.at[t, aligned(chip_of(mask) * 256, 256, 16), :]

    loads = [
        net.local(wo, wo_v),
        net.local(hg_at(0, 0), hg_v.at[0, 0]),
        net.local(hg_at(0, 4), hg_v.at[0, 1]),
        net.local(hg_at(1, 0), hg_v.at[1, 0]),
        net.local(hg_at(1, 2), hg_v.at[1, 1]),
        net.local(mx.at[z], mx_v),
        net.local(att, att_v),
        net.local(wq, wq_v),
        net.local(hat, hat_v),
    ]
    net.barrier(PARTNERS + [("d", 6)])
    mx_copies = [
        net.send(mx_far, mx_r2, ("z", 2)),
        net.send(mx.at[zs[1]], mx_r1, ("z", 1)),
    ]
    half = width // 2

    def norm_back(value, grad):
        inv = rms(value)
        inner = jnp.mean(value * grad, axis=-1, keepdims=True)
        return inv * grad - value * (inv * inv * inv * inner)

    dh[...] = cot[...].astype(F32) + norm_back(hmid[...], dn2[...])
    dbr[chip] = dh[...].astype(BF)
    plane_b = Plane(net, lambda m, s: dbr.at[chip_of(m), :, pl.ds(s * half, half)], lambda m: [])
    plane_b.start()
    small = [
        net.send(att.at[:, :, aligned((1 - core) * 256, 256, 128)], att_s, CORE)
    ] + [
        net.send(
            hat.at[:, :, aligned(i * 512 + (1 - core) * 256, 256, 128)],
            hat_s.at[:, :, pl.ds(i * 256, 256)],
            CORE,
        )
        for i in range(4)
    ]
    plane_b.forward()
    f_1 = [
        net.send(hg_at(0, 6), f_r1.at[0, 1], X),
        net.send(hg_at(1, 6), f_r1.at[1, 1], Y),
        net.send(hg_at(0, 2), f_r1.at[0, 0], X),
        net.send(hg_at(1, 4), f_r1.at[1, 0], Y),
    ]
    plane_b.spread()
    loads[0].wait()
    d_copies = []
    weight = wo_v[...].reshape(span, width)
    for m in (2, 3, 1, 0):
        dsend[m] = right_dot(dbr[zs[m]], weight).astype(BF)
        if m:
            d_copies.append(net.send(dsend.at[m], gh.at[here, :], ("z", m)))
    gh[here, :] = dsend[0]
    dbr_copy = net.send(dbr, dbr_s, CORE)
    for copy in loads[1:]:
        copy.wait()
    for copy in d_copies:
        copy.wait_recv()

    scale = HEAD_SIZE ** (-0.5)
    kk, vv = twice(qkv[:, span:])
    dk_acc[...] = jnp.zeros_like(dk_acc)
    dv_acc[...] = jnp.zeros_like(dv_acc)

    def pair(p, carry):
        cols = aligned(p * 128, 128, 128)
        for qb in range(4):
            keys = (qb + 1) * tok
            rows = slice(qb * tok, (qb + 1) * tok)
            q = qkv[rows, cols]
            g = gh[rows, cols]
            lane = lax.broadcasted_iota(jnp.int32, (tok, 128), 1)
            row = lax.broadcasted_iota(jnp.int32, (tok, keys), 0) + qb * tok
            col = lax.broadcasted_iota(jnp.int32, (tok, keys), 1)
            outs = []
            for h in range(2):
                lanes = (lane < 64) if h == 0 else (lane >= 64)
                qh = jnp.where(lanes, q, jnp.zeros_like(q))
                gg = jnp.where(lanes, g, jnp.zeros_like(g))
                log = jnp.sum(
                    jnp.where(lane == 2 * p + h, lse[rows, :], 0.0), axis=-1, keepdims=True
                )
                s = right_dot(qh, kk[:keys]) * scale
                probs = jnp.exp(jnp.where(col <= row, s, -1e30) - log)
                pg = right_dot(gg, vv[:keys])
                delta = jnp.sum(probs * pg, axis=-1, keepdims=True)
                ds = (probs * (pg - delta)).astype(BF)
                outs.append(dot(ds, kk[:keys]) * scale)
                dk_acc[:keys, :] += left_dot(ds, qh)
                dv_acc[:keys, :] += left_dot(probs.astype(BF), gg)
            dqkv[rows, cols] = jnp.where(lane < 64, outs[0], outs[1]).astype(BF)
        return carry

    lax.fori_loop(0, span // 128, pair, 0)
    dk = dk_acc[...]
    dv = dv_acc[...]
    lane = lax.broadcasted_iota(jnp.int32, dk.shape, 1)
    dqkv[:, span:] = jnp.where(
        lane < 64, (dk + pltpu.roll(dk, 64, 1)) * scale, dv + pltpu.roll(dv, 64, 1)
    ).astype(BF)
    b_copies = [net.send(dqkv.at[slot(m), :], dback.at[z], ("z", m)) for m in (2, 3, 1)]
    dback[z] = dqkv[here, :]

    f_2 = []
    for t, name in ((0, Y), (1, X)):
        f_1[t].wait_recv()
        f_k[t] = (hg_v[t, 1].astype(F32) + f_r1[t, 1].astype(F32)).astype(BF)
        f_2.append(net.send(f_k.at[t], f_r2.at[t], name))

    class Line:
        def __init__(self, parts, r1, s, r2):
            self.parts, self.r1, self.s, self.r2 = parts, r1, s, r2
            self.sent = [
                net.send(parts.at[zs[3]], r1.at[1], ("z", 1)),
                net.send(parts.at[zs[1]], r1.at[0], ("z", 1)),
            ]

        def middle(self):
            self.sent[0].wait_recv()
            self.s[...] = (self.parts[zs[2]].astype(F32) + self.r1[1].astype(F32)).astype(BF)
            self.far = net.send(self.s, self.r2, ("z", 2))

        def total(self):
            self.sent[1].wait_recv()
            self.far.wait_recv()
            own = self.parts[z].astype(F32) + self.r1[0].astype(F32)
            return own + self.r2[...].astype(F32)

    small[0].wait_recv()
    dbr_copy.wait_recv()
    mine = att_v[:, :, aligned(core * 256, 256, 128)].reshape(4 * tok, 256).T
    theirs = att_s[...].reshape(4 * tok, 256).T

    def out_chunk(i, carry):
        cols = aligned(i * 512, 512, 128)
        total = dot(mine, dbr[:, :, cols].reshape(4 * tok, 512))
        total += dot(theirs, dbr_s[:, :, cols].reshape(4 * tok, 512))
        g2_p[:, :, cols] = total.astype(BF).reshape(4, 64, 512)
        return carry

    lax.fori_loop(0, width // 512, out_chunk, 0)
    line_o = Line(g2_p, g2_r1, g2_s, g2_r2)

    for copy in b_copies:
        copy.wait_recv()
    for s in range(4):
        for j in range(group // 128):
            cols = slice(j * 128, (j + 1) * 128)
            last = j == group // 128 - 1
            c_ref, s_ref = (cos_k, sin_k) if last else (cos_q, sin_q)
            value = dback[s, :, cols].astype(F32)
            dpre[s, :, cols] = rotary(value, c_ref[...], -s_ref[...]).astype(BF)
    dpre_copy = net.send(dpre, dpre_s, CORE)

    left = dpre[...].reshape(4 * tok, group)

    def dhat_chunk(i, carry):
        cols = aligned(i * 256, 256, 128)
        rows = wq_v[lax.div(i, 2), lax.rem(i, 2)].reshape(256, group)
        part[:, :, cols] = right_dot(left, rows).astype(BF).reshape(4, tok, 256)
        return carry

    lax.fori_loop(0, width // 256, dhat_chunk, 0)
    sums = Sums(net, part, r1, mid, r2)
    for m in (6, 2, 4):
        sums.first(m)

    for copy in small[1:]:
        copy.wait_recv()
    dpre_copy.wait_recv()
    right = dpre_s[...].reshape(4 * tok, group)

    def first_chunk(i, carry):
        own = hat_v[:, :, aligned(i * 512 + core * 256, 256, 128)].reshape(4 * tok, 256).T
        sib = hat_s[:, :, aligned(i * 256, 256, 128)].reshape(4 * tok, 256).T
        total = dot(own, left) + dot(sib, right)
        g1_p[:, i] = total.astype(BF).reshape(4, 64, group)
        return carry

    lax.fori_loop(0, 4, first_chunk, 0)
    line_q = Line(g1_p, g1_r1, g1_s, g1_r2)
    line_o.middle()
    f_copies = []
    for t in (0, 1):
        f_1[2 + t].wait_recv()
        f_2[t].wait_recv()
        total = hg_v[t, 0].astype(F32) + f_r1[t, 0].astype(F32) + f_r2[t].astype(F32)
        for i in range(4):
            fs[i, t] = total[i * 64 : (i + 1) * 64, :].astype(BF)
    sums.second()
    line_q.middle()
    f_copies = [net.send(fs.at[zs[m]], fb.at[z], ("z", m)) for m in (2, 3, 1)]
    fb[z] = fs[z]
    for copy in mx_copies:
        copy.wait_recv()
    total = mx_v[...].astype(F32) + mx_r1[...].astype(F32) + mx_r2[...].astype(F32)
    mixed[...] = (hmid[...] + total).astype(BF)
    g2_out[...] = line_o.total()
    for side in (0, 1):
        dn2[:, side * half : (side + 1) * half] = sums.total(side)
    tok_out[...] = (dh[...] + norm_back(x_ref[...].astype(F32), dn2[...])).astype(BF)
    g1_f[...] = line_q.total().astype(BF)
    g_copies = [net.send(g1_f.at[chip_of(m)], g1_out.at[chip], ("d", m)) for m in (6, 2, 4)]
    g1_out[chip] = g1_f[chip]
    for copy in g_copies + f_copies:
        copy.wait_recv()
    net.finish()


def third_call(x, hmid, cot, dn2, qkv, lse, tables4, mx, mx_far, wq, wo, hat, att, hg):
    tok, width = x.shape
    group = qkv.shape[1]
    span = group - 128
    ff = hg.shape[-1]
    sds = jax.ShapeDtypeStruct
    v = pltpu.VMEM
    return pl.pallas_call(
        third_kernel,
        name="third",
        out_shape=[
            sds((tok, width), BF), sds((tok, width), BF), sds((64, width), F32),
            sds((4, 64, group), BF), sds((4, 2, 64, ff), BF),
        ],
        in_specs=[VMEM] * 10 + [ANY] * 7,
        out_specs=[VMEM] * 5,
        scratch_shapes=[
            v((4, 2, 4, 64, group), BF), v((2, 4, 64, width), BF), v((4, tok, width), BF),
            v((4, tok, width // 2), BF), v((4, tok, span), BF), v((4, tok, span // 2), BF),
            v((tok, width), BF), v((tok, width), BF), v((tok, width), BF),
            v((2, 2, 256, ff), BF), v((2, 2, 256, ff), BF), v((2, 256, ff), BF), v((2, 256, ff), BF),
            v((4, 2, 64, ff), BF), v((tok, width), F32), v((4, tok, width), BF),
            v((4, tok, width), BF), v((4, tok, span), BF), v((4 * tok, span), BF),
            v((4 * tok, group), BF), v((4 * tok, 128), F32), v((4 * tok, 128), F32),
            v((4, tok, group), BF), v((4, tok, group), BF), v((4, tok, group), BF),
            v((4, tok, width), BF), v((2, 2, tok, width // 2), BF), v((2, tok, width // 2), BF),
            v((2, tok, width // 2), BF),
            v((4, 64, width), BF), v((2, 64, width), BF), v((64, width), BF), v((64, width), BF),
            v((4, 4, 64, group), BF), v((2, 4, 64, group), BF), v((4, 64, group), BF),
            v((4, 64, group), BF), v((4, 64, group), BF),
            pltpu.SemaphoreType.DMA((80,)),
            pltpu.SemaphoreType.DMA((80,)),
        ],
        compiler_params=pltpu.CompilerParams(
            collective_id=3, has_side_effects=True, vmem_limit_bytes=60 * 2**20
        ),
    )(x, hmid, cot, dn2, qkv, lse, *tables4, mx, mx_far, wq, wo, hat, att, hg)


def last_kernel(
    fb, g1, wq, wk, wv, w_gate, w_up, gain1, gain2,
    gq, gk, gv, g_gate, g_up, g_gain1, g_gain2,
):
    span = g1.shape[2] - 128
    lane = lax.broadcasted_iota(jnp.int32, (g1.shape[1], 128), 1)
    scale = gain1[...]

    def put(out, weight, cols, value):
        out[:, cols] = value * scale
        return jnp.sum(value * weight[:, cols].astype(F32), axis=1, keepdims=True)

    total = jnp.zeros_like(g_gain1)
    for g in range(4):
        total += put(gq, wq, slice(g * span, (g + 1) * span), g1[g, :, :span].astype(F32))
    for g in (0, 2):
        one = g1[g, :, span:].astype(F32)
        two = g1[g + 1, :, span:].astype(F32)
        cols = slice(g * 64, g * 64 + 128)
        total += put(gk, wk, cols, jnp.where(lane < 64, one, pltpu.roll(two, 64, 1)))
        total += put(gv, wv, cols, jnp.where(lane < 64, pltpu.roll(one, 64, 1), two))
    g_gain1[...] = total
    size = fb.shape[-1] // 8
    total = jnp.zeros_like(g_gain2)
    for t, (out, weight) in enumerate(((g_gate, w_gate), (g_up, w_up))):
        for d in range(0, 8, 2):
            parts = [
                fb[i, t, :, e * size : (e + 1) * size].astype(F32) for e in (d, d + 1) for i in range(4)
            ]
            joined = jnp.concatenate(parts, axis=1)
            cols = pl.ds(d * 4 * size, 8 * size)
            total += jnp.sum(joined * weight[:, cols].astype(F32), axis=1, keepdims=True)
            out[:, cols] = joined * gain2[...]
    g_gain2[...] = total


def last_call(fb, g1, wq, wk, wv, w_gate, w_up, gain1, gain2):
    rows, ff = w_gate.shape
    sds = jax.ShapeDtypeStruct
    return pl.pallas_call(
        last_kernel,
        name="last",
        out_shape=[
            sds(wq.shape, F32), sds(wk.shape, F32), sds(wv.shape, F32),
            sds((rows, ff), F32), sds((rows, ff), F32), sds((rows, 1), F32), sds((rows, 1), F32),
        ],
        in_specs=[VMEM] * 9,
        out_specs=[VMEM] * 7,
        compiler_params=pltpu.CompilerParams(vmem_limit_bytes=40 * 2**20),
    )(fb, g1, wq, wk, wv, w_gate, w_up, gain1, gain2)


def shards(
    tokens, norm_first, w_query, w_key, w_value, w_out, norm_second, w_gate, w_up, w_down, cotangent
):
    count = tokens.shape[0]
    gain1 = norm_first.astype(F32)[:, None]
    gain2 = norm_second.astype(F32)[:, None]
    cosine, sine = tables(lax.axis_index("seq") * count + jnp.arange(count))
    cosine, sine = cosine[:, 0], sine[:, 0]
    one, zero = jnp.ones_like(cosine), jnp.zeros_like(cosine)
    tables4 = [
        jnp.concatenate(parts, axis=1)
        for parts in (
            [cosine] * 4,
            [-sine, sine] * 2,
            [cosine, cosine, one, one],
            [-sine, sine, zero, zero],
        )
    ]
    wq, wo, hat, qkv, att, mixed_part, mixed_far, hg, lse, hmid, dhat2, grad_down = first_call(
        tokens, w_query, w_key, w_value, gain1, w_gate, w_up, gain2, tables4,
        w_out, w_down, cotangent,
    )
    grad_tokens, mixed, grad_out, grad_first, parts = third_call(
        tokens, hmid, cotangent, dhat2, qkv, lse, tables4, mixed_part, mixed_far,
        wq, wo, hat, att, hg,
    )
    grad_query, grad_key, grad_value, grad_gate, grad_up, grad_gain1, grad_gain2 = last_call(
        parts, grad_first, w_query, w_key, w_value, w_gate, w_up, gain1, gain2
    )
    return (
        mixed,
        grad_tokens,
        grad_gain1[:, 0],
        grad_query,
        grad_key,
        grad_value,
        grad_out,
        grad_gain2[:, 0],
        grad_gate,
        grad_up,
        grad_down,
    )


def solution(mesh):
    special = mesh.shape['dp'] == 8 and mesh.shape['seq'] == KEY_VALUE_HEADS
    rows = P(("dp", "seq"), None)
    line = P(("dp", "seq"))
    return jax.shard_map(
        shards if special else general_shards,
        mesh=mesh,
        in_specs=(rows, line, rows, rows, rows, rows, line, rows, rows, rows, rows),
        out_specs=(rows, rows, line, rows, rows, rows, rows, line, rows, rows, rows),
        check_vma=False,
    )
```

```python
import jax
import jax.numpy as jnp
from jax import lax
from jax.experimental import pallas as pl
from jax.experimental.pallas import tpu as pltpu
from jax.sharding import PartitionSpec as P

H = 32
KEY_VALUE_HEADS = 4
HEAD_SIZE = 64
EPS = 1e-05
BF = jnp.bfloat16
F32 = jnp.float32


def tables(positions):
    freq = 10000.0 ** (-jnp.arange(0, HEAD_SIZE // 2, dtype=F32) * 2.0 / HEAD_SIZE)
    angle = positions.astype(F32)[:, None] * freq[None, :]
    return (jnp.cos(angle)[:, None, :], jnp.sin(angle)[:, None, :])


def rotate(heads, cosine, sine):
    half = heads.shape[-1] // 2
    first = heads[..., :half]
    second = heads[..., half:]
    return jnp.concatenate(
        [first * cosine - second * sine, second * cosine + first * sine], axis=-1
    )


def dot(left, right):
    return jnp.dot(left, right, preferred_element_type=F32)


def left_dot(left, right):
    return lax.dot_general(left, right, (((0,), (0,)), ((), ())), preferred_element_type=F32)


def right_dot(left, right):
    return lax.dot_general(left, right, (((1,), (1,)), ((), ())), preferred_element_type=F32)


def bits_of(count):
    return [1 << k for k in range(count.bit_length() - 1)]


class Axis:
    def __init__(self, name):
        self.name = name
        self.size = lax.axis_size(name)
        self.me = lax.axis_index(name)

    def swap(self, value, mask):
        return lax.ppermute(value, self.name, [(i, i ^ mask) for i in range(self.size)])

    def all(self, value):
        return [value if m == 0 else self.swap(value, m) for m in range(self.size)]

    def exchange(self, stacked):
        return [
            lax.dynamic_index_in_dim(stacked, self.me ^ m, 0, keepdims=False)
            if m == 0
            else self.swap(
                lax.dynamic_index_in_dim(stacked, self.me ^ m, 0, keepdims=False), m
            )
            for m in range(self.size)
        ]

    def natural(self, pieces):
        stack = jnp.stack(pieces)
        return [
            lax.dynamic_index_in_dim(stack, self.me ^ i, 0, keepdims=False)
            for i in range(self.size)
        ]


def orders(size):
    even = [m for m in range(size) if m % 2 == 0]
    return even, [m + 1 for m in even]


def chip_bits(size, turn):
    bits = bits_of(size)[1:]
    return bits if turn == 0 else bits[::-1]


def gather_chips(dp, piece, turn):
    pieces = {0: piece}
    for bit in chip_bits(dp.size, turn):
        pieces.update({m ^ bit: dp.swap(p, bit) for m, p in list(pieces.items())})
    return pieces


def gather_rows(dp, piece, turn):
    pieces = gather_chips(dp, piece, turn)
    even = jnp.concatenate([pieces[m] for m in orders(dp.size)[0]], axis=0)
    return even, dp.swap(even, 1)


def scatter_chips(dp, blocks, turn):
    for bit in chip_bits(dp.size, turn):
        for m in [m for m in blocks if m & bit]:
            other = dp.swap(blocks.pop(m).astype(BF), bit)
            blocks[m ^ bit] = blocks[m ^ bit].astype(F32) + other.astype(F32)
    return blocks[0]


def scatter_rows(dp, even_fn, odd, turn):
    rows = odd.shape[0] * 2 // dp.size
    other = dp.swap(odd, 1)
    even = (even_fn() + other.astype(F32)).astype(BF)
    blocks = {
        m: even[i * rows : (i + 1) * rows] for i, m in enumerate(orders(dp.size)[0])
    }
    return scatter_chips(dp, blocks, turn)


def mask_columns(dp, value):
    width = value.shape[1] // dp.size
    return tuple(
        jnp.concatenate(
            [lax.dynamic_slice_in_dim(value, (dp.me ^ m) * width, width, 1) for m in group],
            axis=1,
        )
        for group in orders(dp.size)
    )


def natural_columns(dp, even, odd):
    both = jnp.concatenate([even, odd], axis=1)
    width = both.shape[1] // dp.size
    half = dp.size // 2
    parts = []
    for i in range(dp.size):
        mask = dp.me ^ i
        place = mask // 2 + (mask % 2) * half
        parts.append(lax.dynamic_slice_in_dim(both, place * width, width, 1))
    return jnp.concatenate(parts, axis=1)


def attend(queries, keys, values, visible):
    scores = jnp.einsum("qhd,kd->hqk", queries, keys, preferred_element_type=F32)
    scores = jnp.where(visible[None], scores * HEAD_SIZE ** (-0.5), -1e30)
    top = jnp.max(scores, axis=-1, keepdims=True)
    expo = jnp.exp(scores - top)
    total = jnp.sum(expo, axis=-1, keepdims=True)
    probs = (expo / total).astype(BF)
    result = jnp.einsum("hqk,kd->qhd", probs, values, preferred_element_type=F32)
    return result.astype(BF), top + jnp.log(total)


def attend_back(queries, keys, values, grad_heads, logsum, visible):
    scale = HEAD_SIZE ** (-0.5)
    scores = jnp.einsum("qhd,kd->hqk", queries, keys, preferred_element_type=F32)
    scores = jnp.where(visible[None], scores * scale, -1e30)
    probs = jnp.exp(scores - logsum)
    pgrad = jnp.einsum("qhd,kd->hqk", grad_heads, values, preferred_element_type=F32)
    delta = jnp.sum(probs * pgrad, axis=-1, keepdims=True)
    sgrad = (probs * (pgrad - delta)).astype(BF)
    qgrad = jnp.einsum("hqk,kd->qhd", sgrad, keys, preferred_element_type=F32) * scale
    kgrad = jnp.einsum("hqk,qhd->kd", sgrad, queries, preferred_element_type=F32) * scale
    vgrad = jnp.einsum("hqk,qhd->kd", probs.astype(BF), grad_heads, preferred_element_type=F32)
    return qgrad.astype(BF), kgrad.astype(BF), vgrad.astype(BF)


def general_shards(
    tokens, norm_first, w_query, w_key, w_value, w_out, norm_second, w_gate, w_up, w_down, cotangent
):
    dp, seq = Axis("dp"), Axis("seq")
    groups = seq.size
    count, width = tokens.shape
    ff = w_gate.shape[1]
    per = H // groups
    repeat = groups // KEY_VALUE_HEADS
    heads_wide = H * HEAD_SIZE
    keys_wide = KEY_VALUE_HEADS * HEAD_SIZE
    gain1 = norm_first.astype(F32)[:, None]
    gain2 = norm_second.astype(F32)[:, None]

    w_first = jnp.concatenate([w_query, w_key, w_value], axis=1)
    w_first_scaled = (w_first.astype(F32) * gain1).astype(BF)
    wide = w_first.shape[1]

    def by_part(weight):
        rows = weight.shape[0]
        scaled = (weight.astype(F32) * gain2).astype(BF)
        parts = scaled.reshape(rows, dp.size, groups, ff // dp.size // groups)
        return parts.transpose(2, 0, 1, 3).reshape(groups, rows, ff // groups)

    down = [gather_chips(dp, w_down[:, t * width // 2 : (t + 1) * width // 2], t) for t in (0, 1)]
    first_rows = jnp.concatenate(seq.natural(seq.all(w_first_scaled)), axis=0)
    first = [gather_rows(dp, first_rows[:, t * wide // 2 : (t + 1) * wide // 2], t) for t in (0, 1)]
    out_rows = jnp.concatenate(seq.natural(seq.all(w_out)), axis=0)
    outw = [gather_rows(dp, out_rows[:, t * width // 2 : (t + 1) * width // 2], t) for t in (0, 1)]
    gate_up = seq.exchange(jnp.stack([by_part(w_gate), by_part(w_up)], axis=1))
    gate_up = jnp.concatenate(seq.natural(gate_up), axis=1)
    (gate_even, gate_odd), (up_even, up_odd) = [
        gather_rows(dp, gate_up[t], t) for t in (0, 1)
    ]
    cot_all = jnp.concatenate(seq.all(cotangent), axis=0)

    rows_down = w_down.shape[0]
    down_full = []
    for t in (0, 1):
        even = jnp.stack([down[t][m] for m in orders(dp.size)[0]])
        odd = dp.swap(even, 1)
        full = jnp.zeros((rows_down * dp.size, width // 2), BF)
        for i, m in enumerate(orders(dp.size)[0]):
            full = lax.dynamic_update_slice(full, even[i], ((dp.me ^ m) * rows_down, 0))
            full = lax.dynamic_update_slice(full, odd[i], ((dp.me ^ m ^ 1) * rows_down, 0))
        down_full.append(full)

    inputs = tokens.astype(F32)
    inv1 = lax.rsqrt(jnp.mean(inputs * inputs, axis=-1, keepdims=True) + EPS)
    hat1 = (inputs * inv1).astype(BF)
    hat1_even, hat1_odd = mask_columns(dp, hat1)
    cosine, sine = tables(seq.me * count + jnp.arange(count))
    pre = jnp.concatenate(
        [dot(hat1_even, first[t][0]) + dot(hat1_odd, first[t][1]) for t in (0, 1)], axis=1
    )
    qpre = pre[:, :heads_wide].reshape(count, H, HEAD_SIZE)
    kpre = pre[:, heads_wide : heads_wide + keys_wide].reshape(count, KEY_VALUE_HEADS, HEAD_SIZE)
    vround = pre[:, heads_wide + keys_wide :].astype(BF)
    qrot = rotate(qpre, cosine, sine).reshape(count, heads_wide).astype(BF)
    krot = rotate(kpre, cosine, sine).reshape(count, keys_wide).astype(BF)
    span = per * HEAD_SIZE
    packed = []
    for g in range(groups):
        head = g // repeat * HEAD_SIZE
        packed.append(
            jnp.concatenate(
                [
                    qrot[:, g * span : (g + 1) * span],
                    krot[:, head : head + HEAD_SIZE],
                    vround[:, head : head + HEAD_SIZE],
                ],
                axis=1,
            )
        )
    qkv = jnp.concatenate(seq.exchange(jnp.stack(packed)), axis=0)
    length = qkv.shape[0]
    queries = qkv[:, :span].reshape(length, per, HEAD_SIZE)
    keys = qkv[:, span : span + HEAD_SIZE]
    values = qkv[:, span + HEAD_SIZE :]
    place = jnp.concatenate(
        [(seq.me ^ m) * count + jnp.arange(count, dtype=jnp.int32) for m in range(groups)]
    )
    visible = place[None, :] <= place[:, None]
    out_heads, logsum = attend(queries, keys, values, visible)
    out_heads = out_heads.reshape(length, span)

    def back_home(value):
        return seq.natural(
            [
                value[:count] if m == 0 else seq.swap(value[m * count : (m + 1) * count], m)
                for m in range(groups)
            ]
        )

    attn = jnp.concatenate(back_home(out_heads), axis=1)
    attn_even, attn_odd = mask_columns(dp, attn)
    branch = jnp.concatenate(
        [dot(attn_even, outw[t][0]) + dot(attn_odd, outw[t][1]) for t in (0, 1)], axis=1
    )
    hmid = inputs + branch

    inv2 = lax.rsqrt(jnp.mean(hmid * hmid, axis=-1, keepdims=True) + EPS)
    hat2 = jnp.concatenate(mask_columns(dp, (hmid * inv2).astype(BF)), axis=1)
    hat2_all = jnp.concatenate(seq.all(hat2), axis=0)
    hat2_even, hat2_odd = hat2_all[:, : width // 2], hat2_all[:, width // 2 :]
    gate = dot(hat2_even, gate_even) + dot(hat2_odd, gate_odd)
    upper = dot(hat2_even, up_even) + dot(hat2_odd, up_odd)
    sigma = jax.nn.sigmoid(gate)
    hidden = (gate * sigma * upper).astype(BF)
    halves = [cot_all[:, : width // 2], cot_all[:, width // 2 :]]
    dhidden = right_dot(halves[0], down_full[0]) + right_dot(halves[1], down_full[1])
    dgate = (dhidden * upper * sigma * (1.0 + gate * (1.0 - sigma))).astype(BF)
    dupper = (dhidden * gate * sigma).astype(BF)
    dhat2 = jnp.concatenate(
        [
            right_dot(dgate, gate_even) + right_dot(dupper, up_even),
            right_dot(dgate, gate_odd) + right_dot(dupper, up_odd),
        ],
        axis=1,
    ).astype(BF)

    def sum_home(value):
        total = value[:count].astype(F32)
        for m in range(1, groups):
            total = total + seq.swap(value[m * count : (m + 1) * count], m).astype(F32)
        return total

    dhat2 = sum_home(dhat2)
    dgain2 = natural_columns(dp, dhat2[:, : width // 2], dhat2[:, width // 2 :])
    inner = jnp.mean(hmid * dgain2, axis=-1, keepdims=True)
    dh = cotangent.astype(F32) + inv2 * dgain2 - hmid * inv2 * inv2 * inv2 * inner
    dbranch = dh.astype(BF)

    dattn = natural_columns(
        dp,
        *[
            sum(
                right_dot(dbranch[:, t * width // 2 : (t + 1) * width // 2], outw[t][s])
                for t in (0, 1)
            ).astype(BF)
            for s in (0, 1)
        ],
    )
    grad_heads = jnp.concatenate(
        seq.exchange(dattn.reshape(count, groups, span).transpose(1, 0, 2)), axis=0
    ).reshape(length, per, HEAD_SIZE)
    dq, dk, dv = attend_back(queries, keys, values, grad_heads, logsum, visible)
    dqkv = back_home(jnp.concatenate([dq.reshape(length, span), dk, dv], axis=1))
    dq = jnp.concatenate([piece[:, :span] for piece in dqkv], axis=1)
    dk = [piece[:, span : span + HEAD_SIZE].astype(F32) for piece in dqkv]
    dv = [piece[:, span + HEAD_SIZE :].astype(F32) for piece in dqkv]
    dk = jnp.stack(
        [sum(dk[i * repeat : (i + 1) * repeat]) for i in range(KEY_VALUE_HEADS)], axis=1
    )
    dv = jnp.concatenate(
        [sum(dv[i * repeat : (i + 1) * repeat]) for i in range(KEY_VALUE_HEADS)], axis=1
    )
    dq = rotate(dq.astype(F32).reshape(count, H, HEAD_SIZE), cosine, -sine)
    dk = rotate(dk, cosine, -sine)
    dpre = jnp.concatenate(
        [dq.reshape(count, heads_wide), dk.reshape(count, keys_wide), dv], axis=1
    ).astype(BF)
    dhalf = [dpre[:, t * wide // 2 : (t + 1) * wide // 2] for t in (0, 1)]
    dhat1 = [sum(right_dot(dhalf[t], first[t][s]) for t in (0, 1)) for s in (0, 1)]
    dgain1 = natural_columns(dp, *dhat1)
    inner = jnp.mean(inputs * dgain1, axis=-1, keepdims=True)
    grad_inputs = dh + inv1 * dgain1 - inputs * inv1 * inv1 * inv1 * inner

    mixed_part = jnp.concatenate([dot(hidden, down_full[t]) for t in (0, 1)], axis=1).astype(BF)
    mixed = hmid + sum_home(mixed_part)

    grad_down = []
    for t in (0, 1):
        part = left_dot(hidden, halves[t]).astype(BF)
        blocks = [
            lax.dynamic_slice_in_dim(part, (dp.me ^ m) * rows_down, rows_down, 0)
            for m in range(dp.size)
        ]
        even, odd = orders(dp.size)
        other = dp.swap(jnp.stack([blocks[m] for m in odd]), 1)
        summed = {
            m: (blocks[m].astype(F32) + other[i].astype(F32)).astype(BF)
            for i, m in enumerate(even)
        }
        grad_down.append(scatter_chips(dp, summed, t))
    grad_down = jnp.concatenate(grad_down, axis=1)

    def ff_grad(grad, turn):
        odd = left_dot(hat2_odd, grad).astype(BF)
        return scatter_rows(dp, lambda: left_dot(hat2_even, grad), odd, turn)

    rows = w_gate.shape[0]
    sent = jnp.stack([ff_grad(dgate, 0).astype(BF), ff_grad(dupper, 1).astype(BF)])
    sent = sent.reshape(2, groups, rows, ff // groups).transpose(1, 0, 2, 3)
    got = jnp.stack(seq.natural(seq.exchange(sent)))
    got = got.reshape(groups, 2, rows, dp.size, ff // groups // dp.size)
    got = got.transpose(1, 2, 3, 0, 4).reshape(2, rows, ff).astype(F32)
    grad_gate, grad_up = got[0] * gain2, got[1] * gain2
    grad_gain2 = jnp.sum(got[0] * w_gate.astype(F32) + got[1] * w_up.astype(F32), axis=1)

    def proj_grad(even, odd, grads):
        parts = []
        for t in (0, 1):
            send = left_dot(odd, grads[t]).astype(BF)
            parts.append(
                scatter_rows(dp, lambda grad=grads[t]: left_dot(even, grad), send, t)
            )
        own = jnp.concatenate(parts, axis=1)
        own = own.astype(BF).reshape(groups, rows, own.shape[1])
        return sum(piece.astype(F32) for piece in seq.exchange(own))

    grad_out = proj_grad(
        attn_even,
        attn_odd,
        [dbranch[:, t * width // 2 : (t + 1) * width // 2] for t in (0, 1)],
    )
    grad_first = proj_grad(hat1_even, hat1_odd, dhalf)
    grad_gain1 = jnp.sum(grad_first * w_first.astype(F32), axis=1)
    grad_first = grad_first * gain1
    return (
        mixed.astype(BF),
        grad_inputs.astype(BF),
        grad_gain1,
        grad_first[:, :heads_wide],
        grad_first[:, heads_wide : heads_wide + keys_wide],
        grad_first[:, heads_wide + keys_wide :],
        grad_out,
        grad_gain2,
        grad_gate,
        grad_up,
        grad_down,
    )


MESH = pl.DeviceIdType.MESH
ANY = pl.BlockSpec(memory_space=pl.ANY)
VMEM = pl.BlockSpec(memory_space=pltpu.VMEM)


class Net:
    def __init__(self, send_sems, recv_sems):
        self.send_sems, self.recv_sems, self.used = send_sems, recv_sems, 0
        self.open = []
        dp, z = lax.axis_index("dp"), lax.axis_index("seq")
        self.dp, self.z = dp, z
        self.dps = {
            0: dp,
            1: dp + 1 - 2 * lax.rem(dp, 2),
            2: dp + 2 - 4 * lax.rem(lax.div(dp, 2), 2),
            4: lax.rem(dp + 4, 8),
        }
        self.dps[6] = lax.rem(self.dps[2] + 4, 8)
        for mask in (2, 4, 6):
            self.dps[mask + 1] = self.dps[mask] + 1 - 2 * lax.rem(dp, 2)
        self.zs = {0: z, 1: z + 1 - 2 * lax.rem(z, 2), 2: lax.rem(z + 2, 4), 3: 3 - z}

    def target(self, name):
        kind, mask = name
        return (self.dps[mask], self.z) if kind == "d" else (self.dp, self.zs[mask])

    def barrier(self, names):
        sem = pltpu.get_barrier_semaphore()
        for name in names:
            pl.semaphore_signal(sem, inc=1, device_id=self.target(name), device_id_type=MESH)
        pl.semaphore_wait(sem, len(names))

    def send(self, src, dst, name):
        copy = pltpu.make_async_remote_copy(
            src_ref=src,
            dst_ref=dst,
            send_sem=self.send_sems.at[self.used],
            recv_sem=self.recv_sems.at[self.used],
            device_id=self.target(name),
            device_id_type=MESH,
        )
        self.used += 1
        copy.start()
        self.open.append(copy)
        return copy

    def local(self, src, dst):
        copy = pltpu.make_async_copy(src, dst, self.send_sems.at[self.used])
        self.used += 1
        copy.start()
        return copy

    def sent(self, copies):
        for copy in copies:
            copy.wait_send()
        done = [id(copy) for copy in copies]
        self.open = [copy for copy in self.open if id(copy) not in done]

    def finish(self):
        for copy in self.open:
            copy.wait_send()


X, Y, CORE = ("d", 2), ("d", 4), ("d", 1)
PARTNERS = [X, Y, CORE, ("z", 1), ("z", 2), ("z", 3)]


class Plane:
    def __init__(self, net, at, both):
        self.net, self.at, self.both = net, at, both

    def push(self, mask, half, name):
        ref = self.at(mask, half)
        return self.net.send(ref, ref, name)

    def start(self):
        self.xa = self.push(0, 0, X)
        self.yb = self.push(0, 1, Y)
        self.ya = self.push(0, 0, Y)
        self.xb = self.push(0, 1, X)
        self.cores = [self.core(0)]

    def core(self, mask):
        return [self.net.send(ref, ref, CORE) for ref in self.both(mask)]

    def forward(self):
        self.xa.wait_recv()
        self.ya2 = self.push(2, 0, Y)
        self.yb.wait_recv()
        self.xb2 = self.push(4, 1, X)

    def spread(self):
        self.ya.wait_recv()
        self.cores.append(self.core(4))
        self.xb.wait_recv()
        self.cores.append(self.core(2))
        self.ya2.wait_recv()
        self.xb2.wait_recv()
        self.cores.append(self.core(6))

    def finish(self):
        for copies in self.cores:
            for copy in copies:
                copy.wait_recv()

    def sent(self):
        copies = [self.xa, self.yb, self.ya, self.xb, self.ya2, self.xb2]
        self.net.sent(copies + [copy for group in self.cores for copy in group])


def rotary(value, cosine, sine):
    lane = lax.broadcasted_iota(jnp.int32, value.shape, 1)
    partner = jnp.where(
        lax.rem(lane, 64) < 32, pltpu.roll(value, 96, 1), pltpu.roll(value, 32, 1)
    )
    return value * cosine + partner * sine


def column(row):
    n = row.shape[1]
    shape = (n, n)
    same = lax.broadcasted_iota(jnp.int32, shape, 0) == lax.broadcasted_iota(jnp.int32, shape, 1)
    return jnp.sum(jnp.where(same, row.astype(F32), 0.0), axis=1, keepdims=True)


def line(value):
    n = value.shape[0]
    shape = (n, n)
    same = lax.broadcasted_iota(jnp.int32, shape, 0) == lax.broadcasted_iota(jnp.int32, shape, 1)
    return jnp.sum(jnp.where(same, value, 0.0), axis=0, keepdims=True)


def rms(value):
    return lax.rsqrt(jnp.mean(value * value, axis=-1, keepdims=True) + EPS)


def twice(pair):
    lane = lax.broadcasted_iota(jnp.int32, pair.shape, 1)
    other = pltpu.roll(pair.astype(F32), 64, 1).astype(BF)
    return jnp.where(lane < 64, pair, other), jnp.where(lane < 64, other, pair)


def aligned(start, count, unit):
    return pl.ds(pl.multiple_of(start, unit), count)


class Sums:
    def __init__(self, net, part, r1, mid, r2):
        self.net, self.part, self.r1, self.mid, self.r2 = net, part, r1, mid, r2
        self.width = r2.shape[-1]

    def cols(self, side):
        return pl.ds(side * self.width, self.width)

    def block(self, mask):
        return lax.div(self.net.dps[mask], 2)

    def push(self, mask, side, place, name):
        src = self.part.at[self.block(mask), :, self.cols(side)]
        return self.net.send(src, self.r1.at[side, place], name)

    def first(self, mask):
        if mask == 6:
            self.near = [self.push(6, 0, 1, X), self.push(6, 1, 1, Y)]
        elif mask == 2:
            self.own = [self.push(2, 0, 0, X)]
        elif mask == 4:
            self.own.append(self.push(4, 1, 0, Y))

    def second(self):
        self.far = []
        for side, (mask, name) in enumerate(((4, Y), (2, X))):
            self.near[side].wait_recv()
            mine = self.part[self.block(mask), :, self.cols(side)]
            self.mid[side] = (mine.astype(F32) + self.r1[side, 1].astype(F32)).astype(BF)
            self.far.append(self.net.send(self.mid.at[side], self.r2.at[side], name))

    def sent(self):
        self.net.sent(self.near + self.own + self.far)

    def total(self, side):
        self.own[side].wait_recv()
        self.far[side].wait_recv()
        mine = self.part[self.block(0), :, self.cols(side)]
        return mine.astype(F32) + self.r1[side, 0].astype(F32) + self.r2[side].astype(F32)


def first_kernel(
    x_ref, wq, wk, wv, gain1, w_gate, w_up, gain2, cos_q, sin_q, cos_k, sin_k, wo, wd, cot,
    wq_out, wo_out, hat_out, qkv_out, att_out, mx_out, mx_far, hg_out, lse, hmid, dn_out, gdown,
    wq_s, wf, wq_v, wo_v, hat, qkv_send, qkv, heads, att, part, r1, mid, r2,
    wg_v, wd_v, n_v, n_sib, c_v, c_sib, hid, dg, du,
    mx_r, hd, hd_r1, hd_k, hd_r2, sib_r, send_sems, recv_sems,
):
    net = Net(send_sems, recv_sems)
    dp, z, dps, zs = net.dp, net.z, net.dps, net.zs
    tok, width = x_ref.shape
    group = qkv.shape[1]
    span = heads.shape[1]
    ff = wf.shape[-1]
    core, chip = lax.rem(dp, 2), lax.div(dp, 2)
    here = aligned(z * tok, tok, 16)

    own = [
        net.local(wo, wo_v.at[core, z]),
        net.local(wd, wd_v.at[aligned(dp * 176, 176, 16), :]),
        net.local(cot, c_v.at[here, :]),
    ]
    net.barrier(PARTNERS + [("d", 6)])

    scale = column(gain1[...])
    lane = lax.broadcasted_iota(jnp.int32, (wq.shape[0], 128), 1)
    for g in range(4):
        wq_s[g, :, :span] = (wq[:, g * span : (g + 1) * span].astype(F32) * scale).astype(BF)
        start = g // 2 * 128
        k = wk[:, start : start + 128].astype(F32)
        v = wv[:, start : start + 128].astype(F32)
        if g % 2 == 0:
            both = jnp.where(lane < 64, k, pltpu.roll(v, 64, 1))
        else:
            both = jnp.where(lane < 64, pltpu.roll(k, 64, 1), v)
        wq_s[g, :, span:] = (both * scale).astype(BF)

    def chip_of(mask):
        return lax.div(dps[mask], 2)

    w_1 = [
        net.send(wq_s.at[chip_of(m)], wq_v.at[chip, core, z], ("d", m)) for m in (6, 2, 4)
    ]
    own_q = net.local(wq_s.at[chip], wq_v.at[chip, core, z])
    x = x_ref[...].astype(F32)
    hat[chip] = (x * rms(x)).astype(BF)

    def half_of(ref, side):
        w = ref.shape[-1] // 2
        return pl.ds(side * w, w)

    def block(ref, size, cores):
        def at(mask, side):
            return ref.at[aligned(dps[mask] * size, size, 16), half_of(ref, side)]

        return at, lambda mask: [ref.at[aligned(dps[mask] * size, size, 16), :]] if cores else []

    plane_h = Plane(net, lambda m, s: hat.at[chip_of(m), :, half_of(hat, s)], lambda m: [])
    plane_h.start()
    down = Plane(net, *block(wd_v, 176, True))
    own[1].wait()
    down.start()

    def wq_at(mask):
        return wq_v.at[:, core, zs[mask]]

    def wo_at(mask):
        return wo_v.at[core, zs[mask]]

    class Line:
        def __init__(self, at):
            self.at = at
            self.far = self.push(0, ("z", 2))
            self.near = self.push(0, ("z", 1))
            self.cores = [self.push(0, CORE)]

        def push(self, mask, name):
            return net.send(self.at(mask), self.at(mask), name)

        def forward(self):
            self.far.wait_recv()
            self.last = self.push(2, ("z", 1))
            self.cores.append(self.push(2, CORE))

        def spread(self):
            self.near.wait_recv()
            self.cores.append(self.push(1, CORE))
            self.last.wait_recv()
            self.cores.append(self.push(3, CORE))

        def finish(self):
            for copy in self.cores:
                copy.wait_recv()

    scale = column(gain2[...])
    size = ff // 8
    for t, weight in enumerate((w_gate, w_up)):
        for i in range(4):
            parts = [weight[:, (d * 4 + i) * size : (d * 4 + i + 1) * size] for d in range(8)]
            joined = jnp.concatenate([p.astype(F32) for p in parts], axis=1)
            wf[i, t] = (joined * scale).astype(BF)
    own_f = net.local(wf.at[z], wg_v.at[:, aligned((dp * 4 + z) * 64, 64, 16), :])

    f_rows = aligned((dp * 4 + z) * 64, 64, 16)

    def f_send(t):
        return [
            net.send(wf.at[zs[m], t], wg_v.at[t, f_rows, :], ("z", m)) for m in (2, 3, 1)
        ]

    def f_plane(t):
        def rows(mask, start, count):
            return wg_v.at[t, aligned(dps[mask] * 256 + start, count, 16), :]

        return Plane(
            net, lambda m, s: rows(m, s * 128, 128), lambda m: [rows(m, 0, 256)]
        )

    own[0].wait()
    line_o = Line(wo_at)
    own_q.wait()
    for copy in w_1:
        copy.wait_recv()

    line_q = Line(wq_at)
    plane_h.forward()
    line_q.forward()
    gate_copies = f_send(0)
    plane_h.spread()
    line_q.spread()
    down.forward()
    line_q.finish()

    weight = wq_v[...].reshape(width, group)

    def project(s, carry):
        pre = jnp.dot(hat[s], weight, preferred_element_type=F32)
        for j in range(group // 128):
            last = j == group // 128 - 1
            c_ref, s_ref = (cos_k, sin_k) if last else (cos_q, sin_q)
            value = rotary(pre[:, j * 128 : (j + 1) * 128], c_ref[...], s_ref[...])
            qkv_send[s, :, j * 128 : (j + 1) * 128] = value.astype(BF)
        return carry

    lax.fori_loop(0, 4, project, 0)
    q_copies = [net.send(qkv_send.at[zs[m]], qkv.at[here, :], ("z", m)) for m in (2, 3, 1)]
    own_q = net.local(qkv_send.at[z], qkv.at[here, :])
    line_o.forward()
    up_copies = f_send(1)
    down.spread()
    own_q.wait()
    for copy in q_copies:
        copy.wait_recv()

    kk, vv = twice(qkv[:, span:])

    def pair(p, carry):
        cols = aligned(p * 128, 128, 128)
        for qb in range(4):
            keys = (qb + 1) * tok
            q = qkv[qb * tok : (qb + 1) * tok, cols]
            lane = lax.broadcasted_iota(jnp.int32, (tok, 128), 1)
            row = lax.broadcasted_iota(jnp.int32, (tok, keys), 0) + qb * tok
            col = lax.broadcasted_iota(jnp.int32, (tok, keys), 1)
            outs = []
            for h in range(2):
                mine = (lane < 64) if h == 0 else (lane >= 64)
                qh = jnp.where(mine, q, jnp.zeros_like(q))
                s = right_dot(qh, kk[:keys]) * HEAD_SIZE ** (-0.5)
                s = jnp.where(col <= row, s, -1e30)
                top = jnp.max(s, axis=-1, keepdims=True)
                e = jnp.exp(s - top)
                total = jnp.sum(e, axis=-1, keepdims=True)
                probs = (e * (1.0 / total)).astype(BF)
                outs.append(dot(probs, vv[:keys]))
                old = lse[qb * tok : (qb + 1) * tok, :]
                lse[qb * tok : (qb + 1) * tok, :] = jnp.where(
                    lane == 2 * p + h, top + jnp.log(total), old
                )
            heads[qb * tok : (qb + 1) * tok, cols] = jnp.where(
                lane < 64, outs[0], outs[1]
            ).astype(BF)
        return carry

    lse[...] = jnp.zeros_like(lse)
    lax.fori_loop(0, span // 128, pair, 0)
    h_copies = [
        net.send(heads.at[aligned(zs[m] * tok, tok, 16), :], att.at[z], ("z", m))
        for m in (2, 3, 1)
    ]
    own_h = net.local(heads.at[here, :], att.at[z])

    own_f.wait()
    for copy in gate_copies:
        copy.wait_recv()
    plane_g, plane_u = f_plane(0), f_plane(1)
    plane_g.start()
    line_o.spread()
    line_o.finish()
    own_h.wait()
    for copy in h_copies:
        copy.wait_recv()


    c_near = net.send(cot, c_v.at[here, :], ("z", 1))
    c_far = net.send(cot, c_v.at[here, :], ("z", 2))
    sums = Sums(net, part, r1, mid, r2)
    for m in (6, 2, 4, 0):
        s = chip_of(m)
        for c in range(4):
            cols = pl.ds(c * (width // 4), width // 4)
            weight = wo_v[:, :, :, cols].reshape(span, width // 4)
            part[s, :, cols] = dot(att[s], weight).astype(BF)
        sums.first(m)
    sums.second()
    plane_g.forward()
    for copy in up_copies:
        copy.wait_recv()
    plane_u.start()
    for side in (0, 1):
        cols = half_of(hmid, side)
        hmid[:, cols] = x_ref[:, cols].astype(F32) + sums.total(side)
    value = hmid[...]
    n_v[here, :] = (value * rms(value)).astype(BF)

    def slot(mask):
        return aligned(zs[mask] * tok, tok, 16)

    def tokens(ref, mask, name):
        return net.send(ref.at[slot(mask), :], ref.at[slot(mask), :], name)

    n_far = tokens(n_v, 0, ("z", 2))
    n_near = tokens(n_v, 0, ("z", 1))
    outs = [
        net.local(wq_v, wq_out), net.local(wo_v, wo_out), net.local(qkv, qkv_out),
        net.local(att, att_out), net.local(hat, hat_out),
    ]
    c_far.wait_recv()
    c_last = tokens(c_v, 2, ("z", 1))
    plane_g.spread()
    plane_u.forward()
    n_far.wait_recv()
    n_last = tokens(n_v, 2, ("z", 1))
    plane_u.spread()

    half = width // 2
    near_pair = lax.div(z, 2)
    far = aligned((1 - near_pair) * 2 * tok, 2 * tok, 16)
    near = aligned(near_pair * 2 * tok, 2 * tok, 16)
    dn_part = part

    def chunks(fn, total, size):
        whole = total // size

        def step(i, carry):
            fn(i * size, size)
            return carry

        lax.fori_loop(0, whole, step, 0)
        if total % size:
            fn(whole * size, total - whole * size)

    def front(rows):
        def chunk(start, size):
            cols = aligned(start, size, 128)
            n = n_v[rows, :]
            gate = dot(n, wg_v[0, :, cols])
            upper = dot(n, wg_v[1, :, cols])
            dhid = right_dot(c_v[rows, :], wd_v[cols, :])
            sigma = jax.nn.sigmoid(gate)
            silu = gate * sigma
            hid[0, rows, cols] = (silu * upper).astype(BF)
            dg[0, rows, cols] = (dhid * upper * sigma * (1.0 + gate * (1.0 - sigma))).astype(BF)
            du[0, rows, cols] = (dhid * silu).astype(BF)

        chunks(chunk, ff, 256)
        return [
            net.send(ref.at[0, rows, :], ref.at[1, rows, :], CORE) for ref in (hid, dg, du)
        ]

    def back(rows, first_slot, side):
        def chunk(start, size):
            cols = aligned(start + side * half, size, 128)
            total = right_dot(dg[0, rows, :], wg_v[0, cols, :])
            total += right_dot(du[0, rows, :], wg_v[1, cols, :])
            dn_part[pl.ds(first_slot, 2), :, cols] = total.astype(BF).reshape(2, tok, size)

        chunks(chunk, half, 256)

    def piece(side):
        return pl.ds(side * half, half)

    sums.sent()
    n_near.wait_recv()
    c_near.wait_recv()
    for plane in (down, plane_g, plane_u):
        plane.finish()
    own[2].wait()
    sib = front(near)
    dn_b = []
    for side in (0, 1):
        back(near, near_pair * 2, side)
        dn_b.append(
            net.send(
                dn_part.at[zs[1], :, piece(side)], r1.at[side, 0], ("z", 1)
            )
        )
    c_last.wait_recv()
    c_copy = net.send(c_v.at[:, aligned((1 - core) * half, half, 128)], c_sib, CORE)
    n_last.wait_recv()
    n_copies = [
        net.send(
            n_v.at[:, aligned((i * 2 + 1 - core) * 256, 256, 128)],
            n_sib.at[:, pl.ds(i * 256, 256)],
            CORE,
        )
        for i in range(4)
    ]
    sib += front(far)
    dn_a = []
    for side in (0, 1):
        back(far, (1 - near_pair) * 2, side)
        dn_a.append(
            net.send(
                dn_part.at[zs[3], :, piece(side)], r1.at[side, 1], ("z", 1)
            )
        )
    c_copy.wait_recv()
    for copy in sib:
        copy.wait_recv()

    ccols = aligned(core * half, half, 128)

    def down_chunk(start, size):
        cols = aligned(start, size, 128)
        total = left_dot(hid[0, :, cols], c_v[:, ccols])
        total += left_dot(hid[1, :, cols], c_sib[...])
        hd[cols, :] = total.astype(BF)

    chunks(down_chunk, ff, 256)
    chip_rows = ff // 4
    quarter = half // 2

    def hd_at(mask, side):
        return aligned(chip_of(mask) * chip_rows, chip_rows, 16), pl.ds(side * quarter, quarter)

    def hd_send(mask, side, place, name):
        r, c = hd_at(mask, side)
        return net.send(hd.at[r, c], hd_r1.at[side, place], name)

    hd_1 = [hd_send(6, 0, 1, X), hd_send(6, 1, 1, Y), hd_send(2, 0, 0, X), hd_send(4, 1, 0, Y)]
    dn_c = []
    for side in (0, 1):
        dn_a[side].wait_recv()
        cols = piece(side)
        mid[side] = (
            dn_part[zs[2], :, cols].astype(F32) + r1[side, 1].astype(F32)
        ).astype(BF)
        dn_c.append(net.send(mid.at[side], r2.at[side], ("z", 2)))

    for copy in outs:
        copy.wait()
    plane_h.sent()

    def mix_chunk(start, size):
        cols = aligned(start, size, 128)
        hat[:, :, cols] = dot(hid[0], wd_v[:, cols]).astype(BF).reshape(4, tok, size)

    chunks(mix_chunk, width, 256)
    mx_copy = net.local(hat, mx_out)
    mx_a = net.send(hat.at[zs[3]], mx_r, ("z", 1))

    hd_1[0].wait_recv()
    hd_1[1].wait_recv()
    hd_2 = []
    for side, (mask, name) in enumerate(((4, Y), (2, X))):
        r, c = hd_at(mask, side)
        hd_k[side] = (hd[r, c].astype(F32) + hd_r1[side, 1].astype(F32)).astype(BF)
        hd_2.append(net.send(hd_k.at[side], hd_r2.at[side], name))

    for copy in n_copies:
        copy.wait_recv()
    plane_g.sent()
    plane_u.sent()

    def block(b, carry):
        cols = aligned((b * 2 + core) * 256, 256, 128)
        left = n_v[:, cols].T
        other = n_sib[:, aligned(b * 256, 256, 128)].T
        for t, grad in enumerate((dg, du)):
            total = dot(left, grad[0]) + dot(other, grad[1])
            wg_v[t, aligned(b * 256, 256, 16), :] = total.astype(BF)
        return carry

    lax.fori_loop(0, 4, block, 0)
    hg_copy = net.local(wg_v.at[:, pl.ds(0, 1024), :], hg_out)
    for side in (0, 1):
        dn_b[side].wait_recv()
        dn_c[side].wait_recv()
        cols = piece(side)
        dn_out[:, cols] = (
            dn_part[z, :, cols].astype(F32)
            + r1[side, 0].astype(F32)
            + r2[side].astype(F32)
        )
    mx_a.wait_recv()
    net.sent(dn_c)
    far_copies = []
    for side in (0, 1):
        cols = piece(side)
        mid[side] = (hat[zs[2], :, cols].astype(F32) + mx_r[:, cols].astype(F32)).astype(BF)
        far_copies.append(net.local(mid.at[side], mx_far.at[:, cols]))
    hd_1[2].wait_recv()
    hd_1[3].wait_recv()
    rows_half = chip_rows // 2
    for side in (0, 1):
        hd_2[side].wait_recv()

        def total(start):
            _, c = hd_at(0, side)
            return (
                hd[aligned(chip * chip_rows + start, rows_half, 16), c].astype(F32)
                + hd_r1[side, 0, aligned(start, rows_half, 16), :].astype(F32)
                + hd_r2[side, aligned(start, rows_half, 16), :].astype(F32)
            )

        net.sent([hd_2[side]])
        hd_k[side, :rows_half] = total((1 - core) * rows_half).astype(BF)
        gdown[:, aligned(core * half + side * quarter, quarter, 128)] = total(core * rows_half)
    last = net.send(hd_k.at[:, pl.ds(0, rows_half), :], sib_r, CORE)
    last.wait_recv()
    for side in (0, 1):
        start = (1 - core) * half + side * quarter
        gdown[:, aligned(start, quarter, 128)] = sib_r[side].astype(F32)
    hg_copy.wait()
    mx_copy.wait()
    for copy in far_copies:
        copy.wait()
    net.finish()


def first_call(x, wq, wk, wv, gain1, w_gate, w_up, gain2, tables4, wo, wd, cot):
    tok, width = x.shape
    ff = w_gate.shape[1] // 4
    span = width // 4
    group = span + 128
    sds = jax.ShapeDtypeStruct
    v = pltpu.VMEM
    half = width // 2
    return pl.pallas_call(
        first_kernel,
        name="first",
        out_shape=[
            sds((4, 2, 4, 64, group), BF), sds((2, 4, 64, width), BF), sds((4, tok, width), BF),
            sds((4 * tok, group), BF), sds((4, tok, span), BF), sds((4, tok, width), BF),
            sds((tok, width), BF), sds((2, 1024, ff), BF), sds((4 * tok, 128), F32), sds((tok, width), F32),
            sds((tok, width), F32), sds((ff // 8, width), F32),
        ],
        in_specs=[VMEM] * 15,
        out_specs=[ANY] * 8 + [VMEM] * 4,
        scratch_shapes=[
            v((4, 64, group), BF), v((4, 2, 64, ff), BF), v((4, 2, 4, 64, group), BF),
            v((2, 4, 64, width), BF), v((4, tok, width), BF), v((4, tok, group), BF),
            v((4 * tok, group), BF), v((4 * tok, span), BF), v((4, tok, span), BF),
            v((4, tok, width), BF), v((2, 2, tok, half), BF), v((2, tok, half), BF),
            v((2, tok, half), BF),
            v((2, width, ff), BF), v((ff, width), BF), v((4 * tok, width), BF),
            v((4 * tok, half), BF), v((4 * tok, width), BF), v((4 * tok, half), BF),
            v((2, 4 * tok, ff), BF), v((2, 4 * tok, ff), BF), v((2, 4 * tok, ff), BF),
            v((tok, width), BF), v((ff, half), BF), v((2, 2, ff // 4, half // 2), BF), v((2, ff // 4, half // 2), BF),
            v((2, ff // 4, half // 2), BF), v((2, ff // 8, half // 2), BF),
            pltpu.SemaphoreType.DMA((144,)),
            pltpu.SemaphoreType.DMA((144,)),
        ],
        compiler_params=pltpu.CompilerParams(
            collective_id=1, has_side_effects=True, vmem_limit_bytes=62 * 2**20
        ),
    )(x, wq, wk, wv, gain1, w_gate, w_up, gain2, *tables4, wo, wd, cot)


def third_kernel(
    x_ref, hmid, cot, dn2, qkv, lse, cos_q, sin_q, cos_k, sin_k,
    mx, mx_far, wq, wo, hat, att, hg,
    tok_out, mixed, g2_out, g1_out, fb,
    wq_v, wo_v, hat_v, hat_s, att_v, att_s, mx_v, mx_r1, mx_r2,
    hg_v, f_r1, f_k, f_r2, fs, dh, dbr, dbr_s, dsend, gh, dqkv, dk_acc, dv_acc, dback,
    dpre, dpre_s, part, r1, mid, r2, g2_p, g2_r1, g2_s, g2_r2, g1_p, g1_r1, g1_s, g1_r2, g1_f,
    send_sems, recv_sems,
):
    net = Net(send_sems, recv_sems)
    dp, z, dps, zs = net.dp, net.z, net.dps, net.zs
    tok, width = x_ref.shape
    group = qkv.shape[1]
    span = group - 128
    here = aligned(z * tok, tok, 16)
    core, chip = lax.rem(dp, 2), lax.div(dp, 2)

    def chip_of(mask):
        return lax.div(dps[mask], 2)

    def slot(mask):
        return aligned(zs[mask] * tok, tok, 16)

    def hg_at(t, mask, side):
        return hg.at[t, aligned(chip_of(mask) * 256 + side * 128, 128, 16), :]

    loads = [
        net.local(wo, wo_v),
        net.local(hg.at[:, aligned(chip * 256, 256, 16), :], hg_v.at[0]),
        net.local(hg.at[:, aligned(chip_of(4) * 256, 128, 16), :], hg_v.at[1, :, pl.ds(0, 128)]),
        net.local(
            hg.at[:, aligned(chip_of(2) * 256 + 128, 128, 16), :], hg_v.at[1, :, pl.ds(128, 128)]
        ),
        net.local(mx.at[z], mx_v),
        net.local(att, att_v),
        net.local(wq, wq_v),
        net.local(hat, hat_v),
    ]
    net.barrier(PARTNERS + [("d", 6)])
    def f_send(t, place, mask, side, name):
        return net.send(hg_at(t, mask, side), f_r1.at[place, t, pl.ds(side * 128, 128)], name)

    def f_near(t):
        return [f_send(t, 1, 6, 0, X), f_send(t, 1, 6, 1, Y)]

    def f_own(t):
        return [f_send(t, 0, 2, 0, X), f_send(t, 0, 4, 1, Y)]

    def f_second(t, sent):
        for copy in sent:
            copy.wait_recv()
        f_k[t] = (hg_v[1, t].astype(F32) + f_r1[1, t].astype(F32)).astype(BF)
        return [
            net.send(f_k.at[t, pl.ds(side * 128, 128)], f_r2.at[t, pl.ds(side * 128, 128)], name)
            for side, name in ((0, Y), (1, X))
        ]

    def f_rows(t, sent):
        for copy in sent:
            copy.wait_recv()
        total = hg_v[0, t].astype(F32) + f_r1[0, t].astype(F32) + f_r2[t].astype(F32)
        for i in range(4):
            fs[i, t] = total[i * 64 : (i + 1) * 64, :].astype(BF)
        fb[z, t] = fs[z, t]
        return [net.send(fs.at[zs[m], t], fb.at[z, t], ("z", m)) for m in (2, 3, 1)]

    gate_1 = f_near(0)
    mx_copies = [
        net.send(mx_far, mx_r2, ("z", 2)),
        net.send(mx.at[zs[1]], mx_r1, ("z", 1)),
    ]
    half = width // 2

    def norm_back(value, grad):
        inv = rms(value)
        inner = jnp.mean(value * grad, axis=-1, keepdims=True)
        return inv * grad - value * (inv * inv * inv * inner)

    dh[...] = cot[...].astype(F32) + norm_back(hmid[...], dn2[...])
    dbr[chip] = dh[...].astype(BF)
    plane_b = Plane(net, lambda m, s: dbr.at[chip_of(m), :, pl.ds(s * half, half)], lambda m: [])
    plane_b.start()
    small = [
        net.send(att.at[:, :, aligned((1 - core) * 256, 256, 128)], att_s, CORE)
    ] + [
        net.send(
            hat.at[:, :, aligned(i * 512 + (1 - core) * 256, 256, 128)],
            hat_s.at[:, :, pl.ds(i * 256, 256)],
            CORE,
        )
        for i in range(4)
    ]
    plane_b.forward()
    for copy in loads[1:4]:
        copy.wait()
    gate_2 = f_second(0, gate_1) + f_own(0)
    up_1 = f_near(1)
    up_2 = f_own(1)
    plane_b.spread()
    loads[0].wait()
    d_copies = []
    weight = wo_v[...].reshape(span, width)
    for m in (2, 3, 1, 0):
        dsend[m] = right_dot(dbr[zs[m]], weight).astype(BF)
        if m:
            d_copies.append(net.send(dsend.at[m], gh.at[here, :], ("z", m)))
    gh[here, :] = dsend[0]
    dbr_copy = net.send(dbr, dbr_s, CORE)
    for copy in loads[4:]:
        copy.wait()

    class Line:
        def __init__(self, parts, r1, s, r2):
            self.parts, self.r1, self.s, self.r2 = parts, r1, s, r2
            self.sent = [
                net.send(parts.at[zs[3]], r1.at[1], ("z", 1)),
                net.send(parts.at[zs[1]], r1.at[0], ("z", 1)),
            ]

        def middle(self):
            self.sent[0].wait_recv()
            self.s[...] = (self.parts[zs[2]].astype(F32) + self.r1[1].astype(F32)).astype(BF)
            self.far = net.send(self.s, self.r2, ("z", 2))

        def total(self):
            self.sent[1].wait_recv()
            self.far.wait_recv()
            own = self.parts[z].astype(F32) + self.r1[0].astype(F32)
            return own + self.r2[...].astype(F32)

    small[0].wait_recv()
    dbr_copy.wait_recv()
    mine = att_v[:, :, aligned(core * 256, 256, 128)].reshape(4 * tok, 256).T
    theirs = att_s[...].reshape(4 * tok, 256).T

    def out_chunk(i, carry):
        cols = aligned(i * 512, 512, 128)
        total = dot(mine, dbr[:, :, cols].reshape(4 * tok, 512))
        total += dot(theirs, dbr_s[:, :, cols].reshape(4 * tok, 512))
        g2_p[:, :, cols] = total.astype(BF).reshape(4, 64, 512)
        return carry

    lax.fori_loop(0, width // 512, out_chunk, 0)
    line_o = Line(g2_p, g2_r1, g2_s, g2_r2)

    for copy in d_copies:
        copy.wait_recv()
    f_copies = f_rows(0, gate_2)

    scale = HEAD_SIZE ** (-0.5)
    kk, vv = twice(qkv[:, span:])
    dk_acc[...] = jnp.zeros_like(dk_acc)
    dv_acc[...] = jnp.zeros_like(dv_acc)

    def pair(p, carry):
        cols = aligned(p * 128, 128, 128)
        for qb in range(4):
            keys = (qb + 1) * tok
            rows = slice(qb * tok, (qb + 1) * tok)
            q = qkv[rows, cols]
            g = gh[rows, cols]
            lane = lax.broadcasted_iota(jnp.int32, (tok, 128), 1)
            row = lax.broadcasted_iota(jnp.int32, (tok, keys), 0) + qb * tok
            col = lax.broadcasted_iota(jnp.int32, (tok, keys), 1)
            outs = []
            for h in range(2):
                lanes = (lane < 64) if h == 0 else (lane >= 64)
                qh = jnp.where(lanes, q, jnp.zeros_like(q))
                gg = jnp.where(lanes, g, jnp.zeros_like(g))
                log = jnp.sum(
                    jnp.where(lane == 2 * p + h, lse[rows, :], 0.0), axis=-1, keepdims=True
                )
                s = right_dot(qh, kk[:keys]) * scale
                probs = jnp.exp(jnp.where(col <= row, s, -1e30) - log)
                pg = right_dot(gg, vv[:keys])
                delta = jnp.sum(probs * pg, axis=-1, keepdims=True)
                ds = (probs * (pg - delta)).astype(BF)
                outs.append(dot(ds, kk[:keys]) * scale)
                dk_acc[:keys, :] += left_dot(ds, qh)
                dv_acc[:keys, :] += left_dot(probs.astype(BF), gg)
            dqkv[rows, cols] = jnp.where(lane < 64, outs[0], outs[1]).astype(BF)
        return carry

    lax.fori_loop(0, span // 128, pair, 0)
    dk = dk_acc[...]
    dv = dv_acc[...]
    lane = lax.broadcasted_iota(jnp.int32, dk.shape, 1)
    dqkv[:, span:] = jnp.where(
        lane < 64, (dk + pltpu.roll(dk, 64, 1)) * scale, dv + pltpu.roll(dv, 64, 1)
    ).astype(BF)
    b_copies = [net.send(dqkv.at[slot(m), :], dback.at[z], ("z", m)) for m in (2, 3, 1)]
    dback[z] = dqkv[here, :]
    line_o.middle()

    up_2 += f_second(1, up_1)
    for copy in b_copies:
        copy.wait_recv()
    for s in range(4):
        for j in range(group // 128):
            cols = slice(j * 128, (j + 1) * 128)
            last = j == group // 128 - 1
            c_ref, s_ref = (cos_k, sin_k) if last else (cos_q, sin_q)
            value = dback[s, :, cols].astype(F32)
            dpre[s, :, cols] = rotary(value, c_ref[...], -s_ref[...]).astype(BF)
    dpre_copy = net.send(dpre, dpre_s, CORE)

    left = dpre[...].reshape(4 * tok, group)

    def dhat_chunk(i, carry):
        cols = aligned(i * 256, 256, 128)
        rows = wq_v[lax.div(i, 2), lax.rem(i, 2)].reshape(256, group)
        part[:, :, cols] = right_dot(left, rows).astype(BF).reshape(4, tok, 256)
        return carry

    lax.fori_loop(0, width // 256, dhat_chunk, 0)
    sums = Sums(net, part, r1, mid, r2)
    for m in (6, 2, 4):
        sums.first(m)

    for copy in small[1:]:
        copy.wait_recv()
    dpre_copy.wait_recv()
    right = dpre_s[...].reshape(4 * tok, group)

    def first_chunk(i, carry):
        own = hat_v[:, :, aligned(i * 512 + core * 256, 256, 128)].reshape(4 * tok, 256).T
        sib = hat_s[:, :, aligned(i * 256, 256, 128)].reshape(4 * tok, 256).T
        total = dot(own, left) + dot(sib, right)
        g1_p[:, i] = total.astype(BF).reshape(4, 64, group)
        return carry

    lax.fori_loop(0, 4, first_chunk, 0)
    line_q = Line(g1_p, g1_r1, g1_s, g1_r2)
    f_copies += f_rows(1, up_2)
    sums.second()
    line_q.middle()
    for copy in mx_copies:
        copy.wait_recv()
    total = mx_v[...].astype(F32) + mx_r1[...].astype(F32) + mx_r2[...].astype(F32)
    mixed[...] = (hmid[...] + total).astype(BF)
    g2_out[...] = line_o.total()
    for side in (0, 1):
        dn2[:, side * half : (side + 1) * half] = sums.total(side)
    tok_out[...] = (dh[...] + norm_back(x_ref[...].astype(F32), dn2[...])).astype(BF)
    g1_f[...] = line_q.total().astype(BF)
    g_copies = [net.send(g1_f.at[chip_of(m)], g1_out.at[chip], ("d", m)) for m in (6, 2, 4)]
    g1_out[chip] = g1_f[chip]
    for copy in g_copies + f_copies:
        copy.wait_recv()
    net.finish()


def third_call(x, hmid, cot, dn2, qkv, lse, tables4, mx, mx_far, wq, wo, hat, att, hg):
    tok, width = x.shape
    group = qkv.shape[1]
    span = group - 128
    ff = hg.shape[-1]
    sds = jax.ShapeDtypeStruct
    v = pltpu.VMEM
    return pl.pallas_call(
        third_kernel,
        name="third",
        out_shape=[
            sds((tok, width), BF), sds((tok, width), BF), sds((64, width), F32),
            sds((4, 64, group), BF), sds((4, 2, 64, ff), BF),
        ],
        in_specs=[VMEM] * 10 + [ANY] * 7,
        out_specs=[VMEM] * 5,
        scratch_shapes=[
            v((4, 2, 4, 64, group), BF), v((2, 4, 64, width), BF), v((4, tok, width), BF),
            v((4, tok, width // 2), BF), v((4, tok, span), BF), v((4, tok, span // 2), BF),
            v((tok, width), BF), v((tok, width), BF), v((tok, width), BF),
            v((2, 2, 256, ff), BF), v((2, 2, 256, ff), BF), v((2, 256, ff), BF), v((2, 256, ff), BF),
            v((4, 2, 64, ff), BF), v((tok, width), F32), v((4, tok, width), BF),
            v((4, tok, width), BF), v((4, tok, span), BF), v((4 * tok, span), BF),
            v((4 * tok, group), BF), v((4 * tok, 128), F32), v((4 * tok, 128), F32),
            v((4, tok, group), BF), v((4, tok, group), BF), v((4, tok, group), BF),
            v((4, tok, width), BF), v((2, 2, tok, width // 2), BF), v((2, tok, width // 2), BF),
            v((2, tok, width // 2), BF),
            v((4, 64, width), BF), v((2, 64, width), BF), v((64, width), BF), v((64, width), BF),
            v((4, 4, 64, group), BF), v((2, 4, 64, group), BF), v((4, 64, group), BF),
            v((4, 64, group), BF), v((4, 64, group), BF),
            pltpu.SemaphoreType.DMA((80,)),
            pltpu.SemaphoreType.DMA((80,)),
        ],
        compiler_params=pltpu.CompilerParams(
            collective_id=3, has_side_effects=True, vmem_limit_bytes=60 * 2**20
        ),
    )(x, hmid, cot, dn2, qkv, lse, *tables4, mx, mx_far, wq, wo, hat, att, hg)


def last_kernel(
    fb, g1, wq, wk, wv, gain1, gain2, w_gate_in, w_up_in, tok_in, mixed_in, g2_in, gd_in,
    gq, gk, gv, g_gate, g_up, g_gain1, g_gain2, tok_out, mixed_out, g2_out, gd_out,
    w_gate, w_up, sems,
):
    copies = [
        pltpu.make_async_copy(src, dst, sems.at[i])
        for i, (src, dst) in enumerate(
            (
                (w_gate_in, w_gate), (w_up_in, w_up), (tok_in, tok_out),
                (mixed_in, mixed_out), (g2_in, g2_out), (gd_in, gd_out),
            )
        )
    ]
    for copy in copies:
        copy.start()
    span = g1.shape[2] - 128
    lane = lax.broadcasted_iota(jnp.int32, (g1.shape[1], 128), 1)
    scale = column(gain1[...])
    scale2 = column(gain2[...])

    def put(out, weight, cols, value):
        out[:, cols] = value * scale
        return jnp.sum(value * weight[:, cols].astype(F32), axis=1, keepdims=True)

    total = jnp.zeros((g1.shape[1], 1), F32)
    for g in range(4):
        total += put(gq, wq, slice(g * span, (g + 1) * span), g1[g, :, :span].astype(F32))
    for g in (0, 2):
        one = g1[g, :, span:].astype(F32)
        two = g1[g + 1, :, span:].astype(F32)
        cols = slice(g * 64, g * 64 + 128)
        total += put(gk, wk, cols, jnp.where(lane < 64, one, pltpu.roll(two, 64, 1)))
        total += put(gv, wv, cols, jnp.where(lane < 64, pltpu.roll(one, 64, 1), two))
    g_gain1[...] = line(total)
    size = fb.shape[-1] // 8
    total = jnp.zeros((g1.shape[1], 1), F32)
    for t, (out, weight) in enumerate(((g_gate, w_gate), (g_up, w_up))):
        copies[t].wait()
        for d in range(0, 8, 2):
            parts = [
                fb[i, t, :, e * size : (e + 1) * size].astype(F32) for e in (d, d + 1) for i in range(4)
            ]
            joined = jnp.concatenate(parts, axis=1)
            cols = pl.ds(d * 4 * size, 8 * size)
            total += jnp.sum(joined * weight[:, cols].astype(F32), axis=1, keepdims=True)
            out[:, cols] = joined * scale2
    g_gain2[...] = line(total)
    for copy in copies[2:]:
        copy.wait()


def last_call(fb, g1, wq, wk, wv, gain1, gain2, w_gate, w_up, tok, mixed, g2, gd):
    rows, ff = w_gate.shape
    sds = jax.ShapeDtypeStruct
    return pl.pallas_call(
        last_kernel,
        name="last",
        out_shape=[
            sds(wq.shape, F32), sds(wk.shape, F32), sds(wv.shape, F32),
            sds((rows, ff), F32), sds((rows, ff), F32), sds((1, rows), F32), sds((1, rows), F32),
            sds(tok.shape, BF), sds(mixed.shape, BF), sds(g2.shape, F32), sds(gd.shape, F32),
        ],
        in_specs=[VMEM] * 7 + [ANY] * 6,
        out_specs=[VMEM] * 11,
        scratch_shapes=[
            pltpu.VMEM((rows, ff), BF), pltpu.VMEM((rows, ff), BF), pltpu.SemaphoreType.DMA((6,)),
        ],
        compiler_params=pltpu.CompilerParams(vmem_limit_bytes=60 * 2**20),
    )(fb, g1, wq, wk, wv, gain1, gain2, w_gate, w_up, tok, mixed, g2, gd)


def shards(
    tokens, norm_first, w_query, w_key, w_value, w_out, norm_second, w_gate, w_up, w_down, cotangent
):
    count = tokens.shape[0]
    gain1, gain2 = norm_first[None, :], norm_second[None, :]
    cosine, sine = tables(lax.axis_index("seq") * count + jnp.arange(count))
    cosine, sine = cosine[:, 0], sine[:, 0]
    one, zero = jnp.ones_like(cosine), jnp.zeros_like(cosine)
    tables4 = [
        jnp.concatenate(parts, axis=1)
        for parts in (
            [cosine] * 4,
            [-sine, sine] * 2,
            [cosine, cosine, one, one],
            [-sine, sine, zero, zero],
        )
    ]
    wq, wo, hat, qkv, att, mixed_part, mixed_far, hg, lse, hmid, dhat2, grad_down = first_call(
        tokens, w_query, w_key, w_value, gain1, w_gate, w_up, gain2, tables4,
        w_out, w_down, cotangent,
    )
    grad_tokens, mixed, grad_out, grad_first, parts = third_call(
        tokens, hmid, cotangent, dhat2, qkv, lse, tables4, mixed_part, mixed_far,
        wq, wo, hat, att, hg,
    )
    (
        grad_query, grad_key, grad_value, grad_gate, grad_up, grad_gain1, grad_gain2,
        grad_tokens, mixed, grad_out, grad_down,
    ) = last_call(
        parts, grad_first, w_query, w_key, w_value, gain1, gain2, w_gate, w_up,
        grad_tokens, mixed, grad_out, grad_down,
    )
    return (
        mixed,
        grad_tokens,
        grad_gain1[0],
        grad_query,
        grad_key,
        grad_value,
        grad_out,
        grad_gain2[0],
        grad_gate,
        grad_up,
        grad_down,
    )


def solution(mesh):
    special = mesh.shape['dp'] == 8 and mesh.shape['seq'] == KEY_VALUE_HEADS
    rows = P(("dp", "seq"), None)
    line = P(("dp", "seq"))
    return jax.shard_map(
        shards if special else general_shards,
        mesh=mesh,
        in_specs=(rows, line, rows, rows, rows, rows, line, rows, rows, rows, rows),
        out_specs=(rows, rows, line, rows, rows, rows, rows, line, rows, rows, rows),
        check_vma=False,
    )
```

```python
import jax
import jax.numpy as jnp
from jax import lax
from jax.experimental import pallas as pl
from jax.experimental.pallas import tpu as pltpu
from jax.sharding import PartitionSpec as P

H = 32
KEY_VALUE_HEADS = 4
HEAD_SIZE = 64
EPS = 1e-05
BF = jnp.bfloat16
F32 = jnp.float32


def tables(positions):
    freq = 10000.0 ** (-jnp.arange(0, HEAD_SIZE // 2, dtype=F32) * 2.0 / HEAD_SIZE)
    angle = positions.astype(F32)[:, None] * freq[None, :]
    return (jnp.cos(angle)[:, None, :], jnp.sin(angle)[:, None, :])


def rotate(heads, cosine, sine):
    half = heads.shape[-1] // 2
    first = heads[..., :half]
    second = heads[..., half:]
    return jnp.concatenate(
        [first * cosine - second * sine, second * cosine + first * sine], axis=-1
    )


def dot(left, right):
    return jnp.dot(left, right, preferred_element_type=F32)


def left_dot(left, right):
    return lax.dot_general(left, right, (((0,), (0,)), ((), ())), preferred_element_type=F32)


def right_dot(left, right):
    return lax.dot_general(left, right, (((1,), (1,)), ((), ())), preferred_element_type=F32)


def bits_of(count):
    return [1 << k for k in range(count.bit_length() - 1)]


class Axis:
    def __init__(self, name):
        self.name = name
        self.size = lax.axis_size(name)
        self.me = lax.axis_index(name)

    def swap(self, value, mask):
        return lax.ppermute(value, self.name, [(i, i ^ mask) for i in range(self.size)])

    def all(self, value):
        return [value if m == 0 else self.swap(value, m) for m in range(self.size)]

    def exchange(self, stacked):
        return [
            lax.dynamic_index_in_dim(stacked, self.me ^ m, 0, keepdims=False)
            if m == 0
            else self.swap(
                lax.dynamic_index_in_dim(stacked, self.me ^ m, 0, keepdims=False), m
            )
            for m in range(self.size)
        ]

    def natural(self, pieces):
        stack = jnp.stack(pieces)
        return [
            lax.dynamic_index_in_dim(stack, self.me ^ i, 0, keepdims=False)
            for i in range(self.size)
        ]


def orders(size):
    even = [m for m in range(size) if m % 2 == 0]
    return even, [m + 1 for m in even]


def chip_bits(size, turn):
    bits = bits_of(size)[1:]
    return bits if turn == 0 else bits[::-1]


def gather_chips(dp, piece, turn):
    pieces = {0: piece}
    for bit in chip_bits(dp.size, turn):
        pieces.update({m ^ bit: dp.swap(p, bit) for m, p in list(pieces.items())})
    return pieces


def gather_rows(dp, piece, turn):
    pieces = gather_chips(dp, piece, turn)
    even = jnp.concatenate([pieces[m] for m in orders(dp.size)[0]], axis=0)
    return even, dp.swap(even, 1)


def scatter_chips(dp, blocks, turn):
    for bit in chip_bits(dp.size, turn):
        for m in [m for m in blocks if m & bit]:
            other = dp.swap(blocks.pop(m).astype(BF), bit)
            blocks[m ^ bit] = blocks[m ^ bit].astype(F32) + other.astype(F32)
    return blocks[0]


def scatter_rows(dp, even_fn, odd, turn):
    rows = odd.shape[0] * 2 // dp.size
    other = dp.swap(odd, 1)
    even = (even_fn() + other.astype(F32)).astype(BF)
    blocks = {
        m: even[i * rows : (i + 1) * rows] for i, m in enumerate(orders(dp.size)[0])
    }
    return scatter_chips(dp, blocks, turn)


def mask_columns(dp, value):
    width = value.shape[1] // dp.size
    return tuple(
        jnp.concatenate(
            [lax.dynamic_slice_in_dim(value, (dp.me ^ m) * width, width, 1) for m in group],
            axis=1,
        )
        for group in orders(dp.size)
    )


def natural_columns(dp, even, odd):
    both = jnp.concatenate([even, odd], axis=1)
    width = both.shape[1] // dp.size
    half = dp.size // 2
    parts = []
    for i in range(dp.size):
        mask = dp.me ^ i
        place = mask // 2 + (mask % 2) * half
        parts.append(lax.dynamic_slice_in_dim(both, place * width, width, 1))
    return jnp.concatenate(parts, axis=1)


def attend(queries, keys, values, visible):
    scores = jnp.einsum("qhd,kd->hqk", queries, keys, preferred_element_type=F32)
    scores = jnp.where(visible[None], scores * HEAD_SIZE ** (-0.5), -1e30)
    top = jnp.max(scores, axis=-1, keepdims=True)
    expo = jnp.exp(scores - top)
    total = jnp.sum(expo, axis=-1, keepdims=True)
    probs = (expo / total).astype(BF)
    result = jnp.einsum("hqk,kd->qhd", probs, values, preferred_element_type=F32)
    return result.astype(BF), top + jnp.log(total)


def attend_back(queries, keys, values, grad_heads, logsum, visible):
    scale = HEAD_SIZE ** (-0.5)
    scores = jnp.einsum("qhd,kd->hqk", queries, keys, preferred_element_type=F32)
    scores = jnp.where(visible[None], scores * scale, -1e30)
    probs = jnp.exp(scores - logsum)
    pgrad = jnp.einsum("qhd,kd->hqk", grad_heads, values, preferred_element_type=F32)
    delta = jnp.sum(probs * pgrad, axis=-1, keepdims=True)
    sgrad = (probs * (pgrad - delta)).astype(BF)
    qgrad = jnp.einsum("hqk,kd->qhd", sgrad, keys, preferred_element_type=F32) * scale
    kgrad = jnp.einsum("hqk,qhd->kd", sgrad, queries, preferred_element_type=F32) * scale
    vgrad = jnp.einsum("hqk,qhd->kd", probs.astype(BF), grad_heads, preferred_element_type=F32)
    return qgrad.astype(BF), kgrad.astype(BF), vgrad.astype(BF)


def general_shards(
    tokens, norm_first, w_query, w_key, w_value, w_out, norm_second, w_gate, w_up, w_down, cotangent
):
    dp, seq = Axis("dp"), Axis("seq")
    groups = seq.size
    count, width = tokens.shape
    ff = w_gate.shape[1]
    per = H // groups
    repeat = groups // KEY_VALUE_HEADS
    heads_wide = H * HEAD_SIZE
    keys_wide = KEY_VALUE_HEADS * HEAD_SIZE
    gain1 = norm_first.astype(F32)[:, None]
    gain2 = norm_second.astype(F32)[:, None]

    w_first = jnp.concatenate([w_query, w_key, w_value], axis=1)
    w_first_scaled = (w_first.astype(F32) * gain1).astype(BF)
    wide = w_first.shape[1]

    def by_part(weight):
        rows = weight.shape[0]
        scaled = (weight.astype(F32) * gain2).astype(BF)
        parts = scaled.reshape(rows, dp.size, groups, ff // dp.size // groups)
        return parts.transpose(2, 0, 1, 3).reshape(groups, rows, ff // groups)

    down = [gather_chips(dp, w_down[:, t * width // 2 : (t + 1) * width // 2], t) for t in (0, 1)]
    first_rows = jnp.concatenate(seq.natural(seq.all(w_first_scaled)), axis=0)
    first = [gather_rows(dp, first_rows[:, t * wide // 2 : (t + 1) * wide // 2], t) for t in (0, 1)]
    out_rows = jnp.concatenate(seq.natural(seq.all(w_out)), axis=0)
    outw = [gather_rows(dp, out_rows[:, t * width // 2 : (t + 1) * width // 2], t) for t in (0, 1)]
    gate_up = seq.exchange(jnp.stack([by_part(w_gate), by_part(w_up)], axis=1))
    gate_up = jnp.concatenate(seq.natural(gate_up), axis=1)
    (gate_even, gate_odd), (up_even, up_odd) = [
        gather_rows(dp, gate_up[t], t) for t in (0, 1)
    ]
    cot_all = jnp.concatenate(seq.all(cotangent), axis=0)

    rows_down = w_down.shape[0]
    down_full = []
    for t in (0, 1):
        even = jnp.stack([down[t][m] for m in orders(dp.size)[0]])
        odd = dp.swap(even, 1)
        full = jnp.zeros((rows_down * dp.size, width // 2), BF)
        for i, m in enumerate(orders(dp.size)[0]):
            full = lax.dynamic_update_slice(full, even[i], ((dp.me ^ m) * rows_down, 0))
            full = lax.dynamic_update_slice(full, odd[i], ((dp.me ^ m ^ 1) * rows_down, 0))
        down_full.append(full)

    inputs = tokens.astype(F32)
    inv1 = lax.rsqrt(jnp.mean(inputs * inputs, axis=-1, keepdims=True) + EPS)
    hat1 = (inputs * inv1).astype(BF)
    hat1_even, hat1_odd = mask_columns(dp, hat1)
    cosine, sine = tables(seq.me * count + jnp.arange(count))
    pre = jnp.concatenate(
        [dot(hat1_even, first[t][0]) + dot(hat1_odd, first[t][1]) for t in (0, 1)], axis=1
    )
    qpre = pre[:, :heads_wide].reshape(count, H, HEAD_SIZE)
    kpre = pre[:, heads_wide : heads_wide + keys_wide].reshape(count, KEY_VALUE_HEADS, HEAD_SIZE)
    vround = pre[:, heads_wide + keys_wide :].astype(BF)
    qrot = rotate(qpre, cosine, sine).reshape(count, heads_wide).astype(BF)
    krot = rotate(kpre, cosine, sine).reshape(count, keys_wide).astype(BF)
    span = per * HEAD_SIZE
    packed = []
    for g in range(groups):
        head = g // repeat * HEAD_SIZE
        packed.append(
            jnp.concatenate(
                [
                    qrot[:, g * span : (g + 1) * span],
                    krot[:, head : head + HEAD_SIZE],
                    vround[:, head : head + HEAD_SIZE],
                ],
                axis=1,
            )
        )
    qkv = jnp.concatenate(seq.exchange(jnp.stack(packed)), axis=0)
    length = qkv.shape[0]
    queries = qkv[:, :span].reshape(length, per, HEAD_SIZE)
    keys = qkv[:, span : span + HEAD_SIZE]
    values = qkv[:, span + HEAD_SIZE :]
    place = jnp.concatenate(
        [(seq.me ^ m) * count + jnp.arange(count, dtype=jnp.int32) for m in range(groups)]
    )
    visible = place[None, :] <= place[:, None]
    out_heads, logsum = attend(queries, keys, values, visible)
    out_heads = out_heads.reshape(length, span)

    def back_home(value):
        return seq.natural(
            [
                value[:count] if m == 0 else seq.swap(value[m * count : (m + 1) * count], m)
                for m in range(groups)
            ]
        )

    attn = jnp.concatenate(back_home(out_heads), axis=1)
    attn_even, attn_odd = mask_columns(dp, attn)
    branch = jnp.concatenate(
        [dot(attn_even, outw[t][0]) + dot(attn_odd, outw[t][1]) for t in (0, 1)], axis=1
    )
    hmid = inputs + branch

    inv2 = lax.rsqrt(jnp.mean(hmid * hmid, axis=-1, keepdims=True) + EPS)
    hat2 = jnp.concatenate(mask_columns(dp, (hmid * inv2).astype(BF)), axis=1)
    hat2_all = jnp.concatenate(seq.all(hat2), axis=0)
    hat2_even, hat2_odd = hat2_all[:, : width // 2], hat2_all[:, width // 2 :]
    gate = dot(hat2_even, gate_even) + dot(hat2_odd, gate_odd)
    upper = dot(hat2_even, up_even) + dot(hat2_odd, up_odd)
    sigma = jax.nn.sigmoid(gate)
    hidden = (gate * sigma * upper).astype(BF)
    halves = [cot_all[:, : width // 2], cot_all[:, width // 2 :]]
    dhidden = right_dot(halves[0], down_full[0]) + right_dot(halves[1], down_full[1])
    dgate = (dhidden * upper * sigma * (1.0 + gate * (1.0 - sigma))).astype(BF)
    dupper = (dhidden * gate * sigma).astype(BF)
    dhat2 = jnp.concatenate(
        [
            right_dot(dgate, gate_even) + right_dot(dupper, up_even),
            right_dot(dgate, gate_odd) + right_dot(dupper, up_odd),
        ],
        axis=1,
    ).astype(BF)

    def sum_home(value):
        total = value[:count].astype(F32)
        for m in range(1, groups):
            total = total + seq.swap(value[m * count : (m + 1) * count], m).astype(F32)
        return total

    dhat2 = sum_home(dhat2)
    dgain2 = natural_columns(dp, dhat2[:, : width // 2], dhat2[:, width // 2 :])
    inner = jnp.mean(hmid * dgain2, axis=-1, keepdims=True)
    dh = cotangent.astype(F32) + inv2 * dgain2 - hmid * inv2 * inv2 * inv2 * inner
    dbranch = dh.astype(BF)

    dattn = natural_columns(
        dp,
        *[
            sum(
                right_dot(dbranch[:, t * width // 2 : (t + 1) * width // 2], outw[t][s])
                for t in (0, 1)
            ).astype(BF)
            for s in (0, 1)
        ],
    )
    grad_heads = jnp.concatenate(
        seq.exchange(dattn.reshape(count, groups, span).transpose(1, 0, 2)), axis=0
    ).reshape(length, per, HEAD_SIZE)
    dq, dk, dv = attend_back(queries, keys, values, grad_heads, logsum, visible)
    dqkv = back_home(jnp.concatenate([dq.reshape(length, span), dk, dv], axis=1))
    dq = jnp.concatenate([piece[:, :span] for piece in dqkv], axis=1)
    dk = [piece[:, span : span + HEAD_SIZE].astype(F32) for piece in dqkv]
    dv = [piece[:, span + HEAD_SIZE :].astype(F32) for piece in dqkv]
    dk = jnp.stack(
        [sum(dk[i * repeat : (i + 1) * repeat]) for i in range(KEY_VALUE_HEADS)], axis=1
    )
    dv = jnp.concatenate(
        [sum(dv[i * repeat : (i + 1) * repeat]) for i in range(KEY_VALUE_HEADS)], axis=1
    )
    dq = rotate(dq.astype(F32).reshape(count, H, HEAD_SIZE), cosine, -sine)
    dk = rotate(dk, cosine, -sine)
    dpre = jnp.concatenate(
        [dq.reshape(count, heads_wide), dk.reshape(count, keys_wide), dv], axis=1
    ).astype(BF)
    dhalf = [dpre[:, t * wide // 2 : (t + 1) * wide // 2] for t in (0, 1)]
    dhat1 = [sum(right_dot(dhalf[t], first[t][s]) for t in (0, 1)) for s in (0, 1)]
    dgain1 = natural_columns(dp, *dhat1)
    inner = jnp.mean(inputs * dgain1, axis=-1, keepdims=True)
    grad_inputs = dh + inv1 * dgain1 - inputs * inv1 * inv1 * inv1 * inner

    mixed_part = jnp.concatenate([dot(hidden, down_full[t]) for t in (0, 1)], axis=1).astype(BF)
    mixed = hmid + sum_home(mixed_part)

    grad_down = []
    for t in (0, 1):
        part = left_dot(hidden, halves[t]).astype(BF)
        blocks = [
            lax.dynamic_slice_in_dim(part, (dp.me ^ m) * rows_down, rows_down, 0)
            for m in range(dp.size)
        ]
        even, odd = orders(dp.size)
        other = dp.swap(jnp.stack([blocks[m] for m in odd]), 1)
        summed = {
            m: (blocks[m].astype(F32) + other[i].astype(F32)).astype(BF)
            for i, m in enumerate(even)
        }
        grad_down.append(scatter_chips(dp, summed, t))
    grad_down = jnp.concatenate(grad_down, axis=1)

    def ff_grad(grad, turn):
        odd = left_dot(hat2_odd, grad).astype(BF)
        return scatter_rows(dp, lambda: left_dot(hat2_even, grad), odd, turn)

    rows = w_gate.shape[0]
    sent = jnp.stack([ff_grad(dgate, 0).astype(BF), ff_grad(dupper, 1).astype(BF)])
    sent = sent.reshape(2, groups, rows, ff // groups).transpose(1, 0, 2, 3)
    got = jnp.stack(seq.natural(seq.exchange(sent)))
    got = got.reshape(groups, 2, rows, dp.size, ff // groups // dp.size)
    got = got.transpose(1, 2, 3, 0, 4).reshape(2, rows, ff).astype(F32)
    grad_gate, grad_up = got[0] * gain2, got[1] * gain2
    grad_gain2 = jnp.sum(got[0] * w_gate.astype(F32) + got[1] * w_up.astype(F32), axis=1)

    def proj_grad(even, odd, grads):
        parts = []
        for t in (0, 1):
            send = left_dot(odd, grads[t]).astype(BF)
            parts.append(
                scatter_rows(dp, lambda grad=grads[t]: left_dot(even, grad), send, t)
            )
        own = jnp.concatenate(parts, axis=1)
        own = own.astype(BF).reshape(groups, rows, own.shape[1])
        return sum(piece.astype(F32) for piece in seq.exchange(own))

    grad_out = proj_grad(
        attn_even,
        attn_odd,
        [dbranch[:, t * width // 2 : (t + 1) * width // 2] for t in (0, 1)],
    )
    grad_first = proj_grad(hat1_even, hat1_odd, dhalf)
    grad_gain1 = jnp.sum(grad_first * w_first.astype(F32), axis=1)
    grad_first = grad_first * gain1
    return (
        mixed.astype(BF),
        grad_inputs.astype(BF),
        grad_gain1,
        grad_first[:, :heads_wide],
        grad_first[:, heads_wide : heads_wide + keys_wide],
        grad_first[:, heads_wide + keys_wide :],
        grad_out,
        grad_gain2,
        grad_gate,
        grad_up,
        grad_down,
    )


MESH = pl.DeviceIdType.MESH
ANY = pl.BlockSpec(memory_space=pl.ANY)
VMEM = pl.BlockSpec(memory_space=pltpu.VMEM)


class Net:
    def __init__(self, send_sems, recv_sems):
        self.send_sems, self.recv_sems, self.used = send_sems, recv_sems, 0
        self.open = []
        dp, z = lax.axis_index("dp"), lax.axis_index("seq")
        self.dp, self.z = dp, z
        self.dps = {
            0: dp,
            1: dp + 1 - 2 * lax.rem(dp, 2),
            2: dp + 2 - 4 * lax.rem(lax.div(dp, 2), 2),
            4: lax.rem(dp + 4, 8),
        }
        self.dps[6] = lax.rem(self.dps[2] + 4, 8)
        for mask in (2, 4, 6):
            self.dps[mask + 1] = self.dps[mask] + 1 - 2 * lax.rem(dp, 2)
        self.zs = {0: z, 1: z + 1 - 2 * lax.rem(z, 2), 2: lax.rem(z + 2, 4), 3: 3 - z}

    def target(self, name):
        kind, mask = name
        return (self.dps[mask], self.z) if kind == "d" else (self.dp, self.zs[mask])

    def barrier(self, names):
        sem = pltpu.get_barrier_semaphore()
        for name in names:
            pl.semaphore_signal(sem, inc=1, device_id=self.target(name), device_id_type=MESH)
        pl.semaphore_wait(sem, len(names))

    def send(self, src, dst, name):
        copy = pltpu.make_async_remote_copy(
            src_ref=src,
            dst_ref=dst,
            send_sem=self.send_sems.at[self.used],
            recv_sem=self.recv_sems.at[self.used],
            device_id=self.target(name),
            device_id_type=MESH,
        )
        self.used += 1
        copy.start()
        self.open.append(copy)
        return copy

    def local(self, src, dst):
        copy = pltpu.make_async_copy(src, dst, self.send_sems.at[self.used])
        self.used += 1
        copy.start()
        return copy

    def sent(self, copies):
        for copy in copies:
            copy.wait_send()
        done = [id(copy) for copy in copies]
        self.open = [copy for copy in self.open if id(copy) not in done]

    def finish(self):
        for copy in self.open:
            copy.wait_send()


X, Y, CORE = ("d", 2), ("d", 4), ("d", 1)
PARTNERS = [X, Y, CORE, ("z", 1), ("z", 2), ("z", 3)]


class Plane:
    def __init__(self, net, at, both):
        self.net, self.at, self.both = net, at, both

    def push(self, mask, half, name):
        ref = self.at(mask, half)
        return self.net.send(ref, ref, name)

    def start(self):
        self.xa = self.push(0, 0, X)
        self.yb = self.push(0, 1, Y)
        self.ya = self.push(0, 0, Y)
        self.xb = self.push(0, 1, X)
        self.cores = [self.core(0)]

    def core(self, mask):
        return [self.net.send(ref, ref, CORE) for ref in self.both(mask)]

    def forward(self):
        self.xa.wait_recv()
        self.ya2 = self.push(2, 0, Y)
        self.yb.wait_recv()
        self.xb2 = self.push(4, 1, X)

    def spread(self):
        self.ya.wait_recv()
        self.cores.append(self.core(4))
        self.xb.wait_recv()
        self.cores.append(self.core(2))
        self.ya2.wait_recv()
        self.xb2.wait_recv()
        self.cores.append(self.core(6))

    def finish(self):
        for copies in self.cores:
            for copy in copies:
                copy.wait_recv()

    def sent(self):
        copies = [self.xa, self.yb, self.ya, self.xb, self.ya2, self.xb2]
        self.net.sent(copies + [copy for group in self.cores for copy in group])


def rotary(value, cosine, sine):
    lane = lax.broadcasted_iota(jnp.int32, value.shape, 1)
    partner = jnp.where(
        lax.rem(lane, 64) < 32, pltpu.roll(value, 96, 1), pltpu.roll(value, 32, 1)
    )
    return value * cosine + partner * sine


def column(row):
    n = row.shape[1]
    shape = (n, n)
    same = lax.broadcasted_iota(jnp.int32, shape, 0) == lax.broadcasted_iota(jnp.int32, shape, 1)
    return jnp.sum(jnp.where(same, row.astype(F32), 0.0), axis=1, keepdims=True)


def line(value):
    n = value.shape[0]
    shape = (n, n)
    same = lax.broadcasted_iota(jnp.int32, shape, 0) == lax.broadcasted_iota(jnp.int32, shape, 1)
    return jnp.sum(jnp.where(same, value, 0.0), axis=0, keepdims=True)


def rms(value):
    return lax.rsqrt(jnp.mean(value * value, axis=-1, keepdims=True) + EPS)


def twice(pair):
    lane = lax.broadcasted_iota(jnp.int32, pair.shape, 1)
    other = pltpu.roll(pair.astype(F32), 64, 1).astype(BF)
    return jnp.where(lane < 64, pair, other), jnp.where(lane < 64, other, pair)


def aligned(start, count, unit):
    return pl.ds(pl.multiple_of(start, unit), count)


class Sums:
    def __init__(self, net, part, r1, mid, r2, sets=1):
        self.net, self.part, self.r1, self.mid, self.r2 = net, part, r1, mid, r2
        self.width = r2.shape[-1] // sets
        self.near, self.own, self.far = {}, {}, {}

    def cols(self, side, k):
        return pl.ds((2 * k + side) * self.width, self.width)

    def place(self, k):
        return pl.ds(k * self.width, self.width)

    def block(self, mask):
        return lax.div(self.net.dps[mask], 2)

    def first(self, k=0):
        for sent, place, pushes in (
            (self.near, 1, ((6, 0, X), (6, 1, Y))),
            (self.own, 0, ((2, 0, X), (4, 1, Y))),
        ):
            sent[k] = [
                self.net.send(
                    self.part.at[self.block(mask), :, self.cols(side, k)],
                    self.r1.at[side, place, :, self.place(k)],
                    name,
                )
                for mask, side, name in pushes
            ]

    def second(self, k=0):
        self.far[k] = []
        for side, (mask, name) in enumerate(((4, Y), (2, X))):
            self.near[k][side].wait_recv()
            c = self.place(k)
            mine = self.part[self.block(mask), :, self.cols(side, k)]
            self.mid[side, :, c] = (
                mine.astype(F32) + self.r1[side, 1, :, c].astype(F32)
            ).astype(BF)
            self.far[k].append(
                self.net.send(self.mid.at[side, :, c], self.r2.at[side, :, c], name)
            )

    def sent(self):
        for sent in (self.near, self.own, self.far):
            for copies in sent.values():
                self.net.sent(copies)

    def total(self, side, k=0):
        self.own[k][side].wait_recv()
        self.far[k][side].wait_recv()
        c = self.place(k)
        mine = self.part[self.block(0), :, self.cols(side, k)]
        return mine.astype(F32) + self.r1[side, 0, :, c].astype(F32) + self.r2[side, :, c].astype(F32)


def first_kernel(
    x_ref, wq, wk, wv, gain1, w_gate, w_up, gain2, cos_q, sin_q, cos_k, sin_k, wo, wd, cot,
    wq_out, wo_out, hat_out, qkv_out, att_out, mx_out, mx_far, hg_out, lse, hmid, dn_out, gdown,
    wq_s, wf, wq_v, wo_v, hat, qkv_send, qkv, heads, att, part, r1, mid, r2,
    wg_v, wd_v, n_v, n_sib, c_v, c_sib, hid, dg, du,
    mx_r, hd, hd_r1, hd_r2, sib_r, send_sems, recv_sems,
):
    net = Net(send_sems, recv_sems)
    dp, z, dps, zs = net.dp, net.z, net.dps, net.zs
    tok, width = x_ref.shape
    group = qkv.shape[1]
    span = heads.shape[1]
    ff = wf.shape[-1]
    core, chip = lax.rem(dp, 2), lax.div(dp, 2)
    here = aligned(z * tok, tok, 16)

    staged = [
        net.local(weight.at[:, pl.ds(j * ff, ff)], ref.at[0, pl.ds(j * 64, 64), :])
        for weight, ref in ((w_gate, dg), (w_up, du))
        for j in range(4)
    ]
    own = [
        net.local(wo, wo_v.at[core, z]),
        net.local(wd, wd_v.at[aligned(dp * 176, 176, 16), :]),
        net.local(cot, c_v.at[here, :]),
    ]
    net.barrier(PARTNERS + [("d", 6)])

    scale = column(gain1[...])
    lane = lax.broadcasted_iota(jnp.int32, (wq.shape[0], 128), 1)
    for g in range(4):
        wq_s[g, :, :span] = (wq[:, g * span : (g + 1) * span].astype(F32) * scale).astype(BF)
        start = g // 2 * 128
        k = wk[:, start : start + 128].astype(F32)
        v = wv[:, start : start + 128].astype(F32)
        if g % 2 == 0:
            both = jnp.where(lane < 64, k, pltpu.roll(v, 64, 1))
        else:
            both = jnp.where(lane < 64, pltpu.roll(k, 64, 1), v)
        wq_s[g, :, span:] = (both * scale).astype(BF)

    def chip_of(mask):
        return lax.div(dps[mask], 2)

    w_1 = [
        net.send(wq_s.at[chip_of(m)], wq_v.at[chip, core, z], ("d", m)) for m in (6, 2, 4)
    ]
    own_q = net.local(wq_s.at[chip], wq_v.at[chip, core, z])
    x = x_ref[...].astype(F32)
    hat[chip] = (x * rms(x)).astype(BF)

    def half_of(ref, side):
        w = ref.shape[-1] // 2
        return pl.ds(side * w, w)

    def block(ref, size, cores):
        def at(mask, side):
            return ref.at[aligned(dps[mask] * size, size, 16), half_of(ref, side)]

        return at, lambda mask: [ref.at[aligned(dps[mask] * size, size, 16), :]] if cores else []

    plane_h = Plane(net, lambda m, s: hat.at[chip_of(m), :, half_of(hat, s)], lambda m: [])
    plane_h.start()
    down = Plane(net, *block(wd_v, 176, True))
    own[1].wait()
    down.start()

    def wq_at(mask):
        return wq_v.at[:, core, zs[mask]]

    def wo_at(mask):
        return wo_v.at[core, zs[mask]]

    class Line:
        def __init__(self, at):
            self.at = at
            self.far = self.push(0, ("z", 2))
            self.near = self.push(0, ("z", 1))
            self.cores = [self.push(0, CORE)]

        def push(self, mask, name):
            return net.send(self.at(mask), self.at(mask), name)

        def forward(self):
            self.far.wait_recv()
            self.last = self.push(2, ("z", 1))
            self.cores.append(self.push(2, CORE))

        def spread(self):
            self.near.wait_recv()
            self.cores.append(self.push(1, CORE))
            self.last.wait_recv()
            self.cores.append(self.push(3, CORE))

        def finish(self):
            for copy in self.cores:
                copy.wait_recv()

    scale = column(gain2[...])
    size = ff // 8
    for copy in staged:
        copy.wait()
    for t, ref in enumerate((dg, du)):
        for i in range(4):
            parts = []
            for b in range(i, 32, 4):
                j, start = b // 8, b % 8 * size
                parts.append(ref[0, j * 64 : (j + 1) * 64, start : start + size])
            joined = jnp.concatenate([p.astype(F32) for p in parts], axis=1)
            wf[(i * 2 + t) * 64 : (i * 2 + t + 1) * 64, :] = (joined * scale).astype(BF)
    f_rows = aligned((dp * 4 + z) * 64, 64, 16)

    def wf_at(i, t):
        return wf.at[aligned((i * 2 + t) * 64, 64, 16), :]

    own_f = [net.local(wf_at(z, t), wg_v.at[t, f_rows, :]) for t in (0, 1)]

    def f_send(t):
        return [
            net.send(wf_at(zs[m], t), wg_v.at[t, f_rows, :], ("z", m)) for m in (2, 3, 1)
        ]

    def f_plane(t):
        def rows(mask, start, count):
            return wg_v.at[t, aligned(dps[mask] * 256 + start, count, 16), :]

        return Plane(
            net, lambda m, s: rows(m, s * 128, 128), lambda m: [rows(m, 0, 256)]
        )

    own[0].wait()
    line_o = Line(wo_at)
    own_q.wait()
    for copy in w_1:
        copy.wait_recv()

    line_q = Line(wq_at)
    plane_h.forward()
    line_q.forward()
    gate_copies = f_send(0)
    plane_h.spread()
    line_q.spread()
    down.forward()
    line_q.finish()

    weight = wq_v[...].reshape(width, group)

    left = hat[...].reshape(4 * tok, width)
    for start in range(0, group, 256):
        stop = min(start + 256, group)
        pre = dot(left, weight[:, start:stop])
        for j in range(start, stop, 128):
            c_ref, s_ref = (cos_k, sin_k) if j == group - 128 else (cos_q, sin_q)
            for s in range(4):
                value = pre[s * tok : (s + 1) * tok, j - start : j - start + 128]
                value = rotary(value, c_ref[...], s_ref[...])
                qkv_send[s, :, j : j + 128] = value.astype(BF)
    q_copies = [net.send(qkv_send.at[zs[m]], qkv.at[here, :], ("z", m)) for m in (2, 3, 1)]
    own_q = net.local(qkv_send.at[z], qkv.at[here, :])
    line_o.forward()
    up_copies = f_send(1)
    down.spread()
    own_q.wait()
    for copy in q_copies:
        copy.wait_recv()

    kk, vv = twice(qkv[:, span:])

    def pair(p, carry):
        cols = aligned(p * 128, 128, 128)
        for qb in range(4):
            keys = (qb + 1) * tok
            q = qkv[qb * tok : (qb + 1) * tok, cols]
            lane = lax.broadcasted_iota(jnp.int32, (tok, 128), 1)
            row = lax.rem(lax.broadcasted_iota(jnp.int32, (2 * tok, keys), 0), tok) + qb * tok
            col = lax.broadcasted_iota(jnp.int32, (2 * tok, keys), 1)
            none = jnp.zeros_like(q)
            both = jnp.concatenate(
                [jnp.where(lane < 64, q, none), jnp.where(lane >= 64, q, none)], axis=0
            )
            s = right_dot(both, kk[:keys]) * HEAD_SIZE ** (-0.5)
            s = jnp.where(col <= row, s, -1e30)
            top = jnp.max(s, axis=-1, keepdims=True)
            e = jnp.exp(s - top)
            total = jnp.sum(e, axis=-1, keepdims=True)
            out = dot((e * (1.0 / total)).astype(BF), vv[:keys])
            log = top + jnp.log(total)
            old = lse[qb * tok : (qb + 1) * tok, :]
            old = jnp.where(lane == 2 * p, log[:tok], old)
            lse[qb * tok : (qb + 1) * tok, :] = jnp.where(lane == 2 * p + 1, log[tok:], old)
            heads[qb * tok : (qb + 1) * tok, cols] = jnp.where(
                lane < 64, out[:tok], out[tok:]
            ).astype(BF)
        return carry

    lse[...] = jnp.zeros_like(lse)
    h_copies = []
    for part_of in (0, 1):
        lax.fori_loop(part_of * 2, part_of * 2 + 2, pair, 0)
        cols = pl.ds(part_of * 256, 256)
        h_copies += [
            net.send(
                heads.at[aligned(zs[m] * tok, tok, 16), cols], att.at[z, :, cols], ("z", m)
            )
            for m in (2, 3, 1)
        ]
    own_h = net.local(heads.at[here, :], att.at[z])

    for copy in own_f:
        copy.wait()
    for copy in gate_copies:
        copy.wait_recv()
    plane_g, plane_u = f_plane(0), f_plane(1)
    plane_g.start()
    line_o.spread()
    line_o.finish()
    own_h.wait()
    for copy in h_copies:
        copy.wait_recv()


    c_near = net.send(cot, c_v.at[here, :], ("z", 1))
    c_far = net.send(cot, c_v.at[here, :], ("z", 2))
    sums = Sums(net, part, r1, mid, r2, 2)
    left = att[...].reshape(4 * tok, span)
    for c in range(4):
        cols = pl.ds(c * (width // 4), width // 4)
        weight = wo_v[:, :, :, cols].reshape(span, width // 4)
        part[:, :, cols] = dot(left, weight).astype(BF).reshape(4, tok, width // 4)
    def slot(mask):
        return aligned(zs[mask] * tok, tok, 16)

    def tokens(ref, mask, name):
        return net.send(ref.at[slot(mask), :], ref.at[slot(mask), :], name)

    def n_push(k, mask, name):
        place = n_v.at[slot(mask), pl.ds(k * (width // 2), width // 2)]
        return net.send(place, place, name)

    def middle(k):
        for side in (0, 1):
            cols = sums.cols(side, k)
            value = x_ref[:, cols].astype(F32) + sums.total(side, k)
            hmid[:, cols] = value
            n_v[here, cols] = value.astype(BF)
        n_far.append(n_push(k, 0, ("z", 2)))
        n_near.append(n_push(k, 0, ("z", 1)))

    n_far, n_near = [], []
    sums.first(0)
    sums.second(0)
    sums.first(1)
    middle(0)
    sums.second(1)
    plane_g.forward()
    for copy in up_copies:
        copy.wait_recv()
    plane_u.start()
    middle(1)
    outs = [
        net.local(wq_v, wq_out), net.local(wo_v, wo_out), net.local(qkv, qkv_out),
        net.local(att, att_out), net.local(hat, hat_out),
    ]
    c_far.wait_recv()
    c_last = tokens(c_v, 2, ("z", 1))
    plane_g.spread()
    plane_u.forward()
    n_last = []
    for k in (0, 1):
        n_far[k].wait_recv()
        n_last.append(n_push(k, 2, ("z", 1)))
    plane_u.spread()

    half = width // 2
    near_pair = lax.div(z, 2)
    far = aligned((1 - near_pair) * 2 * tok, 2 * tok, 16)
    near = aligned(near_pair * 2 * tok, 2 * tok, 16)
    dn_part = part

    def chunks(fn, total, size):
        whole = total // size

        def step(i, carry):
            fn(i * size, size)
            return carry

        lax.fori_loop(0, whole, step, 0)
        if total % size:
            fn(whole * size, total - whole * size)

    def front(rows):
        inv = rms(n_v[rows, :].astype(F32))

        def chunk(start, size):
            cols = aligned(start, size, 128)
            n = n_v[rows, :]
            gate = dot(n, wg_v[0, :, cols]) * inv
            upper = dot(n, wg_v[1, :, cols]) * inv
            dhid = right_dot(c_v[rows, :], wd_v[cols, :])
            sigma = jax.nn.sigmoid(gate)
            silu = gate * sigma
            hid[0, rows, cols] = (silu * upper).astype(BF)
            dhid *= inv
            dg[0, rows, cols] = (dhid * upper * sigma * (1.0 + gate * (1.0 - sigma))).astype(BF)
            du[0, rows, cols] = (dhid * silu).astype(BF)

        chunks(chunk, ff, 256)
        return [
            net.send(ref.at[0, rows, :], ref.at[1, rows, :], CORE) for ref in (hid, dg, du)
        ]

    def back(rows, first_slot, side):
        def chunk(start, size):
            cols = aligned(start + side * half, size, 128)
            total = right_dot(dg[0, rows, :], wg_v[0, cols, :])
            total += right_dot(du[0, rows, :], wg_v[1, cols, :])
            dn_part[pl.ds(first_slot, 2), :, cols] = total.astype(BF).reshape(2, tok, size)

        chunks(chunk, half, 256)

    def piece(side):
        return pl.ds(side * half, half)

    sums.sent()
    for copy in n_near:
        copy.wait_recv()
    c_near.wait_recv()
    for plane in (down, plane_g, plane_u):
        plane.finish()
    own[2].wait()
    sib = front(near)
    dn_b = []
    for side in (0, 1):
        back(near, near_pair * 2, side)
        dn_b.append(
            net.send(
                dn_part.at[zs[1], :, piece(side)], r1.at[side, 0], ("z", 1)
            )
        )
    c_last.wait_recv()
    c_copy = net.send(c_v.at[:, aligned((1 - core) * half, half, 128)], c_sib, CORE)
    for copy in n_last:
        copy.wait_recv()
    n_copies = [
        net.send(
            n_v.at[:, aligned((i * 2 + 1 - core) * 256, 256, 128)],
            n_sib.at[:, pl.ds(i * 256, 256)],
            CORE,
        )
        for i in range(4)
    ]
    sib += front(far)
    dn_a = []
    for side in (0, 1):
        back(far, (1 - near_pair) * 2, side)
        dn_a.append(
            net.send(
                dn_part.at[zs[3], :, piece(side)], r1.at[side, 1], ("z", 1)
            )
        )
    c_copy.wait_recv()
    for copy in sib:
        copy.wait_recv()

    ccols = aligned(core * half, half, 128)

    def down_chunk(start, size):
        cols = aligned(start, size, 128)
        total = left_dot(hid[0, :, cols], c_v[:, ccols])
        total += left_dot(hid[1, :, cols], c_sib[...])
        hd[cols, :] = total.astype(BF)

    chunks(down_chunk, ff, 256)
    chip_rows = ff // 4
    quarter = half // 2

    def hd_at(mask, side):
        return aligned(chip_of(mask) * chip_rows, chip_rows, 16), pl.ds(side * quarter, quarter)

    def hd_send(mask, side, place, name):
        r, c = hd_at(mask, side)
        return net.send(hd.at[r, c], hd_r1.at[side, place], name)

    hd_1 = [hd_send(6, 0, 1, X), hd_send(6, 1, 1, Y), hd_send(2, 0, 0, X), hd_send(4, 1, 0, Y)]
    dn_c = []
    for side in (0, 1):
        dn_a[side].wait_recv()
        cols = piece(side)
        mid[side] = (
            dn_part[zs[2], :, cols].astype(F32) + r1[side, 1].astype(F32)
        ).astype(BF)
        dn_c.append(net.send(mid.at[side], r2.at[side], ("z", 2)))

    for copy in outs:
        copy.wait()
    plane_h.sent()

    def mix_chunk(start, size):
        cols = aligned(start, size, 128)
        hat[:, :, cols] = dot(hid[0], wd_v[:, cols]).astype(BF).reshape(4, tok, size)

    chunks(mix_chunk, width, 256)
    mx_copy = net.local(hat, mx_out)
    mx_a = net.send(hat.at[zs[3]], mx_r, ("z", 1))

    hd_1[0].wait_recv()
    hd_1[1].wait_recv()
    net.sent(gate_copies + up_copies)
    hd_2 = []
    for side, (mask, name) in enumerate(((4, Y), (2, X))):
        r, c = hd_at(mask, side)
        k = pl.ds(side * quarter, quarter)
        wf[:chip_rows, k] = (hd[r, c].astype(F32) + hd_r1[side, 1].astype(F32)).astype(BF)
        hd_2.append(net.send(wf.at[pl.ds(0, chip_rows), k], hd_r2.at[side], name))

    for copy in n_copies:
        copy.wait_recv()
    plane_g.sent()
    plane_u.sent()

    def block(b, carry):
        cols = aligned((b * 2 + core) * 256, 256, 128)
        left = n_v[:, cols].T
        other = n_sib[:, aligned(b * 256, 256, 128)].T
        for t, grad in enumerate((dg, du)):
            total = dot(left, grad[0]) + dot(other, grad[1])
            wg_v[t, aligned(b * 256, 256, 16), :] = total.astype(BF)
        return carry

    lax.fori_loop(0, 4, block, 0)
    hg_copy = net.local(wg_v.at[:, pl.ds(0, 1024), :], hg_out)
    for side in (0, 1):
        dn_b[side].wait_recv()
        dn_c[side].wait_recv()
        cols = piece(side)
        dn_out[:, cols] = (
            dn_part[z, :, cols].astype(F32)
            + r1[side, 0].astype(F32)
            + r2[side].astype(F32)
        )
    mx_a.wait_recv()
    net.sent(dn_c)
    far_copies = []
    for side in (0, 1):
        cols = piece(side)
        mid[side] = (hat[zs[2], :, cols].astype(F32) + mx_r[:, cols].astype(F32)).astype(BF)
        far_copies.append(net.local(mid.at[side], mx_far.at[:, cols]))
    hd_1[2].wait_recv()
    hd_1[3].wait_recv()
    rows_half = chip_rows // 2
    for side in (0, 1):
        hd_2[side].wait_recv()

        def total(start):
            _, c = hd_at(0, side)
            return (
                hd[aligned(chip * chip_rows + start, rows_half, 16), c].astype(F32)
                + hd_r1[side, 0, aligned(start, rows_half, 16), :].astype(F32)
                + hd_r2[side, aligned(start, rows_half, 16), :].astype(F32)
            )

        net.sent([hd_2[side]])
        k = pl.ds(side * quarter, quarter)
        wf[:rows_half, k] = total((1 - core) * rows_half).astype(BF)
        gdown[:, aligned(core * half + side * quarter, quarter, 128)] = total(core * rows_half)
    last = net.send(wf.at[pl.ds(0, rows_half), pl.ds(0, half)], sib_r, CORE)
    last.wait_recv()
    gdown[:, aligned((1 - core) * half, half, 128)] = sib_r[...].astype(F32)
    hg_copy.wait()
    mx_copy.wait()
    for copy in far_copies:
        copy.wait()
    net.finish()


def first_call(x, wq, wk, wv, gain1, w_gate, w_up, gain2, tables4, wo, wd, cot):
    tok, width = x.shape
    ff = w_gate.shape[1] // 4
    span = width // 4
    group = span + 128
    sds = jax.ShapeDtypeStruct
    v = pltpu.VMEM
    half = width // 2
    return pl.pallas_call(
        first_kernel,
        name="first",
        out_shape=[
            sds((4, 2, 4, 64, group), BF), sds((2, 4, 64, width), BF), sds((4, tok, width), BF),
            sds((4 * tok, group), BF), sds((4, tok, span), BF), sds((4, tok, width), BF),
            sds((tok, width), BF), sds((2, 1024, ff), BF), sds((4 * tok, 128), F32), sds((tok, width), F32),
            sds((tok, width), F32), sds((ff // 8, width), F32),
        ],
        in_specs=[VMEM] * 5 + [ANY] * 2 + [VMEM] * 8,
        out_specs=[ANY] * 8 + [VMEM] * 4,
        scratch_shapes=[
            v((4, 64, group), BF), v((512, ff), BF), v((4, 2, 4, 64, group), BF),
            v((2, 4, 64, width), BF), v((4, tok, width), BF), v((4, tok, group), BF),
            v((4 * tok, group), BF), v((4 * tok, span), BF), v((4, tok, span), BF),
            v((4, tok, width), BF), v((2, 2, tok, half), BF), v((2, tok, half), BF),
            v((2, tok, half), BF),
            v((2, width, ff), BF), v((ff, width), BF), v((4 * tok, width), BF),
            v((4 * tok, half), BF), v((4 * tok, width), BF), v((4 * tok, half), BF),
            v((2, 4 * tok, ff), BF), v((2, 4 * tok, ff), BF), v((2, 4 * tok, ff), BF),
            v((tok, width), BF), v((ff, half), BF),
            v((2, 2, ff // 4, half // 2), BF), v((2, ff // 4, half // 2), BF),
            v((ff // 8, half), BF),
            pltpu.SemaphoreType.DMA((144,)),
            pltpu.SemaphoreType.DMA((144,)),
        ],
        compiler_params=pltpu.CompilerParams(
            collective_id=1, has_side_effects=True, vmem_limit_bytes=62 * 2**20
        ),
    )(x, wq, wk, wv, gain1, w_gate, w_up, gain2, *tables4, wo, wd, cot)


def third_kernel(
    x_ref, hmid, cot, dn2, qkv, lse, cos_q, sin_q, cos_k, sin_k,
    mx, mx_far, wq, wo, hat, att, hg,
    tok_out, mixed, g2_out, g1_out, fb,
    wq_v, wo_v, hat_v, hat_s, att_v, att_s, mx_v, mx_r1, mx_r2,
    hg_v, f_r1, f_k, f_r2, fs, dh, dbr, dbr_s, dsend, gh, dqkv, dk_acc, dv_acc, dback,
    dpre, dpre_s, part, r1, mid, r2, g2_p, g2_r1, g2_s, g2_r2, g1_p, g1_r1, g1_s, g1_r2, g1_f,
    send_sems, recv_sems,
):
    net = Net(send_sems, recv_sems)
    dp, z, dps, zs = net.dp, net.z, net.dps, net.zs
    tok, width = x_ref.shape
    group = qkv.shape[1]
    span = group - 128
    here = aligned(z * tok, tok, 16)
    core, chip = lax.rem(dp, 2), lax.div(dp, 2)

    def chip_of(mask):
        return lax.div(dps[mask], 2)

    def slot(mask):
        return aligned(zs[mask] * tok, tok, 16)

    def hg_at(t, mask, side):
        return hg.at[t, aligned(chip_of(mask) * 256 + side * 128, 128, 16), :]

    loads = [
        net.local(wo, wo_v),
        net.local(hg.at[:, aligned(chip * 256, 256, 16), :], hg_v.at[0]),
        net.local(hg.at[:, aligned(chip_of(4) * 256, 128, 16), :], hg_v.at[1, :, pl.ds(0, 128)]),
        net.local(
            hg.at[:, aligned(chip_of(2) * 256 + 128, 128, 16), :], hg_v.at[1, :, pl.ds(128, 128)]
        ),
        net.local(mx.at[z], mx_v),
        net.local(att, att_v),
        net.local(wq, wq_v),
        net.local(hat, hat_v),
    ]
    net.barrier(PARTNERS + [("d", 6)])
    def f_send(t, place, mask, side, name):
        return net.send(hg_at(t, mask, side), f_r1.at[place, t, pl.ds(side * 128, 128)], name)

    def f_near(t):
        return [f_send(t, 1, 6, 0, X), f_send(t, 1, 6, 1, Y)]

    def f_own(t):
        return [f_send(t, 0, 2, 0, X), f_send(t, 0, 4, 1, Y)]

    def f_second(t, sent):
        for copy in sent:
            copy.wait_recv()
        f_k[t] = (hg_v[1, t].astype(F32) + f_r1[1, t].astype(F32)).astype(BF)
        return [
            net.send(f_k.at[t, pl.ds(side * 128, 128)], f_r2.at[t, pl.ds(side * 128, 128)], name)
            for side, name in ((0, Y), (1, X))
        ]

    def f_rows(t, sent):
        for copy in sent:
            copy.wait_recv()
        total = hg_v[0, t].astype(F32) + f_r1[0, t].astype(F32) + f_r2[t].astype(F32)
        for i in range(4):
            fs[i, t] = total[i * 64 : (i + 1) * 64, :].astype(BF)
        fb[z, t] = fs[z, t]
        return [net.send(fs.at[zs[m], t], fb.at[z, t], ("z", m)) for m in (2, 3, 1)]

    gate_1 = f_near(0)
    mx_copies = [
        net.send(mx_far, mx_r2, ("z", 2)),
        net.send(mx.at[zs[1]], mx_r1, ("z", 1)),
    ]
    half = width // 2

    def norm_back(value, grad):
        inv = rms(value)
        inner = jnp.mean(value * grad, axis=-1, keepdims=True)
        return inv * grad - value * (inv * inv * inv * inner)

    value, grad = hmid[...], dn2[...]
    inv = rms(value)
    inner = jnp.mean(value * grad, axis=-1, keepdims=True)
    dh[...] = cot[...].astype(F32) + grad - value * (inv * inv * inner)
    dbr[chip] = dh[...].astype(BF)
    plane_b = Plane(net, lambda m, s: dbr.at[chip_of(m), :, pl.ds(s * half, half)], lambda m: [])
    plane_b.start()
    small = [
        net.send(att.at[:, :, aligned((1 - core) * 256, 256, 128)], att_s, CORE)
    ] + [
        net.send(
            hat.at[:, :, aligned(i * 512 + (1 - core) * 256, 256, 128)],
            hat_s.at[:, :, pl.ds(i * 256, 256)],
            CORE,
        )
        for i in range(4)
    ]
    plane_b.forward()
    for copy in loads[1:4]:
        copy.wait()
    gate_2 = f_second(0, gate_1) + f_own(0)
    up_1 = f_near(1)
    up_2 = f_own(1)
    plane_b.spread()
    loads[0].wait()
    weight = wo_v[...].reshape(span, width)
    dsend[...] = (
        right_dot(dbr[...].reshape(4 * tok, width), weight).astype(BF).reshape(4, tok, span)
    )
    d_copies = [net.send(dsend.at[zs[m]], gh.at[here, :], ("z", m)) for m in (2, 3, 1)]
    gh[here, :] = dsend[z]
    dbr_copy = net.send(dbr, dbr_s, CORE)
    for copy in loads[4:]:
        copy.wait()

    class Line:
        def __init__(self, parts, r1, s, r2):
            self.parts, self.r1, self.s, self.r2 = parts, r1, s, r2
            self.sent = [
                net.send(parts.at[zs[3]], r1.at[1], ("z", 1)),
                net.send(parts.at[zs[1]], r1.at[0], ("z", 1)),
            ]

        def middle(self):
            self.sent[0].wait_recv()
            self.s[...] = (self.parts[zs[2]].astype(F32) + self.r1[1].astype(F32)).astype(BF)
            self.far = net.send(self.s, self.r2, ("z", 2))

        def total(self):
            self.sent[1].wait_recv()
            self.far.wait_recv()
            own = self.parts[z].astype(F32) + self.r1[0].astype(F32)
            return own + self.r2[...].astype(F32)

    small[0].wait_recv()
    dbr_copy.wait_recv()
    mine = att_v[:, :, aligned(core * 256, 256, 128)].reshape(4 * tok, 256).T
    theirs = att_s[...].reshape(4 * tok, 256).T

    def out_chunk(i, carry):
        cols = aligned(i * 512, 512, 128)
        total = dot(mine, dbr[:, :, cols].reshape(4 * tok, 512))
        total += dot(theirs, dbr_s[:, :, cols].reshape(4 * tok, 512))
        g2_p[:, :, cols] = total.astype(BF).reshape(4, 64, 512)
        return carry

    lax.fori_loop(0, width // 512, out_chunk, 0)
    line_o = Line(g2_p, g2_r1, g2_s, g2_r2)

    for copy in d_copies:
        copy.wait_recv()
    f_copies = f_rows(0, gate_2)

    scale = HEAD_SIZE ** (-0.5)
    kk, vv = twice(qkv[:, span:])
    dk_acc[...] = jnp.zeros_like(dk_acc)
    dv_acc[...] = jnp.zeros_like(dv_acc)

    def pair(p, carry):
        cols = aligned(p * 128, 128, 128)
        for qb in range(4):
            keys = (qb + 1) * tok
            rows = slice(qb * tok, (qb + 1) * tok)
            q = qkv[rows, cols]
            g = gh[rows, cols]
            lane = lax.broadcasted_iota(jnp.int32, (tok, 128), 1)
            row = lax.rem(lax.broadcasted_iota(jnp.int32, (2 * tok, keys), 0), tok) + qb * tok
            col = lax.broadcasted_iota(jnp.int32, (2 * tok, keys), 1)
            none = jnp.zeros_like(q)

            def both(value):
                return jnp.concatenate(
                    [jnp.where(lane < 64, value, none), jnp.where(lane >= 64, value, none)], axis=0
                )

            qq, gg = both(q), both(g)
            logs = lse[rows, :]
            log = jnp.concatenate(
                [
                    jnp.sum(jnp.where(lane == 2 * p + h, logs, 0.0), axis=-1, keepdims=True)
                    for h in range(2)
                ],
                axis=0,
            )
            s = right_dot(qq, kk[:keys]) * scale
            probs = jnp.exp(jnp.where(col <= row, s, -1e30) - log)
            pg = right_dot(gg, vv[:keys])
            delta = jnp.sum(probs * pg, axis=-1, keepdims=True)
            ds = (probs * (pg - delta)).astype(BF)
            out = dot(ds, kk[:keys]) * scale
            dk_acc[:keys, :] += left_dot(ds, qq)
            dv_acc[:keys, :] += left_dot(probs.astype(BF), gg)
            dqkv[rows, cols] = jnp.where(lane < 64, out[:tok], out[tok:]).astype(BF)
        return carry

    def send_back(start, count):
        cols = pl.ds(start, count)
        return [net.send(dqkv.at[slot(m), cols], dback.at[z, :, cols], ("z", m)) for m in (2, 3, 1)]

    lax.fori_loop(0, 2, pair, 0)
    b_copies = send_back(0, 256)
    lax.fori_loop(2, 4, pair, 0)
    dk = dk_acc[...]
    dv = dv_acc[...]
    lane = lax.broadcasted_iota(jnp.int32, dk.shape, 1)
    dqkv[:, span:] = jnp.where(
        lane < 64, (dk + pltpu.roll(dk, 64, 1)) * scale, dv + pltpu.roll(dv, 64, 1)
    ).astype(BF)
    b_copies += send_back(256, group - 256)
    dback[z] = dqkv[here, :]
    line_o.middle()

    up_2 += f_second(1, up_1)
    for copy in b_copies:
        copy.wait_recv()
    for s in range(4):
        for j in range(group // 128):
            cols = slice(j * 128, (j + 1) * 128)
            last = j == group // 128 - 1
            c_ref, s_ref = (cos_k, sin_k) if last else (cos_q, sin_q)
            value = dback[s, :, cols].astype(F32)
            dpre[s, :, cols] = rotary(value, c_ref[...], -s_ref[...]).astype(BF)
    dpre_copy = net.send(dpre, dpre_s, CORE)

    left = dpre[...].reshape(4 * tok, group)

    def dhat_chunk(i, carry):
        cols = aligned(i * 256, 256, 128)
        rows = wq_v[lax.div(i, 2), lax.rem(i, 2)].reshape(256, group)
        part[:, :, cols] = right_dot(left, rows).astype(BF).reshape(4, tok, 256)
        return carry

    lax.fori_loop(0, width // 256, dhat_chunk, 0)
    sums = Sums(net, part, r1, mid, r2)
    sums.first()

    for copy in small[1:]:
        copy.wait_recv()
    dpre_copy.wait_recv()
    right = dpre_s[...].reshape(4 * tok, group)

    def first_chunk(i, carry):
        own = hat_v[:, :, aligned(i * 512 + core * 256, 256, 128)].reshape(4 * tok, 256).T
        sib = hat_s[:, :, aligned(i * 256, 256, 128)].reshape(4 * tok, 256).T
        total = dot(own, left) + dot(sib, right)
        g1_p[:, i] = total.astype(BF).reshape(4, 64, group)
        return carry

    lax.fori_loop(0, 4, first_chunk, 0)
    line_q = Line(g1_p, g1_r1, g1_s, g1_r2)
    f_copies += f_rows(1, up_2)
    sums.second()
    line_q.middle()
    for copy in mx_copies:
        copy.wait_recv()
    total = mx_v[...].astype(F32) + mx_r1[...].astype(F32) + mx_r2[...].astype(F32)
    mixed[...] = (hmid[...] + total).astype(BF)
    g2_out[...] = line_o.total()
    for side in (0, 1):
        dn2[:, side * half : (side + 1) * half] = sums.total(side)
    tok_out[...] = (dh[...] + norm_back(x_ref[...].astype(F32), dn2[...])).astype(BF)
    g1_f[...] = line_q.total().astype(BF)
    g_copies = [net.send(g1_f.at[chip_of(m)], g1_out.at[chip], ("d", m)) for m in (6, 2, 4)]
    g1_out[chip] = g1_f[chip]
    for copy in g_copies + f_copies:
        copy.wait_recv()
    net.finish()


def third_call(x, hmid, cot, dn2, qkv, lse, tables4, mx, mx_far, wq, wo, hat, att, hg):
    tok, width = x.shape
    group = qkv.shape[1]
    span = group - 128
    ff = hg.shape[-1]
    sds = jax.ShapeDtypeStruct
    v = pltpu.VMEM
    return pl.pallas_call(
        third_kernel,
        name="third",
        out_shape=[
            sds((tok, width), BF), sds((tok, width), BF), sds((64, width), F32),
            sds((4, 64, group), BF), sds((4, 2, 64, ff), BF),
        ],
        in_specs=[VMEM] * 10 + [ANY] * 7,
        out_specs=[VMEM] * 5,
        scratch_shapes=[
            v((4, 2, 4, 64, group), BF), v((2, 4, 64, width), BF), v((4, tok, width), BF),
            v((4, tok, width // 2), BF), v((4, tok, span), BF), v((4, tok, span // 2), BF),
            v((tok, width), BF), v((tok, width), BF), v((tok, width), BF),
            v((2, 2, 256, ff), BF), v((2, 2, 256, ff), BF), v((2, 256, ff), BF), v((2, 256, ff), BF),
            v((4, 2, 64, ff), BF), v((tok, width), F32), v((4, tok, width), BF),
            v((4, tok, width), BF), v((4, tok, span), BF), v((4 * tok, span), BF),
            v((4 * tok, group), BF), v((4 * tok, 128), F32), v((4 * tok, 128), F32),
            v((4, tok, group), BF), v((4, tok, group), BF), v((4, tok, group), BF),
            v((4, tok, width), BF), v((2, 2, tok, width // 2), BF), v((2, tok, width // 2), BF),
            v((2, tok, width // 2), BF),
            v((4, 64, width), BF), v((2, 64, width), BF), v((64, width), BF), v((64, width), BF),
            v((4, 4, 64, group), BF), v((2, 4, 64, group), BF), v((4, 64, group), BF),
            v((4, 64, group), BF), v((4, 64, group), BF),
            pltpu.SemaphoreType.DMA((80,)),
            pltpu.SemaphoreType.DMA((80,)),
        ],
        compiler_params=pltpu.CompilerParams(
            collective_id=3, has_side_effects=True, vmem_limit_bytes=60 * 2**20
        ),
    )(x, hmid, cot, dn2, qkv, lse, *tables4, mx, mx_far, wq, wo, hat, att, hg)


def last_kernel(
    fb, g1, wq, wk, wv, gain1, gain2, w_gate_in, w_up_in, tok_in, mixed_in, g2_in, gd_in,
    gq, gk, gv, g_gate, g_up, g_gain1, g_gain2, tok_out, mixed_out, g2_out, gd_out,
    w_gate, w_up, sems,
):
    copies = [
        pltpu.make_async_copy(src, dst, sems.at[i])
        for i, (src, dst) in enumerate(
            (
                (w_gate_in, w_gate), (w_up_in, w_up), (tok_in, tok_out),
                (mixed_in, mixed_out), (g2_in, g2_out), (gd_in, gd_out),
            )
        )
    ]
    for copy in copies:
        copy.start()
    span = g1.shape[2] - 128
    lane = lax.broadcasted_iota(jnp.int32, (g1.shape[1], 128), 1)
    scale = column(gain1[...])
    scale2 = column(gain2[...])

    def put(out, weight, cols, value):
        out[:, cols] = value * scale
        return jnp.sum(value * weight[:, cols].astype(F32), axis=1, keepdims=True)

    total = jnp.zeros((g1.shape[1], 1), F32)
    for g in range(4):
        total += put(gq, wq, slice(g * span, (g + 1) * span), g1[g, :, :span].astype(F32))
    for g in (0, 2):
        one = g1[g, :, span:].astype(F32)
        two = g1[g + 1, :, span:].astype(F32)
        cols = slice(g * 64, g * 64 + 128)
        total += put(gk, wk, cols, jnp.where(lane < 64, one, pltpu.roll(two, 64, 1)))
        total += put(gv, wv, cols, jnp.where(lane < 64, pltpu.roll(one, 64, 1), two))
    g_gain1[...] = line(total)
    size = fb.shape[-1] // 8
    total = jnp.zeros((g1.shape[1], 1), F32)
    for t, (out, weight) in enumerate(((g_gate, w_gate), (g_up, w_up))):
        copies[t].wait()
        for d in range(0, 8, 2):
            parts = [
                fb[i, t, :, e * size : (e + 1) * size].astype(F32) for e in (d, d + 1) for i in range(4)
            ]
            joined = jnp.concatenate(parts, axis=1)
            cols = pl.ds(d * 4 * size, 8 * size)
            total += jnp.sum(joined * weight[:, cols].astype(F32), axis=1, keepdims=True)
            out[:, cols] = joined * scale2
    g_gain2[...] = line(total)
    for copy in copies[2:]:
        copy.wait()


def last_call(fb, g1, wq, wk, wv, gain1, gain2, w_gate, w_up, tok, mixed, g2, gd):
    rows, ff = w_gate.shape
    sds = jax.ShapeDtypeStruct
    return pl.pallas_call(
        last_kernel,
        name="last",
        out_shape=[
            sds(wq.shape, F32), sds(wk.shape, F32), sds(wv.shape, F32),
            sds((rows, ff), F32), sds((rows, ff), F32), sds((1, rows), F32), sds((1, rows), F32),
            sds(tok.shape, BF), sds(mixed.shape, BF), sds(g2.shape, F32), sds(gd.shape, F32),
        ],
        in_specs=[VMEM] * 7 + [ANY] * 6,
        out_specs=[VMEM] * 11,
        scratch_shapes=[
            pltpu.VMEM((rows, ff), BF), pltpu.VMEM((rows, ff), BF), pltpu.SemaphoreType.DMA((6,)),
        ],
        compiler_params=pltpu.CompilerParams(vmem_limit_bytes=60 * 2**20),
    )(fb, g1, wq, wk, wv, gain1, gain2, w_gate, w_up, tok, mixed, g2, gd)


def shards(
    tokens, norm_first, w_query, w_key, w_value, w_out, norm_second, w_gate, w_up, w_down, cotangent
):
    count = tokens.shape[0]
    gain1, gain2 = norm_first[None, :], norm_second[None, :]
    cosine, sine = tables(lax.axis_index("seq") * count + jnp.arange(count))
    cosine, sine = cosine[:, 0], sine[:, 0]
    one, zero = jnp.ones_like(cosine), jnp.zeros_like(cosine)
    tables4 = [
        jnp.concatenate(parts, axis=1)
        for parts in (
            [cosine] * 4,
            [-sine, sine] * 2,
            [cosine, cosine, one, one],
            [-sine, sine, zero, zero],
        )
    ]
    wq, wo, hat, qkv, att, mixed_part, mixed_far, hg, lse, hmid, dhat2, grad_down = first_call(
        tokens, w_query, w_key, w_value, gain1, w_gate, w_up, gain2, tables4,
        w_out, w_down, cotangent,
    )
    grad_tokens, mixed, grad_out, grad_first, parts = third_call(
        tokens, hmid, cotangent, dhat2, qkv, lse, tables4, mixed_part, mixed_far,
        wq, wo, hat, att, hg,
    )
    (
        grad_query, grad_key, grad_value, grad_gate, grad_up, grad_gain1, grad_gain2,
        grad_tokens, mixed, grad_out, grad_down,
    ) = last_call(
        parts, grad_first, w_query, w_key, w_value, gain1, gain2, w_gate, w_up,
        grad_tokens, mixed, grad_out, grad_down,
    )
    return (
        mixed,
        grad_tokens,
        grad_gain1[0],
        grad_query,
        grad_key,
        grad_value,
        grad_out,
        grad_gain2[0],
        grad_gate,
        grad_up,
        grad_down,
    )


def solution(mesh):
    special = mesh.shape['dp'] == 8 and mesh.shape['seq'] == KEY_VALUE_HEADS
    rows = P(("dp", "seq"), None)
    line = P(("dp", "seq"))
    return jax.shard_map(
        shards if special else general_shards,
        mesh=mesh,
        in_specs=(rows, line, rows, rows, rows, rows, line, rows, rows, rows, rows),
        out_specs=(rows, rows, line, rows, rows, rows, rows, line, rows, rows, rows),
        check_vma=False,
    )
```

```python
import jax
import jax.numpy as jnp
from jax import lax
from jax.experimental import pallas as pl
from jax.experimental.pallas import tpu as pltpu
from jax.sharding import PartitionSpec as P

H = 32
KEY_VALUE_HEADS = 4
HEAD_SIZE = 64
EPS = 1e-05
BF = jnp.bfloat16
F32 = jnp.float32


def tables(positions):
    freq = 10000.0 ** (-jnp.arange(0, HEAD_SIZE // 2, dtype=F32) * 2.0 / HEAD_SIZE)
    angle = positions.astype(F32)[:, None] * freq[None, :]
    return (jnp.cos(angle)[:, None, :], jnp.sin(angle)[:, None, :])


def rotate(heads, cosine, sine):
    half = heads.shape[-1] // 2
    first = heads[..., :half]
    second = heads[..., half:]
    return jnp.concatenate(
        [first * cosine - second * sine, second * cosine + first * sine], axis=-1
    )


def dot(left, right):
    return jnp.dot(left, right, preferred_element_type=F32)


def left_dot(left, right):
    return lax.dot_general(left, right, (((0,), (0,)), ((), ())), preferred_element_type=F32)


def right_dot(left, right):
    return lax.dot_general(left, right, (((1,), (1,)), ((), ())), preferred_element_type=F32)


def bits_of(count):
    return [1 << k for k in range(count.bit_length() - 1)]


class Axis:
    def __init__(self, name):
        self.name = name
        self.size = lax.axis_size(name)
        self.me = lax.axis_index(name)

    def swap(self, value, mask):
        return lax.ppermute(value, self.name, [(i, i ^ mask) for i in range(self.size)])

    def all(self, value):
        return [value if m == 0 else self.swap(value, m) for m in range(self.size)]

    def exchange(self, stacked):
        return [
            lax.dynamic_index_in_dim(stacked, self.me ^ m, 0, keepdims=False)
            if m == 0
            else self.swap(
                lax.dynamic_index_in_dim(stacked, self.me ^ m, 0, keepdims=False), m
            )
            for m in range(self.size)
        ]

    def natural(self, pieces):
        stack = jnp.stack(pieces)
        return [
            lax.dynamic_index_in_dim(stack, self.me ^ i, 0, keepdims=False)
            for i in range(self.size)
        ]


def orders(size):
    even = [m for m in range(size) if m % 2 == 0]
    return even, [m + 1 for m in even]


def chip_bits(size, turn):
    bits = bits_of(size)[1:]
    return bits if turn == 0 else bits[::-1]


def gather_chips(dp, piece, turn):
    pieces = {0: piece}
    for bit in chip_bits(dp.size, turn):
        pieces.update({m ^ bit: dp.swap(p, bit) for m, p in list(pieces.items())})
    return pieces


def gather_rows(dp, piece, turn):
    pieces = gather_chips(dp, piece, turn)
    even = jnp.concatenate([pieces[m] for m in orders(dp.size)[0]], axis=0)
    return even, dp.swap(even, 1)


def scatter_chips(dp, blocks, turn):
    for bit in chip_bits(dp.size, turn):
        for m in [m for m in blocks if m & bit]:
            other = dp.swap(blocks.pop(m).astype(BF), bit)
            blocks[m ^ bit] = blocks[m ^ bit].astype(F32) + other.astype(F32)
    return blocks[0]


def scatter_rows(dp, even_fn, odd, turn):
    rows = odd.shape[0] * 2 // dp.size
    other = dp.swap(odd, 1)
    even = (even_fn() + other.astype(F32)).astype(BF)
    blocks = {
        m: even[i * rows : (i + 1) * rows] for i, m in enumerate(orders(dp.size)[0])
    }
    return scatter_chips(dp, blocks, turn)


def mask_columns(dp, value):
    width = value.shape[1] // dp.size
    return tuple(
        jnp.concatenate(
            [lax.dynamic_slice_in_dim(value, (dp.me ^ m) * width, width, 1) for m in group],
            axis=1,
        )
        for group in orders(dp.size)
    )


def natural_columns(dp, even, odd):
    both = jnp.concatenate([even, odd], axis=1)
    width = both.shape[1] // dp.size
    half = dp.size // 2
    parts = []
    for i in range(dp.size):
        mask = dp.me ^ i
        place = mask // 2 + (mask % 2) * half
        parts.append(lax.dynamic_slice_in_dim(both, place * width, width, 1))
    return jnp.concatenate(parts, axis=1)


def attend(queries, keys, values, visible):
    scores = jnp.einsum("qhd,kd->hqk", queries, keys, preferred_element_type=F32)
    scores = jnp.where(visible[None], scores * HEAD_SIZE ** (-0.5), -1e30)
    top = jnp.max(scores, axis=-1, keepdims=True)
    expo = jnp.exp(scores - top)
    total = jnp.sum(expo, axis=-1, keepdims=True)
    probs = (expo / total).astype(BF)
    result = jnp.einsum("hqk,kd->qhd", probs, values, preferred_element_type=F32)
    return result.astype(BF), top + jnp.log(total)


def attend_back(queries, keys, values, grad_heads, logsum, visible):
    scale = HEAD_SIZE ** (-0.5)
    scores = jnp.einsum("qhd,kd->hqk", queries, keys, preferred_element_type=F32)
    scores = jnp.where(visible[None], scores * scale, -1e30)
    probs = jnp.exp(scores - logsum)
    pgrad = jnp.einsum("qhd,kd->hqk", grad_heads, values, preferred_element_type=F32)
    delta = jnp.sum(probs * pgrad, axis=-1, keepdims=True)
    sgrad = (probs * (pgrad - delta)).astype(BF)
    qgrad = jnp.einsum("hqk,kd->qhd", sgrad, keys, preferred_element_type=F32) * scale
    kgrad = jnp.einsum("hqk,qhd->kd", sgrad, queries, preferred_element_type=F32) * scale
    vgrad = jnp.einsum("hqk,qhd->kd", probs.astype(BF), grad_heads, preferred_element_type=F32)
    return qgrad.astype(BF), kgrad.astype(BF), vgrad.astype(BF)


def general_shards(
    tokens, norm_first, w_query, w_key, w_value, w_out, norm_second, w_gate, w_up, w_down, cotangent
):
    dp, seq = Axis("dp"), Axis("seq")
    groups = seq.size
    count, width = tokens.shape
    ff = w_gate.shape[1]
    per = H // groups
    repeat = groups // KEY_VALUE_HEADS
    heads_wide = H * HEAD_SIZE
    keys_wide = KEY_VALUE_HEADS * HEAD_SIZE
    gain1 = norm_first.astype(F32)[:, None]
    gain2 = norm_second.astype(F32)[:, None]

    w_first = jnp.concatenate([w_query, w_key, w_value], axis=1)
    w_first_scaled = (w_first.astype(F32) * gain1).astype(BF)
    wide = w_first.shape[1]

    def by_part(weight):
        rows = weight.shape[0]
        scaled = (weight.astype(F32) * gain2).astype(BF)
        parts = scaled.reshape(rows, dp.size, groups, ff // dp.size // groups)
        return parts.transpose(2, 0, 1, 3).reshape(groups, rows, ff // groups)

    down = [gather_chips(dp, w_down[:, t * width // 2 : (t + 1) * width // 2], t) for t in (0, 1)]
    first_rows = jnp.concatenate(seq.natural(seq.all(w_first_scaled)), axis=0)
    first = [gather_rows(dp, first_rows[:, t * wide // 2 : (t + 1) * wide // 2], t) for t in (0, 1)]
    out_rows = jnp.concatenate(seq.natural(seq.all(w_out)), axis=0)
    outw = [gather_rows(dp, out_rows[:, t * width // 2 : (t + 1) * width // 2], t) for t in (0, 1)]
    gate_up = seq.exchange(jnp.stack([by_part(w_gate), by_part(w_up)], axis=1))
    gate_up = jnp.concatenate(seq.natural(gate_up), axis=1)
    (gate_even, gate_odd), (up_even, up_odd) = [
        gather_rows(dp, gate_up[t], t) for t in (0, 1)
    ]
    cot_all = jnp.concatenate(seq.all(cotangent), axis=0)

    rows_down = w_down.shape[0]
    down_full = []
    for t in (0, 1):
        even = jnp.stack([down[t][m] for m in orders(dp.size)[0]])
        odd = dp.swap(even, 1)
        full = jnp.zeros((rows_down * dp.size, width // 2), BF)
        for i, m in enumerate(orders(dp.size)[0]):
            full = lax.dynamic_update_slice(full, even[i], ((dp.me ^ m) * rows_down, 0))
            full = lax.dynamic_update_slice(full, odd[i], ((dp.me ^ m ^ 1) * rows_down, 0))
        down_full.append(full)

    inputs = tokens.astype(F32)
    inv1 = lax.rsqrt(jnp.mean(inputs * inputs, axis=-1, keepdims=True) + EPS)
    hat1 = (inputs * inv1).astype(BF)
    hat1_even, hat1_odd = mask_columns(dp, hat1)
    cosine, sine = tables(seq.me * count + jnp.arange(count))
    pre = jnp.concatenate(
        [dot(hat1_even, first[t][0]) + dot(hat1_odd, first[t][1]) for t in (0, 1)], axis=1
    )
    qpre = pre[:, :heads_wide].reshape(count, H, HEAD_SIZE)
    kpre = pre[:, heads_wide : heads_wide + keys_wide].reshape(count, KEY_VALUE_HEADS, HEAD_SIZE)
    vround = pre[:, heads_wide + keys_wide :].astype(BF)
    qrot = rotate(qpre, cosine, sine).reshape(count, heads_wide).astype(BF)
    krot = rotate(kpre, cosine, sine).reshape(count, keys_wide).astype(BF)
    span = per * HEAD_SIZE
    packed = []
    for g in range(groups):
        head = g // repeat * HEAD_SIZE
        packed.append(
            jnp.concatenate(
                [
                    qrot[:, g * span : (g + 1) * span],
                    krot[:, head : head + HEAD_SIZE],
                    vround[:, head : head + HEAD_SIZE],
                ],
                axis=1,
            )
        )
    qkv = jnp.concatenate(seq.exchange(jnp.stack(packed)), axis=0)
    length = qkv.shape[0]
    queries = qkv[:, :span].reshape(length, per, HEAD_SIZE)
    keys = qkv[:, span : span + HEAD_SIZE]
    values = qkv[:, span + HEAD_SIZE :]
    place = jnp.concatenate(
        [(seq.me ^ m) * count + jnp.arange(count, dtype=jnp.int32) for m in range(groups)]
    )
    visible = place[None, :] <= place[:, None]
    out_heads, logsum = attend(queries, keys, values, visible)
    out_heads = out_heads.reshape(length, span)

    def back_home(value):
        return seq.natural(
            [
                value[:count] if m == 0 else seq.swap(value[m * count : (m + 1) * count], m)
                for m in range(groups)
            ]
        )

    attn = jnp.concatenate(back_home(out_heads), axis=1)
    attn_even, attn_odd = mask_columns(dp, attn)
    branch = jnp.concatenate(
        [dot(attn_even, outw[t][0]) + dot(attn_odd, outw[t][1]) for t in (0, 1)], axis=1
    )
    hmid = inputs + branch

    inv2 = lax.rsqrt(jnp.mean(hmid * hmid, axis=-1, keepdims=True) + EPS)
    hat2 = jnp.concatenate(mask_columns(dp, (hmid * inv2).astype(BF)), axis=1)
    hat2_all = jnp.concatenate(seq.all(hat2), axis=0)
    hat2_even, hat2_odd = hat2_all[:, : width // 2], hat2_all[:, width // 2 :]
    gate = dot(hat2_even, gate_even) + dot(hat2_odd, gate_odd)
    upper = dot(hat2_even, up_even) + dot(hat2_odd, up_odd)
    sigma = jax.nn.sigmoid(gate)
    hidden = (gate * sigma * upper).astype(BF)
    halves = [cot_all[:, : width // 2], cot_all[:, width // 2 :]]
    dhidden = right_dot(halves[0], down_full[0]) + right_dot(halves[1], down_full[1])
    dgate = (dhidden * upper * sigma * (1.0 + gate * (1.0 - sigma))).astype(BF)
    dupper = (dhidden * gate * sigma).astype(BF)
    dhat2 = jnp.concatenate(
        [
            right_dot(dgate, gate_even) + right_dot(dupper, up_even),
            right_dot(dgate, gate_odd) + right_dot(dupper, up_odd),
        ],
        axis=1,
    ).astype(BF)

    def sum_home(value):
        total = value[:count].astype(F32)
        for m in range(1, groups):
            total = total + seq.swap(value[m * count : (m + 1) * count], m).astype(F32)
        return total

    dhat2 = sum_home(dhat2)
    dgain2 = natural_columns(dp, dhat2[:, : width // 2], dhat2[:, width // 2 :])
    inner = jnp.mean(hmid * dgain2, axis=-1, keepdims=True)
    dh = cotangent.astype(F32) + inv2 * dgain2 - hmid * inv2 * inv2 * inv2 * inner
    dbranch = dh.astype(BF)

    dattn = natural_columns(
        dp,
        *[
            sum(
                right_dot(dbranch[:, t * width // 2 : (t + 1) * width // 2], outw[t][s])
                for t in (0, 1)
            ).astype(BF)
            for s in (0, 1)
        ],
    )
    grad_heads = jnp.concatenate(
        seq.exchange(dattn.reshape(count, groups, span).transpose(1, 0, 2)), axis=0
    ).reshape(length, per, HEAD_SIZE)
    dq, dk, dv = attend_back(queries, keys, values, grad_heads, logsum, visible)
    dqkv = back_home(jnp.concatenate([dq.reshape(length, span), dk, dv], axis=1))
    dq = jnp.concatenate([piece[:, :span] for piece in dqkv], axis=1)
    dk = [piece[:, span : span + HEAD_SIZE].astype(F32) for piece in dqkv]
    dv = [piece[:, span + HEAD_SIZE :].astype(F32) for piece in dqkv]
    dk = jnp.stack(
        [sum(dk[i * repeat : (i + 1) * repeat]) for i in range(KEY_VALUE_HEADS)], axis=1
    )
    dv = jnp.concatenate(
        [sum(dv[i * repeat : (i + 1) * repeat]) for i in range(KEY_VALUE_HEADS)], axis=1
    )
    dq = rotate(dq.astype(F32).reshape(count, H, HEAD_SIZE), cosine, -sine)
    dk = rotate(dk, cosine, -sine)
    dpre = jnp.concatenate(
        [dq.reshape(count, heads_wide), dk.reshape(count, keys_wide), dv], axis=1
    ).astype(BF)
    dhalf = [dpre[:, t * wide // 2 : (t + 1) * wide // 2] for t in (0, 1)]
    dhat1 = [sum(right_dot(dhalf[t], first[t][s]) for t in (0, 1)) for s in (0, 1)]
    dgain1 = natural_columns(dp, *dhat1)
    inner = jnp.mean(inputs * dgain1, axis=-1, keepdims=True)
    grad_inputs = dh + inv1 * dgain1 - inputs * inv1 * inv1 * inv1 * inner

    mixed_part = jnp.concatenate([dot(hidden, down_full[t]) for t in (0, 1)], axis=1).astype(BF)
    mixed = hmid + sum_home(mixed_part)

    grad_down = []
    for t in (0, 1):
        part = left_dot(hidden, halves[t]).astype(BF)
        blocks = [
            lax.dynamic_slice_in_dim(part, (dp.me ^ m) * rows_down, rows_down, 0)
            for m in range(dp.size)
        ]
        even, odd = orders(dp.size)
        other = dp.swap(jnp.stack([blocks[m] for m in odd]), 1)
        summed = {
            m: (blocks[m].astype(F32) + other[i].astype(F32)).astype(BF)
            for i, m in enumerate(even)
        }
        grad_down.append(scatter_chips(dp, summed, t))
    grad_down = jnp.concatenate(grad_down, axis=1)

    def ff_grad(grad, turn):
        odd = left_dot(hat2_odd, grad).astype(BF)
        return scatter_rows(dp, lambda: left_dot(hat2_even, grad), odd, turn)

    rows = w_gate.shape[0]
    sent = jnp.stack([ff_grad(dgate, 0).astype(BF), ff_grad(dupper, 1).astype(BF)])
    sent = sent.reshape(2, groups, rows, ff // groups).transpose(1, 0, 2, 3)
    got = jnp.stack(seq.natural(seq.exchange(sent)))
    got = got.reshape(groups, 2, rows, dp.size, ff // groups // dp.size)
    got = got.transpose(1, 2, 3, 0, 4).reshape(2, rows, ff).astype(F32)
    grad_gate, grad_up = got[0] * gain2, got[1] * gain2
    grad_gain2 = jnp.sum(got[0] * w_gate.astype(F32) + got[1] * w_up.astype(F32), axis=1)

    def proj_grad(even, odd, grads):
        parts = []
        for t in (0, 1):
            send = left_dot(odd, grads[t]).astype(BF)
            parts.append(
                scatter_rows(dp, lambda grad=grads[t]: left_dot(even, grad), send, t)
            )
        own = jnp.concatenate(parts, axis=1)
        own = own.astype(BF).reshape(groups, rows, own.shape[1])
        return sum(piece.astype(F32) for piece in seq.exchange(own))

    grad_out = proj_grad(
        attn_even,
        attn_odd,
        [dbranch[:, t * width // 2 : (t + 1) * width // 2] for t in (0, 1)],
    )
    grad_first = proj_grad(hat1_even, hat1_odd, dhalf)
    grad_gain1 = jnp.sum(grad_first * w_first.astype(F32), axis=1)
    grad_first = grad_first * gain1
    return (
        mixed.astype(BF),
        grad_inputs.astype(BF),
        grad_gain1,
        grad_first[:, :heads_wide],
        grad_first[:, heads_wide : heads_wide + keys_wide],
        grad_first[:, heads_wide + keys_wide :],
        grad_out,
        grad_gain2,
        grad_gate,
        grad_up,
        grad_down,
    )


MESH = pl.DeviceIdType.MESH
ANY = pl.BlockSpec(memory_space=pl.ANY)
VMEM = pl.BlockSpec(memory_space=pltpu.VMEM)


class Net:
    def __init__(self, send_sems, recv_sems):
        self.send_sems, self.recv_sems, self.used = send_sems, recv_sems, 0
        self.open = []
        dp, z = lax.axis_index("dp"), lax.axis_index("seq")
        self.dp, self.z = dp, z
        self.dps = {
            0: dp,
            1: dp + 1 - 2 * lax.rem(dp, 2),
            2: dp + 2 - 4 * lax.rem(lax.div(dp, 2), 2),
            4: lax.rem(dp + 4, 8),
        }
        self.dps[6] = lax.rem(self.dps[2] + 4, 8)
        for mask in (2, 4, 6):
            self.dps[mask + 1] = self.dps[mask] + 1 - 2 * lax.rem(dp, 2)
        self.zs = {0: z, 1: z + 1 - 2 * lax.rem(z, 2), 2: lax.rem(z + 2, 4), 3: 3 - z}

    def target(self, name):
        kind, mask = name
        return (self.dps[mask], self.z) if kind == "d" else (self.dp, self.zs[mask])

    def barrier(self, names):
        sem = pltpu.get_barrier_semaphore()
        for name in names:
            pl.semaphore_signal(sem, inc=1, device_id=self.target(name), device_id_type=MESH)
        pl.semaphore_wait(sem, len(names))

    def send(self, src, dst, name):
        copy = pltpu.make_async_remote_copy(
            src_ref=src,
            dst_ref=dst,
            send_sem=self.send_sems.at[self.used],
            recv_sem=self.recv_sems.at[self.used],
            device_id=self.target(name),
            device_id_type=MESH,
        )
        self.used += 1
        copy.start()
        self.open.append(copy)
        return copy

    def local(self, src, dst):
        copy = pltpu.make_async_copy(src, dst, self.send_sems.at[self.used])
        self.used += 1
        copy.start()
        return copy

    def sent(self, copies):
        for copy in copies:
            copy.wait_send()
        done = [id(copy) for copy in copies]
        self.open = [copy for copy in self.open if id(copy) not in done]

    def finish(self):
        for copy in self.open:
            copy.wait_send()


X, Y, CORE = ("d", 2), ("d", 4), ("d", 1)
PARTNERS = [X, Y, CORE, ("z", 1), ("z", 2), ("z", 3)]


class Plane:
    def __init__(self, net, at, both):
        self.net, self.at, self.both = net, at, both

    def push(self, mask, half, name):
        ref = self.at(mask, half)
        return self.net.send(ref, ref, name)

    def start(self):
        self.xa = self.push(0, 0, X)
        self.yb = self.push(0, 1, Y)
        self.ya = self.push(0, 0, Y)
        self.xb = self.push(0, 1, X)
        self.cores = [self.core(0)]

    def core(self, mask):
        return [self.net.send(ref, ref, CORE) for ref in self.both(mask)]

    def forward(self):
        self.xa.wait_recv()
        self.ya2 = self.push(2, 0, Y)
        self.yb.wait_recv()
        self.xb2 = self.push(4, 1, X)

    def spread(self):
        self.ya.wait_recv()
        self.cores.append(self.core(4))
        self.xb.wait_recv()
        self.cores.append(self.core(2))
        self.ya2.wait_recv()
        self.xb2.wait_recv()
        self.cores.append(self.core(6))

    def finish(self):
        for copies in self.cores:
            for copy in copies:
                copy.wait_recv()

    def sent(self):
        copies = [self.xa, self.yb, self.ya, self.xb, self.ya2, self.xb2]
        self.net.sent(copies + [copy for group in self.cores for copy in group])


def rotary(value, cosine, sine):
    lane = lax.broadcasted_iota(jnp.int32, value.shape, 1)
    partner = jnp.where(
        lax.rem(lane, 64) < 32, pltpu.roll(value, 96, 1), pltpu.roll(value, 32, 1)
    )
    return value * cosine + partner * sine


def column(row):
    n = row.shape[1]
    shape = (n, n)
    same = lax.broadcasted_iota(jnp.int32, shape, 0) == lax.broadcasted_iota(jnp.int32, shape, 1)
    return jnp.sum(jnp.where(same, row.astype(F32), 0.0), axis=1, keepdims=True)


def line(value):
    n = value.shape[0]
    shape = (n, n)
    same = lax.broadcasted_iota(jnp.int32, shape, 0) == lax.broadcasted_iota(jnp.int32, shape, 1)
    return jnp.sum(jnp.where(same, value, 0.0), axis=0, keepdims=True)


def rms(value):
    return lax.rsqrt(jnp.mean(value * value, axis=-1, keepdims=True) + EPS)


def twice(pair):
    lane = lax.broadcasted_iota(jnp.int32, pair.shape, 1)
    other = pltpu.roll(pair.astype(F32), 64, 1).astype(BF)
    return jnp.where(lane < 64, pair, other), jnp.where(lane < 64, other, pair)


def aligned(start, count, unit):
    return pl.ds(pl.multiple_of(start, unit), count)


class Sums:
    def __init__(self, net, part, r1, mid, r2, sets=1):
        self.net, self.part, self.r1, self.mid, self.r2 = net, part, r1, mid, r2
        self.width = r2.shape[-1] // sets
        self.near, self.own, self.far = {}, {}, {}

    def cols(self, side, k):
        return pl.ds((2 * k + side) * self.width, self.width)

    def place(self, k):
        return pl.ds(k * self.width, self.width)

    def block(self, mask):
        return lax.div(self.net.dps[mask], 2)

    def first(self, k=0):
        for sent, place, pushes in (
            (self.near, 1, ((6, 0, X), (6, 1, Y))),
            (self.own, 0, ((2, 0, X), (4, 1, Y))),
        ):
            sent[k] = [
                self.net.send(
                    self.part.at[self.block(mask), :, self.cols(side, k)],
                    self.r1.at[side, place, :, self.place(k)],
                    name,
                )
                for mask, side, name in pushes
            ]

    def second(self, k=0):
        self.far[k] = []
        for side, (mask, name) in enumerate(((4, Y), (2, X))):
            self.near[k][side].wait_recv()
            c = self.place(k)
            mine = self.part[self.block(mask), :, self.cols(side, k)]
            self.mid[side, :, c] = (
                mine.astype(F32) + self.r1[side, 1, :, c].astype(F32)
            ).astype(BF)
            self.far[k].append(
                self.net.send(self.mid.at[side, :, c], self.r2.at[side, :, c], name)
            )

    def sent(self):
        for sent in (self.near, self.own, self.far):
            for copies in sent.values():
                self.net.sent(copies)

    def total(self, side, k=0):
        self.own[k][side].wait_recv()
        self.far[k][side].wait_recv()
        c = self.place(k)
        mine = self.part[self.block(0), :, self.cols(side, k)]
        return mine.astype(F32) + self.r1[side, 0, :, c].astype(F32) + self.r2[side, :, c].astype(F32)


def first_kernel(
    x_ref, wq, wk, wv, gain1, w_gate, w_up, gain2, cos_q, sin_q, cos_k, sin_k, wo, wd, cot,
    wq_out, wo_out, hat_out, qkv_out, att_out, mx_out, mx_far, hg_out, lse, hmid, dn_out, gdown,
    wq_s, wf, wq_v, wo_v, hat, qkv_send, qkv, heads, att, part, r1, mid, r2,
    wg_v, wd_v, n_v, n_sib, c_v, c_sib, hid, dg, du,
    mx_r, hd, hd_r1, hd_r2, sib_r, send_sems, recv_sems,
):
    net = Net(send_sems, recv_sems)
    dp, z, dps, zs = net.dp, net.z, net.dps, net.zs
    tok, width = x_ref.shape
    group = qkv.shape[1]
    span = heads.shape[1]
    ff = wf.shape[-1]
    core, chip = lax.rem(dp, 2), lax.div(dp, 2)
    here = aligned(z * tok, tok, 16)

    staged = [
        net.local(weight.at[:, pl.ds(j * ff, ff)], ref.at[0, pl.ds(j * 64, 64), :])
        for weight, ref in ((w_gate, dg), (w_up, du))
        for j in range(4)
    ]
    own = [
        net.local(wo, wo_v.at[core, z]),
        net.local(wd, wd_v.at[aligned(dp * 176, 176, 16), :]),
        net.local(cot, c_v.at[here, :]),
    ]
    net.barrier(PARTNERS + [("d", 6)])

    scale = column(gain1[...])
    lane = lax.broadcasted_iota(jnp.int32, (wq.shape[0], 128), 1)
    for g in range(4):
        wq_s[g, :, :span] = (wq[:, g * span : (g + 1) * span].astype(F32) * scale).astype(BF)
        start = g // 2 * 128
        k = wk[:, start : start + 128].astype(F32)
        v = wv[:, start : start + 128].astype(F32)
        if g % 2 == 0:
            both = jnp.where(lane < 64, k, pltpu.roll(v, 64, 1))
        else:
            both = jnp.where(lane < 64, pltpu.roll(k, 64, 1), v)
        wq_s[g, :, span:] = (both * scale).astype(BF)

    def chip_of(mask):
        return lax.div(dps[mask], 2)

    w_1 = [
        net.send(wq_s.at[chip_of(m)], wq_v.at[chip, core, z], ("d", m)) for m in (6, 2, 4)
    ]
    own_q = net.local(wq_s.at[chip], wq_v.at[chip, core, z])
    x = x_ref[...].astype(F32)
    hat[chip] = (x * rms(x)).astype(BF)

    def half_of(ref, side):
        w = ref.shape[-1] // 2
        return pl.ds(side * w, w)

    def block(ref, size, cores):
        def at(mask, side):
            return ref.at[aligned(dps[mask] * size, size, 16), half_of(ref, side)]

        return at, lambda mask: [ref.at[aligned(dps[mask] * size, size, 16), :]] if cores else []

    plane_h = Plane(net, lambda m, s: hat.at[chip_of(m), :, half_of(hat, s)], lambda m: [])
    plane_h.start()
    down = Plane(net, *block(wd_v, 176, True))
    own[1].wait()
    down.start()

    def wq_at(mask):
        return wq_v.at[:, core, zs[mask]]

    def wo_at(mask):
        return wo_v.at[core, zs[mask]]

    class Line:
        def __init__(self, at):
            self.at = at
            self.far = self.push(0, ("z", 2))
            self.near = self.push(0, ("z", 1))
            self.cores = [self.push(0, CORE)]

        def push(self, mask, name):
            return net.send(self.at(mask), self.at(mask), name)

        def forward(self):
            self.far.wait_recv()
            self.last = self.push(2, ("z", 1))
            self.cores.append(self.push(2, CORE))

        def spread(self):
            self.near.wait_recv()
            self.cores.append(self.push(1, CORE))
            self.last.wait_recv()
            self.cores.append(self.push(3, CORE))

        def finish(self):
            for copy in self.cores:
                copy.wait_recv()

    scale = column(gain2[...])
    size = ff // 8
    for copy in staged:
        copy.wait()
    for t, ref in enumerate((dg, du)):
        for i in range(4):
            parts = []
            for b in range(i, 32, 4):
                j, start = b // 8, b % 8 * size
                parts.append(ref[0, j * 64 : (j + 1) * 64, start : start + size])
            joined = jnp.concatenate([p.astype(F32) for p in parts], axis=1)
            wf[(i * 2 + t) * 64 : (i * 2 + t + 1) * 64, :] = (joined * scale).astype(BF)
    f_rows = aligned((dp * 4 + z) * 64, 64, 16)

    def wf_at(i, t):
        return wf.at[aligned((i * 2 + t) * 64, 64, 16), :]

    own_f = [net.local(wf_at(z, t), wg_v.at[t, f_rows, :]) for t in (0, 1)]

    def f_send(t):
        return [
            net.send(wf_at(zs[m], t), wg_v.at[t, f_rows, :], ("z", m)) for m in (2, 3, 1)
        ]

    def f_plane(t):
        def rows(mask, start, count):
            return wg_v.at[t, aligned(dps[mask] * 256 + start, count, 16), :]

        return Plane(
            net, lambda m, s: rows(m, s * 128, 128), lambda m: [rows(m, 0, 256)]
        )

    own[0].wait()
    line_o = Line(wo_at)
    own_q.wait()
    for copy in w_1:
        copy.wait_recv()

    line_q = Line(wq_at)
    plane_h.forward()
    line_q.forward()
    gate_copies = f_send(0)
    plane_h.spread()
    line_q.spread()
    down.forward()
    line_q.finish()

    weight = wq_v[...].reshape(width, group)

    left = hat[...].reshape(4 * tok, width)
    for start in range(0, group, 256):
        stop = min(start + 256, group)
        pre = dot(left, weight[:, start:stop])
        for j in range(start, stop, 128):
            c_ref, s_ref = (cos_k, sin_k) if j == group - 128 else (cos_q, sin_q)
            for s in range(4):
                value = pre[s * tok : (s + 1) * tok, j - start : j - start + 128]
                value = rotary(value, c_ref[...], s_ref[...])
                qkv_send[s, :, j : j + 128] = value.astype(BF)
    q_copies = [net.send(qkv_send.at[zs[m]], qkv.at[here, :], ("z", m)) for m in (2, 3, 1)]
    own_q = net.local(qkv_send.at[z], qkv.at[here, :])
    line_o.forward()
    up_copies = f_send(1)
    down.spread()
    own_q.wait()
    for copy in q_copies:
        copy.wait_recv()

    kk, vv = twice(qkv[:, span:])

    def pair(p, carry):
        cols = aligned(p * 128, 128, 128)
        for qb in range(4):
            keys = (qb + 1) * tok
            q = qkv[qb * tok : (qb + 1) * tok, cols]
            lane = lax.broadcasted_iota(jnp.int32, (tok, 128), 1)
            row = lax.rem(lax.broadcasted_iota(jnp.int32, (2 * tok, keys), 0), tok) + qb * tok
            col = lax.broadcasted_iota(jnp.int32, (2 * tok, keys), 1)
            none = jnp.zeros_like(q)
            both = jnp.concatenate(
                [jnp.where(lane < 64, q, none), jnp.where(lane >= 64, q, none)], axis=0
            )
            s = right_dot(both, kk[:keys]) * HEAD_SIZE ** (-0.5)
            s = jnp.where(col <= row, s, -1e30)
            top = jnp.max(s, axis=-1, keepdims=True)
            e = jnp.exp(s - top)
            total = jnp.sum(e, axis=-1, keepdims=True)
            out = dot((e * (1.0 / total)).astype(BF), vv[:keys])
            log = top + jnp.log(total)
            old = lse[qb * tok : (qb + 1) * tok, :]
            old = jnp.where(lane == 2 * p, log[:tok], old)
            lse[qb * tok : (qb + 1) * tok, :] = jnp.where(lane == 2 * p + 1, log[tok:], old)
            heads[qb * tok : (qb + 1) * tok, cols] = jnp.where(
                lane < 64, out[:tok], out[tok:]
            ).astype(BF)
        return carry

    lse[...] = jnp.zeros_like(lse)
    h_copies = []
    for part_of in (0, 1):
        lax.fori_loop(part_of * 2, part_of * 2 + 2, pair, 0)
        cols = pl.ds(part_of * 256, 256)
        h_copies += [
            net.send(
                heads.at[aligned(zs[m] * tok, tok, 16), cols], att.at[z, :, cols], ("z", m)
            )
            for m in (2, 3, 1)
        ]
    own_h = net.local(heads.at[here, :], att.at[z])

    for copy in own_f:
        copy.wait()
    for copy in gate_copies:
        copy.wait_recv()
    plane_g, plane_u = f_plane(0), f_plane(1)
    plane_g.start()
    line_o.spread()
    line_o.finish()
    own_h.wait()
    for copy in h_copies:
        copy.wait_recv()


    c_near = net.send(cot, c_v.at[here, :], ("z", 1))
    c_far = net.send(cot, c_v.at[here, :], ("z", 2))
    sums = Sums(net, part, r1, mid, r2, 2)
    left = att[...].reshape(4 * tok, span)
    for c in range(4):
        cols = pl.ds(c * (width // 4), width // 4)
        weight = wo_v[:, :, :, cols].reshape(span, width // 4)
        part[:, :, cols] = dot(left, weight).astype(BF).reshape(4, tok, width // 4)
    def slot(mask):
        return aligned(zs[mask] * tok, tok, 16)

    def tokens(ref, mask, name):
        return net.send(ref.at[slot(mask), :], ref.at[slot(mask), :], name)

    def n_push(k, mask, name):
        place = n_v.at[slot(mask), pl.ds(k * (width // 2), width // 2)]
        return net.send(place, place, name)

    def middle(k):
        for side in (0, 1):
            cols = sums.cols(side, k)
            value = x_ref[:, cols].astype(F32) + sums.total(side, k)
            hmid[:, cols] = value
            n_v[here, cols] = value.astype(BF)
        n_far.append(n_push(k, 0, ("z", 2)))
        n_near.append(n_push(k, 0, ("z", 1)))

    n_far, n_near = [], []
    sums.first(0)
    sums.second(0)
    sums.first(1)
    middle(0)
    sums.second(1)
    plane_g.forward()
    for copy in up_copies:
        copy.wait_recv()
    plane_u.start()
    middle(1)
    outs = [
        net.local(wq_v, wq_out), net.local(wo_v, wo_out), net.local(qkv, qkv_out),
        net.local(att, att_out), net.local(hat, hat_out),
    ]
    c_far.wait_recv()
    c_last = tokens(c_v, 2, ("z", 1))
    plane_g.spread()
    plane_u.forward()
    n_last = []
    for k in (0, 1):
        n_far[k].wait_recv()
        n_last.append(n_push(k, 2, ("z", 1)))
    plane_u.spread()

    half = width // 2
    near_pair = lax.div(z, 2)
    far = aligned((1 - near_pair) * 2 * tok, 2 * tok, 16)
    near = aligned(near_pair * 2 * tok, 2 * tok, 16)
    dn_part = part

    def chunks(fn, total, size):
        whole = total // size

        def step(i, carry):
            fn(i * size, size)
            return carry

        lax.fori_loop(0, whole, step, 0)
        if total % size:
            fn(whole * size, total - whole * size)

    def front(rows):
        inv = rms(n_v[rows, :].astype(F32))

        def chunk(start, size):
            cols = aligned(start, size, 128)
            n = n_v[rows, :]
            gate = dot(n, wg_v[0, :, cols]) * inv
            upper = dot(n, wg_v[1, :, cols]) * inv
            dhid = right_dot(c_v[rows, :], wd_v[cols, :])
            sigma = jax.nn.sigmoid(gate)
            silu = gate * sigma
            hid[0, rows, cols] = (silu * upper).astype(BF)
            dhid *= inv
            dg[0, rows, cols] = (dhid * upper * sigma * (1.0 + gate * (1.0 - sigma))).astype(BF)
            du[0, rows, cols] = (dhid * silu).astype(BF)

        chunks(chunk, ff, 256)
        return [
            net.send(ref.at[0, rows, :], ref.at[1, rows, :], CORE) for ref in (hid, dg, du)
        ]

    def back(rows, first_slot, side):
        def chunk(start, size):
            cols = aligned(start + side * half, size, 128)
            total = right_dot(dg[0, rows, :], wg_v[0, cols, :])
            total += right_dot(du[0, rows, :], wg_v[1, cols, :])
            dn_part[pl.ds(first_slot, 2), :, cols] = total.astype(BF).reshape(2, tok, size)

        chunks(chunk, half, 256)

    def piece(side):
        return pl.ds(side * half, half)

    sums.sent()
    for copy in n_near:
        copy.wait_recv()
    c_near.wait_recv()
    for plane in (down, plane_g, plane_u):
        plane.finish()
    own[2].wait()
    sib = front(near)
    dn_b = []
    for side in (0, 1):
        back(near, near_pair * 2, side)
        dn_b.append(
            net.send(
                dn_part.at[zs[1], :, piece(side)], r1.at[side, 0], ("z", 1)
            )
        )
    c_last.wait_recv()
    c_copy = net.send(c_v.at[:, aligned((1 - core) * half, half, 128)], c_sib, CORE)
    for copy in n_last:
        copy.wait_recv()
    n_copies = [
        net.send(
            n_v.at[:, aligned((i * 2 + 1 - core) * 256, 256, 128)],
            n_sib.at[:, pl.ds(i * 256, 256)],
            CORE,
        )
        for i in range(4)
    ]
    sib += front(far)
    dn_a = []
    for side in (0, 1):
        back(far, (1 - near_pair) * 2, side)
        dn_a.append(
            net.send(
                dn_part.at[zs[3], :, piece(side)], r1.at[side, 1], ("z", 1)
            )
        )
    c_copy.wait_recv()
    for copy in sib:
        copy.wait_recv()

    ccols = aligned(core * half, half, 128)

    def down_chunk(start, size):
        cols = aligned(start, size, 128)
        total = left_dot(hid[0, :, cols], c_v[:, ccols])
        total += left_dot(hid[1, :, cols], c_sib[...])
        hd[cols, :] = total.astype(BF)

    chunks(down_chunk, ff, 256)
    chip_rows = ff // 4
    quarter = half // 2

    def hd_at(mask, side):
        return aligned(chip_of(mask) * chip_rows, chip_rows, 16), pl.ds(side * quarter, quarter)

    def hd_send(mask, side, place, name):
        r, c = hd_at(mask, side)
        return net.send(hd.at[r, c], hd_r1.at[side, place], name)

    hd_1 = [hd_send(6, 0, 1, X), hd_send(6, 1, 1, Y), hd_send(2, 0, 0, X), hd_send(4, 1, 0, Y)]
    dn_c = []
    for side in (0, 1):
        dn_a[side].wait_recv()
        cols = piece(side)
        mid[side] = (
            dn_part[zs[2], :, cols].astype(F32) + r1[side, 1].astype(F32)
        ).astype(BF)
        dn_c.append(net.send(mid.at[side], r2.at[side], ("z", 2)))

    for copy in outs:
        copy.wait()
    plane_h.sent()

    def mix_chunk(start, size):
        cols = aligned(start, size, 128)
        hat[:, :, cols] = dot(hid[0], wd_v[:, cols]).astype(BF).reshape(4, tok, size)

    chunks(mix_chunk, width, 256)
    mx_copy = net.local(hat, mx_out)
    mx_a = net.send(hat.at[zs[3]], mx_r, ("z", 1))

    hd_1[0].wait_recv()
    hd_1[1].wait_recv()
    net.sent(gate_copies + up_copies)
    hd_2 = []
    for side, (mask, name) in enumerate(((4, Y), (2, X))):
        r, c = hd_at(mask, side)
        k = pl.ds(side * quarter, quarter)
        wf[:chip_rows, k] = (hd[r, c].astype(F32) + hd_r1[side, 1].astype(F32)).astype(BF)
        hd_2.append(net.send(wf.at[pl.ds(0, chip_rows), k], hd_r2.at[side], name))

    for copy in n_copies:
        copy.wait_recv()
    plane_g.sent()
    plane_u.sent()

    def block(b, carry):
        cols = aligned((b * 2 + core) * 256, 256, 128)
        left = n_v[:, cols].T
        other = n_sib[:, aligned(b * 256, 256, 128)].T
        for t, grad in enumerate((dg, du)):
            total = dot(left, grad[0]) + dot(other, grad[1])
            wg_v[t, aligned(b * 256, 256, 16), :] = total.astype(BF)
        return carry

    lax.fori_loop(0, 4, block, 0)
    hg_copy = net.local(wg_v.at[:, pl.ds(0, 1024), :], hg_out)
    for side in (0, 1):
        dn_b[side].wait_recv()
        dn_c[side].wait_recv()
        cols = piece(side)
        dn_out[:, cols] = (
            dn_part[z, :, cols].astype(F32)
            + r1[side, 0].astype(F32)
            + r2[side].astype(F32)
        )
    mx_a.wait_recv()
    net.sent(dn_c)
    far_copies = []
    for side in (0, 1):
        cols = piece(side)
        mid[side] = (hat[zs[2], :, cols].astype(F32) + mx_r[:, cols].astype(F32)).astype(BF)
        far_copies.append(net.local(mid.at[side], mx_far.at[:, cols]))
    hd_1[2].wait_recv()
    hd_1[3].wait_recv()
    rows_half = chip_rows // 2
    for side in (0, 1):
        hd_2[side].wait_recv()

        def total(start):
            _, c = hd_at(0, side)
            return (
                hd[aligned(chip * chip_rows + start, rows_half, 16), c].astype(F32)
                + hd_r1[side, 0, aligned(start, rows_half, 16), :].astype(F32)
                + hd_r2[side, aligned(start, rows_half, 16), :].astype(F32)
            )

        net.sent([hd_2[side]])
        k = pl.ds(side * quarter, quarter)
        wf[:rows_half, k] = total((1 - core) * rows_half).astype(BF)
        gdown[:, aligned(core * half + side * quarter, quarter, 128)] = total(core * rows_half)
    last = net.send(wf.at[pl.ds(0, rows_half), pl.ds(0, half)], sib_r, CORE)
    last.wait_recv()
    gdown[:, aligned((1 - core) * half, half, 128)] = sib_r[...].astype(F32)
    hg_copy.wait()
    mx_copy.wait()
    for copy in far_copies:
        copy.wait()
    net.finish()


def first_call(x, wq, wk, wv, gain1, w_gate, w_up, gain2, tables4, wo, wd, cot):
    tok, width = x.shape
    ff = w_gate.shape[1] // 4
    span = width // 4
    group = span + 128
    sds = jax.ShapeDtypeStruct
    v = pltpu.VMEM
    half = width // 2
    return pl.pallas_call(
        first_kernel,
        name="first",
        out_shape=[
            sds((4, 2, 4, 64, group), BF), sds((2, 4, 64, width), BF), sds((4, tok, width), BF),
            sds((4 * tok, group), BF), sds((4, tok, span), BF), sds((4, tok, width), BF),
            sds((tok, width), BF), sds((2, 1024, ff), BF), sds((4 * tok, 128), F32), sds((tok, width), F32),
            sds((tok, width), F32), sds((ff // 8, width), F32),
        ],
        in_specs=[VMEM] * 5 + [ANY] * 2 + [VMEM] * 5 + [ANY] * 3,
        out_specs=[ANY] * 8 + [VMEM] * 4,
        scratch_shapes=[
            v((4, 64, group), BF), v((512, ff), BF), v((4, 2, 4, 64, group), BF),
            v((2, 4, 64, width), BF), v((4, tok, width), BF), v((4, tok, group), BF),
            v((4 * tok, group), BF), v((4 * tok, span), BF), v((4, tok, span), BF),
            v((4, tok, width), BF), v((2, 2, tok, half), BF), v((2, tok, half), BF),
            v((2, tok, half), BF),
            v((2, width, ff), BF), v((ff, width), BF), v((4 * tok, width), BF),
            v((4 * tok, half), BF), v((4 * tok, width), BF), v((4 * tok, half), BF),
            v((2, 4 * tok, ff), BF), v((2, 4 * tok, ff), BF), v((2, 4 * tok, ff), BF),
            v((tok, width), BF), v((ff, half), BF),
            v((2, 2, ff // 4, half // 2), BF), v((2, ff // 4, half // 2), BF),
            v((ff // 8, half), BF),
            pltpu.SemaphoreType.DMA((144,)),
            pltpu.SemaphoreType.DMA((144,)),
        ],
        compiler_params=pltpu.CompilerParams(
            collective_id=1, has_side_effects=True, vmem_limit_bytes=62 * 2**20
        ),
    )(x, wq, wk, wv, gain1, w_gate, w_up, gain2, *tables4, wo, wd, cot)


def third_kernel(
    hmid, cot, dn2, cos_q, sin_q, cos_k, sin_k,
    x_in, qkv_in, lse_in, mx, mx_far, wq, wo, hat, att, hg,
    tok_out, mixed, g2_out, g1_out, fb,
    x_ref, qkv, lse, wq_v, wo_v, hat_v, hat_s, att_v, att_s, mx_v, mx_r1, mx_r2,
    hg_v, f_r1, f_k, f_r2, fs, dh, dbr, dbr_s, dsend, gh, dqkv, dk_acc, dv_acc, dback,
    dpre, dpre_s, part, r1, mid, r2, g2_p, g2_r1, g2_s, g2_r2, g1_p, g1_r1, g1_s, g1_r2, g1_f,
    send_sems, recv_sems,
):
    net = Net(send_sems, recv_sems)
    dp, z, dps, zs = net.dp, net.z, net.dps, net.zs
    tok, width = x_ref.shape
    group = qkv.shape[1]
    span = group - 128
    here = aligned(z * tok, tok, 16)
    core, chip = lax.rem(dp, 2), lax.div(dp, 2)

    def chip_of(mask):
        return lax.div(dps[mask], 2)

    def slot(mask):
        return aligned(zs[mask] * tok, tok, 16)

    def hg_at(t, mask, side):
        return hg.at[t, aligned(chip_of(mask) * 256 + side * 128, 128, 16), :]

    loads = [
        net.local(wo, wo_v),
        net.local(hg.at[:, aligned(chip * 256, 256, 16), :], hg_v.at[0]),
        net.local(hg.at[:, aligned(chip_of(4) * 256, 128, 16), :], hg_v.at[1, :, pl.ds(0, 128)]),
        net.local(
            hg.at[:, aligned(chip_of(2) * 256 + 128, 128, 16), :], hg_v.at[1, :, pl.ds(128, 128)]
        ),
        net.local(mx.at[z], mx_v),
        net.local(att, att_v),
        net.local(wq, wq_v),
        net.local(hat, hat_v),
        net.local(x_in, x_ref),
        net.local(qkv_in, qkv),
        net.local(lse_in, lse),
    ]
    net.barrier(PARTNERS + [("d", 6)])
    def f_send(t, place, mask, side, name):
        return net.send(hg_at(t, mask, side), f_r1.at[place, t, pl.ds(side * 128, 128)], name)

    def f_near(t):
        return [f_send(t, 1, 6, 0, X), f_send(t, 1, 6, 1, Y)]

    def f_own(t):
        return [f_send(t, 0, 2, 0, X), f_send(t, 0, 4, 1, Y)]

    def f_second(t, sent):
        for copy in sent:
            copy.wait_recv()
        f_k[t] = (hg_v[1, t].astype(F32) + f_r1[1, t].astype(F32)).astype(BF)
        return [
            net.send(f_k.at[t, pl.ds(side * 128, 128)], f_r2.at[t, pl.ds(side * 128, 128)], name)
            for side, name in ((0, Y), (1, X))
        ]

    own_f = []

    def f_rows(t, sent):
        for copy in sent:
            copy.wait_recv()
        total = hg_v[0, t].astype(F32) + f_r1[0, t].astype(F32) + f_r2[t].astype(F32)
        for i in range(4):
            fs[i, t] = total[i * 64 : (i + 1) * 64, :].astype(BF)
        own_f.append(net.local(fs.at[z, t], fb.at[z, t]))
        return [net.send(fs.at[zs[m], t], fb.at[z, t], ("z", m)) for m in (2, 3, 1)]

    gate_1 = f_near(0)
    mx_copies = [
        net.send(mx_far, mx_r2, ("z", 2)),
        net.send(mx.at[zs[1]], mx_r1, ("z", 1)),
    ]
    half = width // 2

    def norm_back(value, grad):
        inv = rms(value)
        inner = jnp.mean(value * grad, axis=-1, keepdims=True)
        return inv * grad - value * (inv * inv * inv * inner)

    value, grad = hmid[...], dn2[...]
    inv = rms(value)
    inner = jnp.mean(value * grad, axis=-1, keepdims=True)
    dh[...] = cot[...].astype(F32) + grad - value * (inv * inv * inner)
    dbr[chip] = dh[...].astype(BF)
    plane_b = Plane(net, lambda m, s: dbr.at[chip_of(m), :, pl.ds(s * half, half)], lambda m: [])
    plane_b.start()
    small = [
        net.send(att.at[:, :, aligned((1 - core) * 256, 256, 128)], att_s, CORE)
    ] + [
        net.send(
            hat.at[:, :, aligned(i * 512 + (1 - core) * 256, 256, 128)],
            hat_s.at[:, :, pl.ds(i * 256, 256)],
            CORE,
        )
        for i in range(4)
    ]
    plane_b.forward()
    for copy in loads[1:4]:
        copy.wait()
    gate_2 = f_second(0, gate_1) + f_own(0)
    up_1 = f_near(1)
    up_2 = f_own(1)
    plane_b.spread()
    loads[0].wait()
    weight = wo_v[...].reshape(span, width)
    dsend[...] = (
        right_dot(dbr[...].reshape(4 * tok, width), weight).astype(BF).reshape(4, tok, span)
    )
    d_copies = [net.send(dsend.at[zs[m]], gh.at[here, :], ("z", m)) for m in (2, 3, 1)]
    gh[here, :] = dsend[z]
    dbr_copy = net.send(dbr, dbr_s, CORE)
    for copy in loads[4:]:
        copy.wait()

    class Line:
        def __init__(self, parts, r1, s, r2):
            self.parts, self.r1, self.s, self.r2 = parts, r1, s, r2
            self.sent = [
                net.send(parts.at[zs[3]], r1.at[1], ("z", 1)),
                net.send(parts.at[zs[1]], r1.at[0], ("z", 1)),
            ]

        def middle(self):
            self.sent[0].wait_recv()
            self.s[...] = (self.parts[zs[2]].astype(F32) + self.r1[1].astype(F32)).astype(BF)
            self.far = net.send(self.s, self.r2, ("z", 2))

        def total(self):
            self.sent[1].wait_recv()
            self.far.wait_recv()
            own = self.parts[z].astype(F32) + self.r1[0].astype(F32)
            return own + self.r2[...].astype(F32)

    small[0].wait_recv()
    dbr_copy.wait_recv()
    mine = att_v[:, :, aligned(core * 256, 256, 128)].reshape(4 * tok, 256).T
    theirs = att_s[...].reshape(4 * tok, 256).T

    def out_chunk(i, carry):
        cols = aligned(i * 512, 512, 128)
        total = dot(mine, dbr[:, :, cols].reshape(4 * tok, 512))
        total += dot(theirs, dbr_s[:, :, cols].reshape(4 * tok, 512))
        g2_p[:, :, cols] = total.astype(BF).reshape(4, 64, 512)
        return carry

    lax.fori_loop(0, width // 512, out_chunk, 0)
    line_o = Line(g2_p, g2_r1, g2_s, g2_r2)

    for copy in d_copies:
        copy.wait_recv()
    f_copies = f_rows(0, gate_2)

    scale = HEAD_SIZE ** (-0.5)
    kk, vv = twice(qkv[:, span:])
    dk_acc[...] = jnp.zeros_like(dk_acc)
    dv_acc[...] = jnp.zeros_like(dv_acc)

    def pair(p, carry):
        cols = aligned(p * 128, 128, 128)
        for qb in range(4):
            keys = (qb + 1) * tok
            rows = slice(qb * tok, (qb + 1) * tok)
            q = qkv[rows, cols]
            g = gh[rows, cols]
            lane = lax.broadcasted_iota(jnp.int32, (tok, 128), 1)
            row = lax.rem(lax.broadcasted_iota(jnp.int32, (2 * tok, keys), 0), tok) + qb * tok
            col = lax.broadcasted_iota(jnp.int32, (2 * tok, keys), 1)
            none = jnp.zeros_like(q)

            def both(value):
                return jnp.concatenate(
                    [jnp.where(lane < 64, value, none), jnp.where(lane >= 64, value, none)], axis=0
                )

            qq, gg = both(q), both(g)
            logs = lse[rows, :]
            log = jnp.concatenate(
                [
                    jnp.sum(jnp.where(lane == 2 * p + h, logs, 0.0), axis=-1, keepdims=True)
                    for h in range(2)
                ],
                axis=0,
            )
            s = right_dot(qq, kk[:keys]) * scale
            probs = jnp.exp(jnp.where(col <= row, s, -1e30) - log)
            pg = right_dot(gg, vv[:keys])
            delta = jnp.sum(probs * pg, axis=-1, keepdims=True)
            ds = (probs * (pg - delta)).astype(BF)
            out = dot(ds, kk[:keys]) * scale
            dk_acc[:keys, :] += left_dot(ds, qq)
            dv_acc[:keys, :] += left_dot(probs.astype(BF), gg)
            dqkv[rows, cols] = jnp.where(lane < 64, out[:tok], out[tok:]).astype(BF)
        return carry

    def send_back(start, count):
        cols = pl.ds(start, count)
        return [net.send(dqkv.at[slot(m), cols], dback.at[z, :, cols], ("z", m)) for m in (2, 3, 1)]

    lax.fori_loop(0, 2, pair, 0)
    b_copies = send_back(0, 256)
    lax.fori_loop(2, 4, pair, 0)
    dk = dk_acc[...]
    dv = dv_acc[...]
    lane = lax.broadcasted_iota(jnp.int32, dk.shape, 1)
    dqkv[:, span:] = jnp.where(
        lane < 64, (dk + pltpu.roll(dk, 64, 1)) * scale, dv + pltpu.roll(dv, 64, 1)
    ).astype(BF)
    b_copies += send_back(256, group - 256)
    dback[z] = dqkv[here, :]
    line_o.middle()

    up_2 += f_second(1, up_1)
    for copy in b_copies:
        copy.wait_recv()
    for s in range(4):
        for j in range(group // 128):
            cols = slice(j * 128, (j + 1) * 128)
            last = j == group // 128 - 1
            c_ref, s_ref = (cos_k, sin_k) if last else (cos_q, sin_q)
            value = dback[s, :, cols].astype(F32)
            dpre[s, :, cols] = rotary(value, c_ref[...], -s_ref[...]).astype(BF)
    dpre_copy = net.send(dpre, dpre_s, CORE)

    left = dpre[...].reshape(4 * tok, group)

    def dhat_chunk(i, carry):
        cols = aligned(i * 256, 256, 128)
        rows = wq_v[lax.div(i, 2), lax.rem(i, 2)].reshape(256, group)
        part[:, :, cols] = right_dot(left, rows).astype(BF).reshape(4, tok, 256)
        return carry

    lax.fori_loop(0, width // 256, dhat_chunk, 0)
    sums = Sums(net, part, r1, mid, r2)
    sums.first()

    for copy in small[1:]:
        copy.wait_recv()
    dpre_copy.wait_recv()
    right = dpre_s[...].reshape(4 * tok, group)

    def first_chunk(i, carry):
        own = hat_v[:, :, aligned(i * 512 + core * 256, 256, 128)].reshape(4 * tok, 256).T
        sib = hat_s[:, :, aligned(i * 256, 256, 128)].reshape(4 * tok, 256).T
        total = dot(own, left) + dot(sib, right)
        g1_p[:, i] = total.astype(BF).reshape(4, 64, group)
        return carry

    lax.fori_loop(0, 4, first_chunk, 0)
    line_q = Line(g1_p, g1_r1, g1_s, g1_r2)
    f_copies += f_rows(1, up_2)
    sums.second()
    line_q.middle()
    for copy in mx_copies:
        copy.wait_recv()
    total = mx_v[...].astype(F32) + mx_r1[...].astype(F32) + mx_r2[...].astype(F32)
    mixed[...] = (hmid[...] + total).astype(BF)
    g2_out[...] = line_o.total()
    for side in (0, 1):
        dn2[:, side * half : (side + 1) * half] = sums.total(side)
    tok_out[...] = (dh[...] + norm_back(x_ref[...].astype(F32), dn2[...])).astype(BF)
    g1_f[...] = line_q.total().astype(BF)
    g_copies = [net.send(g1_f.at[chip_of(m)], g1_out.at[chip], ("d", m)) for m in (6, 2, 4)]
    g1_out[chip] = g1_f[chip]
    for copy in g_copies + f_copies:
        copy.wait_recv()
    for copy in own_f:
        copy.wait()
    net.finish()


def third_call(x, hmid, cot, dn2, qkv, lse, tables4, mx, mx_far, wq, wo, hat, att, hg):
    tok, width = x.shape
    group = qkv.shape[1]
    span = group - 128
    ff = hg.shape[-1]
    sds = jax.ShapeDtypeStruct
    v = pltpu.VMEM
    return pl.pallas_call(
        third_kernel,
        name="third",
        out_shape=[
            sds((tok, width), BF), sds((tok, width), BF), sds((64, width), F32),
            sds((4, 64, group), BF), sds((4, 2, 64, ff), BF),
        ],
        in_specs=[VMEM] * 7 + [ANY] * 10,
        out_specs=[VMEM] * 4 + [ANY],
        scratch_shapes=[
            v((tok, width), BF), v((4 * tok, group), BF), v((4 * tok, 128), F32),
            v((4, 2, 4, 64, group), BF), v((2, 4, 64, width), BF), v((4, tok, width), BF),
            v((4, tok, width // 2), BF), v((4, tok, span), BF), v((4, tok, span // 2), BF),
            v((tok, width), BF), v((tok, width), BF), v((tok, width), BF),
            v((2, 2, 256, ff), BF), v((2, 2, 256, ff), BF), v((2, 256, ff), BF), v((2, 256, ff), BF),
            v((4, 2, 64, ff), BF), v((tok, width), F32), v((4, tok, width), BF),
            v((4, tok, width), BF), v((4, tok, span), BF), v((4 * tok, span), BF),
            v((4 * tok, group), BF), v((4 * tok, 128), F32), v((4 * tok, 128), F32),
            v((4, tok, group), BF), v((4, tok, group), BF), v((4, tok, group), BF),
            v((4, tok, width), BF), v((2, 2, tok, width // 2), BF), v((2, tok, width // 2), BF),
            v((2, tok, width // 2), BF),
            v((4, 64, width), BF), v((2, 64, width), BF), v((64, width), BF), v((64, width), BF),
            v((4, 4, 64, group), BF), v((2, 4, 64, group), BF), v((4, 64, group), BF),
            v((4, 64, group), BF), v((4, 64, group), BF),
            pltpu.SemaphoreType.DMA((80,)),
            pltpu.SemaphoreType.DMA((80,)),
        ],
        compiler_params=pltpu.CompilerParams(
            collective_id=3, has_side_effects=True, vmem_limit_bytes=60 * 2**20
        ),
    )(hmid, cot, dn2, *tables4, x, qkv, lse, mx, mx_far, wq, wo, hat, att, hg)


def last_kernel(
    fb, g1, wq, wk, wv, gain1, gain2, w_gate_in, w_up_in, tok_in, mixed_in, g2_in, gd_in,
    gq, gk, gv, g_gate, g_up, g_gain1, g_gain2, tok_out, mixed_out, g2_out, gd_out,
    w_gate, w_up, sems,
):
    copies = [
        pltpu.make_async_copy(src, dst, sems.at[i])
        for i, (src, dst) in enumerate(
            (
                (w_gate_in, w_gate), (w_up_in, w_up), (tok_in, tok_out),
                (mixed_in, mixed_out), (g2_in, g2_out), (gd_in, gd_out),
            )
        )
    ]
    for copy in copies:
        copy.start()
    span = g1.shape[2] - 128
    lane = lax.broadcasted_iota(jnp.int32, (g1.shape[1], 128), 1)
    scale = column(gain1[...])
    scale2 = column(gain2[...])

    def put(out, weight, cols, value):
        out[:, cols] = value * scale
        return jnp.sum(value * weight[:, cols].astype(F32), axis=1, keepdims=True)

    total = jnp.zeros((g1.shape[1], 1), F32)
    for g in range(4):
        total += put(gq, wq, slice(g * span, (g + 1) * span), g1[g, :, :span].astype(F32))
    for g in (0, 2):
        one = g1[g, :, span:].astype(F32)
        two = g1[g + 1, :, span:].astype(F32)
        cols = slice(g * 64, g * 64 + 128)
        total += put(gk, wk, cols, jnp.where(lane < 64, one, pltpu.roll(two, 64, 1)))
        total += put(gv, wv, cols, jnp.where(lane < 64, pltpu.roll(one, 64, 1), two))
    g_gain1[...] = line(total)
    size = fb.shape[-1] // 8
    total = jnp.zeros((g1.shape[1], 1), F32)
    for t, (out, weight) in enumerate(((g_gate, w_gate), (g_up, w_up))):
        copies[t].wait()
        for d in range(0, 8, 2):
            parts = [
                fb[i, t, :, e * size : (e + 1) * size].astype(F32) for e in (d, d + 1) for i in range(4)
            ]
            joined = jnp.concatenate(parts, axis=1)
            cols = pl.ds(d * 4 * size, 8 * size)
            total += jnp.sum(joined * weight[:, cols].astype(F32), axis=1, keepdims=True)
            out[:, cols] = joined * scale2
    g_gain2[...] = line(total)
    for copy in copies[2:]:
        copy.wait()


def last_call(fb, g1, wq, wk, wv, gain1, gain2, w_gate, w_up, tok, mixed, g2, gd):
    rows, ff = w_gate.shape
    sds = jax.ShapeDtypeStruct
    return pl.pallas_call(
        last_kernel,
        name="last",
        out_shape=[
            sds(wq.shape, F32), sds(wk.shape, F32), sds(wv.shape, F32),
            sds((rows, ff), F32), sds((rows, ff), F32), sds((1, rows), F32), sds((1, rows), F32),
            sds(tok.shape, BF), sds(mixed.shape, BF), sds(g2.shape, F32), sds(gd.shape, F32),
        ],
        in_specs=[VMEM] * 7 + [ANY] * 6,
        out_specs=[VMEM] * 11,
        scratch_shapes=[
            pltpu.VMEM((rows, ff), BF), pltpu.VMEM((rows, ff), BF), pltpu.SemaphoreType.DMA((6,)),
        ],
        compiler_params=pltpu.CompilerParams(vmem_limit_bytes=60 * 2**20),
    )(fb, g1, wq, wk, wv, gain1, gain2, w_gate, w_up, tok, mixed, g2, gd)


def shards(
    tokens, norm_first, w_query, w_key, w_value, w_out, norm_second, w_gate, w_up, w_down, cotangent
):
    count = tokens.shape[0]
    gain1, gain2 = norm_first[None, :], norm_second[None, :]
    cosine, sine = tables(lax.axis_index("seq") * count + jnp.arange(count))
    cosine, sine = cosine[:, 0], sine[:, 0]
    one, zero = jnp.ones_like(cosine), jnp.zeros_like(cosine)
    tables4 = [
        jnp.concatenate(parts, axis=1)
        for parts in (
            [cosine] * 4,
            [-sine, sine] * 2,
            [cosine, cosine, one, one],
            [-sine, sine, zero, zero],
        )
    ]
    wq, wo, hat, qkv, att, mixed_part, mixed_far, hg, lse, hmid, dhat2, grad_down = first_call(
        tokens, w_query, w_key, w_value, gain1, w_gate, w_up, gain2, tables4,
        w_out, w_down, cotangent,
    )
    grad_tokens, mixed, grad_out, grad_first, parts = third_call(
        tokens, hmid, cotangent, dhat2, qkv, lse, tables4, mixed_part, mixed_far,
        wq, wo, hat, att, hg,
    )
    (
        grad_query, grad_key, grad_value, grad_gate, grad_up, grad_gain1, grad_gain2,
        grad_tokens, mixed, grad_out, grad_down,
    ) = last_call(
        parts, grad_first, w_query, w_key, w_value, gain1, gain2, w_gate, w_up,
        grad_tokens, mixed, grad_out, grad_down,
    )
    return (
        mixed,
        grad_tokens,
        grad_gain1[0],
        grad_query,
        grad_key,
        grad_value,
        grad_out,
        grad_gain2[0],
        grad_gate,
        grad_up,
        grad_down,
    )


def solution(mesh):
    special = mesh.shape['dp'] == 8 and mesh.shape['seq'] == KEY_VALUE_HEADS
    rows = P(("dp", "seq"), None)
    line = P(("dp", "seq"))
    return jax.shard_map(
        shards if special else general_shards,
        mesh=mesh,
        in_specs=(rows, line, rows, rows, rows, rows, line, rows, rows, rows, rows),
        out_specs=(rows, rows, line, rows, rows, rows, rows, line, rows, rows, rows),
        check_vma=False,
    )
```

```python
import jax
import jax.numpy as jnp
from jax import lax
from jax.experimental import pallas as pl
from jax.experimental.pallas import tpu as pltpu
from jax.sharding import PartitionSpec as P

H = 32
KEY_VALUE_HEADS = 4
HEAD_SIZE = 64
EPS = 1e-05
BF = jnp.bfloat16
F32 = jnp.float32


def tables(positions):
    freq = 10000.0 ** (-jnp.arange(0, HEAD_SIZE // 2, dtype=F32) * 2.0 / HEAD_SIZE)
    angle = positions.astype(F32)[:, None] * freq[None, :]
    return (jnp.cos(angle)[:, None, :], jnp.sin(angle)[:, None, :])


def rotate(heads, cosine, sine):
    half = heads.shape[-1] // 2
    first = heads[..., :half]
    second = heads[..., half:]
    return jnp.concatenate(
        [first * cosine - second * sine, second * cosine + first * sine], axis=-1
    )


def dot(left, right):
    return jnp.dot(left, right, preferred_element_type=F32)


def left_dot(left, right):
    return lax.dot_general(left, right, (((0,), (0,)), ((), ())), preferred_element_type=F32)


def right_dot(left, right):
    return lax.dot_general(left, right, (((1,), (1,)), ((), ())), preferred_element_type=F32)


def bits_of(count):
    return [1 << k for k in range(count.bit_length() - 1)]


class Axis:
    def __init__(self, name):
        self.name = name
        self.size = lax.axis_size(name)
        self.me = lax.axis_index(name)

    def swap(self, value, mask):
        return lax.ppermute(value, self.name, [(i, i ^ mask) for i in range(self.size)])

    def all(self, value):
        return [value if m == 0 else self.swap(value, m) for m in range(self.size)]

    def exchange(self, stacked):
        return [
            lax.dynamic_index_in_dim(stacked, self.me ^ m, 0, keepdims=False)
            if m == 0
            else self.swap(
                lax.dynamic_index_in_dim(stacked, self.me ^ m, 0, keepdims=False), m
            )
            for m in range(self.size)
        ]

    def natural(self, pieces):
        stack = jnp.stack(pieces)
        return [
            lax.dynamic_index_in_dim(stack, self.me ^ i, 0, keepdims=False)
            for i in range(self.size)
        ]


def orders(size):
    even = [m for m in range(size) if m % 2 == 0]
    return even, [m + 1 for m in even]


def chip_bits(size, turn):
    bits = bits_of(size)[1:]
    return bits if turn == 0 else bits[::-1]


def gather_chips(dp, piece, turn):
    pieces = {0: piece}
    for bit in chip_bits(dp.size, turn):
        pieces.update({m ^ bit: dp.swap(p, bit) for m, p in list(pieces.items())})
    return pieces


def gather_rows(dp, piece, turn):
    pieces = gather_chips(dp, piece, turn)
    even = jnp.concatenate([pieces[m] for m in orders(dp.size)[0]], axis=0)
    return even, dp.swap(even, 1)


def scatter_chips(dp, blocks, turn):
    for bit in chip_bits(dp.size, turn):
        for m in [m for m in blocks if m & bit]:
            other = dp.swap(blocks.pop(m).astype(BF), bit)
            blocks[m ^ bit] = blocks[m ^ bit].astype(F32) + other.astype(F32)
    return blocks[0]


def scatter_rows(dp, even_fn, odd, turn):
    rows = odd.shape[0] * 2 // dp.size
    other = dp.swap(odd, 1)
    even = (even_fn() + other.astype(F32)).astype(BF)
    blocks = {
        m: even[i * rows : (i + 1) * rows] for i, m in enumerate(orders(dp.size)[0])
    }
    return scatter_chips(dp, blocks, turn)


def mask_columns(dp, value):
    width = value.shape[1] // dp.size
    return tuple(
        jnp.concatenate(
            [lax.dynamic_slice_in_dim(value, (dp.me ^ m) * width, width, 1) for m in group],
            axis=1,
        )
        for group in orders(dp.size)
    )


def natural_columns(dp, even, odd):
    both = jnp.concatenate([even, odd], axis=1)
    width = both.shape[1] // dp.size
    half = dp.size // 2
    parts = []
    for i in range(dp.size):
        mask = dp.me ^ i
        place = mask // 2 + (mask % 2) * half
        parts.append(lax.dynamic_slice_in_dim(both, place * width, width, 1))
    return jnp.concatenate(parts, axis=1)


def attend(queries, keys, values, visible):
    scores = jnp.einsum("qhd,kd->hqk", queries, keys, preferred_element_type=F32)
    scores = jnp.where(visible[None], scores * HEAD_SIZE ** (-0.5), -1e30)
    top = jnp.max(scores, axis=-1, keepdims=True)
    expo = jnp.exp(scores - top)
    total = jnp.sum(expo, axis=-1, keepdims=True)
    probs = (expo / total).astype(BF)
    result = jnp.einsum("hqk,kd->qhd", probs, values, preferred_element_type=F32)
    return result.astype(BF), top + jnp.log(total)


def attend_back(queries, keys, values, grad_heads, logsum, visible):
    scale = HEAD_SIZE ** (-0.5)
    scores = jnp.einsum("qhd,kd->hqk", queries, keys, preferred_element_type=F32)
    scores = jnp.where(visible[None], scores * scale, -1e30)
    probs = jnp.exp(scores - logsum)
    pgrad = jnp.einsum("qhd,kd->hqk", grad_heads, values, preferred_element_type=F32)
    delta = jnp.sum(probs * pgrad, axis=-1, keepdims=True)
    sgrad = (probs * (pgrad - delta)).astype(BF)
    qgrad = jnp.einsum("hqk,kd->qhd", sgrad, keys, preferred_element_type=F32) * scale
    kgrad = jnp.einsum("hqk,qhd->kd", sgrad, queries, preferred_element_type=F32) * scale
    vgrad = jnp.einsum("hqk,qhd->kd", probs.astype(BF), grad_heads, preferred_element_type=F32)
    return qgrad.astype(BF), kgrad.astype(BF), vgrad.astype(BF)


def general_shards(
    tokens, norm_first, w_query, w_key, w_value, w_out, norm_second, w_gate, w_up, w_down, cotangent
):
    dp, seq = Axis("dp"), Axis("seq")
    groups = seq.size
    count, width = tokens.shape
    ff = w_gate.shape[1]
    per = H // groups
    repeat = groups // KEY_VALUE_HEADS
    heads_wide = H * HEAD_SIZE
    keys_wide = KEY_VALUE_HEADS * HEAD_SIZE
    gain1 = norm_first.astype(F32)[:, None]
    gain2 = norm_second.astype(F32)[:, None]

    w_first = jnp.concatenate([w_query, w_key, w_value], axis=1)
    w_first_scaled = (w_first.astype(F32) * gain1).astype(BF)
    wide = w_first.shape[1]

    def by_part(weight):
        rows = weight.shape[0]
        scaled = (weight.astype(F32) * gain2).astype(BF)
        parts = scaled.reshape(rows, dp.size, groups, ff // dp.size // groups)
        return parts.transpose(2, 0, 1, 3).reshape(groups, rows, ff // groups)

    down = [gather_chips(dp, w_down[:, t * width // 2 : (t + 1) * width // 2], t) for t in (0, 1)]
    first_rows = jnp.concatenate(seq.natural(seq.all(w_first_scaled)), axis=0)
    first = [gather_rows(dp, first_rows[:, t * wide // 2 : (t + 1) * wide // 2], t) for t in (0, 1)]
    out_rows = jnp.concatenate(seq.natural(seq.all(w_out)), axis=0)
    outw = [gather_rows(dp, out_rows[:, t * width // 2 : (t + 1) * width // 2], t) for t in (0, 1)]
    gate_up = seq.exchange(jnp.stack([by_part(w_gate), by_part(w_up)], axis=1))
    gate_up = jnp.concatenate(seq.natural(gate_up), axis=1)
    (gate_even, gate_odd), (up_even, up_odd) = [
        gather_rows(dp, gate_up[t], t) for t in (0, 1)
    ]
    cot_all = jnp.concatenate(seq.all(cotangent), axis=0)

    rows_down = w_down.shape[0]
    down_full = []
    for t in (0, 1):
        even = jnp.stack([down[t][m] for m in orders(dp.size)[0]])
        odd = dp.swap(even, 1)
        full = jnp.zeros((rows_down * dp.size, width // 2), BF)
        for i, m in enumerate(orders(dp.size)[0]):
            full = lax.dynamic_update_slice(full, even[i], ((dp.me ^ m) * rows_down, 0))
            full = lax.dynamic_update_slice(full, odd[i], ((dp.me ^ m ^ 1) * rows_down, 0))
        down_full.append(full)

    inputs = tokens.astype(F32)
    inv1 = lax.rsqrt(jnp.mean(inputs * inputs, axis=-1, keepdims=True) + EPS)
    hat1 = (inputs * inv1).astype(BF)
    hat1_even, hat1_odd = mask_columns(dp, hat1)
    cosine, sine = tables(seq.me * count + jnp.arange(count))
    pre = jnp.concatenate(
        [dot(hat1_even, first[t][0]) + dot(hat1_odd, first[t][1]) for t in (0, 1)], axis=1
    )
    qpre = pre[:, :heads_wide].reshape(count, H, HEAD_SIZE)
    kpre = pre[:, heads_wide : heads_wide + keys_wide].reshape(count, KEY_VALUE_HEADS, HEAD_SIZE)
    vround = pre[:, heads_wide + keys_wide :].astype(BF)
    qrot = rotate(qpre, cosine, sine).reshape(count, heads_wide).astype(BF)
    krot = rotate(kpre, cosine, sine).reshape(count, keys_wide).astype(BF)
    span = per * HEAD_SIZE
    packed = []
    for g in range(groups):
        head = g // repeat * HEAD_SIZE
        packed.append(
            jnp.concatenate(
                [
                    qrot[:, g * span : (g + 1) * span],
                    krot[:, head : head + HEAD_SIZE],
                    vround[:, head : head + HEAD_SIZE],
                ],
                axis=1,
            )
        )
    qkv = jnp.concatenate(seq.exchange(jnp.stack(packed)), axis=0)
    length = qkv.shape[0]
    queries = qkv[:, :span].reshape(length, per, HEAD_SIZE)
    keys = qkv[:, span : span + HEAD_SIZE]
    values = qkv[:, span + HEAD_SIZE :]
    place = jnp.concatenate(
        [(seq.me ^ m) * count + jnp.arange(count, dtype=jnp.int32) for m in range(groups)]
    )
    visible = place[None, :] <= place[:, None]
    out_heads, logsum = attend(queries, keys, values, visible)
    out_heads = out_heads.reshape(length, span)

    def back_home(value):
        return seq.natural(
            [
                value[:count] if m == 0 else seq.swap(value[m * count : (m + 1) * count], m)
                for m in range(groups)
            ]
        )

    attn = jnp.concatenate(back_home(out_heads), axis=1)
    attn_even, attn_odd = mask_columns(dp, attn)
    branch = jnp.concatenate(
        [dot(attn_even, outw[t][0]) + dot(attn_odd, outw[t][1]) for t in (0, 1)], axis=1
    )
    hmid = inputs + branch

    inv2 = lax.rsqrt(jnp.mean(hmid * hmid, axis=-1, keepdims=True) + EPS)
    hat2 = jnp.concatenate(mask_columns(dp, (hmid * inv2).astype(BF)), axis=1)
    hat2_all = jnp.concatenate(seq.all(hat2), axis=0)
    hat2_even, hat2_odd = hat2_all[:, : width // 2], hat2_all[:, width // 2 :]
    gate = dot(hat2_even, gate_even) + dot(hat2_odd, gate_odd)
    upper = dot(hat2_even, up_even) + dot(hat2_odd, up_odd)
    sigma = jax.nn.sigmoid(gate)
    hidden = (gate * sigma * upper).astype(BF)
    halves = [cot_all[:, : width // 2], cot_all[:, width // 2 :]]
    dhidden = right_dot(halves[0], down_full[0]) + right_dot(halves[1], down_full[1])
    dgate = (dhidden * upper * sigma * (1.0 + gate * (1.0 - sigma))).astype(BF)
    dupper = (dhidden * gate * sigma).astype(BF)
    dhat2 = jnp.concatenate(
        [
            right_dot(dgate, gate_even) + right_dot(dupper, up_even),
            right_dot(dgate, gate_odd) + right_dot(dupper, up_odd),
        ],
        axis=1,
    ).astype(BF)

    def sum_home(value):
        total = value[:count].astype(F32)
        for m in range(1, groups):
            total = total + seq.swap(value[m * count : (m + 1) * count], m).astype(F32)
        return total

    dhat2 = sum_home(dhat2)
    dgain2 = natural_columns(dp, dhat2[:, : width // 2], dhat2[:, width // 2 :])
    inner = jnp.mean(hmid * dgain2, axis=-1, keepdims=True)
    dh = cotangent.astype(F32) + inv2 * dgain2 - hmid * inv2 * inv2 * inv2 * inner
    dbranch = dh.astype(BF)

    dattn = natural_columns(
        dp,
        *[
            sum(
                right_dot(dbranch[:, t * width // 2 : (t + 1) * width // 2], outw[t][s])
                for t in (0, 1)
            ).astype(BF)
            for s in (0, 1)
        ],
    )
    grad_heads = jnp.concatenate(
        seq.exchange(dattn.reshape(count, groups, span).transpose(1, 0, 2)), axis=0
    ).reshape(length, per, HEAD_SIZE)
    dq, dk, dv = attend_back(queries, keys, values, grad_heads, logsum, visible)
    dqkv = back_home(jnp.concatenate([dq.reshape(length, span), dk, dv], axis=1))
    dq = jnp.concatenate([piece[:, :span] for piece in dqkv], axis=1)
    dk = [piece[:, span : span + HEAD_SIZE].astype(F32) for piece in dqkv]
    dv = [piece[:, span + HEAD_SIZE :].astype(F32) for piece in dqkv]
    dk = jnp.stack(
        [sum(dk[i * repeat : (i + 1) * repeat]) for i in range(KEY_VALUE_HEADS)], axis=1
    )
    dv = jnp.concatenate(
        [sum(dv[i * repeat : (i + 1) * repeat]) for i in range(KEY_VALUE_HEADS)], axis=1
    )
    dq = rotate(dq.astype(F32).reshape(count, H, HEAD_SIZE), cosine, -sine)
    dk = rotate(dk, cosine, -sine)
    dpre = jnp.concatenate(
        [dq.reshape(count, heads_wide), dk.reshape(count, keys_wide), dv], axis=1
    ).astype(BF)
    dhalf = [dpre[:, t * wide // 2 : (t + 1) * wide // 2] for t in (0, 1)]
    dhat1 = [sum(right_dot(dhalf[t], first[t][s]) for t in (0, 1)) for s in (0, 1)]
    dgain1 = natural_columns(dp, *dhat1)
    inner = jnp.mean(inputs * dgain1, axis=-1, keepdims=True)
    grad_inputs = dh + inv1 * dgain1 - inputs * inv1 * inv1 * inv1 * inner

    mixed_part = jnp.concatenate([dot(hidden, down_full[t]) for t in (0, 1)], axis=1).astype(BF)
    mixed = hmid + sum_home(mixed_part)

    grad_down = []
    for t in (0, 1):
        part = left_dot(hidden, halves[t]).astype(BF)
        blocks = [
            lax.dynamic_slice_in_dim(part, (dp.me ^ m) * rows_down, rows_down, 0)
            for m in range(dp.size)
        ]
        even, odd = orders(dp.size)
        other = dp.swap(jnp.stack([blocks[m] for m in odd]), 1)
        summed = {
            m: (blocks[m].astype(F32) + other[i].astype(F32)).astype(BF)
            for i, m in enumerate(even)
        }
        grad_down.append(scatter_chips(dp, summed, t))
    grad_down = jnp.concatenate(grad_down, axis=1)

    def ff_grad(grad, turn):
        odd = left_dot(hat2_odd, grad).astype(BF)
        return scatter_rows(dp, lambda: left_dot(hat2_even, grad), odd, turn)

    rows = w_gate.shape[0]
    sent = jnp.stack([ff_grad(dgate, 0).astype(BF), ff_grad(dupper, 1).astype(BF)])
    sent = sent.reshape(2, groups, rows, ff // groups).transpose(1, 0, 2, 3)
    got = jnp.stack(seq.natural(seq.exchange(sent)))
    got = got.reshape(groups, 2, rows, dp.size, ff // groups // dp.size)
    got = got.transpose(1, 2, 3, 0, 4).reshape(2, rows, ff).astype(F32)
    grad_gate, grad_up = got[0] * gain2, got[1] * gain2
    grad_gain2 = jnp.sum(got[0] * w_gate.astype(F32) + got[1] * w_up.astype(F32), axis=1)

    def proj_grad(even, odd, grads):
        parts = []
        for t in (0, 1):
            send = left_dot(odd, grads[t]).astype(BF)
            parts.append(
                scatter_rows(dp, lambda grad=grads[t]: left_dot(even, grad), send, t)
            )
        own = jnp.concatenate(parts, axis=1)
        own = own.astype(BF).reshape(groups, rows, own.shape[1])
        return sum(piece.astype(F32) for piece in seq.exchange(own))

    grad_out = proj_grad(
        attn_even,
        attn_odd,
        [dbranch[:, t * width // 2 : (t + 1) * width // 2] for t in (0, 1)],
    )
    grad_first = proj_grad(hat1_even, hat1_odd, dhalf)
    grad_gain1 = jnp.sum(grad_first * w_first.astype(F32), axis=1)
    grad_first = grad_first * gain1
    return (
        mixed.astype(BF),
        grad_inputs.astype(BF),
        grad_gain1,
        grad_first[:, :heads_wide],
        grad_first[:, heads_wide : heads_wide + keys_wide],
        grad_first[:, heads_wide + keys_wide :],
        grad_out,
        grad_gain2,
        grad_gate,
        grad_up,
        grad_down,
    )


MESH = pl.DeviceIdType.MESH
ANY = pl.BlockSpec(memory_space=pl.ANY)
VMEM = pl.BlockSpec(memory_space=pltpu.VMEM)


class Net:
    def __init__(self, send_sems, recv_sems):
        self.send_sems, self.recv_sems, self.used = send_sems, recv_sems, 0
        self.open = []
        dp, z = lax.axis_index("dp"), lax.axis_index("seq")
        self.dp, self.z = dp, z
        self.dps = {
            0: dp,
            1: dp + 1 - 2 * lax.rem(dp, 2),
            2: dp + 2 - 4 * lax.rem(lax.div(dp, 2), 2),
            4: lax.rem(dp + 4, 8),
        }
        self.dps[6] = lax.rem(self.dps[2] + 4, 8)
        for mask in (2, 4, 6):
            self.dps[mask + 1] = self.dps[mask] + 1 - 2 * lax.rem(dp, 2)
        self.zs = {0: z, 1: z + 1 - 2 * lax.rem(z, 2), 2: lax.rem(z + 2, 4), 3: 3 - z}

    def target(self, name):
        kind, mask = name
        return (self.dps[mask], self.z) if kind == "d" else (self.dp, self.zs[mask])

    def barrier(self, names):
        sem = pltpu.get_barrier_semaphore()
        for name in names:
            pl.semaphore_signal(sem, inc=1, device_id=self.target(name), device_id_type=MESH)
        pl.semaphore_wait(sem, len(names))

    def send(self, src, dst, name):
        copy = pltpu.make_async_remote_copy(
            src_ref=src,
            dst_ref=dst,
            send_sem=self.send_sems.at[self.used],
            recv_sem=self.recv_sems.at[self.used],
            device_id=self.target(name),
            device_id_type=MESH,
        )
        self.used += 1
        copy.start()
        self.open.append(copy)
        return copy

    def local(self, src, dst):
        copy = pltpu.make_async_copy(src, dst, self.send_sems.at[self.used])
        self.used += 1
        copy.start()
        return copy

    def sent(self, copies):
        for copy in copies:
            copy.wait_send()
        done = [id(copy) for copy in copies]
        self.open = [copy for copy in self.open if id(copy) not in done]

    def finish(self):
        for copy in self.open:
            copy.wait_send()


X, Y, CORE = ("d", 2), ("d", 4), ("d", 1)
PARTNERS = [X, Y, CORE, ("z", 1), ("z", 2), ("z", 3)]


class Plane:
    def __init__(self, net, at, both):
        self.net, self.at, self.both = net, at, both

    def push(self, mask, half, name):
        ref = self.at(mask, half)
        return self.net.send(ref, ref, name)

    def start(self):
        self.xa = self.push(0, 0, X)
        self.yb = self.push(0, 1, Y)
        self.ya = self.push(0, 0, Y)
        self.xb = self.push(0, 1, X)
        self.cores = [self.core(0)]

    def core(self, mask):
        return [self.net.send(ref, ref, CORE) for ref in self.both(mask)]

    def forward(self):
        self.xa.wait_recv()
        self.ya2 = self.push(2, 0, Y)
        self.yb.wait_recv()
        self.xb2 = self.push(4, 1, X)

    def spread(self):
        self.ya.wait_recv()
        self.cores.append(self.core(4))
        self.xb.wait_recv()
        self.cores.append(self.core(2))
        self.ya2.wait_recv()
        self.xb2.wait_recv()
        self.cores.append(self.core(6))

    def finish(self):
        for copies in self.cores:
            for copy in copies:
                copy.wait_recv()

    def sent(self):
        copies = [self.xa, self.yb, self.ya, self.xb, self.ya2, self.xb2]
        self.net.sent(copies + [copy for group in self.cores for copy in group])


def rotary(value, cosine, sine):
    lane = lax.broadcasted_iota(jnp.int32, value.shape, 1)
    partner = jnp.where(
        lax.rem(lane, 64) < 32, pltpu.roll(value, 96, 1), pltpu.roll(value, 32, 1)
    )
    return value * cosine + partner * sine


def column(row):
    n = row.shape[1]
    shape = (n, n)
    same = lax.broadcasted_iota(jnp.int32, shape, 0) == lax.broadcasted_iota(jnp.int32, shape, 1)
    return jnp.sum(jnp.where(same, row.astype(F32), 0.0), axis=1, keepdims=True)


def line(value):
    n = value.shape[0]
    shape = (n, n)
    same = lax.broadcasted_iota(jnp.int32, shape, 0) == lax.broadcasted_iota(jnp.int32, shape, 1)
    return jnp.sum(jnp.where(same, value, 0.0), axis=0, keepdims=True)


def rms(value):
    return lax.rsqrt(jnp.mean(value * value, axis=-1, keepdims=True) + EPS)


def twice(pair):
    lane = lax.broadcasted_iota(jnp.int32, pair.shape, 1)
    other = pltpu.roll(pair.astype(F32), 64, 1).astype(BF)
    return jnp.where(lane < 64, pair, other), jnp.where(lane < 64, other, pair)


def aligned(start, count, unit):
    return pl.ds(pl.multiple_of(start, unit), count)


class Sums:
    def __init__(self, net, part, r1, mid, r2, sets=1):
        self.net, self.part, self.r1, self.mid, self.r2 = net, part, r1, mid, r2
        self.width = r2.shape[-1] // sets
        self.near, self.own, self.far = {}, {}, {}

    def cols(self, side, k):
        return pl.ds((2 * k + side) * self.width, self.width)

    def place(self, k):
        return pl.ds(k * self.width, self.width)

    def block(self, mask):
        return lax.div(self.net.dps[mask], 2)

    def first(self, k=0):
        for sent, place, pushes in (
            (self.near, 1, ((6, 0, X), (6, 1, Y))),
            (self.own, 0, ((2, 0, X), (4, 1, Y))),
        ):
            sent[k] = [
                self.net.send(
                    self.part.at[self.block(mask), :, self.cols(side, k)],
                    self.r1.at[side, place, :, self.place(k)],
                    name,
                )
                for mask, side, name in pushes
            ]

    def second(self, k=0):
        self.far[k] = []
        for side, (mask, name) in enumerate(((4, Y), (2, X))):
            self.near[k][side].wait_recv()
            c = self.place(k)
            mine = self.part[self.block(mask), :, self.cols(side, k)]
            self.mid[side, :, c] = (
                mine.astype(F32) + self.r1[side, 1, :, c].astype(F32)
            ).astype(BF)
            self.far[k].append(
                self.net.send(self.mid.at[side, :, c], self.r2.at[side, :, c], name)
            )

    def sent(self):
        for sent in (self.near, self.own, self.far):
            for copies in sent.values():
                self.net.sent(copies)

    def total(self, side, k=0):
        self.own[k][side].wait_recv()
        self.far[k][side].wait_recv()
        c = self.place(k)
        mine = self.part[self.block(0), :, self.cols(side, k)]
        return mine.astype(F32) + self.r1[side, 0, :, c].astype(F32) + self.r2[side, :, c].astype(F32)


def first_kernel(
    x_ref, wq, wk, wv, gain1, w_gate, w_up, gain2, cos_q, sin_q, cos_k, sin_k, wo, wd, cot,
    wq_out, wo_out, hat_out, qkv_out, att_out, mx_out, mx_far, hg_out, lse_out, hmid_out, dn_out, gdown,
    lse, hmid, wq_s, wf, wq_v, wo_v, hat, qkv_send, qkv, heads, att, part, r1, mid, r2,
    wg_v, wd_v, n_v, n_sib, c_v, c_sib, hid, dg, du,
    mx_r, hd, hd_r1, hd_r2, sib_r, send_sems, recv_sems,
):
    net = Net(send_sems, recv_sems)
    dp, z, dps, zs = net.dp, net.z, net.dps, net.zs
    tok, width = x_ref.shape
    group = qkv.shape[1]
    span = heads.shape[1]
    ff = wf.shape[-1]
    core, chip = lax.rem(dp, 2), lax.div(dp, 2)
    here = aligned(z * tok, tok, 16)

    staged = [
        net.local(weight.at[:, pl.ds(j * ff, ff)], ref.at[0, pl.ds(j * 64, 64), :])
        for weight, ref in ((w_gate, dg), (w_up, du))
        for j in range(4)
    ]
    own = [
        net.local(wo, wo_v.at[core, z]),
        net.local(wd, wd_v.at[aligned(dp * 176, 176, 16), :]),
        net.local(cot, c_v.at[here, :]),
    ]
    net.barrier(PARTNERS + [("d", 6)])

    scale = column(gain1[...])
    lane = lax.broadcasted_iota(jnp.int32, (wq.shape[0], 128), 1)
    for g in range(4):
        wq_s[g, :, :span] = (wq[:, g * span : (g + 1) * span].astype(F32) * scale).astype(BF)
        start = g // 2 * 128
        k = wk[:, start : start + 128].astype(F32)
        v = wv[:, start : start + 128].astype(F32)
        if g % 2 == 0:
            both = jnp.where(lane < 64, k, pltpu.roll(v, 64, 1))
        else:
            both = jnp.where(lane < 64, pltpu.roll(k, 64, 1), v)
        wq_s[g, :, span:] = (both * scale).astype(BF)

    def chip_of(mask):
        return lax.div(dps[mask], 2)

    w_1 = [
        net.send(wq_s.at[chip_of(m)], wq_v.at[chip, core, z], ("d", m)) for m in (6, 2, 4)
    ]
    own_q = net.local(wq_s.at[chip], wq_v.at[chip, core, z])
    x = x_ref[...].astype(F32)
    hat[chip] = (x * rms(x)).astype(BF)

    def half_of(ref, side):
        w = ref.shape[-1] // 2
        return pl.ds(side * w, w)

    def block(ref, size, cores):
        def at(mask, side):
            return ref.at[aligned(dps[mask] * size, size, 16), half_of(ref, side)]

        return at, lambda mask: [ref.at[aligned(dps[mask] * size, size, 16), :]] if cores else []

    plane_h = Plane(net, lambda m, s: hat.at[chip_of(m), :, half_of(hat, s)], lambda m: [])
    plane_h.start()
    down = Plane(net, *block(wd_v, 176, True))
    own[1].wait()
    down.start()

    def wq_at(mask):
        return wq_v.at[:, core, zs[mask]]

    def wo_at(mask):
        return wo_v.at[core, zs[mask]]

    class Line:
        def __init__(self, at):
            self.at = at
            self.far = self.push(0, ("z", 2))
            self.near = self.push(0, ("z", 1))
            self.cores = [self.push(0, CORE)]

        def push(self, mask, name):
            return net.send(self.at(mask), self.at(mask), name)

        def forward(self):
            self.far.wait_recv()
            self.last = self.push(2, ("z", 1))
            self.cores.append(self.push(2, CORE))

        def spread(self):
            self.near.wait_recv()
            self.cores.append(self.push(1, CORE))
            self.last.wait_recv()
            self.cores.append(self.push(3, CORE))

        def finish(self):
            for copy in self.cores:
                copy.wait_recv()

    scale = column(gain2[...])
    size = ff // 8
    for copy in staged:
        copy.wait()
    for t, ref in enumerate((dg, du)):
        for i in range(4):
            parts = []
            for b in range(i, 32, 4):
                j, start = b // 8, b % 8 * size
                parts.append(ref[0, j * 64 : (j + 1) * 64, start : start + size])
            joined = jnp.concatenate([p.astype(F32) for p in parts], axis=1)
            wf[(i * 2 + t) * 64 : (i * 2 + t + 1) * 64, :] = (joined * scale).astype(BF)
    f_rows = aligned((dp * 4 + z) * 64, 64, 16)

    def wf_at(i, t):
        return wf.at[aligned((i * 2 + t) * 64, 64, 16), :]

    own_f = [net.local(wf_at(z, t), wg_v.at[t, f_rows, :]) for t in (0, 1)]

    def f_send(t):
        return [
            net.send(wf_at(zs[m], t), wg_v.at[t, f_rows, :], ("z", m)) for m in (2, 3, 1)
        ]

    def f_plane(t):
        def rows(mask, start, count):
            return wg_v.at[t, aligned(dps[mask] * 256 + start, count, 16), :]

        return Plane(
            net, lambda m, s: rows(m, s * 128, 128), lambda m: [rows(m, 0, 256)]
        )

    own[0].wait()
    line_o = Line(wo_at)
    own_q.wait()
    for copy in w_1:
        copy.wait_recv()

    line_q = Line(wq_at)
    plane_h.forward()
    line_q.forward()
    gate_copies = f_send(0)
    plane_h.spread()
    line_q.spread()
    down.forward()
    line_q.finish()

    weight = wq_v[...].reshape(width, group)

    left = hat[...].reshape(4 * tok, width)
    for start in range(0, group, 256):
        stop = min(start + 256, group)
        pre = dot(left, weight[:, start:stop])
        for j in range(start, stop, 128):
            c_ref, s_ref = (cos_k, sin_k) if j == group - 128 else (cos_q, sin_q)
            for s in range(4):
                value = pre[s * tok : (s + 1) * tok, j - start : j - start + 128]
                value = rotary(value, c_ref[...], s_ref[...])
                qkv_send[s, :, j : j + 128] = value.astype(BF)
    q_copies = [net.send(qkv_send.at[zs[m]], qkv.at[here, :], ("z", m)) for m in (2, 3, 1)]
    own_q = net.local(qkv_send.at[z], qkv.at[here, :])
    line_o.forward()
    up_copies = f_send(1)
    down.spread()
    own_q.wait()
    for copy in q_copies:
        copy.wait_recv()

    kk, vv = twice(qkv[:, span:])

    def pair(p, carry):
        cols = aligned(p * 128, 128, 128)
        for qb in range(4):
            keys = (qb + 1) * tok
            q = qkv[qb * tok : (qb + 1) * tok, cols]
            lane = lax.broadcasted_iota(jnp.int32, (tok, 128), 1)
            row = lax.rem(lax.broadcasted_iota(jnp.int32, (2 * tok, keys), 0), tok) + qb * tok
            col = lax.broadcasted_iota(jnp.int32, (2 * tok, keys), 1)
            none = jnp.zeros_like(q)
            both = jnp.concatenate(
                [jnp.where(lane < 64, q, none), jnp.where(lane >= 64, q, none)], axis=0
            )
            s = right_dot(both, kk[:keys]) * HEAD_SIZE ** (-0.5)
            s = jnp.where(col <= row, s, -1e30)
            top = jnp.max(s, axis=-1, keepdims=True)
            e = jnp.exp(s - top)
            total = jnp.sum(e, axis=-1, keepdims=True)
            out = dot((e * (1.0 / total)).astype(BF), vv[:keys])
            log = top + jnp.log(total)
            old = lse[qb * tok : (qb + 1) * tok, :]
            old = jnp.where(lane == 2 * p, log[:tok], old)
            lse[qb * tok : (qb + 1) * tok, :] = jnp.where(lane == 2 * p + 1, log[tok:], old)
            heads[qb * tok : (qb + 1) * tok, cols] = jnp.where(
                lane < 64, out[:tok], out[tok:]
            ).astype(BF)
        return carry

    lse[...] = jnp.zeros_like(lse)
    h_copies = []
    for part_of in (0, 1):
        lax.fori_loop(part_of * 2, part_of * 2 + 2, pair, 0)
        cols = pl.ds(part_of * 256, 256)
        h_copies += [
            net.send(
                heads.at[aligned(zs[m] * tok, tok, 16), cols], att.at[z, :, cols], ("z", m)
            )
            for m in (2, 3, 1)
        ]
    own_h = net.local(heads.at[here, :], att.at[z])

    for copy in own_f:
        copy.wait()
    for copy in gate_copies:
        copy.wait_recv()
    plane_g, plane_u = f_plane(0), f_plane(1)
    plane_g.start()
    line_o.spread()
    line_o.finish()
    own_h.wait()
    for copy in h_copies:
        copy.wait_recv()


    c_near = net.send(cot, c_v.at[here, :], ("z", 1))
    c_far = net.send(cot, c_v.at[here, :], ("z", 2))
    sums = Sums(net, part, r1, mid, r2, 2)
    left = att[...].reshape(4 * tok, span)
    for c in range(4):
        cols = pl.ds(c * (width // 4), width // 4)
        weight = wo_v[:, :, :, cols].reshape(span, width // 4)
        part[:, :, cols] = dot(left, weight).astype(BF).reshape(4, tok, width // 4)
    def slot(mask):
        return aligned(zs[mask] * tok, tok, 16)

    def tokens(ref, mask, name):
        return net.send(ref.at[slot(mask), :], ref.at[slot(mask), :], name)

    def n_push(k, mask, name):
        place = n_v.at[slot(mask), pl.ds(k * (width // 2), width // 2)]
        return net.send(place, place, name)

    def middle(k):
        for side in (0, 1):
            cols = sums.cols(side, k)
            value = x_ref[:, cols].astype(F32) + sums.total(side, k)
            hmid[:, cols] = value
            n_v[here, cols] = value.astype(BF)
        n_far.append(n_push(k, 0, ("z", 2)))
        n_near.append(n_push(k, 0, ("z", 1)))

    n_far, n_near = [], []
    sums.first(0)
    sums.second(0)
    sums.first(1)
    middle(0)
    sums.second(1)
    plane_g.forward()
    for copy in up_copies:
        copy.wait_recv()
    plane_u.start()
    middle(1)
    outs = [
        net.local(wq_v, wq_out), net.local(wo_v, wo_out), net.local(qkv, qkv_out),
        net.local(att, att_out), net.local(hat, hat_out),
        net.local(lse, lse_out), net.local(hmid, hmid_out),
    ]
    c_far.wait_recv()
    c_last = tokens(c_v, 2, ("z", 1))
    plane_g.spread()
    plane_u.forward()
    n_last = []
    for k in (0, 1):
        n_far[k].wait_recv()
        n_last.append(n_push(k, 2, ("z", 1)))
    plane_u.spread()

    half = width // 2
    near_pair = lax.div(z, 2)
    far = aligned((1 - near_pair) * 2 * tok, 2 * tok, 16)
    near = aligned(near_pair * 2 * tok, 2 * tok, 16)
    dn_part = part

    def chunks(fn, total, size):
        whole = total // size

        def step(i, carry):
            fn(i * size, size)
            return carry

        lax.fori_loop(0, whole, step, 0)
        if total % size:
            fn(whole * size, total - whole * size)

    def front(rows):
        inv = rms(n_v[rows, :].astype(F32))

        def chunk(start, size):
            cols = aligned(start, size, 128)
            n = n_v[rows, :]
            gate = dot(n, wg_v[0, :, cols]) * inv
            upper = dot(n, wg_v[1, :, cols]) * inv
            dhid = right_dot(c_v[rows, :], wd_v[cols, :])
            sigma = jax.nn.sigmoid(gate)
            silu = gate * sigma
            hid[0, rows, cols] = (silu * upper).astype(BF)
            dhid *= inv
            dg[0, rows, cols] = (dhid * upper * sigma * (1.0 + gate * (1.0 - sigma))).astype(BF)
            du[0, rows, cols] = (dhid * silu).astype(BF)

        chunks(chunk, ff, 256)
        return [
            net.send(ref.at[0, rows, :], ref.at[1, rows, :], CORE) for ref in (hid, dg, du)
        ]

    def back(rows, first_slot, side):
        def chunk(start, size):
            cols = aligned(start + side * half, size, 128)
            total = right_dot(dg[0, rows, :], wg_v[0, cols, :])
            total += right_dot(du[0, rows, :], wg_v[1, cols, :])
            dn_part[pl.ds(first_slot, 2), :, cols] = total.astype(BF).reshape(2, tok, size)

        chunks(chunk, half, 256)

    def piece(side):
        return pl.ds(side * half, half)

    sums.sent()
    for copy in n_near:
        copy.wait_recv()
    c_near.wait_recv()
    for plane in (down, plane_g, plane_u):
        plane.finish()
    own[2].wait()
    sib = front(near)
    dn_b = []
    for side in (0, 1):
        back(near, near_pair * 2, side)
        dn_b.append(
            net.send(
                dn_part.at[zs[1], :, piece(side)], r1.at[side, 0], ("z", 1)
            )
        )
    c_last.wait_recv()
    c_copy = net.send(c_v.at[:, aligned((1 - core) * half, half, 128)], c_sib, CORE)
    for copy in n_last:
        copy.wait_recv()
    n_copies = [
        net.send(
            n_v.at[:, aligned((i * 2 + 1 - core) * 256, 256, 128)],
            n_sib.at[:, pl.ds(i * 256, 256)],
            CORE,
        )
        for i in range(4)
    ]
    sib += front(far)
    dn_a = []
    for side in (0, 1):
        back(far, (1 - near_pair) * 2, side)
        dn_a.append(
            net.send(
                dn_part.at[zs[3], :, piece(side)], r1.at[side, 1], ("z", 1)
            )
        )
    c_copy.wait_recv()
    for copy in sib:
        copy.wait_recv()

    ccols = aligned(core * half, half, 128)

    def down_chunk(start, size):
        cols = aligned(start, size, 128)
        total = left_dot(hid[0, :, cols], c_v[:, ccols])
        total += left_dot(hid[1, :, cols], c_sib[...])
        hd[cols, :] = total.astype(BF)

    chunks(down_chunk, ff, 256)
    chip_rows = ff // 4
    quarter = half // 2

    def hd_at(mask, side):
        return aligned(chip_of(mask) * chip_rows, chip_rows, 16), pl.ds(side * quarter, quarter)

    def hd_send(mask, side, place, name):
        r, c = hd_at(mask, side)
        return net.send(hd.at[r, c], hd_r1.at[side, place], name)

    hd_1 = [hd_send(6, 0, 1, X), hd_send(6, 1, 1, Y), hd_send(2, 0, 0, X), hd_send(4, 1, 0, Y)]
    dn_c = []
    for side in (0, 1):
        dn_a[side].wait_recv()
        cols = piece(side)
        mid[side] = (
            dn_part[zs[2], :, cols].astype(F32) + r1[side, 1].astype(F32)
        ).astype(BF)
        dn_c.append(net.send(mid.at[side], r2.at[side], ("z", 2)))

    for copy in outs:
        copy.wait()
    plane_h.sent()

    def mix_chunk(start, size):
        cols = aligned(start, size, 128)
        hat[:, :, cols] = dot(hid[0], wd_v[:, cols]).astype(BF).reshape(4, tok, size)

    chunks(mix_chunk, width, 256)
    mx_copy = net.local(hat, mx_out)
    mx_a = net.send(hat.at[zs[3]], mx_r, ("z", 1))

    hd_1[0].wait_recv()
    hd_1[1].wait_recv()
    net.sent(gate_copies + up_copies)
    hd_2 = []
    for side, (mask, name) in enumerate(((4, Y), (2, X))):
        r, c = hd_at(mask, side)
        k = pl.ds(side * quarter, quarter)
        wf[:chip_rows, k] = (hd[r, c].astype(F32) + hd_r1[side, 1].astype(F32)).astype(BF)
        hd_2.append(net.send(wf.at[pl.ds(0, chip_rows), k], hd_r2.at[side], name))

    for copy in n_copies:
        copy.wait_recv()
    plane_g.sent()
    plane_u.sent()

    def block(b, carry):
        cols = aligned((b * 2 + core) * 256, 256, 128)
        left = n_v[:, cols].T
        other = n_sib[:, aligned(b * 256, 256, 128)].T
        for t, grad in enumerate((dg, du)):
            total = dot(left, grad[0]) + dot(other, grad[1])
            wg_v[t, aligned(b * 256, 256, 16), :] = total.astype(BF)
        return carry

    lax.fori_loop(0, 4, block, 0)
    hg_copy = net.local(wg_v.at[:, pl.ds(0, 1024), :], hg_out)
    for side in (0, 1):
        dn_b[side].wait_recv()
        dn_c[side].wait_recv()
        cols = piece(side)
        dn_out[:, cols] = (
            dn_part[z, :, cols].astype(F32)
            + r1[side, 0].astype(F32)
            + r2[side].astype(F32)
        )
    mx_a.wait_recv()
    net.sent(dn_c)
    far_copies = []
    for side in (0, 1):
        cols = piece(side)
        mid[side] = (hat[zs[2], :, cols].astype(F32) + mx_r[:, cols].astype(F32)).astype(BF)
        far_copies.append(net.local(mid.at[side], mx_far.at[:, cols]))
    hd_1[2].wait_recv()
    hd_1[3].wait_recv()
    rows_half = chip_rows // 2
    for side in (0, 1):
        hd_2[side].wait_recv()

        def total(start):
            _, c = hd_at(0, side)
            return (
                hd[aligned(chip * chip_rows + start, rows_half, 16), c].astype(F32)
                + hd_r1[side, 0, aligned(start, rows_half, 16), :].astype(F32)
                + hd_r2[side, aligned(start, rows_half, 16), :].astype(F32)
            )

        net.sent([hd_2[side]])
        k = pl.ds(side * quarter, quarter)
        wf[:rows_half, k] = total((1 - core) * rows_half).astype(BF)
        gdown[:, aligned(core * half + side * quarter, quarter, 128)] = total(core * rows_half)
    last = net.send(wf.at[pl.ds(0, rows_half), pl.ds(0, half)], sib_r, CORE)
    last.wait_recv()
    gdown[:, aligned((1 - core) * half, half, 128)] = sib_r[...].astype(F32)
    hg_copy.wait()
    mx_copy.wait()
    for copy in far_copies:
        copy.wait()
    net.finish()


def first_call(x, wq, wk, wv, gain1, w_gate, w_up, gain2, tables4, wo, wd, cot):
    tok, width = x.shape
    ff = w_gate.shape[1] // 4
    span = width // 4
    group = span + 128
    sds = jax.ShapeDtypeStruct
    v = pltpu.VMEM
    half = width // 2
    return pl.pallas_call(
        first_kernel,
        name="first",
        out_shape=[
            sds((4, 2, 4, 64, group), BF), sds((2, 4, 64, width), BF), sds((4, tok, width), BF),
            sds((4 * tok, group), BF), sds((4, tok, span), BF), sds((4, tok, width), BF),
            sds((tok, width), BF), sds((2, 1024, ff), BF), sds((4 * tok, 128), F32), sds((tok, width), F32),
            sds((tok, width), F32), sds((ff // 8, width), F32),
        ],
        in_specs=[VMEM] * 5 + [ANY] * 2 + [VMEM] * 5 + [ANY] * 3,
        out_specs=[ANY] * 10 + [VMEM] * 2,
        scratch_shapes=[
            v((4 * tok, 128), F32), v((tok, width), F32),
            v((4, 64, group), BF), v((512, ff), BF), v((4, 2, 4, 64, group), BF),
            v((2, 4, 64, width), BF), v((4, tok, width), BF), v((4, tok, group), BF),
            v((4 * tok, group), BF), v((4 * tok, span), BF), v((4, tok, span), BF),
            v((4, tok, width), BF), v((2, 2, tok, half), BF), v((2, tok, half), BF),
            v((2, tok, half), BF),
            v((2, width, ff), BF), v((ff, width), BF), v((4 * tok, width), BF),
            v((4 * tok, half), BF), v((4 * tok, width), BF), v((4 * tok, half), BF),
            v((2, 4 * tok, ff), BF), v((2, 4 * tok, ff), BF), v((2, 4 * tok, ff), BF),
            v((tok, width), BF), v((ff, half), BF),
            v((2, 2, ff // 4, half // 2), BF), v((2, ff // 4, half // 2), BF),
            v((ff // 8, half), BF),
            pltpu.SemaphoreType.DMA((144,)),
            pltpu.SemaphoreType.DMA((144,)),
        ],
        compiler_params=pltpu.CompilerParams(
            collective_id=1, has_side_effects=True, vmem_limit_bytes=62 * 2**20
        ),
    )(x, wq, wk, wv, gain1, w_gate, w_up, gain2, *tables4, wo, wd, cot)


def third_kernel(
    hmid, cot, dn2, cos_q, sin_q, cos_k, sin_k,
    x_in, qkv_in, lse_in, mx, mx_far, wq, wo, hat, att, hg,
    tok_out, mixed, g2_out, g1_out, fb,
    x_ref, qkv, lse, wq_v, wo_v, hat_v, hat_s, att_v, att_s, mx_v, mx_r1, mx_r2,
    hg_v, f_r1, f_k, f_r2, fs, dh, dbr, dbr_s, dsend, gh, dqkv, dk_acc, dv_acc, dback,
    dpre, dpre_s, part, r1, mid, r2, g2_p, g2_r1, g2_s, g2_r2, g1_p, g1_r1, g1_s, g1_r2, g1_f,
    send_sems, recv_sems,
):
    net = Net(send_sems, recv_sems)
    dp, z, dps, zs = net.dp, net.z, net.dps, net.zs
    tok, width = x_ref.shape
    group = qkv.shape[1]
    span = group - 128
    here = aligned(z * tok, tok, 16)
    core, chip = lax.rem(dp, 2), lax.div(dp, 2)

    def chip_of(mask):
        return lax.div(dps[mask], 2)

    def slot(mask):
        return aligned(zs[mask] * tok, tok, 16)

    def hg_at(t, mask, side):
        return hg.at[t, aligned(chip_of(mask) * 256 + side * 128, 128, 16), :]

    loads = [
        net.local(wo, wo_v),
        net.local(hg.at[:, aligned(chip * 256, 256, 16), :], hg_v.at[0]),
        net.local(hg.at[:, aligned(chip_of(4) * 256, 128, 16), :], hg_v.at[1, :, pl.ds(0, 128)]),
        net.local(
            hg.at[:, aligned(chip_of(2) * 256 + 128, 128, 16), :], hg_v.at[1, :, pl.ds(128, 128)]
        ),
        net.local(mx.at[z], mx_v),
        net.local(att, att_v),
        net.local(wq, wq_v),
        net.local(hat, hat_v),
        net.local(x_in, x_ref),
        net.local(qkv_in, qkv),
        net.local(lse_in, lse),
    ]
    net.barrier(PARTNERS + [("d", 6)])
    def f_send(t, place, mask, side, name):
        return net.send(hg_at(t, mask, side), f_r1.at[place, t, pl.ds(side * 128, 128)], name)

    def f_near(t):
        return [f_send(t, 1, 6, 0, X), f_send(t, 1, 6, 1, Y)]

    def f_own(t):
        return [f_send(t, 0, 2, 0, X), f_send(t, 0, 4, 1, Y)]

    def f_second(t, sent):
        for copy in sent:
            copy.wait_recv()
        f_k[t] = (hg_v[1, t].astype(F32) + f_r1[1, t].astype(F32)).astype(BF)
        return [
            net.send(f_k.at[t, pl.ds(side * 128, 128)], f_r2.at[t, pl.ds(side * 128, 128)], name)
            for side, name in ((0, Y), (1, X))
        ]

    own_f = []

    def f_rows(t, sent):
        for copy in sent:
            copy.wait_recv()
        total = hg_v[0, t].astype(F32) + f_r1[0, t].astype(F32) + f_r2[t].astype(F32)
        for i in range(4):
            fs[i, t] = total[i * 64 : (i + 1) * 64, :].astype(BF)
        own_f.append(net.local(fs.at[z, t], fb.at[z, t]))
        return [net.send(fs.at[zs[m], t], fb.at[z, t], ("z", m)) for m in (2, 3, 1)]

    gate_1 = f_near(0)
    mx_copies = [
        net.send(mx_far, mx_r2, ("z", 2)),
        net.send(mx.at[zs[1]], mx_r1, ("z", 1)),
    ]
    half = width // 2

    def norm_back(value, grad):
        inv = rms(value)
        inner = jnp.mean(value * grad, axis=-1, keepdims=True)
        return inv * grad - value * (inv * inv * inv * inner)

    value, grad = hmid[...], dn2[...]
    inv = rms(value)
    inner = jnp.mean(value * grad, axis=-1, keepdims=True)
    dh[...] = cot[...].astype(F32) + grad - value * (inv * inv * inner)
    dbr[chip] = dh[...].astype(BF)
    plane_b = Plane(net, lambda m, s: dbr.at[chip_of(m), :, pl.ds(s * half, half)], lambda m: [])
    plane_b.start()
    small = [
        net.send(att.at[:, :, aligned((1 - core) * 256, 256, 128)], att_s, CORE)
    ] + [
        net.send(
            hat.at[:, :, aligned(i * 512 + (1 - core) * 256, 256, 128)],
            hat_s.at[:, :, pl.ds(i * 256, 256)],
            CORE,
        )
        for i in range(4)
    ]
    plane_b.forward()
    for copy in loads[1:4]:
        copy.wait()
    gate_2 = f_second(0, gate_1) + f_own(0)
    up_1 = f_near(1)
    up_2 = f_own(1)
    plane_b.spread()
    loads[0].wait()
    weight = wo_v[...].reshape(span, width)
    dsend[...] = (
        right_dot(dbr[...].reshape(4 * tok, width), weight).astype(BF).reshape(4, tok, span)
    )
    d_copies = [net.send(dsend.at[zs[m]], gh.at[here, :], ("z", m)) for m in (2, 3, 1)]
    gh[here, :] = dsend[z]
    dbr_copy = net.send(dbr, dbr_s, CORE)
    for copy in loads[4:]:
        copy.wait()

    class Line:
        def __init__(self, parts, r1, s, r2):
            self.parts, self.r1, self.s, self.r2 = parts, r1, s, r2
            self.sent = [
                net.send(parts.at[zs[3]], r1.at[1], ("z", 1)),
                net.send(parts.at[zs[1]], r1.at[0], ("z", 1)),
            ]

        def middle(self):
            self.sent[0].wait_recv()
            self.s[...] = (self.parts[zs[2]].astype(F32) + self.r1[1].astype(F32)).astype(BF)
            self.far = net.send(self.s, self.r2, ("z", 2))

        def total(self):
            self.sent[1].wait_recv()
            self.far.wait_recv()
            own = self.parts[z].astype(F32) + self.r1[0].astype(F32)
            return own + self.r2[...].astype(F32)

    small[0].wait_recv()
    dbr_copy.wait_recv()
    mine = att_v[:, :, aligned(core * 256, 256, 128)].reshape(4 * tok, 256).T
    theirs = att_s[...].reshape(4 * tok, 256).T

    def out_chunk(i, carry):
        cols = aligned(i * 512, 512, 128)
        total = dot(mine, dbr[:, :, cols].reshape(4 * tok, 512))
        total += dot(theirs, dbr_s[:, :, cols].reshape(4 * tok, 512))
        g2_p[:, :, cols] = total.astype(BF).reshape(4, 64, 512)
        return carry

    lax.fori_loop(0, width // 512, out_chunk, 0)
    line_o = Line(g2_p, g2_r1, g2_s, g2_r2)

    for copy in d_copies:
        copy.wait_recv()
    f_copies = f_rows(0, gate_2)

    scale = HEAD_SIZE ** (-0.5)
    kk, vv = twice(qkv[:, span:])
    dk_acc[...] = jnp.zeros_like(dk_acc)
    dv_acc[...] = jnp.zeros_like(dv_acc)

    def pair(p, carry):
        cols = aligned(p * 128, 128, 128)
        for qb in range(4):
            keys = (qb + 1) * tok
            rows = slice(qb * tok, (qb + 1) * tok)
            q = qkv[rows, cols]
            g = gh[rows, cols]
            lane = lax.broadcasted_iota(jnp.int32, (tok, 128), 1)
            row = lax.rem(lax.broadcasted_iota(jnp.int32, (2 * tok, keys), 0), tok) + qb * tok
            col = lax.broadcasted_iota(jnp.int32, (2 * tok, keys), 1)
            none = jnp.zeros_like(q)

            def both(value):
                return jnp.concatenate(
                    [jnp.where(lane < 64, value, none), jnp.where(lane >= 64, value, none)], axis=0
                )

            qq, gg = both(q), both(g)
            logs = lse[rows, :]
            log = jnp.concatenate(
                [
                    jnp.sum(jnp.where(lane == 2 * p + h, logs, 0.0), axis=-1, keepdims=True)
                    for h in range(2)
                ],
                axis=0,
            )
            s = right_dot(qq, kk[:keys]) * scale
            probs = jnp.exp(jnp.where(col <= row, s, -1e30) - log)
            pg = right_dot(gg, vv[:keys])
            delta = jnp.sum(probs * pg, axis=-1, keepdims=True)
            ds = (probs * (pg - delta)).astype(BF)
            out = dot(ds, kk[:keys]) * scale
            dk_acc[:keys, :] += left_dot(ds, qq)
            dv_acc[:keys, :] += left_dot(probs.astype(BF), gg)
            dqkv[rows, cols] = jnp.where(lane < 64, out[:tok], out[tok:]).astype(BF)
        return carry

    def send_back(start, count):
        cols = pl.ds(start, count)
        return [net.send(dqkv.at[slot(m), cols], dback.at[z, :, cols], ("z", m)) for m in (2, 3, 1)]

    lax.fori_loop(0, 2, pair, 0)
    b_copies = send_back(0, 256)
    lax.fori_loop(2, 4, pair, 0)
    dk = dk_acc[...]
    dv = dv_acc[...]
    lane = lax.broadcasted_iota(jnp.int32, dk.shape, 1)
    dqkv[:, span:] = jnp.where(
        lane < 64, (dk + pltpu.roll(dk, 64, 1)) * scale, dv + pltpu.roll(dv, 64, 1)
    ).astype(BF)
    b_copies += send_back(256, group - 256)
    dback[z] = dqkv[here, :]
    line_o.middle()

    up_2 += f_second(1, up_1)
    for copy in b_copies:
        copy.wait_recv()
    for s in range(4):
        for j in range(group // 128):
            cols = slice(j * 128, (j + 1) * 128)
            last = j == group // 128 - 1
            c_ref, s_ref = (cos_k, sin_k) if last else (cos_q, sin_q)
            value = dback[s, :, cols].astype(F32)
            dpre[s, :, cols] = rotary(value, c_ref[...], -s_ref[...]).astype(BF)
    dpre_copy = net.send(dpre, dpre_s, CORE)

    left = dpre[...].reshape(4 * tok, group)

    def dhat_chunk(i, carry):
        cols = aligned(i * 256, 256, 128)
        rows = wq_v[lax.div(i, 2), lax.rem(i, 2)].reshape(256, group)
        part[:, :, cols] = right_dot(left, rows).astype(BF).reshape(4, tok, 256)
        return carry

    lax.fori_loop(0, width // 256, dhat_chunk, 0)
    sums = Sums(net, part, r1, mid, r2)
    sums.first()

    for copy in small[1:]:
        copy.wait_recv()
    dpre_copy.wait_recv()
    right = dpre_s[...].reshape(4 * tok, group)

    def first_chunk(i, carry):
        own = hat_v[:, :, aligned(i * 512 + core * 256, 256, 128)].reshape(4 * tok, 256).T
        sib = hat_s[:, :, aligned(i * 256, 256, 128)].reshape(4 * tok, 256).T
        total = dot(own, left) + dot(sib, right)
        g1_p[:, i] = total.astype(BF).reshape(4, 64, group)
        return carry

    lax.fori_loop(0, 4, first_chunk, 0)
    line_q = Line(g1_p, g1_r1, g1_s, g1_r2)
    f_copies += f_rows(1, up_2)
    sums.second()
    line_q.middle()
    for copy in mx_copies:
        copy.wait_recv()
    total = mx_v[...].astype(F32) + mx_r1[...].astype(F32) + mx_r2[...].astype(F32)
    mixed[...] = (hmid[...] + total).astype(BF)
    g2_out[...] = line_o.total()
    for side in (0, 1):
        dn2[:, side * half : (side + 1) * half] = sums.total(side)
    tok_out[...] = (dh[...] + norm_back(x_ref[...].astype(F32), dn2[...])).astype(BF)
    g1_f[...] = line_q.total().astype(BF)
    g_copies = [net.send(g1_f.at[chip_of(m)], g1_out.at[chip], ("d", m)) for m in (6, 2, 4)]
    g1_out[chip] = g1_f[chip]
    for copy in g_copies + f_copies:
        copy.wait_recv()
    for copy in own_f:
        copy.wait()
    net.finish()


def third_call(x, hmid, cot, dn2, qkv, lse, tables4, mx, mx_far, wq, wo, hat, att, hg):
    tok, width = x.shape
    group = qkv.shape[1]
    span = group - 128
    ff = hg.shape[-1]
    sds = jax.ShapeDtypeStruct
    v = pltpu.VMEM
    return pl.pallas_call(
        third_kernel,
        name="third",
        out_shape=[
            sds((tok, width), BF), sds((tok, width), BF), sds((64, width), F32),
            sds((4, 64, group), BF), sds((4, 2, 64, ff), BF),
        ],
        in_specs=[VMEM] * 7 + [ANY] * 10,
        out_specs=[VMEM] * 4 + [ANY],
        scratch_shapes=[
            v((tok, width), BF), v((4 * tok, group), BF), v((4 * tok, 128), F32),
            v((4, 2, 4, 64, group), BF), v((2, 4, 64, width), BF), v((4, tok, width), BF),
            v((4, tok, width // 2), BF), v((4, tok, span), BF), v((4, tok, span // 2), BF),
            v((tok, width), BF), v((tok, width), BF), v((tok, width), BF),
            v((2, 2, 256, ff), BF), v((2, 2, 256, ff), BF), v((2, 256, ff), BF), v((2, 256, ff), BF),
            v((4, 2, 64, ff), BF), v((tok, width), F32), v((4, tok, width), BF),
            v((4, tok, width), BF), v((4, tok, span), BF), v((4 * tok, span), BF),
            v((4 * tok, group), BF), v((4 * tok, 128), F32), v((4 * tok, 128), F32),
            v((4, tok, group), BF), v((4, tok, group), BF), v((4, tok, group), BF),
            v((4, tok, width), BF), v((2, 2, tok, width // 2), BF), v((2, tok, width // 2), BF),
            v((2, tok, width // 2), BF),
            v((4, 64, width), BF), v((2, 64, width), BF), v((64, width), BF), v((64, width), BF),
            v((4, 4, 64, group), BF), v((2, 4, 64, group), BF), v((4, 64, group), BF),
            v((4, 64, group), BF), v((4, 64, group), BF),
            pltpu.SemaphoreType.DMA((80,)),
            pltpu.SemaphoreType.DMA((80,)),
        ],
        compiler_params=pltpu.CompilerParams(
            collective_id=3, has_side_effects=True, vmem_limit_bytes=60 * 2**20
        ),
    )(hmid, cot, dn2, *tables4, x, qkv, lse, mx, mx_far, wq, wo, hat, att, hg)


def last_kernel(
    fb, g1, wq, wk, wv, gain1, gain2, w_gate_in, w_up_in, tok_in, mixed_in, g2_in, gd_in,
    gq, gk, gv, g_gate, g_up, g_gain1, g_gain2, tok_out, mixed_out, g2_out, gd_out,
    w_gate, w_up, sems,
):
    copies = [
        pltpu.make_async_copy(src, dst, sems.at[i])
        for i, (src, dst) in enumerate(
            (
                (w_gate_in, w_gate), (w_up_in, w_up), (tok_in, tok_out),
                (mixed_in, mixed_out), (g2_in, g2_out), (gd_in, gd_out),
            )
        )
    ]
    for copy in copies:
        copy.start()
    span = g1.shape[2] - 128
    lane = lax.broadcasted_iota(jnp.int32, (g1.shape[1], 128), 1)
    scale = column(gain1[...])
    scale2 = column(gain2[...])

    def put(out, weight, cols, value):
        out[:, cols] = value * scale
        return jnp.sum(value * weight[:, cols].astype(F32), axis=1, keepdims=True)

    total = jnp.zeros((g1.shape[1], 1), F32)
    for g in range(4):
        total += put(gq, wq, slice(g * span, (g + 1) * span), g1[g, :, :span].astype(F32))
    for g in (0, 2):
        one = g1[g, :, span:].astype(F32)
        two = g1[g + 1, :, span:].astype(F32)
        cols = slice(g * 64, g * 64 + 128)
        total += put(gk, wk, cols, jnp.where(lane < 64, one, pltpu.roll(two, 64, 1)))
        total += put(gv, wv, cols, jnp.where(lane < 64, pltpu.roll(one, 64, 1), two))
    g_gain1[...] = line(total)
    size = fb.shape[-1] // 8
    total = jnp.zeros((g1.shape[1], 1), F32)
    for t, (out, weight) in enumerate(((g_gate, w_gate), (g_up, w_up))):
        copies[t].wait()
        for d in range(0, 8, 2):
            parts = [
                fb[i, t, :, e * size : (e + 1) * size].astype(F32) for e in (d, d + 1) for i in range(4)
            ]
            joined = jnp.concatenate(parts, axis=1)
            cols = pl.ds(d * 4 * size, 8 * size)
            total += jnp.sum(joined * weight[:, cols].astype(F32), axis=1, keepdims=True)
            out[:, cols] = joined * scale2
    g_gain2[...] = line(total)
    for copy in copies[2:]:
        copy.wait()


def last_call(fb, g1, wq, wk, wv, gain1, gain2, w_gate, w_up, tok, mixed, g2, gd):
    rows, ff = w_gate.shape
    sds = jax.ShapeDtypeStruct
    return pl.pallas_call(
        last_kernel,
        name="last",
        out_shape=[
            sds(wq.shape, F32), sds(wk.shape, F32), sds(wv.shape, F32),
            sds((rows, ff), F32), sds((rows, ff), F32), sds((1, rows), F32), sds((1, rows), F32),
            sds(tok.shape, BF), sds(mixed.shape, BF), sds(g2.shape, F32), sds(gd.shape, F32),
        ],
        in_specs=[VMEM] * 7 + [ANY] * 6,
        out_specs=[VMEM] * 11,
        scratch_shapes=[
            pltpu.VMEM((rows, ff), BF), pltpu.VMEM((rows, ff), BF), pltpu.SemaphoreType.DMA((6,)),
        ],
        compiler_params=pltpu.CompilerParams(vmem_limit_bytes=60 * 2**20),
    )(fb, g1, wq, wk, wv, gain1, gain2, w_gate, w_up, tok, mixed, g2, gd)


def shards(
    tokens, norm_first, w_query, w_key, w_value, w_out, norm_second, w_gate, w_up, w_down, cotangent
):
    count = tokens.shape[0]
    gain1, gain2 = norm_first[None, :], norm_second[None, :]
    cosine, sine = tables(lax.axis_index("seq") * count + jnp.arange(count))
    cosine, sine = cosine[:, 0], sine[:, 0]
    one, zero = jnp.ones_like(cosine), jnp.zeros_like(cosine)
    tables4 = [
        jnp.concatenate(parts, axis=1)
        for parts in (
            [cosine] * 4,
            [-sine, sine] * 2,
            [cosine, cosine, one, one],
            [-sine, sine, zero, zero],
        )
    ]
    wq, wo, hat, qkv, att, mixed_part, mixed_far, hg, lse, hmid, dhat2, grad_down = first_call(
        tokens, w_query, w_key, w_value, gain1, w_gate, w_up, gain2, tables4,
        w_out, w_down, cotangent,
    )
    grad_tokens, mixed, grad_out, grad_first, parts = third_call(
        tokens, hmid, cotangent, dhat2, qkv, lse, tables4, mixed_part, mixed_far,
        wq, wo, hat, att, hg,
    )
    (
        grad_query, grad_key, grad_value, grad_gate, grad_up, grad_gain1, grad_gain2,
        grad_tokens, mixed, grad_out, grad_down,
    ) = last_call(
        parts, grad_first, w_query, w_key, w_value, gain1, gain2, w_gate, w_up,
        grad_tokens, mixed, grad_out, grad_down,
    )
    return (
        mixed,
        grad_tokens,
        grad_gain1[0],
        grad_query,
        grad_key,
        grad_value,
        grad_out,
        grad_gain2[0],
        grad_gate,
        grad_up,
        grad_down,
    )


def solution(mesh):
    special = mesh.shape['dp'] == 8 and mesh.shape['seq'] == KEY_VALUE_HEADS
    rows = P(("dp", "seq"), None)
    line = P(("dp", "seq"))
    return jax.shard_map(
        shards if special else general_shards,
        mesh=mesh,
        in_specs=(rows, line, rows, rows, rows, rows, line, rows, rows, rows, rows),
        out_specs=(rows, rows, line, rows, rows, rows, rows, line, rows, rows, rows),
        check_vma=False,
    )
```
